32 devices in a mesh: dp: 8 (over z, y), mp: 4 (over x, core).
Axes of the slice: x: 2, y: 2, z: 4, core: 2. Of those that a mesh axis runs over, the one named last changes fastest.
Arguments:
- token_ids: int32 [2048], P('dp'), may hold values from 0 to 31999
- target_ids: int32 [2048], P('dp'), may hold values from 0 to 31999
- exit_mask: int32 [2, 2048], P(None, 'dp'), may hold values from 0 to 1, as said below
- table: float32 [32000, 2048], P(('dp', 'mp'))
- table_first: float32 [32000, 2048], P(('dp', 'mp'))
- table_second: float32 [32000, 2048], P(('dp', 'mp')), as said below
- qkv_weight: float32 [2048, 3, 2048], P('dp', None, 'mp'), may hold values from -0.125 to 0.125
- qkv_first: float32 [2048, 3, 2048], P('dp', None, 'mp')
- qkv_second: float32 [2048, 3, 2048], P('dp', None, 'mp'), as said below
- out_weight: float32 [2048, 2048], P('mp', 'dp'), may hold values from -0.25 to 0.25
- out_first: float32 [2048, 2048], P('mp', 'dp')
- out_second: float32 [2048, 2048], P('mp', 'dp'), as said below
- gate_up_weight: float32 [2048, 2, 5632], P('dp', None, 'mp'), may hold values from -0.125 to 0.125
- gate_up_first: float32 [2048, 2, 5632], P('dp', None, 'mp')
- gate_up_second: float32 [2048, 2, 5632], P('dp', None, 'mp'), as said below
- down_weight: float32 [5632, 2048], P('mp', 'dp'), may hold values from -0.078125 to 0.078125
- down_first: float32 [5632, 2048], P('mp', 'dp')
- down_second: float32 [5632, 2048], P('mp', 'dp'), as said below
- gains: float32 [3, 2048], P(None, 'dp')
- gains_first: float32 [3, 2048], P(None, 'dp')
- gains_second: float32 [3, 2048], P(None, 'dp'), as said below
Outputs:
- loss_sums: float32 [2], replicated
- exit_counts: float32 [2], replicated
- grad_norm: float32 [], replicated
- table_new: float32 [32000, 2048], P(('dp', 'mp'))
- table_first_new: float32 [32000, 2048], P(('dp', 'mp'))
- table_second_new: float32 [32000, 2048], P(('dp', 'mp'))
- qkv_new: float32 [2048, 3, 2048], P('dp', None, 'mp')
- qkv_first_new: float32 [2048, 3, 2048], P('dp', None, 'mp')
- qkv_second_new: float32 [2048, 3, 2048], P('dp', None, 'mp')
- out_new: float32 [2048, 2048], P('mp', 'dp')
- out_first_new: float32 [2048, 2048], P('mp', 'dp')
- out_second_new: float32 [2048, 2048], P('mp', 'dp')
- gate_up_new: float32 [2048, 2, 5632], P('dp', None, 'mp')
- gate_up_first_new: float32 [2048, 2, 5632], P('dp', None, 'mp')
- gate_up_second_new: float32 [2048, 2, 5632], P('dp', None, 'mp')
- down_new: float32 [5632, 2048], P('mp', 'dp')
- down_first_new: float32 [5632, 2048], P('mp', 'dp')
- down_second_new: float32 [5632, 2048], P('mp', 'dp')
- gains_new: float32 [3, 2048], P(None, 'dp')
- gains_first_new: float32 [3, 2048], P(None, 'dp')
- gains_second_new: float32 [3, 2048], P(None, 'dp')
The draws below stay inside these ranges and needn't reach their ends.
Inputs may be any that keep to these rules, and one draw needn't show every extreme that they name: `exit_mask`: in each exit, the 256 positions of one block of tokens hold at most 64 ones, and some block holds exactly 64. `table_second`: Positive. `qkv_second`: Positive. `out_second`: Positive. `gate_up_second`: Positive. `down_second`: Positive. `gains_second`: Positive.
All inputs are finite; a program needn't handle non-finite values.
Results may differ from the reference program's by a relative error of at most 0.023.
Values may be sent and summed in bfloat16 or wider, within the bound.
A program may use at most 256 MiB of HBM per device.

```python
import math
import jax
import jax.numpy as jnp
import numpy as np
from jax import lax

D = 2048
HEADS = 16
HEAD_DIM = 128
FF = 5632
VOCAB = 32000
TOK_DEV = 256
R_DEV = 64
STEP = 10
TOKENS = 2048


def grad_size():
    return 0.02 / math.sqrt(VOCAB * D + 4 * D * D + 3 * D * FF + 3 * D)


def first_moment(key, shape, boost):
    return jax.random.normal(key, shape, jnp.float32) * (0.11 * boost * grad_size())


def second_moment(key, shape, boost):
    level = jax.random.uniform(key, shape, jnp.float32, 0.0, math.log(4.0))
    return jnp.exp(level) * (0.0526 * (boost * grad_size()) ** 2)


def draw_exit_mask(key, part):
    key = jax.random.fold_in(key, 11)
    block_count = TOKENS // TOK_DEV
    count_key, full_key, order_key = jax.random.split(key, 3)
    block_ids = jnp.arange(block_count, dtype=jnp.int32)
    ramp = R_DEV // 3 + (R_DEV - R_DEV // 3) * block_ids // max(block_count - 1, 1)
    reach = max(1, R_DEV // 6)
    jitter = jax.random.randint(count_key, (2, block_count), -reach, reach + 1)
    filled = jnp.clip(ramp[None, :] + jitter, 1, R_DEV)
    full_block = jax.random.randint(full_key, (2, 1), block_count // 2, block_count)
    filled = jnp.where(block_ids[None, :] == full_block, R_DEV, filled)
    order_keys = jax.random.split(order_key, 2 * block_count)
    orders = jax.vmap(lambda one_key: jax.random.permutation(one_key, TOK_DEV))(order_keys)
    chosen = orders.reshape(2, block_count, TOK_DEV) < filled[:, :, None]
    return chosen.astype(jnp.int32).reshape(2, TOKENS)


def draw_table(key, part):
    key = jax.random.fold_in(key, 23)
    ramp = jnp.arange(VOCAB, dtype=jnp.float32) / (VOCAB - 1)
    values = jax.random.normal(key, (VOCAB, D), jnp.float32)
    spread = 1.0 + 2.0 * ramp
    return values * (spread / math.sqrt(D))[:, None]


def draw_gains(key, part):
    key = jax.random.fold_in(key, 37)
    ramp = jnp.arange(D, dtype=jnp.float32) / (D - 1)
    factor = jax.random.uniform(key, (3, D), jnp.float32, 0.8, 1.2)
    return factor * (0.55 + 0.9 * ramp)[None, :]


def draw_table_first(key, part):
    key = jax.random.fold_in(key, 41)
    return first_moment(key, (VOCAB, D), 1.0)


def draw_table_second(key, part):
    key = jax.random.fold_in(key, 43)
    return second_moment(key, (VOCAB, D), 1.0)


def draw_qkv_first(key, part):
    key = jax.random.fold_in(key, 47)
    return first_moment(key, (D, 3, D), 1.0)


def draw_qkv_second(key, part):
    key = jax.random.fold_in(key, 53)
    return second_moment(key, (D, 3, D), 1.0)


def draw_out_first(key, part):
    key = jax.random.fold_in(key, 59)
    return first_moment(key, (D, D), 1.0)


def draw_out_second(key, part):
    key = jax.random.fold_in(key, 61)
    return second_moment(key, (D, D), 1.0)


def draw_gate_up_first(key, part):
    key = jax.random.fold_in(key, 67)
    return first_moment(key, (D, 2, FF), 1.0)


def draw_gate_up_second(key, part):
    key = jax.random.fold_in(key, 71)
    return second_moment(key, (D, 2, FF), 1.0)


def draw_down_first(key, part):
    key = jax.random.fold_in(key, 73)
    return first_moment(key, (FF, D), 1.0)


def draw_down_second(key, part):
    key = jax.random.fold_in(key, 79)
    return second_moment(key, (FF, D), 1.0)


def draw_gains_first(key, part):
    key = jax.random.fold_in(key, 83)
    return first_moment(key, (3, D), 5.0)


def draw_gains_second(key, part):
    key = jax.random.fold_in(key, 89)
    return second_moment(key, (3, D), 5.0)


def touch_ends(drawn, rng, least, high):
    extent = drawn.shape
    spot = [jax.random.randint(jax.random.fold_in(rng, axis), (), 0, extent[axis]) for axis in range(len(extent))]
    drawn = drawn.at[tuple(spot)].set(least)
    longest = extent.index(max(extent))
    spot[longest] = (spot[longest] + 1) % extent[longest]
    return drawn.at[tuple(spot)].set(high)


def shard_levels(own_key, extent, cuts, least, top_value):
    level, own = 1.0, jax.random.fold_in(own_key, 6)
    for position, blocks in cuts:
        draws = jnp.exp(jax.random.uniform(jax.random.fold_in(own, position), (blocks,), jnp.float32, least / len(cuts), top_value / len(cuts)))
        level = level * jnp.repeat(draws, extent[position] // blocks).reshape([-1 if axis == position else 1 for axis in range(len(extent))])
    return level


def rank_table(number_of, slope):
    weights = [(1 << 20) // math.isqrt(grade ** slope) + 1 for grade in range(1, number_of + 1)]
    scale = 1 + sum(weights) // (1 << 30)
    return np.cumsum(np.array([max(1, weight // scale) for weight in weights]))


def ranked(rng, extent, number_of, slope):
    table = rank_table(number_of, slope)
    pick = jax.random.randint(jax.random.fold_in(rng, 1), extent, 0, int(table[number_of - 1]))
    standing = jnp.searchsorted(jnp.asarray(table, jnp.int32), pick, side="right")
    return jax.random.permutation(jax.random.fold_in(rng, 2), number_of)[standing].astype(jnp.int32)


def noise(own_key, shape, scale, most, cuts=(), held_as=jnp.bfloat16):
    entries = jax.random.normal(own_key, shape, jnp.float32) * scale
    if len(cuts) > 0:
        entries = shard_levels(own_key, shape, cuts, -0.22, 0.18) * entries
    return jnp.clip(entries, min=-most, max=most).astype(held_as)


def setup_inputs(seed: int = 0) -> dict:
    seeds = jax.random.split(jax.random.key(seed), 22)
    token_ids = touch_ends(ranked(seeds[0], (TOKENS,), VOCAB, 1), jax.random.fold_in(seeds[0], 3), 0, VOCAB - 1).astype(jnp.int32)
    target_ids = touch_ends(ranked(seeds[1], (TOKENS,), VOCAB, 1), jax.random.fold_in(seeds[1], 3), 0, VOCAB - 1).astype(jnp.int32)
    exit_mask = draw_exit_mask(jax.random.fold_in(seeds[21], 71), 0)
    table = draw_table(jax.random.fold_in(seeds[21], 71), 0)
    table_first = draw_table_first(jax.random.fold_in(seeds[21], 71), 0)
    table_second = draw_table_second(jax.random.fold_in(seeds[21], 71), 0)
    qkv_weight = noise(seeds[6], (D, 3, D), D ** -0.5, 0.125, ((0, 8), (2, 4)), jnp.float32)
    qkv_first = draw_qkv_first(jax.random.fold_in(seeds[21], 71), 0)
    qkv_second = draw_qkv_second(jax.random.fold_in(seeds[21], 71), 0)
    out_weight = noise(seeds[9], (D, D), (D // 4) ** -0.5, 0.25, ((0, 4), (1, 8)), jnp.float32)
    out_first = draw_out_first(jax.random.fold_in(seeds[21], 71), 0)
    out_second = draw_out_second(jax.random.fold_in(seeds[21], 71), 0)
    gate_up_weight = noise(seeds[12], (D, 2, FF), D ** -0.5, 0.125, ((0, 8), (2, 4)), jnp.float32)
    gate_up_first = draw_gate_up_first(jax.random.fold_in(seeds[21], 71), 0)
    gate_up_second = draw_gate_up_second(jax.random.fold_in(seeds[21], 71), 0)
    down_weight = noise(seeds[15], (FF, D), FF ** -0.5, 0.078125, ((0, 4), (1, 8)), jnp.float32)
    down_first = draw_down_first(jax.random.fold_in(seeds[21], 71), 0)
    down_second = draw_down_second(jax.random.fold_in(seeds[21], 71), 0)
    gains = draw_gains(jax.random.fold_in(seeds[21], 71), 0)
    gains_first = draw_gains_first(jax.random.fold_in(seeds[21], 71), 0)
    gains_second = draw_gains_second(jax.random.fold_in(seeds[21], 71), 0)
    return dict(token_ids=token_ids, target_ids=target_ids, exit_mask=exit_mask, table=table, table_first=table_first, table_second=table_second, qkv_weight=qkv_weight, qkv_first=qkv_first, qkv_second=qkv_second, out_weight=out_weight, out_first=out_first, out_second=out_second, gate_up_weight=gate_up_weight, gate_up_first=gate_up_first, gate_up_second=gate_up_second, down_weight=down_weight, down_first=down_first, down_second=down_second, gains=gains, gains_first=gains_first, gains_second=gains_second)


@jax.custom_vjp
def low(v):
    return lax.optimization_barrier(v.astype(jnp.bfloat16)).astype(jnp.float32)

@jax.custom_vjp
def low_back(v):
    return v

def low_keep(v):
    return (low(v), None)

def low_pass(kept, grad):
    return (grad,)

def back_keep(v):
    return (v, None)

def back_low(kept, grad):
    return (low(grad),)
low.defvjp(low_keep, low_pass)
low_back.defvjp(back_keep, back_low)
EPS_NORM = 1e-05
BETA_ONE = 0.9
BETA_TWO = 0.95
ADAM_EPS = 1e-08
DECAY = 0.1
RATE_MATRIX = 0.02
RATE_GAIN = 1.0
CLIP = 0.02
EXIT_SCALE = (1.0 / 3.0, 2.0 / 3.0)
NEG = -1e+30
exact_mode = lax.Precision.HIGHEST

def rounded(values):
    return low_back(low(values))

def norm_gain(values, gain):
    return values * lax.rsqrt(lax.optimization_barrier(jnp.mean(values * values, axis=-1, keepdims=True)) + EPS_NORM) * gain

def rotary(places, width):
    half_width = width // 2
    frequency = jnp.exp(jnp.arange(half_width, dtype=jnp.float32) * (-math.log(10000.0) / half_width))
    angles = places.astype(jnp.float32)[:, None] * frequency[None, :]
    return (jnp.cos(angles), jnp.sin(angles))

def rotate_pairs(values, cosine, sine_table):
    half_width = values.shape[-1] // 2
    front_half = values[..., :half_width]
    back_half = values[..., half_width:]
    cosine = cosine[:, None, :]
    sine_table = sine_table[:, None, :]
    return jnp.concatenate([front_half * cosine - back_half * sine_table, back_half * cosine + front_half * sine_table], axis=-1)

def attention(query, keys, values, seq_len):
    key_count = keys.shape[0]
    block_rows = min(512, key_count)
    key_place = jnp.arange(key_count, dtype=jnp.int32)
    score_scale = 1.0 / math.sqrt(HEAD_DIM)

    def one_block(row_start):
        query_block = lax.dynamic_slice_in_dim(query, row_start, block_rows, 0)
        query_place = row_start + jnp.arange(block_rows, dtype=jnp.int32)
        scores = low_back(jnp.einsum('qhd,khd->hqk', query_block, keys, precision=exact_mode) * score_scale)
        allowed = ((key_place[None, :] <= query_place[:, None]) & (key_place[None, :] // seq_len == query_place[:, None] // seq_len))[None]
        scores = jnp.where(allowed, scores, NEG)
        row_top = lax.optimization_barrier(jnp.max(scores, axis=-1, keepdims=True))
        weights = jnp.exp(scores - row_top)
        probability = weights / lax.optimization_barrier(jnp.sum(weights, axis=-1, keepdims=True))
        return jnp.einsum('hqk,khd->qhd', low(probability), values, precision=exact_mode)
    starts = jnp.arange(0, key_count, block_rows, dtype=jnp.int32)
    blocks = lax.map(jax.checkpoint(one_block), starts)
    return blocks.reshape(key_count, query.shape[1], query.shape[2])

def exit_entropy(rows, targets, live, table_low):
    vocab_ids = jnp.arange(VOCAB, dtype=jnp.int32)

    def one_block(pieces):
        row_block, target_block, live_block = pieces
        logits = low_back(jnp.dot(row_block, table_low.T, precision=exact_mode))
        row_top = lax.optimization_barrier(jnp.max(logits, axis=-1, keepdims=True))
        row_lse = row_top[:, 0] + jnp.log(lax.optimization_barrier(jnp.sum(jnp.exp(logits - row_top), axis=-1)))
        target_logit = lax.optimization_barrier(jnp.sum(jnp.where(vocab_ids[None, :] == target_block[:, None], logits, 0.0), axis=-1))
        return jnp.sum((row_lse - target_logit) * live_block)
    return jnp.sum(lax.map(jax.checkpoint(one_block), (rows, targets, live)))

def forward(params, token_ids, pick_table, picked_targets, live_slots, counts):
    table, qkv_weight, out_weight, gate_up_weight, down_weight, gains = params
    token_count = token_ids.shape[0]
    seq_len = token_count
    table_low = low(table)
    gain_rows = low(gains)
    resid_zero = low_back(jnp.take(table_low, token_ids, axis=0))
    attn_in = low(norm_gain(resid_zero, gain_rows[0]))
    projected = low_back(jnp.einsum('td,dcf->tcf', attn_in, low(qkv_weight), precision=exact_mode))
    shaped = projected.reshape(token_count, 3, HEADS, HEAD_DIM)
    cosine, sine_table = rotary(jnp.arange(token_count, dtype=jnp.int32), HEAD_DIM)
    query = low(rotate_pairs(shaped[:, 0], cosine, sine_table))
    keys = low(rotate_pairs(shaped[:, 1], cosine, sine_table))
    values = low(shaped[:, 2])
    attn_out = rounded(attention(query, keys, values, seq_len)).reshape(token_count, D)
    resid_one = resid_zero + low_back(jnp.dot(attn_out, low(out_weight), precision=exact_mode))
    mlp_in = low(norm_gain(resid_one, gain_rows[1]))
    gate_up = low_back(jnp.einsum('td,dcf->tcf', mlp_in, low(gate_up_weight), precision=exact_mode))
    hidden = low(gate_up[:, 0] * jax.nn.sigmoid(gate_up[:, 0]) * gate_up[:, 1])
    resid_two = resid_one + low_back(jnp.dot(hidden, low(down_weight), precision=exact_mode))
    exits = jnp.stack([low(norm_gain(resid_one, gain_rows[2])), low(norm_gain(resid_two, gain_rows[2]))])
    exits = exits.reshape(2, token_count // TOK_DEV, TOK_DEV, D)
    chosen = jnp.einsum('ebrt,ebtd->ebrd', pick_table, exits, precision=exact_mode)
    sum_one = exit_entropy(chosen[0], picked_targets[0], live_slots[0], table_low)
    sum_two = exit_entropy(chosen[1], picked_targets[1], live_slots[1], table_low)
    loss = EXIT_SCALE[0] * sum_one / counts[0] + EXIT_SCALE[1] * sum_two / counts[1]
    return (loss, jnp.stack([sum_one, sum_two]))

def adam_update(weight, moment_one, moment_two, gradient, rate, decay):
    moment_one = BETA_ONE * moment_one + (1.0 - BETA_ONE) * gradient
    moment_two = BETA_TWO * moment_two + (1.0 - BETA_TWO) * gradient * gradient
    ratio = moment_one / (1.0 - BETA_ONE ** STEP) / (jnp.sqrt(moment_two / (1.0 - BETA_TWO ** STEP)) + ADAM_EPS)
    return (weight - rate * (ratio + decay * weight), moment_one, moment_two)

def reference(token_ids, target_ids, exit_mask, table, table_first, table_second, qkv_weight, qkv_first, qkv_second, out_weight, out_first, out_second, gate_up_weight, gate_up_first, gate_up_second, down_weight, down_first, down_second, gains, gains_first, gains_second):
    token_count = token_ids.shape[0]
    block_count = token_count // TOK_DEV
    mask_blocks = exit_mask.reshape(2, block_count, TOK_DEV)
    slot_ranks = jnp.cumsum(mask_blocks, axis=2) - 1
    slot_ids = jnp.arange(R_DEV, dtype=jnp.int32)
    pick_int = ((slot_ranks[:, :, None, :] == slot_ids[None, None, :, None]) & (mask_blocks[:, :, None, :] == 1)).astype(jnp.int32)
    target_blocks = target_ids.reshape(block_count, TOK_DEV)
    picked_targets = lax.optimization_barrier(jnp.sum(pick_int * target_blocks[None, :, None, :], axis=3))
    live_slots = (slot_ids[None, None, :] < lax.optimization_barrier(jnp.sum(mask_blocks, axis=2))[:, :, None]).astype(jnp.float32)
    counts = lax.optimization_barrier(jnp.sum(live_slots, axis=(1, 2)))
    pick_table = pick_int.astype(jnp.float32)
    params = (table, qkv_weight, out_weight, gate_up_weight, down_weight, gains)

    def loss_of(weights_now):
        return forward(weights_now, token_ids, pick_table, picked_targets, live_slots, counts)
    loss, pullback, loss_sums = jax.vjp(loss_of, params, has_aux=True)
    grads = pullback(jnp.ones((), jnp.float32))[0]
    squares = jnp.zeros((), jnp.float32)
    for gradient in grads:
        squares = squares + jnp.sum(gradient * gradient)
    grad_norm = jnp.sqrt(squares)
    factor = jnp.minimum(1.0, CLIP / (grad_norm + 1e-06))
    firsts = (table_first, qkv_first, out_first, gate_up_first, down_first, gains_first)
    seconds = (table_second, qkv_second, out_second, gate_up_second, down_second, gains_second)
    results = []
    for place in range(6):
        rate = RATE_GAIN if place == 5 else RATE_MATRIX
        decay = 0.0 if place == 5 else DECAY
        results.append(adam_update(params[place], firsts[place], seconds[place], grads[place] * factor, rate, decay))
    return (loss_sums, counts, grad_norm, results[0][0], results[0][1], results[0][2], results[1][0], results[1][1], results[1][2], results[2][0], results[2][1], results[2][2], results[3][0], results[3][1], results[3][2], results[4][0], results[4][1], results[4][2], results[5][0], results[5][1], results[5][2])
```

```python
import functools
import math

import jax
import jax.numpy as jnp
from jax import lax
from jax.experimental import pallas as pl
from jax.experimental.pallas import tpu as pltpu
from jax.sharding import PartitionSpec as P

HEAD_DIM = 128
R_DEV = 64
STEP = 10


EPS_NORM = 1e-05
BETA_ONE = 0.9
BETA_TWO = 0.95
ADAM_EPS = 1e-08
DECAY = 0.1
RATE_MATRIX = 0.02
RATE_GAIN = 1.0
CLIP = 0.02
EXIT_SCALE = (1.0 / 3.0, 2.0 / 3.0)
NEG = -1e30
BOTH = ("dp", "mp")
MESH = pl.DeviceIdType.MESH
VMEM_LIMIT = 60 * 1024 * 1024
ANY = pl.BlockSpec(memory_space=pl.ANY)


def kernel_mesh():
    return lax.axis_size("dp") == 8 and lax.axis_size("mp") == 4


def place():
    data_index, model_index = lax.axis_index("dp"), lax.axis_index("mp")
    return (data_index // 2, data_index % 2, model_index // 2, model_index % 2)


def z_peers(z):
    return (z, z + 1 - 2 * (z % 2), (z + 2) % 4, 3 - z)


def device(z, y, x, c):
    return (z * 2 + y, x * 2 + c)


def chunk(ref, rows, z, y, x, c):
    start = ((z * 2 + y) * 4 + x * 2 + c) * rows
    return ref.at[pl.ds(pl.multiple_of(start, rows), rows)]


def greet(peers):
    barrier = pltpu.get_barrier_semaphore()
    for peer in peers:
        pl.semaphore_signal(barrier, inc=1, device_id=peer, device_id_type=MESH)
    pl.semaphore_wait(barrier, len(peers))


def comm_params(ident):
    return pltpu.CompilerParams(
        collective_id=ident, has_side_effects=True, vmem_limit_bytes=VMEM_LIMIT
    )


def gather_kernel(rows, x_ref, o_ref, send_sem, recv_sem, own_sem):
    z, y, x, c = place()
    zs = z_peers(z)
    x_side, y_side, c_side = device(z, y, 1 - x, c), device(z, 1 - y, x, c), device(z, y, x, 1 - c)
    greet([device(zs[d], y, x, c) for d in (1, 2, 3)] + [x_side, y_side, c_side])
    origins = ((y, x), (y, 1 - x), (1 - y, x), (1 - y, 1 - x))
    sent = []

    def send(source, target, d, group, core):
        copy = pltpu.make_async_remote_copy(
            src_ref=source[0],
            dst_ref=source[1],
            send_sem=send_sem.at[len(sent)],
            recv_sem=recv_sem.at[(d * 4 + group) * 2 + core],
            device_id=target,
            device_id_type=MESH,
        )
        copy.start()
        sent.append(copy)

    def spot(d, group, core=0):
        oy, ox = origins[group]
        return chunk(o_ref, rows, zs[d], oy, ox, c if core == 0 else 1 - c)

    def arrived(d, group, core):
        here = spot(d, group, core)
        pltpu.make_async_copy(here, here, recv_sem.at[(d * 4 + group) * 2 + core]).wait()

    mine = (x_ref, spot(0, 0))
    own = pltpu.make_async_copy(x_ref, spot(0, 0), own_sem)
    own.start()
    for d in (3, 2, 1):
        send(mine, device(zs[d], y, x, c), d, 0, 0)
    send(mine, x_side, 0, 1, 0)
    send(mine, y_side, 0, 2, 0)
    send(mine, c_side, 0, 0, 1)
    for d in (1, 2, 3):
        arrived(d, 0, 0)
        here = (spot(d, 0), spot(d, 0))
        send(here, x_side, d, 1, 0)
        send(here, y_side, d, 2, 0)
        send(here, c_side, d, 0, 1)
    for d in (0, 1, 2, 3):
        for group, side in ((1, y_side), (2, x_side)):
            arrived(d, group, 0)
            here = (spot(d, group), spot(d, group))
            if (d % 2 == 0) == (group == 1):
                send(here, side, d, 3, 0)
            send(here, c_side, d, group, 1)
    for d in (0, 1, 2, 3):
        arrived(d, 3, 0)
        send((spot(d, 3), spot(d, 3)), c_side, d, 3, 1)
    for d in (0, 1, 2, 3):
        for group in range(4):
            arrived(d, group, 1)
    own.wait()
    for copy in sent:
        copy.wait_send()


def gather_all(value, ident):
    if not kernel_mesh():
        return lax.all_gather(value, BOTH, axis=0, tiled=True)
    rows, width = value.shape
    return pl.pallas_call(
        functools.partial(gather_kernel, rows),
        out_shape=jax.ShapeDtypeStruct((32 * rows, width), value.dtype),
        in_specs=[ANY],
        out_specs=ANY,
        scratch_shapes=[
            pltpu.SemaphoreType.DMA((31,)),
            pltpu.SemaphoreType.DMA((32,)),
            pltpu.SemaphoreType.DMA,
        ],
        compiler_params=comm_params(ident),
    )(value)


def scatter_kernel(
    rows, p_ref, o_ref, core_buf, diag_buf, side_buf, z_buf, held, send_sem, recv_sem
):
    z, y, x, c = place()
    zs = z_peers(z)
    x_side, y_side, c_side = device(z, y, 1 - x, c), device(z, 1 - y, x, c), device(z, y, x, 1 - c)
    greet([device(zs[d], y, x, c) for d in (1, 2, 3)] + [x_side, y_side, c_side])
    origins = ((y, x), (y, 1 - x), (1 - y, x), (1 - y, 1 - x))
    step = 16
    sent = []

    def send(source, target, slot_ref, slot):
        copy = pltpu.make_async_remote_copy(
            src_ref=source,
            dst_ref=slot_ref,
            send_sem=send_sem.at[len(sent)],
            recv_sem=recv_sem.at[slot],
            device_id=target,
            device_id_type=MESH,
        )
        copy.start()
        sent.append(copy)

    def arrived(slot_ref, slot):
        pltpu.make_async_copy(slot_ref, slot_ref, recv_sem.at[slot]).wait()

    def part(d, group, core=0):
        oy, ox = origins[group]
        return chunk(p_ref, rows, zs[d], oy, ox, c if core == 0 else 1 - c)

    def add(target, sources):
        @pl.loop(0, rows // step)
        def _(index):
            at = pl.ds(index * step, step)
            total = sources[0][at].astype(jnp.float32)
            for source in sources[1:]:
                total = total + source[at].astype(jnp.float32)
            target[at] = total.astype(target.dtype)

    order = [(d, 3) for d in range(4)]
    order += [(d, group) for d in range(4) for group in (1, 2)]
    order += [(d, 0) for d in (3, 2, 1, 0)]
    for d, group in order:
        send(part(d, group, 1), c_side, core_buf.at[d * 4 + group], d * 4 + group)
    for d, group in order:
        slot = d * 4 + group
        arrived(core_buf.at[slot], slot)
        terms = [part(d, group), core_buf.at[slot]]
        if group == 3:
            add(held.at[slot], terms)
            send(held.at[slot], y_side if d % 2 == 0 else x_side, diag_buf.at[d], 16 + d)
        elif group in (1, 2):
            if (d % 2 == 0) == (group == 1):
                arrived(diag_buf.at[d], 16 + d)
                terms.append(diag_buf.at[d])
            add(held.at[slot], terms)
            side = d * 2 + group - 1
            target = x_side if group == 1 else y_side
            send(held.at[slot], target, side_buf.at[side], 20 + side)
        else:
            for side in (d * 2, d * 2 + 1):
                arrived(side_buf.at[side], 20 + side)
                terms.append(side_buf.at[side])
            if d == 0:
                for peer in (1, 2, 3):
                    arrived(z_buf.at[peer - 1], 27 + peer)
                    terms.append(z_buf.at[peer - 1])
                add(o_ref, terms)
            else:
                add(held.at[slot], terms)
                send(held.at[slot], device(zs[d], y, x, c), z_buf.at[d - 1], 27 + d)
    for copy in sent:
        copy.wait_send()


def scatter_sum(value, ident):
    if not kernel_mesh():
        return lax.psum_scatter(value, BOTH, scatter_dimension=0, tiled=True).astype(jnp.float32)
    rows, width = value.shape[0] // 32, value.shape[1]
    low = value.dtype
    return pl.pallas_call(
        functools.partial(scatter_kernel, rows),
        out_shape=jax.ShapeDtypeStruct((rows, width), jnp.float32),
        in_specs=[pl.BlockSpec(memory_space=pltpu.VMEM)],
        out_specs=pl.BlockSpec(memory_space=pltpu.VMEM),
        scratch_shapes=[
            pltpu.VMEM((16, rows, width), low),
            pltpu.VMEM((4, rows, width), low),
            pltpu.VMEM((8, rows, width), low),
            pltpu.VMEM((3, rows, width), low),
            pltpu.VMEM((16, rows, width), low),
            pltpu.SemaphoreType.DMA((31,)),
            pltpu.SemaphoreType.DMA((31,)),
        ],
        compiler_params=comm_params(ident),
    )(value)


def exchange_kernel(count, whole, *refs):
    ins, outs = refs[: len(whole)], refs[len(whole) : 2 * len(whole)]
    send_sem, recv_sem, own_sem = refs[2 * len(whole) :]
    me, model_index = lax.axis_index("dp"), lax.axis_index("mp")
    peers = [lax.rem(me + shift, count) for shift in range(1, count)]
    greet([(peer, model_index) for peer in peers])
    owns, sent = [], []
    for array, keep in enumerate(whole):
        own = pltpu.make_async_copy(
            ins[array] if keep else ins[array].at[me], outs[array].at[me], own_sem.at[array]
        )
        own.start()
        owns.append(own)
        for shift in range(count - 1):
            copy = pltpu.make_async_remote_copy(
                src_ref=ins[array] if keep else ins[array].at[peers[shift]],
                dst_ref=outs[array].at[me],
                send_sem=send_sem.at[array, shift],
                recv_sem=recv_sem.at[array, shift],
                device_id=(peers[shift], model_index),
                device_id_type=MESH,
            )
            copy.start()
            sent.append(copy)
    for own in owns:
        own.wait()
    for array in range(len(whole)):
        for shift in range(count - 1):
            source = lax.rem(me + count - 1 - shift, count)
            here = outs[array].at[source]
            pltpu.make_async_copy(here, here, recv_sem.at[array, shift]).wait()
    for copy in sent:
        copy.wait_send()


def exchange(values, whole, ident):
    count = lax.axis_size("dp")
    if not kernel_mesh():
        return [
            lax.all_gather(value, "dp")
            if keep
            else lax.all_to_all(value, "dp", split_axis=0, concat_axis=0, tiled=True)
            for value, keep in zip(values, whole)
        ]
    shapes = [
        jax.ShapeDtypeStruct(((count,) if keep else ()) + value.shape, value.dtype)
        for value, keep in zip(values, whole)
    ]
    return pl.pallas_call(
        functools.partial(exchange_kernel, count, tuple(whole)),
        out_shape=shapes,
        in_specs=[ANY] * len(values),
        out_specs=[ANY] * len(values),
        scratch_shapes=[
            pltpu.SemaphoreType.DMA((len(values), count - 1)),
            pltpu.SemaphoreType.DMA((len(values), count - 1)),
            pltpu.SemaphoreType.DMA((len(values),)),
        ],
        compiler_params=comm_params(ident),
    )(*values)


def norm_fwd(values, gain):
    row_scale = lax.rsqrt(jnp.mean(values * values, axis=-1, keepdims=True) + EPS_NORM)
    unit_rows = values * row_scale
    return (unit_rows * gain, unit_rows, row_scale)


def norm_back(unit_rows, row_scale, gain, gradient):
    weighted = gradient * gain
    back_rows = row_scale * (
        weighted - unit_rows * jnp.mean(weighted * unit_rows, axis=-1, keepdims=True)
    )
    return (back_rows, jnp.sum(gradient * unit_rows, axis=0))


def rotary(places, width):
    half_width = width // 2
    frequency = jnp.exp(
        jnp.arange(half_width, dtype=jnp.float32) * (-math.log(10000.0) / half_width)
    )
    angles = places.astype(jnp.float32)[:, None] * frequency[None, :]
    return (jnp.cos(angles), jnp.sin(angles))


def rotate_pairs(values, cosine, sine_table):
    half_width = values.shape[-1] // 2
    front_half = values[..., :half_width]
    back_half = values[..., half_width:]
    return jnp.concatenate(
        [
            front_half * cosine - back_half * sine_table,
            back_half * cosine + front_half * sine_table,
        ],
        axis=-1,
    )


def dot(left, right, left_dim=1, right_dim=0):
    return lax.dot_general(
        left, right, (((left_dim,), (right_dim,)), ((), ())), preferred_element_type=jnp.float32
    )


def adam_update(weight, moment_one, moment_two, gradient, rate, decay):
    moment_one = BETA_ONE * moment_one + (1.0 - BETA_ONE) * gradient
    moment_two = BETA_TWO * moment_two + (1.0 - BETA_TWO) * gradient * gradient
    ratio = (
        moment_one
        / (1.0 - BETA_ONE**STEP)
        / (jnp.sqrt(moment_two / (1.0 - BETA_TWO**STEP)) + ADAM_EPS)
    )
    return (weight - rate * (ratio + decay * weight), moment_one, moment_two)


def body(
    token_ids,
    target_ids,
    exit_mask,
    table,
    table_first,
    table_second,
    qkv_weight,
    qkv_first,
    qkv_second,
    out_weight,
    out_first,
    out_second,
    gate_up_weight,
    gate_up_first,
    gate_up_second,
    down_weight,
    down_first,
    down_second,
    gains,
    gains_first,
    gains_second,
):
    low = jnp.bfloat16
    data_size, model_size = lax.axis_size("dp"), lax.axis_size("mp")
    data_index, model_index = lax.axis_index("dp"), lax.axis_index("mp")
    devices = data_size * model_size
    block_rows = token_ids.shape[0]
    tokens = block_rows * data_size
    width = table.shape[1]
    width_here = qkv_weight.shape[0]
    heads_here = qkv_weight.shape[2] // HEAD_DIM
    hidden_here = down_weight.shape[0] // data_size
    vocab_here = table.shape[0]
    device_index = data_index * model_size + model_index
    vocab_ids = device_index * vocab_here + jnp.arange(vocab_here, dtype=jnp.int32)
    score_scale = 1.0 / math.sqrt(HEAD_DIM)

    sharers = data_size // heads_here
    shares = sharers // 2
    share_slots = data_size // shares * R_DEV
    exit_here = data_index % sharers % 2
    share_here = data_index % sharers // 2
    slots_here = R_DEV // model_size
    rows_here = block_rows // model_size

    ints, gain_low = exchange(
        [
            jnp.concatenate([token_ids[None], target_ids[None], exit_mask]),
            jnp.pad(gains.astype(low), ((0, 13), (0, 0))),
        ],
        (True, True),
        0,
    )
    gain_rows = jnp.moveaxis(gain_low[:, :3], 0, 1).reshape(3, width).astype(jnp.float32)
    all_ids = ints[:, 0].reshape(tokens)
    mask_blocks = jnp.moveaxis(ints[:, 2:], 0, 1)
    slot_ids = jnp.arange(R_DEV, dtype=jnp.int32)
    slot_ranks = jnp.cumsum(mask_blocks, axis=2) - 1
    pick_int = (
        (slot_ranks[:, :, None, :] == slot_ids[:, None]) & (mask_blocks[:, :, None, :] == 1)
    ).astype(jnp.int32)
    pick_low = pick_int.astype(low)
    token_places = jnp.arange(tokens, dtype=jnp.int32)
    slot_targets = jnp.sum(pick_int * ints[:, 1][None, :, None, :], axis=3).reshape(2, -1)
    slot_places = jnp.sum(
        pick_int * token_places.reshape(1, data_size, 1, block_rows), axis=3
    ).reshape(2, -1)
    live = (slot_ids < jnp.sum(mask_blocks, axis=2)[:, :, None]).astype(jnp.float32).reshape(2, -1)
    counts = jnp.sum(live, axis=1)

    head_major = jnp.moveaxis(
        qkv_weight.astype(low).reshape(width_here, 3, heads_here, HEAD_DIM), 2, 0
    ).reshape(heads_here, width_here, 3 * HEAD_DIM)
    qkv_head, out_head, gate_up_cols, down_rows = exchange(
        [
            jnp.repeat(head_major, sharers, axis=0),
            jnp.repeat(
                out_weight.astype(low).reshape(heads_here, HEAD_DIM, width_here), sharers, axis=0
            ),
            jnp.moveaxis(
                gate_up_weight.astype(low).reshape(width_here, 2, data_size, hidden_here), 2, 0
            ).reshape(data_size, width_here, 2 * hidden_here),
            down_weight.astype(low).reshape(data_size, hidden_here, width_here),
        ],
        (False,) * 4,
        1,
    )
    qkv_head = qkv_head.reshape(width, 3 * HEAD_DIM)
    out_head = jnp.moveaxis(out_head, 0, 1).reshape(HEAD_DIM, width)
    gate_up_cols = gate_up_cols.reshape(width, 2 * hidden_here)
    down_rows = jnp.moveaxis(down_rows, 0, 1).reshape(hidden_here, width)

    table_low = table.astype(low)
    id_hits = (all_ids[:, None] == vocab_ids[None, :]).astype(low)
    resid_here = scatter_sum(dot(id_hits, table_low).astype(low), 2)
    resid_low = gather_all(resid_here.astype(low), 3)
    attn_low = norm_fwd(resid_low.astype(jnp.float32), gain_rows[0])[0].astype(low)

    projected = dot(attn_low, qkv_head)
    cosine, sine_table = rotary(token_places, HEAD_DIM)
    query_low = rotate_pairs(projected[:, :HEAD_DIM], cosine, sine_table).astype(low)
    key_low = rotate_pairs(projected[:, HEAD_DIM : 2 * HEAD_DIM], cosine, sine_table).astype(low)
    value_low = projected[:, 2 * HEAD_DIM :].astype(low)
    pick_share = lax.dynamic_slice_in_dim(
        lax.dynamic_index_in_dim(pick_low, exit_here, 0, keepdims=False),
        share_here * (data_size // shares),
        data_size // shares,
        0,
    )
    query_share = lax.dynamic_slice_in_dim(
        query_low.reshape(data_size, block_rows, HEAD_DIM),
        share_here * (data_size // shares),
        data_size // shares,
        0,
    )
    query_slots = (
        jnp.einsum("brt,btd->brd", pick_share, query_share, preferred_element_type=jnp.float32)
        .astype(low)
        .reshape(share_slots, HEAD_DIM)
    )

    def share_of(per_slot):
        return lax.dynamic_slice(per_slot, (exit_here, share_here * share_slots), (1, share_slots))[
            0
        ]

    places_share, live_share = share_of(slot_places), share_of(live)
    scores = dot(query_slots, key_low, 1, 1) * score_scale
    allowed = token_places[None, :] <= places_share[:, None]
    scores = jnp.where(allowed, scores, NEG)
    weights = jnp.exp(scores - jnp.max(scores, axis=-1, keepdims=True))
    probs = weights / jnp.sum(weights, axis=-1, keepdims=True)
    probs_low = probs.astype(low)
    attn_out = (dot(probs_low, value_low) * live_share[:, None]).astype(low)

    def spread(per_share):
        if shares > 1:
            full = jnp.zeros((data_size * R_DEV, width), per_share.dtype)
            per_share = lax.dynamic_update_slice_in_dim(
                full, per_share, share_here * share_slots, 0
            )
        exits = jnp.arange(2, dtype=jnp.int32)[None, :, None, None]
        rows = per_share.reshape(devices, 1, slots_here, width)
        return jnp.where(exits == exit_here, rows, 0).reshape(-1, width)

    out_slots = scatter_sum(spread(dot(attn_out, out_head).astype(low)), 4)
    block_low = lax.dynamic_slice_in_dim(resid_low, data_index * block_rows, block_rows, 0)
    pick_here = lax.dynamic_slice(
        pick_low,
        (0, data_index, model_index * slots_here, 0),
        (2, 1, slots_here, block_rows),
    ).reshape(2 * slots_here, block_rows)
    resid_one = dot(pick_here, block_low) + out_slots
    exit_one, unit_one, scale_one = norm_fwd(resid_one[:slots_here], gain_rows[2])
    mlp_in, mlp_unit, mlp_scale = norm_fwd(resid_one[slots_here:], gain_rows[1])
    first_rows = gather_all(jnp.concatenate([exit_one, mlp_in]).astype(low), 5).reshape(
        devices, 2, slots_here, width
    )
    exit_rows_one = first_rows[:, 0].reshape(-1, width)
    mlp_low = first_rows[:, 1].reshape(-1, width)

    gate_up = dot(mlp_low, gate_up_cols)
    gate_part, up_part = gate_up[:, :hidden_here], gate_up[:, hidden_here:]
    gate_sigma = jax.nn.sigmoid(gate_part)
    hidden_low = (gate_part * gate_sigma * up_part).astype(low)
    resid_two = resid_one[slots_here:] + scatter_sum(dot(hidden_low, down_rows).astype(low), 6)
    exit_two, unit_two, scale_two = norm_fwd(resid_two, gain_rows[2])
    exit_rows_two = gather_all(exit_two.astype(low), 7)

    exit_rows = (exit_rows_one, exit_rows_two)
    logits = [dot(rows, table_low, 1, 1) for rows in exit_rows]
    hits = [slot_targets[e][:, None] == vocab_ids[None, :] for e in range(2)]
    tops = [jnp.max(values, axis=1) for values in logits]
    masses = [jnp.sum(jnp.exp(values - top[:, None]), axis=1) for values, top in zip(logits, tops)]
    found = [jnp.sum(jnp.where(hit, values, 0.0), axis=1) for hit, values in zip(hits, logits)]
    stats = jnp.concatenate(tops + masses + found).reshape(-1, 128)
    stats = gather_all(stats, 8).reshape(devices, 3, 2, -1)
    row_top = jnp.max(stats[:, 0], axis=0)
    row_mass = jnp.sum(stats[:, 1] * jnp.exp(stats[:, 0] - row_top), axis=0)
    row_lse = row_top + jnp.log(row_mass)
    entropy = row_lse - jnp.sum(stats[:, 2], axis=0)
    loss_sums = jnp.sum(entropy * live, axis=1)
    row_weight = live * (jnp.array(EXIT_SCALE, jnp.float32) / counts)[:, None]
    grad_logits = [
        (
            row_weight[e][:, None]
            * (jnp.exp(logits[e] - row_lse[e][:, None]) - hits[e].astype(jnp.float32))
        ).astype(low)
        for e in range(2)
    ]
    table_head = dot(grad_logits[0], exit_rows_one, 0, 0) + dot(grad_logits[1], exit_rows_two, 0, 0)
    row_terms = jnp.stack(
        [
            dot(grad, table_low).astype(low).reshape(devices, slots_here, width)
            for grad in grad_logits
        ],
        axis=1,
    )
    row_grads = scatter_sum(row_terms.reshape(-1, width), 9)

    dexit_one, final_one = norm_back(unit_one, scale_one, gain_rows[2], row_grads[:slots_here])
    dresid_two, final_two = norm_back(unit_two, scale_two, gain_rows[2], row_grads[slots_here:])
    dtwo_low = gather_all(dresid_two.astype(low), 10)
    down_local = dot(hidden_low, dtwo_low, 0, 0)
    dhidden = dot(dtwo_low, down_rows, 1, 1)
    dgate = dhidden * up_part * gate_sigma * (1.0 + gate_part * (1.0 - gate_sigma))
    dup_part = dhidden * gate_part * gate_sigma
    dgate_up = jnp.concatenate([dgate, dup_part], axis=1).astype(low)
    gate_up_local = dot(mlp_low, dgate_up, 0, 0)
    dmlp_in = scatter_sum(dot(dgate_up, gate_up_cols, 1, 1).astype(low), 11)
    dmlp_rows, mlp_gain_grad = norm_back(mlp_unit, mlp_scale, gain_rows[1], dmlp_in)
    done_here = jnp.concatenate([dexit_one, dresid_two + dmlp_rows]).astype(low)
    done_low = gather_all(done_here, 12).reshape(devices, 2, slots_here, width)

    done_share = lax.dynamic_slice(
        lax.dynamic_index_in_dim(done_low, exit_here, 1, keepdims=False).reshape(-1, width),
        (share_here * share_slots, 0),
        (share_slots, width),
    )
    out_local = dot(attn_out, done_share, 0, 0)
    dattn_low = dot(done_share, out_head, 1, 1).astype(low)
    dprobs = dot(dattn_low, value_low, 1, 1)
    delta = jnp.sum(probs * dprobs, axis=-1, keepdims=True)
    dscores = (probs * (dprobs - delta)).astype(low)
    cosine_share, sine_share = rotary(places_share, HEAD_DIM)
    dquery = rotate_pairs(dot(dscores, key_low) * score_scale, cosine_share, -sine_share).astype(
        low
    )
    dquery_share = jnp.einsum(
        "brt,brd->btd",
        pick_share,
        dquery.reshape(-1, R_DEV, HEAD_DIM),
        preferred_element_type=jnp.float32,
    ).astype(low)
    if shares > 1:
        dquery_share = lax.dynamic_update_slice_in_dim(
            jnp.zeros((data_size, block_rows, HEAD_DIM), low),
            dquery_share,
            share_here * (data_size // shares),
            0,
        )
    dkey = rotate_pairs(dot(dscores, query_slots, 0, 0) * score_scale, cosine, -sine_table)
    dvalue = dot(probs_low, dattn_low, 0, 0)
    dprojected = jnp.concatenate(
        [dquery_share.reshape(tokens, HEAD_DIM), dkey.astype(low), dvalue.astype(low)], axis=1
    )
    qkv_local = dot(attn_low, dprojected, 0, 0)
    dattn_in = scatter_sum(dot(dprojected, qkv_head, 1, 1).astype(low), 13)

    _, attn_unit, attn_scale = norm_fwd(resid_here, gain_rows[0])
    dattn_rows, attn_gain_grad = norm_back(attn_unit, attn_scale, gain_rows[0], dattn_in)
    done_block = lax.dynamic_slice_in_dim(done_low, data_index * model_size, model_size, 0)
    pick_block = lax.dynamic_slice(
        pick_low,
        (0, data_index, 0, model_index * rows_here),
        (2, 1, R_DEV, rows_here),
    ).reshape(2, model_size, slots_here, rows_here)
    dresid_here = jnp.einsum(
        "emst,mesd->td", pick_block, done_block, preferred_element_type=jnp.float32
    )
    dzero_low = gather_all((dresid_here + dattn_rows).astype(low), 14)
    table_grad = table_head + dot(id_hits, dzero_low, 0, 0)

    gain_local = jnp.stack([attn_gain_grad, mlp_gain_grad, final_one + final_two])
    gain_sums = jnp.sum(
        gather_all(gain_local.reshape(-1, 128), 15).reshape(devices, 3, width), axis=0
    )
    qkv_parts, out_parts, gate_up_parts, down_parts = exchange(
        [
            qkv_local.astype(low).reshape(data_size, width_here, 3 * HEAD_DIM),
            jnp.moveaxis(out_local.astype(low).reshape(HEAD_DIM, data_size, width_here), 1, 0),
            gate_up_local.astype(low).reshape(data_size, width_here, 2 * hidden_here),
            jnp.moveaxis(down_local.astype(low).reshape(hidden_here, data_size, width_here), 1, 0),
        ],
        (False,) * 4,
        16,
    )
    qkv_grad = jnp.sum(
        qkv_parts.reshape(heads_here, sharers, width_here, 3, HEAD_DIM).astype(jnp.float32), axis=1
    )
    qkv_grad = jnp.moveaxis(qkv_grad, 0, 2).reshape(qkv_weight.shape)
    out_grad = jnp.sum(
        out_parts.reshape(heads_here, sharers, HEAD_DIM, width_here).astype(jnp.float32), axis=1
    ).reshape(out_weight.shape)
    gate_up_grad = jnp.moveaxis(
        gate_up_parts.reshape(data_size, width_here, 2, hidden_here), 0, 2
    ).reshape(gate_up_weight.shape)
    gate_up_grad = gate_up_grad.astype(jnp.float32)
    down_grad = down_parts.reshape(down_weight.shape).astype(jnp.float32)
    gain_grad = lax.dynamic_slice_in_dim(gain_sums, data_index * width_here, width_here, 1)

    squares = (
        jnp.sum(table_grad * table_grad)
        + jnp.sum(qkv_grad * qkv_grad)
        + jnp.sum(out_grad * out_grad)
        + jnp.sum(gate_up_grad * gate_up_grad)
        + jnp.sum(down_grad * down_grad)
    )
    square_parts = gather_all(jnp.full((8, 128), squares), 17).reshape(devices, 8 * 128)
    grad_norm = jnp.sqrt(jnp.sum(square_parts[:, 0]) + jnp.sum(gain_sums * gain_sums))
    factor = jnp.minimum(1.0, CLIP / (grad_norm + 1e-06))
    table_new = adam_update(
        table, table_first, table_second, table_grad * factor, RATE_MATRIX, DECAY
    )
    qkv_new = adam_update(qkv_weight, qkv_first, qkv_second, qkv_grad * factor, RATE_MATRIX, DECAY)
    out_new = adam_update(out_weight, out_first, out_second, out_grad * factor, RATE_MATRIX, DECAY)
    gate_up_new = adam_update(
        gate_up_weight, gate_up_first, gate_up_second, gate_up_grad * factor, RATE_MATRIX, DECAY
    )
    down_new = adam_update(
        down_weight, down_first, down_second, down_grad * factor, RATE_MATRIX, DECAY
    )
    gains_new = adam_update(gains, gains_first, gains_second, gain_grad * factor, RATE_GAIN, 0.0)
    return (
        loss_sums,
        counts,
        grad_norm,
        *table_new,
        *qkv_new,
        *out_new,
        *gate_up_new,
        *down_new,
        *gains_new,
    )


def solution(mesh):
    rows, sides, cols, gain = P(BOTH, None), P("dp", None, "mp"), P("mp", "dp"), P(None, "dp")
    state = (rows,) * 3 + (sides,) * 3 + (cols,) * 3 + (sides,) * 3 + (cols,) * 3 + (gain,) * 3
    return jax.shard_map(
        body,
        mesh=mesh,
        in_specs=(P("dp"), P("dp"), P(None, "dp")) + state,
        out_specs=(P(), P(), P()) + state,
        check_vma=False,
    )
```

```python
import functools
import math

import jax
import jax.numpy as jnp
from jax import lax
from jax.experimental import pallas as pl
from jax.experimental.layout import Layout, with_layout_constraint
from jax.experimental.pallas import tpu as pltpu
from jax.sharding import PartitionSpec as P

HEAD_DIM = 128
R_DEV = 64
STEP = 10


EPS_NORM = 1e-05
BETA_ONE = 0.9
BETA_TWO = 0.95
ADAM_EPS = 1e-08
DECAY = 0.1
RATE_MATRIX = 0.02
RATE_GAIN = 1.0
CLIP = 0.02
EXIT_SCALE = (1.0 / 3.0, 2.0 / 3.0)
NEG = -1e30
BOTH = ("dp", "mp")
MESH = pl.DeviceIdType.MESH
VMEM_LIMIT = 60 * 1024 * 1024
ANY = pl.BlockSpec(memory_space=pl.ANY)
GROUP = 16


def kernel_mesh():
    return lax.axis_size("dp") == 8 and lax.axis_size("mp") == 4


def comm_params(ident):
    return pltpu.CompilerParams(
        collective_id=ident, has_side_effects=True, vmem_limit_bytes=VMEM_LIMIT
    )


class Links:
    def __init__(self, send_sem, recv_sem, cargo):
        data_index, model_index = lax.axis_index("dp"), lax.axis_index("mp")
        z, y, x, c = data_index // 2, data_index % 2, model_index // 2, model_index % 2
        self.c = c
        self.zs = (z, z + 1 - 2 * (z % 2), (z + 2) % 4, 3 - z)
        self.corners = ((y, x), (y, 1 - x), (1 - y, x), (1 - y, 1 - x))
        self.z_side = [(zd * 2 + y, model_index) for zd in self.zs]
        self.x_side = (data_index, (1 - x) * 2 + c)
        self.y_side = (z * 2 + 1 - y, model_index)
        self.c_side = (data_index, x * 2 + 1 - c)
        self.send_sem, self.recv_sem, self.sent, self.slots = send_sem, recv_sem, [], {}
        peers = self.z_side[1:] + [self.x_side, self.y_side, self.c_side]
        if cargo:
            peers += [(zd * 2 + 1 - y, model_index) for zd in self.zs[1:]]
        barrier = pltpu.get_barrier_semaphore()
        for peer in peers:
            pl.semaphore_signal(barrier, inc=1, device_id=peer, device_id_type=MESH)
        pl.semaphore_wait(barrier, len(peers))

    def first_row(self, rows, d, group, core=0):
        y, x = self.corners[group]
        c = 1 - self.c if core else self.c
        return ((self.zs[d] * 2 + y) * 4 + x * 2 + c) * rows

    def recv(self, name):
        return self.recv_sem.at[self.slots.setdefault(name, len(self.slots))]

    def send(self, source, target, device, name):
        copy = pltpu.make_async_remote_copy(
            src_ref=source,
            dst_ref=target,
            send_sem=self.send_sem.at[len(self.sent)],
            recv_sem=self.recv(name),
            device_id=device,
            device_id_type=MESH,
        )
        copy.start()
        self.sent.append(copy)

    def arrived(self, ref, name):
        pltpu.make_async_copy(ref, ref, self.recv(name)).wait()
        return ref

    def finish(self):
        for copy in self.sent:
            copy.wait_send()


class Cargo:
    def __init__(self, source, target, send_sem, recv_sem, own_sem):
        self.me, self.model_index = lax.axis_index("dp"), lax.axis_index("mp")
        self.source, self.target = source, target
        self.send_sem, self.recv_sem, self.own_sem, self.sent = send_sem, recv_sem, own_sem, []

    def block(self, ref, index):
        if len(ref.shape) == 3:
            return ref.at[index]
        size = ref.shape[1] // 8
        return ref.at[:, pl.ds(pl.multiple_of(index * size, size), size)]

    def start(self):
        self.own = pltpu.make_async_copy(
            self.block(self.source, self.me), self.block(self.target, self.me), self.own_sem
        )
        self.own.start()
        for shift in (4, 3, 5, 2, 6, 1, 7):
            peer = lax.rem(self.me + shift, 8)
            copy = pltpu.make_async_remote_copy(
                src_ref=self.block(self.source, peer),
                dst_ref=self.block(self.target, self.me),
                send_sem=self.send_sem.at[shift - 1],
                recv_sem=self.recv_sem.at[shift - 1],
                device_id=(peer, self.model_index),
                device_id_type=MESH,
            )
            copy.start()
            self.sent.append(copy)

    def finish(self):
        self.own.wait()
        for shift in range(1, 8):
            here = self.block(self.target, lax.rem(self.me + 8 - shift, 8))
            pltpu.make_async_copy(here, here, self.recv_sem.at[shift - 1]).wait()
        for copy in self.sent:
            copy.wait_send()


def swapped(shape):
    if len(shape) == 3:
        return (shape[1], shape[0] * shape[2])
    return (8, shape[0], shape[1] // 8)


class Gather:
    def __init__(self, link, out, steps, own_sem):
        self.link, self.out, self.steps, self.own_sem = link, out, steps, own_sem
        self.owns = []

    def spot(self, g, d, group, core=0):
        rows = self.steps * GROUP
        start = self.link.first_row(rows, d, group, core) + g * GROUP
        return self.out.at[pl.ds(pl.multiple_of(start, GROUP), GROUP)]

    def send(self, g, source, device, here, there):
        self.link.send(source, self.spot(g, *here), device, ("gather", g, *there))

    def arrived(self, g, d, group, core):
        return self.link.arrived(self.spot(g, d, group, core), ("gather", g, d, group, core))

    def begin(self, g, source):
        link = self.link
        own = pltpu.make_async_copy(source, self.spot(g, 0, 0), self.own_sem.at[g])
        own.start()
        self.owns.append(own)
        for d in (1, 2, 3):
            self.send(g, source, link.z_side[d], (0, 0), (d, 0, 0))
        self.send(g, source, link.x_side, (0, 0), (0, 1, 0))
        self.send(g, source, link.y_side, (0, 0), (0, 2, 0))
        self.send(g, source, link.c_side, (0, 0), (0, 0, 1))

    def from_z(self, g, d):
        here = self.arrived(g, d, 0, 0)
        self.send(g, here, self.link.x_side, (d, 0), (d, 1, 0))
        self.send(g, here, self.link.y_side, (d, 0), (d, 2, 0))
        self.send(g, here, self.link.c_side, (d, 0), (d, 0, 1))

    def from_sides(self, g, d):
        for group, side in ((1, self.link.y_side), (2, self.link.x_side)):
            here = self.arrived(g, d, group, 0)
            if (d % 2 == 0) == (group == 1):
                self.send(g, here, side, (d, group), (d, 3, 0))
            self.send(g, here, self.link.c_side, (d, group), (d, group, 1))

    def first(self, g):
        self.from_z(g, 1)
        self.from_sides(g, 0)
        self.from_z(g, 2)
        self.from_z(g, 3)

    def second(self, g):
        for d in (1, 2, 3):
            self.from_sides(g, d)

    def third(self, g):
        for d in range(4):
            here = self.arrived(g, d, 3, 0)
            self.send(g, here, self.link.c_side, (d, 3), (d, 3, 1))

    def finish(self):
        for g in range(self.steps):
            for d in range(4):
                for group in range(4):
                    self.arrived(g, d, group, 1)
        for own in self.owns:
            own.wait()


CORNER = [(d, 3) for d in range(4)]
SIDES = [(1, 1), (3, 1), (0, 2), (2, 2), (0, 1), (2, 1), (1, 2), (3, 2)]
COLUMN = [(d, 0) for d in (3, 2, 1)]


class Scatter:
    def __init__(self, link, partial, rows, order, buffers, own_sem):
        self.link, self.partial, self.rows = link, partial, rows
        self.mine, self.core, self.corner, self.side, self.column = buffers
        self.owns = {}
        for p in order:
            for d, group in CORNER + SIDES + COLUMN + [(0, 0)]:
                k = d * 4 + group
                here = self.mine.at[k, pl.ds(p * GROUP, GROUP)]
                own = pltpu.make_async_copy(self.spot(p, d, group), here, own_sem.at[p * 16 + k])
                own.start()
                self.owns[p, k] = own
                self.send(p, self.spot(p, d, group, 1), self.core, k, link.c_side, "core")

    def spot(self, p, d, group, core=0):
        start = self.link.first_row(self.rows, d, group, core) + p * GROUP
        return self.partial.at[pl.ds(pl.multiple_of(start, GROUP), GROUP)]

    def send(self, p, source, buffer, k, device, name):
        self.link.send(source, buffer.at[k, pl.ds(p * GROUP, GROUP)], device, (name, p, k))

    def term(self, p, buffer, k, name):
        return self.link.arrived(buffer.at[k, pl.ds(p * GROUP, GROUP)], (name, p, k))[...].astype(
            jnp.float32
        )

    def start_terms(self, p, k):
        self.owns[p, k].wait()
        own = self.mine[k, pl.ds(p * GROUP, GROUP)].astype(jnp.float32)
        return own + self.term(p, self.core, k, "core")

    def pass_on(self, p, k, total, buffer, there, device, name):
        here = self.mine.at[k, pl.ds(p * GROUP, GROUP)]
        here[...] = total.astype(here.dtype)
        self.send(p, here, buffer, there, device, name)

    def to_corner(self, p):
        for d, _ in CORNER:
            side = self.link.y_side if d % 2 == 0 else self.link.x_side
            k = d * 4 + 3
            self.pass_on(p, k, self.start_terms(p, k), self.corner, d, side, "corner")

    def to_sides(self, p):
        for d, group in SIDES:
            k = d * 4 + group
            total = self.start_terms(p, k)
            if (d % 2 == 0) == (group == 1):
                total = total + self.term(p, self.corner, d, "corner")
            side = self.link.x_side if group == 1 else self.link.y_side
            self.pass_on(p, k, total, self.side, d * 2 + group - 1, side, "side")

    def column_terms(self, p, d):
        total = self.start_terms(p, d * 4)
        for k in (d * 2, d * 2 + 1):
            total = total + self.term(p, self.side, k, "side")
        return total

    def to_column(self, p):
        for d, _ in COLUMN:
            total = self.column_terms(p, d)
            self.pass_on(p, d * 4, total, self.column, d - 1, self.link.z_side[d], "column")

    def total(self, p):
        total = self.column_terms(p, 0)
        for d in (1, 2, 3):
            total = total + self.term(p, self.column, d - 1, "column")
        return total


def relay_kernel(plan, row_step, *refs):
    refs = list(refs)

    def take(count):
        taken = refs[:count]
        del refs[:count]
        return taken

    (partial,) = take(1)
    ready = take(plan["ready"])
    extras = take(plan["extras"])
    cargo_in = take(plan["cargo"])
    (gathered,) = take(1)
    kept = take(plan["kept"])
    sums = take(plan["sums"])
    cargo_out = take(plan["cargo"])
    buffers = take(5)
    held, send_sem, recv_sem, load_sem, own_sem = take(5)
    order, steps = plan["order"], plan["steps"]
    link = Links(send_sem, recv_sem, plan["cargo"])
    cargo = Cargo(*cargo_in, *cargo_out, *refs) if cargo_in else None
    gather = Gather(link, gathered, steps, own_sem)
    if ready:
        gather.begin(0, ready[0])
    scatter = Scatter(link, partial, plan["rows"], order, buffers, load_sem)
    if cargo:
        cargo.start()
    ticks = len(order) + 7
    agenda = [[] for _ in range(ticks)]
    if ready:
        for tick, step in enumerate((gather.first, gather.second, gather.third)):
            agenda[tick + 2].append((step, 0))

    def last(p):
        rows, keeps, adds = row_step(p, scatter.total(p), extras)
        for ref, value in zip(kept, keeps):
            ref[pl.ds(p * GROUP, GROUP)] = value
        for ref, value in zip(sums, adds):
            ref[...] = value if p == order[0] else ref[...] + value
        if rows is not None:
            g = plan["slot"](p)
            held[g] = rows
            gather.begin(g, held.at[g])

    for q, p in enumerate(order):
        for tick, step in enumerate(
            (scatter.to_corner, scatter.to_sides, scatter.to_column, last)
        ):
            agenda[q + tick].append((step, p))
        if plan["slot"](p) is not None:
            for tick, step in enumerate((gather.first, gather.second, gather.third)):
                agenda[q + 4 + tick].append((step, plan["slot"](p)))
    for tick in agenda:
        for step, index in tick:
            step(index)
    gather.finish()
    link.finish()
    if cargo:
        cargo.finish()


def relay(
    partial, row_step, ident, extras=(), kept=0, sums=0, order=None, slot=None, ready=None, cargo=None
):
    rows, width = partial.shape[0] // (lax.axis_size("dp") * lax.axis_size("mp")), partial.shape[1]
    groups = rows // GROUP
    order = list(range(groups)) if order is None else order
    slot = slot or (lambda p: p)
    steps = sum(slot(p) is not None for p in order) + (ready is not None)
    if not kernel_mesh():
        total = lax.psum_scatter(partial, BOTH, scatter_dimension=0, tiled=True)
        total = total.astype(jnp.float32)
        outs, keeps, adds = [None] * steps, [None] * groups, [0.0] * sums
        if ready is not None:
            outs[0] = ready
        for p in order:
            out, keeps[p], add = row_step(p, total[p * GROUP : (p + 1) * GROUP], extras)
            adds = [one + two for one, two in zip(adds, add)]
            if out is not None:
                outs[slot(p)] = out
        gathered = lax.all_gather(jnp.concatenate(outs), BOTH, axis=0, tiled=True)
        keeps = [jnp.concatenate(parts) for parts in zip(*keeps)]
        moved = [] if cargo is None else [exchange_plain(cargo)]
        return [gathered, *keeps, *adds, *moved]
    plan = dict(
        rows=rows,
        order=order,
        slot=slot,
        steps=steps,
        ready=int(ready is not None),
        extras=len(extras),
        cargo=int(cargo is not None),
        kept=kept,
        sums=sums,
    )
    low = partial.dtype
    vmem = pl.BlockSpec(memory_space=pltpu.VMEM)
    load = [] if cargo is None else [cargo]
    copies = 31 * (groups + steps)
    shapes = [jax.ShapeDtypeStruct((32 * steps * GROUP, width), low)]
    shapes += [jax.ShapeDtypeStruct((rows, width), jnp.float32)] * kept
    shapes += [jax.ShapeDtypeStruct((1, width), jnp.float32)] * sums
    shapes += [jax.ShapeDtypeStruct(swapped(value.shape), value.dtype) for value in load]
    buffers = [pltpu.VMEM((count, rows, width), low) for count in (16, 16, 4, 8, 3)]
    semaphores = [pltpu.SemaphoreType.DMA((count,)) for count in (copies, copies, 16 * groups, steps)]
    semaphores += [pltpu.SemaphoreType.DMA((7,))] * 2 * len(load)
    semaphores += [pltpu.SemaphoreType.DMA] * len(load)
    return pl.pallas_call(
        functools.partial(relay_kernel, plan, row_step),
        out_shape=shapes,
        in_specs=[ANY] * (1 + plan["ready"]) + [vmem] * len(extras) + [ANY] * len(load),
        out_specs=[ANY] + [vmem] * (kept + sums) + [ANY] * len(load),
        scratch_shapes=buffers + [pltpu.VMEM((steps, GROUP, width), low)] + semaphores,
        compiler_params=comm_params(ident),
    )(partial, *([] if ready is None else [ready]), *extras, *load)


def exchange_plain(value):
    count = lax.axis_size("dp")
    if len(value.shape) == 3:
        moved = lax.all_to_all(value, "dp", split_axis=0, concat_axis=0, tiled=True)
        return jnp.moveaxis(moved, 0, 1).reshape(value.shape[1], -1)
    parts = jnp.moveaxis(value.reshape(value.shape[0], count, -1), 1, 0)
    return lax.all_to_all(parts, "dp", split_axis=0, concat_axis=0, tiled=True)


def small_gather_kernel(x_ref, o_ref, send_sem, recv_sem, own_sem):
    data_index, model_index = lax.axis_index("dp"), lax.axis_index("mp")
    me = data_index * 4 + model_index
    own = pltpu.make_async_copy(x_ref, o_ref.at[me], own_sem)
    own.start()
    peers = [lax.rem(me + shift, 32) for shift in range(1, 32)]
    barrier = pltpu.get_barrier_semaphore()
    for peer in peers:
        pl.semaphore_signal(
            barrier, inc=1, device_id=(peer // 4, peer % 4), device_id_type=MESH
        )
    pl.semaphore_wait(barrier, 31)
    sent = []
    for index, peer in enumerate(peers):
        copy = pltpu.make_async_remote_copy(
            src_ref=x_ref,
            dst_ref=o_ref.at[me],
            send_sem=send_sem.at[index],
            recv_sem=recv_sem.at[index],
            device_id=(peer // 4, peer % 4),
            device_id_type=MESH,
        )
        copy.start()
        sent.append(copy)
    for index in range(31):
        here = o_ref.at[lax.rem(me + 31 - index, 32)]
        pltpu.make_async_copy(here, here, recv_sem.at[index]).wait()
    own.wait()
    for copy in sent:
        copy.wait_send()


def gather_small(value, ident):
    if not kernel_mesh():
        return lax.all_gather(value, BOTH)
    vmem = pl.BlockSpec(memory_space=pltpu.VMEM)
    return pl.pallas_call(
        small_gather_kernel,
        out_shape=jax.ShapeDtypeStruct((32,) + value.shape, value.dtype),
        in_specs=[vmem],
        out_specs=vmem,
        scratch_shapes=[
            pltpu.SemaphoreType.DMA((31,)),
            pltpu.SemaphoreType.DMA((31,)),
            pltpu.SemaphoreType.DMA,
        ],
        compiler_params=comm_params(ident),
    )(value)


def greet(peers):
    barrier = pltpu.get_barrier_semaphore()
    for peer in peers:
        pl.semaphore_signal(barrier, inc=1, device_id=peer, device_id_type=MESH)
    pl.semaphore_wait(barrier, len(peers))


def exchange_kernel(count, whole, *refs):
    ins, outs = refs[: len(whole)], refs[len(whole) : 2 * len(whole)]
    send_sem, recv_sem, own_sem = refs[2 * len(whole) :]
    me, model_index = lax.axis_index("dp"), lax.axis_index("mp")
    peers = [lax.rem(me + shift, count) for shift in range(1, count)]
    greet([(peer, model_index) for peer in peers])
    owns, sent = [], []
    for array, keep in enumerate(whole):
        own = pltpu.make_async_copy(
            ins[array] if keep else ins[array].at[me], outs[array].at[me], own_sem.at[array]
        )
        own.start()
        owns.append(own)
        for shift in range(count - 1):
            copy = pltpu.make_async_remote_copy(
                src_ref=ins[array] if keep else ins[array].at[peers[shift]],
                dst_ref=outs[array].at[me],
                send_sem=send_sem.at[array, shift],
                recv_sem=recv_sem.at[array, shift],
                device_id=(peers[shift], model_index),
                device_id_type=MESH,
            )
            copy.start()
            sent.append(copy)
    for own in owns:
        own.wait()
    for array in range(len(whole)):
        for shift in range(count - 1):
            source = lax.rem(me + count - 1 - shift, count)
            here = outs[array].at[source]
            pltpu.make_async_copy(here, here, recv_sem.at[array, shift]).wait()
    for copy in sent:
        copy.wait_send()


def exchange(values, whole, ident):
    count = lax.axis_size("dp")
    if not kernel_mesh():
        return [
            lax.all_gather(value, "dp")
            if keep
            else lax.all_to_all(value, "dp", split_axis=0, concat_axis=0, tiled=True)
            for value, keep in zip(values, whole)
        ]
    shapes = [
        jax.ShapeDtypeStruct(((count,) if keep else ()) + value.shape, value.dtype)
        for value, keep in zip(values, whole)
    ]
    return pl.pallas_call(
        functools.partial(exchange_kernel, count, tuple(whole)),
        out_shape=shapes,
        in_specs=[ANY] * len(values),
        out_specs=[ANY] * len(values),
        scratch_shapes=[
            pltpu.SemaphoreType.DMA((len(values), count - 1)),
            pltpu.SemaphoreType.DMA((len(values), count - 1)),
            pltpu.SemaphoreType.DMA((len(values),)),
        ],
        compiler_params=comm_params(ident),
    )(*values)


def norm_fwd(values, gain):
    row_scale = lax.rsqrt(jnp.mean(values * values, axis=-1, keepdims=True) + EPS_NORM)
    unit_rows = values * row_scale
    return (unit_rows * gain, unit_rows, row_scale)


def norm_back(unit_rows, row_scale, gain, gradient):
    weighted = gradient * gain
    back_rows = row_scale * (
        weighted - unit_rows * jnp.mean(weighted * unit_rows, axis=-1, keepdims=True)
    )
    return (back_rows, jnp.sum(gradient * unit_rows, axis=0))


def rotary(places, width):
    half_width = width // 2
    frequency = jnp.exp(
        jnp.arange(half_width, dtype=jnp.float32) * (-math.log(10000.0) / half_width)
    )
    angles = places.astype(jnp.float32)[:, None] * frequency[None, :]
    return (jnp.cos(angles), jnp.sin(angles))


def rotate_pairs(values, cosine, sine_table):
    half_width = values.shape[-1] // 2
    front_half = values[..., :half_width]
    back_half = values[..., half_width:]
    return jnp.concatenate(
        [
            front_half * cosine - back_half * sine_table,
            back_half * cosine + front_half * sine_table,
        ],
        axis=-1,
    )


def dot(left, right, left_dim=1, right_dim=0):
    return lax.dot_general(
        left, right, (((left_dim,), (right_dim,)), ((), ())), preferred_element_type=jnp.float32
    )


def placed(value, order):
    return with_layout_constraint(value, Layout(major_to_minor=order))


def adam_update(weight, moment_one, moment_two, gradient, rate, decay):
    moment_one = BETA_ONE * moment_one + (1.0 - BETA_ONE) * gradient
    moment_two = BETA_TWO * moment_two + (1.0 - BETA_TWO) * gradient * gradient
    ratio = (
        moment_one
        / (1.0 - BETA_ONE**STEP)
        / (jnp.sqrt(moment_two / (1.0 - BETA_TWO**STEP)) + ADAM_EPS)
    )
    return (weight - rate * (ratio + decay * weight), moment_one, moment_two)


def body(
    token_ids,
    target_ids,
    exit_mask,
    table,
    table_first,
    table_second,
    qkv_weight,
    qkv_first,
    qkv_second,
    out_weight,
    out_first,
    out_second,
    gate_up_weight,
    gate_up_first,
    gate_up_second,
    down_weight,
    down_first,
    down_second,
    gains,
    gains_first,
    gains_second,
):
    low = jnp.bfloat16
    data_size, model_size = lax.axis_size("dp"), lax.axis_size("mp")
    data_index, model_index = lax.axis_index("dp"), lax.axis_index("mp")
    devices = data_size * model_size
    block_rows = token_ids.shape[0]
    tokens = block_rows * data_size
    width = table.shape[1]
    width_here = qkv_weight.shape[0]
    heads_here = qkv_weight.shape[2] // HEAD_DIM
    hidden_here = down_weight.shape[0] // data_size
    vocab_here = table.shape[0]
    device_index = data_index * model_size + model_index
    vocab_ids = device_index * vocab_here + jnp.arange(vocab_here, dtype=jnp.int32)
    score_scale = 1.0 / math.sqrt(HEAD_DIM)

    sharers = data_size // heads_here
    shares = sharers // 2
    share_slots = data_size // shares * R_DEV
    exit_here = data_index % sharers % 2
    share_here = data_index % sharers // 2
    slots_here = R_DEV // model_size
    rows_here = block_rows // model_size

    ints, gain_low = exchange(
        [
            jnp.concatenate([token_ids[None], target_ids[None], exit_mask]),
            jnp.pad(gains.astype(low), ((0, 13), (0, 0))),
        ],
        (True, True),
        0,
    )
    gain_rows = jnp.moveaxis(gain_low[:, :3], 0, 1).reshape(3, width).astype(jnp.float32)
    all_ids = ints[:, 0].reshape(tokens)
    mask_blocks = jnp.moveaxis(ints[:, 2:], 0, 1)
    slot_ids = jnp.arange(R_DEV, dtype=jnp.int32)
    slot_ranks = jnp.cumsum(mask_blocks, axis=2) - 1
    pick_int = (
        (slot_ranks[:, :, None, :] == slot_ids[:, None]) & (mask_blocks[:, :, None, :] == 1)
    ).astype(jnp.int32)
    pick_low = pick_int.astype(low)
    token_places = jnp.arange(tokens, dtype=jnp.int32)
    slot_targets = jnp.sum(pick_int * ints[:, 1][None, :, None, :], axis=3).reshape(2, -1)
    slot_places = jnp.sum(
        pick_int * token_places.reshape(1, data_size, 1, block_rows), axis=3
    ).reshape(2, -1)
    live = (slot_ids < jnp.sum(mask_blocks, axis=2)[:, :, None]).astype(jnp.float32).reshape(2, -1)
    counts = jnp.sum(live, axis=1)

    head_rows = jnp.moveaxis(
        qkv_weight.astype(low).reshape(width_here, 3, heads_here, HEAD_DIM), 0, 3
    )
    head_rows = jnp.concatenate(
        [
            jnp.moveaxis(head_rows, 0, 1).reshape(heads_here, 3 * HEAD_DIM, width_here),
            out_weight.astype(low).reshape(heads_here, HEAD_DIM, width_here),
        ],
        axis=1,
    )
    hidden_rows = jnp.moveaxis(
        gate_up_weight.astype(low).reshape(width_here, 2, data_size, hidden_here), 0, 3
    )
    hidden_rows = jnp.concatenate(
        [
            jnp.moveaxis(hidden_rows, 0, 1).reshape(data_size, 2 * hidden_here, width_here),
            down_weight.astype(low).reshape(data_size, hidden_here, width_here),
        ],
        axis=1,
    )

    table_low = table.astype(low)
    id_hits = (all_ids[:, None] == vocab_ids[None, :]).astype(low)
    resid_low, head_rows = relay(
        dot(id_hits, table_low).astype(low),
        lambda p, total, extras: (total.astype(low), (), ()),
        1,
        cargo=jnp.repeat(head_rows, sharers, axis=0),
    )
    qkv_head, out_head = head_rows[: 3 * HEAD_DIM], head_rows[3 * HEAD_DIM :]
    attn_low = norm_fwd(resid_low.astype(jnp.float32), gain_rows[0])[0].astype(low)

    projected = dot(attn_low, qkv_head, 1, 1)
    cosine, sine_table = rotary(token_places, HEAD_DIM)
    query_low = rotate_pairs(projected[:, :HEAD_DIM], cosine, sine_table).astype(low)
    key_low = rotate_pairs(projected[:, HEAD_DIM : 2 * HEAD_DIM], cosine, sine_table).astype(low)
    value_low = projected[:, 2 * HEAD_DIM :].astype(low)
    pick_share = lax.dynamic_slice_in_dim(
        lax.dynamic_index_in_dim(pick_low, exit_here, 0, keepdims=False),
        share_here * (data_size // shares),
        data_size // shares,
        0,
    )
    query_share = lax.dynamic_slice_in_dim(
        query_low.reshape(data_size, block_rows, HEAD_DIM),
        share_here * (data_size // shares),
        data_size // shares,
        0,
    )
    query_slots = (
        jnp.einsum("brt,btd->brd", pick_share, query_share, preferred_element_type=jnp.float32)
        .astype(low)
        .reshape(share_slots, HEAD_DIM)
    )

    def share_of(per_slot):
        return lax.dynamic_slice(per_slot, (exit_here, share_here * share_slots), (1, share_slots))[
            0
        ]

    places_share, live_share = share_of(slot_places), share_of(live)
    scores = dot(query_slots, key_low, 1, 1) * score_scale
    allowed = token_places[None, :] <= places_share[:, None]
    scores = jnp.where(allowed, scores, NEG)
    weights = jnp.exp(scores - jnp.max(scores, axis=-1, keepdims=True))
    probs = weights / jnp.sum(weights, axis=-1, keepdims=True)
    probs_low = probs.astype(low)
    attn_out = (dot(probs_low, value_low) * live_share[:, None]).astype(low)

    def spread(per_share):
        if shares > 1:
            full = jnp.zeros((data_size * R_DEV, width), per_share.dtype)
            per_share = lax.dynamic_update_slice_in_dim(
                full, per_share, share_here * share_slots, 0
            )
        exits = jnp.arange(2, dtype=jnp.int32)[None, :, None, None]
        rows = per_share.reshape(devices, 1, slots_here, width)
        return jnp.where(exits == exit_here, rows, 0).reshape(-1, width)

    block_low = lax.dynamic_slice_in_dim(resid_low, data_index * block_rows, block_rows, 0)
    pick_here = lax.dynamic_slice(
        pick_low,
        (0, data_index, model_index * slots_here, 0),
        (2, 1, slots_here, block_rows),
    ).reshape(2 * slots_here, block_rows)

    def first_step(p, total, extras):
        resid = extras[0][p * GROUP : (p + 1) * GROUP] + total
        gain = 2 if p == 0 else 1
        return (norm_fwd(resid, extras[1][gain : gain + 1])[0].astype(low), (resid,), ())

    first_rows, resid_one, hidden_rows = relay(
        spread(dot(attn_out, out_head).astype(low)),
        first_step,
        2,
        extras=[dot(pick_here, block_low), gain_rows],
        kept=1,
        cargo=hidden_rows,
    )
    first_rows = first_rows.reshape(devices, 2, slots_here, width)
    exit_rows_one = first_rows[:, 0].reshape(-1, width)
    mlp_low = first_rows[:, 1].reshape(-1, width)

    gate_up_head, down_head = hidden_rows[: 2 * hidden_here], hidden_rows[2 * hidden_here :]
    gate_up = dot(mlp_low, gate_up_head, 1, 1)
    gate_part, up_part = gate_up[:, :hidden_here], gate_up[:, hidden_here:]
    gate_sigma = jax.nn.sigmoid(gate_part)
    hidden_low = (gate_part * gate_sigma * up_part).astype(low)

    def second_step(p, total, extras):
        resid = extras[0][GROUP : 2 * GROUP] + total
        return (norm_fwd(resid, extras[1][2:3])[0].astype(low), (resid,), ())

    exit_rows_two, resid_two = relay(
        dot(hidden_low, down_head).astype(low), second_step, 3, extras=[resid_one, gain_rows], kept=1
    )

    exit_rows = (exit_rows_one, exit_rows_two)
    logits = [dot(rows, table_low, 1, 1) for rows in exit_rows]
    hits = [slot_targets[e][:, None] == vocab_ids[None, :] for e in range(2)]
    tops = [jnp.max(values, axis=1) for values in logits]
    masses = [jnp.sum(jnp.exp(values - top[:, None]), axis=1) for values, top in zip(logits, tops)]
    found = [jnp.sum(jnp.where(hit, values, 0.0), axis=1) for hit, values in zip(hits, logits)]
    stats = jnp.concatenate(tops + masses + found).reshape(-1, 128)
    stats = gather_small(stats, 4).reshape(devices, 3, 2, -1)
    row_top = jnp.max(stats[:, 0], axis=0)
    row_mass = jnp.sum(stats[:, 1] * jnp.exp(stats[:, 0] - row_top), axis=0)
    row_lse = row_top + jnp.log(row_mass)
    entropy = row_lse - jnp.sum(stats[:, 2], axis=0)
    loss_sums = jnp.sum(entropy * live, axis=1)
    row_weight = live * (jnp.array(EXIT_SCALE, jnp.float32) / counts)[:, None]
    grad_logits = [
        (
            row_weight[e][:, None]
            * (jnp.exp(logits[e] - row_lse[e][:, None]) - hits[e].astype(jnp.float32))
        ).astype(low)
        for e in range(2)
    ]
    table_head = dot(grad_logits[0], exit_rows_one, 0, 0) + dot(grad_logits[1], exit_rows_two, 0, 0)
    row_terms = jnp.stack(
        [
            dot(grad, table_low).astype(low).reshape(devices, slots_here, width)
            for grad in grad_logits
        ],
        axis=1,
    )

    def head_step(p, total, extras):
        values = extras[0][:GROUP] if p == 0 else extras[1][...]
        gain = extras[2][2:3]
        _, unit, scale = norm_fwd(values, gain)
        back, gain_grad = norm_back(unit, scale, gain, total)
        return (None if p == 0 else back.astype(low), (back,), (gain_grad[None],))

    dtwo_low, dexits, final_grad = relay(
        row_terms.reshape(-1, width),
        head_step,
        5,
        extras=[resid_one, resid_two, gain_rows],
        kept=1,
        sums=1,
        order=[1, 0],
        slot=lambda p: None if p == 0 else 0,
    )
    down_local = dot(hidden_low, dtwo_low, 0, 0)
    dhidden = dot(dtwo_low, down_head, 1, 1)
    dgate = dhidden * up_part * gate_sigma * (1.0 + gate_part * (1.0 - gate_sigma))
    dup_part = dhidden * gate_part * gate_sigma
    dgate_up = jnp.concatenate([dgate, dup_part], axis=1).astype(low)
    gate_up_local = dot(dgate_up, mlp_low, 0, 0)

    def mlp_step(p, total, extras):
        gain = extras[2][1:2]
        _, unit, scale = norm_fwd(extras[0][GROUP : 2 * GROUP], gain)
        back, gain_grad = norm_back(unit, scale, gain, total)
        return ((extras[1][GROUP : 2 * GROUP] + back).astype(low), (), (gain_grad[None],))

    done_low, mlp_grad, hidden_parts = relay(
        dot(dgate_up, gate_up_head).astype(low),
        mlp_step,
        6,
        extras=[resid_one, dexits, gain_rows],
        sums=1,
        slot=lambda p: 1,
        ready=dexits[:GROUP].astype(low),
        cargo=jnp.concatenate([gate_up_local.astype(low), down_local.astype(low)]),
    )
    done_low = done_low.reshape(devices, 2, slots_here, width)

    done_share = lax.dynamic_slice(
        lax.dynamic_index_in_dim(done_low, exit_here, 1, keepdims=False).reshape(-1, width),
        (share_here * share_slots, 0),
        (share_slots, width),
    )
    out_local = dot(attn_out, done_share, 0, 0)
    dattn_low = dot(done_share, out_head, 1, 1).astype(low)
    dprobs = dot(dattn_low, value_low, 1, 1)
    delta = jnp.sum(probs * dprobs, axis=-1, keepdims=True)
    dscores = (probs * (dprobs - delta)).astype(low)
    cosine_share, sine_share = rotary(places_share, HEAD_DIM)
    dquery = rotate_pairs(dot(dscores, key_low) * score_scale, cosine_share, -sine_share).astype(
        low
    )
    dquery_share = jnp.einsum(
        "brt,brd->btd",
        pick_share,
        dquery.reshape(-1, R_DEV, HEAD_DIM),
        preferred_element_type=jnp.float32,
    ).astype(low)
    if shares > 1:
        dquery_share = lax.dynamic_update_slice_in_dim(
            jnp.zeros((data_size, block_rows, HEAD_DIM), low),
            dquery_share,
            share_here * (data_size // shares),
            0,
        )
    dkey = rotate_pairs(dot(dscores, query_slots, 0, 0) * score_scale, cosine, -sine_table)
    dvalue = dot(probs_low, dattn_low, 0, 0)
    dprojected = jnp.concatenate(
        [dquery_share.reshape(tokens, HEAD_DIM), dkey.astype(low), dvalue.astype(low)], axis=1
    )
    qkv_local = dot(dprojected, attn_low, 0, 0)

    resid_here = lax.dynamic_slice_in_dim(resid_low, device_index * rows_here, rows_here, 0)
    done_block = lax.dynamic_slice_in_dim(done_low, data_index * model_size, model_size, 0)
    pick_block = lax.dynamic_slice(
        pick_low,
        (0, data_index, 0, model_index * rows_here),
        (2, 1, R_DEV, rows_here),
    ).reshape(2, model_size, slots_here, rows_here)
    dresid_here = jnp.einsum(
        "emst,mesd->td", pick_block, done_block, preferred_element_type=jnp.float32
    )

    def zero_step(p, total, extras):
        at = slice(p * GROUP, (p + 1) * GROUP)
        gain = extras[2][:1]
        _, unit, scale = norm_fwd(extras[0][at], gain)
        back, gain_grad = norm_back(unit, scale, gain, total)
        return ((extras[1][at] + back).astype(low), (), (gain_grad[None],))

    dzero_low, attn_grad, head_parts = relay(
        dot(dprojected, qkv_head).astype(low),
        zero_step,
        7,
        extras=[resid_here.astype(jnp.float32), dresid_here, gain_rows],
        sums=1,
        cargo=jnp.concatenate([qkv_local.astype(low), out_local.astype(low)]),
    )
    table_grad = table_head + dot(id_hits, dzero_low, 0, 0)

    gain_sums = jnp.sum(
        gather_small(
            jnp.concatenate([attn_grad, mlp_grad, final_grad]).reshape(-1, 128), 8
        ).reshape(devices, 3, width),
        axis=0,
    )
    head_grad = jnp.sum(
        head_parts.reshape(heads_here, sharers, 4, HEAD_DIM, width_here).astype(jnp.float32), axis=1
    )
    qkv_grad = placed(jnp.transpose(head_grad[:, :3], (3, 1, 0, 2)).reshape(qkv_weight.shape), (1, 0, 2))
    out_grad = head_grad[:, 3].reshape(out_weight.shape)
    hidden_parts = hidden_parts.astype(jnp.float32)
    gate_up_grad = hidden_parts[:, : 2 * hidden_here].reshape(
        data_size, 2, hidden_here, width_here
    )
    gate_up_grad = placed(
        jnp.transpose(gate_up_grad, (3, 1, 0, 2)).reshape(gate_up_weight.shape), (0, 1, 2)
    )
    down_grad = hidden_parts[:, 2 * hidden_here :].reshape(down_weight.shape)
    gain_grad = lax.dynamic_slice_in_dim(gain_sums, data_index * width_here, width_here, 1)

    squares = (
        jnp.sum(table_grad * table_grad)
        + jnp.sum(qkv_grad * qkv_grad)
        + jnp.sum(out_grad * out_grad)
        + jnp.sum(gate_up_grad * gate_up_grad)
        + jnp.sum(down_grad * down_grad)
    )
    square_parts = gather_small(jnp.full((8, 128), squares), 9)[:, 0, 0]
    grad_norm = jnp.sqrt(jnp.sum(square_parts) + jnp.sum(gain_sums * gain_sums))
    factor = jnp.minimum(1.0, CLIP / (grad_norm + 1e-06))
    table_new = adam_update(
        table, table_first, table_second, table_grad * factor, RATE_MATRIX, DECAY
    )
    qkv_new = adam_update(qkv_weight, qkv_first, qkv_second, qkv_grad * factor, RATE_MATRIX, DECAY)
    out_new = adam_update(out_weight, out_first, out_second, out_grad * factor, RATE_MATRIX, DECAY)
    gate_up_new = adam_update(
        gate_up_weight, gate_up_first, gate_up_second, gate_up_grad * factor, RATE_MATRIX, DECAY
    )
    down_new = adam_update(
        down_weight, down_first, down_second, down_grad * factor, RATE_MATRIX, DECAY
    )
    gains_new = adam_update(gains, gains_first, gains_second, gain_grad * factor, RATE_GAIN, 0.0)
    return (
        loss_sums,
        counts,
        grad_norm,
        *table_new,
        *qkv_new,
        *out_new,
        *gate_up_new,
        *down_new,
        *gains_new,
    )


def solution(mesh):
    rows, sides, cols, gain = P(BOTH, None), P("dp", None, "mp"), P("mp", "dp"), P(None, "dp")
    state = (rows,) * 3 + (sides,) * 3 + (cols,) * 3 + (sides,) * 3 + (cols,) * 3 + (gain,) * 3
    return jax.shard_map(
        body,
        mesh=mesh,
        in_specs=(P("dp"), P("dp"), P(None, "dp")) + state,
        out_specs=(P(), P(), P()) + state,
        check_vma=False,
    )
```

```python
import functools
import math

import jax
import jax.numpy as jnp
from jax import lax
from jax.experimental import pallas as pl
from jax.experimental.layout import Layout, with_layout_constraint
from jax.experimental.pallas import tpu as pltpu
from jax.sharding import PartitionSpec as P

HEAD_DIM = 128
R_DEV = 64
STEP = 10


EPS_NORM = 1e-05
BETA_ONE = 0.9
BETA_TWO = 0.95
ADAM_EPS = 1e-08
DECAY = 0.1
RATE_MATRIX = 0.02
RATE_GAIN = 1.0
CLIP = 0.02
EXIT_SCALE = (1.0 / 3.0, 2.0 / 3.0)
NEG = -1e30
BOTH = ("dp", "mp")
MESH = pl.DeviceIdType.MESH
VMEM_LIMIT = 60 * 1024 * 1024
ANY = pl.BlockSpec(memory_space=pl.ANY)
GROUP = 16


def kernel_mesh():
    return lax.axis_size("dp") == 8 and lax.axis_size("mp") == 4


def comm_params(ident):
    return pltpu.CompilerParams(
        collective_id=ident, has_side_effects=True, vmem_limit_bytes=VMEM_LIMIT
    )


class Links:
    def __init__(self, send_sem, recv_sem):
        data_index, model_index = lax.axis_index("dp"), lax.axis_index("mp")
        z, y, x, c = data_index // 2, data_index % 2, model_index // 2, model_index % 2
        self.c = c
        self.zs = (z, z + 1 - 2 * (z % 2), (z + 2) % 4, 3 - z)
        self.corners = ((y, x), (y, 1 - x), (1 - y, x), (1 - y, 1 - x))
        self.z_side = [(zd * 2 + y, model_index) for zd in self.zs]
        self.x_side = (data_index, (1 - x) * 2 + c)
        self.y_side = (z * 2 + 1 - y, model_index)
        self.c_side = (data_index, x * 2 + 1 - c)
        self.send_sem, self.recv_sem, self.sent, self.slots = send_sem, recv_sem, [], {}
        peers = self.z_side[1:] + [self.x_side, self.y_side, self.c_side]
        barrier = pltpu.get_barrier_semaphore()
        for peer in peers:
            pl.semaphore_signal(barrier, inc=1, device_id=peer, device_id_type=MESH)
        pl.semaphore_wait(barrier, len(peers))

    def first_row(self, rows, d, group, core=0):
        y, x = self.corners[group]
        c = 1 - self.c if core else self.c
        return ((self.zs[d] * 2 + y) * 4 + x * 2 + c) * rows

    def recv(self, name):
        return self.recv_sem.at[self.slots.setdefault(name, len(self.slots))]

    def send(self, source, target, device, name):
        copy = pltpu.make_async_remote_copy(
            src_ref=source,
            dst_ref=target,
            send_sem=self.send_sem.at[len(self.sent)],
            recv_sem=self.recv(name),
            device_id=device,
            device_id_type=MESH,
        )
        copy.start()
        self.sent.append(copy)

    def arrived(self, ref, name):
        pltpu.make_async_copy(ref, ref, self.recv(name)).wait()
        return ref

    def finish(self):
        for copy in self.sent:
            copy.wait_send()


class Gather:
    def __init__(self, link, out, steps, own_sem):
        self.link, self.out, self.steps, self.own_sem = link, out, steps, own_sem
        self.owns = []

    def spot(self, g, d, group, core=0):
        rows = self.steps * GROUP
        start = self.link.first_row(rows, d, group, core) + g * GROUP
        return self.out.at[pl.ds(pl.multiple_of(start, GROUP), GROUP)]

    def send(self, g, source, device, here, there):
        self.link.send(source, self.spot(g, *here), device, ("gather", g, *there))

    def arrived(self, g, d, group, core):
        return self.link.arrived(self.spot(g, d, group, core), ("gather", g, d, group, core))

    def begin(self, g, source):
        link = self.link
        own = pltpu.make_async_copy(source, self.spot(g, 0, 0), self.own_sem.at[g])
        own.start()
        self.owns.append(own)
        for d in (1, 2, 3):
            self.send(g, source, link.z_side[d], (0, 0), (d, 0, 0))
        self.send(g, source, link.x_side, (0, 0), (0, 1, 0))
        self.send(g, source, link.y_side, (0, 0), (0, 2, 0))
        self.send(g, source, link.c_side, (0, 0), (0, 0, 1))

    def from_z(self, g, d):
        here = self.arrived(g, d, 0, 0)
        self.send(g, here, self.link.x_side, (d, 0), (d, 1, 0))
        self.send(g, here, self.link.y_side, (d, 0), (d, 2, 0))
        self.send(g, here, self.link.c_side, (d, 0), (d, 0, 1))

    def from_sides(self, g, d):
        for group, side in ((1, self.link.y_side), (2, self.link.x_side)):
            here = self.arrived(g, d, group, 0)
            if (d % 2 == 0) == (group == 1):
                self.send(g, here, side, (d, group), (d, 3, 0))
            self.send(g, here, self.link.c_side, (d, group), (d, group, 1))

    def first(self, g):
        self.from_z(g, 1)
        self.from_sides(g, 0)
        self.from_z(g, 2)
        self.from_z(g, 3)

    def second(self, g):
        for d in (1, 2, 3):
            self.from_sides(g, d)

    def third(self, g):
        for d in range(4):
            here = self.arrived(g, d, 3, 0)
            self.send(g, here, self.link.c_side, (d, 3), (d, 3, 1))

    def finish(self):
        for g in range(self.steps):
            for d in range(4):
                for group in range(4):
                    self.arrived(g, d, group, 1)
        for own in self.owns:
            own.wait()


CORNER = [(d, 3) for d in range(4)]
SIDES = [(1, 1), (3, 1), (0, 2), (2, 2), (0, 1), (2, 1), (1, 2), (3, 2)]
COLUMN = [(d, 0) for d in (3, 2, 1)]


class Scatter:
    def __init__(self, link, partial, rows, order, buffers, own_sem):
        self.link, self.partial, self.rows = link, partial, rows
        self.mine, self.core, self.corner, self.side, self.column = buffers
        self.owns = {}
        for p in order:
            for d, group in CORNER + SIDES + COLUMN + [(0, 0)]:
                k = d * 4 + group
                here = self.mine.at[k, pl.ds(p * GROUP, GROUP)]
                own = pltpu.make_async_copy(self.spot(p, d, group), here, own_sem.at[p * 16 + k])
                own.start()
                self.owns[p, k] = own
                self.send(p, self.spot(p, d, group, 1), self.core, k, link.c_side, "core")

    def spot(self, p, d, group, core=0):
        start = self.link.first_row(self.rows, d, group, core) + p * GROUP
        return self.partial.at[pl.ds(pl.multiple_of(start, GROUP), GROUP)]

    def send(self, p, source, buffer, k, device, name):
        self.link.send(source, buffer.at[k, pl.ds(p * GROUP, GROUP)], device, (name, p, k))

    def term(self, p, buffer, k, name):
        return self.link.arrived(buffer.at[k, pl.ds(p * GROUP, GROUP)], (name, p, k))[...].astype(
            jnp.float32
        )

    def start_terms(self, p, k):
        self.owns[p, k].wait()
        own = self.mine[k, pl.ds(p * GROUP, GROUP)].astype(jnp.float32)
        return own + self.term(p, self.core, k, "core")

    def pass_on(self, p, k, total, buffer, there, device, name):
        here = self.mine.at[k, pl.ds(p * GROUP, GROUP)]
        here[...] = total.astype(here.dtype)
        self.send(p, here, buffer, there, device, name)

    def to_corner(self, p):
        for d, _ in CORNER:
            side = self.link.y_side if d % 2 == 0 else self.link.x_side
            k = d * 4 + 3
            self.pass_on(p, k, self.start_terms(p, k), self.corner, d, side, "corner")

    def to_sides(self, p):
        for d, group in SIDES:
            k = d * 4 + group
            total = self.start_terms(p, k)
            if (d % 2 == 0) == (group == 1):
                total = total + self.term(p, self.corner, d, "corner")
            side = self.link.x_side if group == 1 else self.link.y_side
            self.pass_on(p, k, total, self.side, d * 2 + group - 1, side, "side")

    def column_terms(self, p, d):
        total = self.start_terms(p, d * 4)
        for k in (d * 2, d * 2 + 1):
            total = total + self.term(p, self.side, k, "side")
        return total

    def to_column(self, p):
        for d, _ in COLUMN:
            total = self.column_terms(p, d)
            self.pass_on(p, d * 4, total, self.column, d - 1, self.link.z_side[d], "column")

    def total(self, p):
        total = self.column_terms(p, 0)
        for d in (1, 2, 3):
            total = total + self.term(p, self.column, d - 1, "column")
        return total


def relay_kernel(plan, row_step, *refs):
    refs = list(refs)

    def take(count):
        taken = refs[:count]
        del refs[:count]
        return taken

    (partial,) = take(1)
    ready = take(plan["ready"])
    extras = take(plan["extras"])
    (gathered,) = take(1)
    kept = take(plan["kept"])
    sums = take(plan["sums"])
    buffers = take(5)
    held, send_sem, recv_sem, load_sem, own_sem = take(5)
    order, steps = plan["order"], plan["steps"]
    link = Links(send_sem, recv_sem)
    gather = Gather(link, gathered, steps, own_sem)
    if ready:
        gather.begin(0, ready[0])
    scatter = Scatter(link, partial, plan["rows"], order, buffers, load_sem)
    ticks = len(order) + 7
    agenda = [[] for _ in range(ticks)]
    if ready:
        for tick, step in enumerate((gather.first, gather.second, gather.third)):
            agenda[tick + 2].append((step, 0))

    def last(p):
        rows, keeps, adds = row_step(p, scatter.total(p), extras)
        for ref, value in zip(kept, keeps):
            ref[pl.ds(p * GROUP, GROUP)] = value
        for ref, value in zip(sums, adds):
            ref[...] = value if p == order[0] else ref[...] + value
        if rows is not None:
            g = plan["slot"](p)
            held[g] = rows
            gather.begin(g, held.at[g])

    for q, p in enumerate(order):
        for tick, step in enumerate(
            (scatter.to_corner, scatter.to_sides, scatter.to_column, last)
        ):
            agenda[q + tick].append((step, p))
        if plan["slot"](p) is not None:
            for tick, step in enumerate((gather.first, gather.second, gather.third)):
                agenda[q + 4 + tick].append((step, plan["slot"](p)))
    for tick in agenda:
        for step, index in tick:
            step(index)
    gather.finish()
    link.finish()


def relay(partial, row_step, ident, extras=(), kept=0, sums=0, order=None, slot=None, ready=None):
    rows, width = partial.shape[0] // (lax.axis_size("dp") * lax.axis_size("mp")), partial.shape[1]
    groups = rows // GROUP
    order = list(range(groups)) if order is None else order
    slot = slot or (lambda p: p)
    steps = sum(slot(p) is not None for p in order) + (ready is not None)
    if not kernel_mesh():
        total = lax.psum_scatter(partial, BOTH, scatter_dimension=0, tiled=True)
        total = total.astype(jnp.float32)
        outs, keeps, adds = [None] * steps, [None] * groups, [0.0] * sums
        if ready is not None:
            outs[0] = ready
        for p in order:
            out, keeps[p], add = row_step(p, total[p * GROUP : (p + 1) * GROUP], extras)
            adds = [one + two for one, two in zip(adds, add)]
            if out is not None:
                outs[slot(p)] = out
        gathered = lax.all_gather(jnp.concatenate(outs), BOTH, axis=0, tiled=True)
        keeps = [jnp.concatenate(parts) for parts in zip(*keeps)]
        return [gathered, *keeps, *adds]
    plan = dict(
        rows=rows,
        order=order,
        slot=slot,
        steps=steps,
        ready=int(ready is not None),
        extras=len(extras),
        kept=kept,
        sums=sums,
    )
    low = partial.dtype
    vmem = pl.BlockSpec(memory_space=pltpu.VMEM)
    copies = 31 * (groups + steps)
    shapes = [jax.ShapeDtypeStruct((32 * steps * GROUP, width), low)]
    shapes += [jax.ShapeDtypeStruct((rows, width), jnp.float32)] * kept
    shapes += [jax.ShapeDtypeStruct((1, width), jnp.float32)] * sums
    buffers = [pltpu.VMEM((count, rows, width), low) for count in (16, 16, 4, 8, 3)]
    semaphores = [pltpu.SemaphoreType.DMA((count,)) for count in (copies, copies, 16 * groups, steps)]
    return pl.pallas_call(
        functools.partial(relay_kernel, plan, row_step),
        out_shape=shapes,
        in_specs=[ANY] * (1 + plan["ready"]) + [vmem] * len(extras),
        out_specs=[ANY] + [vmem] * (kept + sums),
        scratch_shapes=buffers + [pltpu.VMEM((steps, GROUP, width), low)] + semaphores,
        compiler_params=comm_params(ident),
        cost_estimate=pl.CostEstimate(flops=1, bytes_accessed=1, transcendentals=0),
    )(partial, *([] if ready is None else [ready]), *extras)


def after(value, *first):
    return lax.optimization_barrier((value, *first))[0]


def swap_blocks(value):
    count = lax.axis_size("dp")
    if len(value.shape) == 3:
        moved = lax.all_to_all(value, "dp", split_axis=0, concat_axis=0, tiled=True)
        return jnp.moveaxis(moved, 0, 1).reshape(value.shape[1], -1)
    parts = jnp.moveaxis(value.reshape(value.shape[0], count, -1), 1, 0)
    return lax.all_to_all(parts, "dp", split_axis=0, concat_axis=0, tiled=True)


def small_gather_kernel(x_ref, o_ref, send_sem, recv_sem, own_sem):
    data_index, model_index = lax.axis_index("dp"), lax.axis_index("mp")
    me = data_index * 4 + model_index
    own = pltpu.make_async_copy(x_ref, o_ref.at[me], own_sem)
    own.start()
    peers = [lax.rem(me + shift, 32) for shift in range(1, 32)]
    barrier = pltpu.get_barrier_semaphore()
    for peer in peers:
        pl.semaphore_signal(
            barrier, inc=1, device_id=(peer // 4, peer % 4), device_id_type=MESH
        )
    pl.semaphore_wait(barrier, 31)
    sent = []
    for index, peer in enumerate(peers):
        copy = pltpu.make_async_remote_copy(
            src_ref=x_ref,
            dst_ref=o_ref.at[me],
            send_sem=send_sem.at[index],
            recv_sem=recv_sem.at[index],
            device_id=(peer // 4, peer % 4),
            device_id_type=MESH,
        )
        copy.start()
        sent.append(copy)
    for index in range(31):
        here = o_ref.at[lax.rem(me + 31 - index, 32)]
        pltpu.make_async_copy(here, here, recv_sem.at[index]).wait()
    own.wait()
    for copy in sent:
        copy.wait_send()


def gather_small(value, ident):
    if not kernel_mesh():
        return lax.all_gather(value, BOTH)
    vmem = pl.BlockSpec(memory_space=pltpu.VMEM)
    return pl.pallas_call(
        small_gather_kernel,
        out_shape=jax.ShapeDtypeStruct((32,) + value.shape, value.dtype),
        in_specs=[vmem],
        out_specs=vmem,
        scratch_shapes=[
            pltpu.SemaphoreType.DMA((31,)),
            pltpu.SemaphoreType.DMA((31,)),
            pltpu.SemaphoreType.DMA,
        ],
        compiler_params=comm_params(ident),
    )(value)


def greet(peers):
    barrier = pltpu.get_barrier_semaphore()
    for peer in peers:
        pl.semaphore_signal(barrier, inc=1, device_id=peer, device_id_type=MESH)
    pl.semaphore_wait(barrier, len(peers))


def exchange_kernel(count, whole, *refs):
    ins, outs = refs[: len(whole)], refs[len(whole) : 2 * len(whole)]
    send_sem, recv_sem, own_sem = refs[2 * len(whole) :]
    me, model_index = lax.axis_index("dp"), lax.axis_index("mp")
    peers = [lax.rem(me + shift, count) for shift in range(1, count)]
    greet([(peer, model_index) for peer in peers])
    owns, sent = [], []
    for array, keep in enumerate(whole):
        own = pltpu.make_async_copy(
            ins[array] if keep else ins[array].at[me], outs[array].at[me], own_sem.at[array]
        )
        own.start()
        owns.append(own)
        for shift in range(count - 1):
            copy = pltpu.make_async_remote_copy(
                src_ref=ins[array] if keep else ins[array].at[peers[shift]],
                dst_ref=outs[array].at[me],
                send_sem=send_sem.at[array, shift],
                recv_sem=recv_sem.at[array, shift],
                device_id=(peers[shift], model_index),
                device_id_type=MESH,
            )
            copy.start()
            sent.append(copy)
    for own in owns:
        own.wait()
    for array in range(len(whole)):
        for shift in range(count - 1):
            source = lax.rem(me + count - 1 - shift, count)
            here = outs[array].at[source]
            pltpu.make_async_copy(here, here, recv_sem.at[array, shift]).wait()
    for copy in sent:
        copy.wait_send()


def exchange(values, whole, ident):
    count = lax.axis_size("dp")
    if not kernel_mesh():
        return [
            lax.all_gather(value, "dp")
            if keep
            else lax.all_to_all(value, "dp", split_axis=0, concat_axis=0, tiled=True)
            for value, keep in zip(values, whole)
        ]
    shapes = [
        jax.ShapeDtypeStruct(((count,) if keep else ()) + value.shape, value.dtype)
        for value, keep in zip(values, whole)
    ]
    return pl.pallas_call(
        functools.partial(exchange_kernel, count, tuple(whole)),
        out_shape=shapes,
        in_specs=[ANY] * len(values),
        out_specs=[ANY] * len(values),
        scratch_shapes=[
            pltpu.SemaphoreType.DMA((len(values), count - 1)),
            pltpu.SemaphoreType.DMA((len(values), count - 1)),
            pltpu.SemaphoreType.DMA((len(values),)),
        ],
        compiler_params=comm_params(ident),
    )(*values)


def turned(values, cosine, sine_table):
    return values * cosine + pltpu.roll(values, HEAD_DIM // 2, 1) * sine_table


def softmax_rows(query, keys, places):
    scores = dot(query, keys, 1, 1) * (1.0 / math.sqrt(HEAD_DIM))
    columns = lax.broadcasted_iota(jnp.int32, scores.shape, 1)
    scores = jnp.where(columns <= places, scores, NEG)
    weights = jnp.exp(scores - jnp.max(scores, axis=-1, keepdims=True))
    return weights / jnp.sum(weights, axis=-1, keepdims=True)


def attend_kernel(
    exit_ref,
    resid_ref,
    gain_ref,
    head_ref,
    cosine_ref,
    sine_ref,
    pick_ref,
    place_ref,
    live_ref,
    attn_ref,
    query_ref,
    key_ref,
    value_ref,
    out_ref,
    partial_ref,
):
    block, blocks = pl.program_id(0), key_ref.shape[0] // resid_ref.shape[0]
    rows, slots = resid_ref.shape[0], pick_ref.shape[1]
    low = jnp.bfloat16
    attn = norm_fwd(resid_ref[...].astype(jnp.float32), gain_ref[...])[0].astype(low)
    attn_ref[...] = attn
    projected = dot(attn, head_ref[: 3 * HEAD_DIM], 1, 1)
    cosine, sine_table = cosine_ref[...], sine_ref[...]
    query = turned(projected[:, :HEAD_DIM], cosine, sine_table).astype(low)
    at = pl.ds(pl.multiple_of(block * rows, rows), rows)
    key_ref[at] = turned(projected[:, HEAD_DIM : 2 * HEAD_DIM], cosine, sine_table).astype(low)
    value_ref[at] = projected[:, 2 * HEAD_DIM :].astype(low)
    at = pl.ds(pl.multiple_of(block * slots, slots), slots)
    query_ref[at] = dot(pick_ref[0], query).astype(low)

    @pl.when(block == blocks - 1)
    def _():
        exit_here = exit_ref[0]
        step = 2 * slots
        for index in range(blocks // 2):
            reach = (index + 1) * 2 * rows
            at = slice(index * step, (index + 1) * step)
            probs = softmax_rows(query_ref[at], key_ref[:reach], place_ref[at]).astype(low)
            out = (dot(probs, value_ref[:reach]) * live_ref[at]).astype(low)
            out_ref[at] = out
            share = dot(out, head_ref[3 * HEAD_DIM :]).astype(low)
            groups = step // partial_ref.shape[2]
            at = slice(index * groups, (index + 1) * groups)
            share = share.reshape(groups, 1, -1, share.shape[1])
            partial_ref[at, pl.ds(exit_here, 1)] = share
            partial_ref[at, pl.ds(1 - exit_here, 1)] = jnp.zeros_like(share)


def attend_back_kernel(
    exit_ref,
    done_ref,
    head_ref,
    out_ref,
    query_ref,
    key_ref,
    value_ref,
    cosine_ref,
    sine_ref,
    slot_cosine_ref,
    slot_sine_ref,
    pick_ref,
    place_ref,
    attn_ref,
    partial_ref,
    parts_ref,
    key_sum,
    value_sum,
    turned_ref,
    head_sum,
):
    block, blocks = pl.program_id(0), key_ref.shape[0] // attn_ref.shape[0]
    rows, slots = attn_ref.shape[0], pick_ref.shape[1]
    low = jnp.bfloat16
    scale = 1.0 / math.sqrt(HEAD_DIM)

    @pl.when(block == 0)
    def _():
        key_sum[...] = jnp.zeros_like(key_sum)
        value_sum[...] = jnp.zeros_like(value_sum)
        step = 2 * slots
        width = done_ref.shape[-1]
        done = done_ref[...].reshape(-1, width)
        parts_ref[3 * HEAD_DIM :] = dot(out_ref[...], done, 0, 0).astype(low)
        dout = dot(done, head_ref[3 * HEAD_DIM :], 1, 1).astype(low)
        for index in range(blocks // 2):
            reach = (index + 1) * 2 * rows
            at = slice(index * step, (index + 1) * step)
            probs = softmax_rows(query_ref[at], key_ref[:reach], place_ref[at])
            dprobs = dot(dout[at], value_ref[:reach], 1, 1)
            delta = jnp.sum(probs * dprobs, axis=-1, keepdims=True)
            dscores = (probs * (dprobs - delta)).astype(low)
            dquery = dot(dscores, key_ref[:reach]) * scale
            dquery = turned(dquery, slot_cosine_ref[at], -slot_sine_ref[at]).astype(low)
            for half in (0, 1):
                where = 2 * index + half
                turned_ref[where * rows : (where + 1) * rows, :HEAD_DIM] = dot(
                    pick_ref[where], dquery[half * slots : (half + 1) * slots], 0, 0
                ).astype(low)
            key_sum[:reach] += dot(dscores, query_ref[at], 0, 0)
            value_sum[:reach] += dot(probs.astype(low), dout[at], 0, 0)
        dkey = turned(key_sum[...] * scale, cosine_ref[...], -sine_ref[...])
        turned_ref[:, HEAD_DIM : 2 * HEAD_DIM] = dkey.astype(low)
        turned_ref[:, 2 * HEAD_DIM :] = value_sum[...].astype(low)

    at = pl.ds(pl.multiple_of(block * rows, rows), rows)
    dprojected = turned_ref[at]
    partial_ref[...] = dot(dprojected, head_ref[: 3 * HEAD_DIM]).astype(low)
    term = dot(dprojected, attn_ref[...], 0, 0)

    @pl.when(block == 0)
    def _():
        head_sum[...] = term

    @pl.when(block > 0)
    def _():
        head_sum[...] += term

    @pl.when(block == blocks - 1)
    def _():
        parts_ref[: 3 * HEAD_DIM] = head_sum[...].astype(low)


def local_params():
    return dict(
        compiler_params=pltpu.CompilerParams(vmem_limit_bytes=VMEM_LIMIT),
        cost_estimate=pl.CostEstimate(flops=1, bytes_accessed=1, transcendentals=0),
    )


def whole_spec(value):
    return pl.BlockSpec(value.shape, lambda b, e: (0,) * len(value.shape))


def attend(exit_here, resid, gain, head, cosine, sine_table, pick, places, live, slots_here):
    (tokens, width), (blocks, slots, rows) = resid.shape, pick.shape
    low = resid.dtype
    devices = blocks * slots // slots_here
    by_block = lambda columns: pl.BlockSpec((rows, columns), lambda b, e: (b, 0))
    outs = [
        jax.ShapeDtypeStruct(shape, low)
        for shape in (
            (tokens, width),
            (blocks * slots, HEAD_DIM),
            (tokens, HEAD_DIM),
            (tokens, HEAD_DIM),
            (blocks * slots, HEAD_DIM),
            (devices, 2, slots_here, width),
        )
    ]
    return pl.pallas_call(
        attend_kernel,
        out_shape=outs,
        grid_spec=pltpu.PrefetchScalarGridSpec(
            num_scalar_prefetch=1,
            grid=(blocks,),
            in_specs=[
                by_block(width),
                whole_spec(gain),
                whole_spec(head),
                by_block(HEAD_DIM),
                by_block(HEAD_DIM),
                pl.BlockSpec((1, slots, rows), lambda b, e: (b, 0, 0)),
                whole_spec(places),
                whole_spec(live),
            ],
            out_specs=[by_block(width)] + [whole_spec(out) for out in outs[1:]],
        ),
        **local_params(),
    )(exit_here, resid, gain, head, cosine, sine_table, pick, places, live)


def attend_back(
    exit_here, done, head, out, query, key, value, cosine, sine_table, slot_turns, pick, places, attn
):
    (tokens, width), (blocks, slots, rows) = attn.shape, pick.shape
    low = attn.dtype
    devices, _, slots_here, _ = done.shape
    by_block = pl.BlockSpec((rows, width), lambda b, e: (b, 0))
    inner = [head, out, query, key, value, cosine, sine_table, *slot_turns, pick, places]
    parts = jax.ShapeDtypeStruct((4 * HEAD_DIM, width), low)
    return pl.pallas_call(
        attend_back_kernel,
        out_shape=[jax.ShapeDtypeStruct((tokens, width), low), parts],
        grid_spec=pltpu.PrefetchScalarGridSpec(
            num_scalar_prefetch=1,
            grid=(blocks,),
            in_specs=[
                pl.BlockSpec((devices, 1, slots_here, width), lambda b, e: (0, e[0], 0, 0))
            ]
            + [whole_spec(value) for value in inner]
            + [by_block],
            out_specs=[by_block, whole_spec(parts)],
            scratch_shapes=[
                pltpu.VMEM((tokens, HEAD_DIM), jnp.float32),
                pltpu.VMEM((tokens, HEAD_DIM), jnp.float32),
                pltpu.VMEM((tokens, 3 * HEAD_DIM), low),
                pltpu.VMEM((3 * HEAD_DIM, width), jnp.float32),
            ],
        ),
        **local_params(),
    )(exit_here, done, *inner, attn)


def norm_fwd(values, gain):
    row_scale = lax.rsqrt(jnp.mean(values * values, axis=-1, keepdims=True) + EPS_NORM)
    unit_rows = values * row_scale
    return (unit_rows * gain, unit_rows, row_scale)


def norm_back(unit_rows, row_scale, gain, gradient):
    weighted = gradient * gain
    back_rows = row_scale * (
        weighted - unit_rows * jnp.mean(weighted * unit_rows, axis=-1, keepdims=True)
    )
    return (back_rows, jnp.sum(gradient * unit_rows, axis=0))


def rotary(places, width):
    half_width = width // 2
    frequency = jnp.exp(
        jnp.arange(half_width, dtype=jnp.float32) * (-math.log(10000.0) / half_width)
    )
    angles = places.astype(jnp.float32)[:, None] * frequency[None, :]
    return (jnp.cos(angles), jnp.sin(angles))


def rotate_pairs(values, cosine, sine_table):
    half_width = values.shape[-1] // 2
    front_half = values[..., :half_width]
    back_half = values[..., half_width:]
    return jnp.concatenate(
        [
            front_half * cosine - back_half * sine_table,
            back_half * cosine + front_half * sine_table,
        ],
        axis=-1,
    )


def dot(left, right, left_dim=1, right_dim=0):
    return lax.dot_general(
        left, right, (((left_dim,), (right_dim,)), ((), ())), preferred_element_type=jnp.float32
    )


def placed(value, order):
    return with_layout_constraint(value, Layout(major_to_minor=order))


def adam_update(weight, moment_one, moment_two, gradient, rate, decay):
    moment_one = BETA_ONE * moment_one + (1.0 - BETA_ONE) * gradient
    moment_two = BETA_TWO * moment_two + (1.0 - BETA_TWO) * gradient * gradient
    ratio = (
        moment_one
        / (1.0 - BETA_ONE**STEP)
        / (jnp.sqrt(moment_two / (1.0 - BETA_TWO**STEP)) + ADAM_EPS)
    )
    return (weight - rate * (ratio + decay * weight), moment_one, moment_two)


def body(
    token_ids,
    target_ids,
    exit_mask,
    table,
    table_first,
    table_second,
    qkv_weight,
    qkv_first,
    qkv_second,
    out_weight,
    out_first,
    out_second,
    gate_up_weight,
    gate_up_first,
    gate_up_second,
    down_weight,
    down_first,
    down_second,
    gains,
    gains_first,
    gains_second,
):
    low = jnp.bfloat16
    data_size, model_size = lax.axis_size("dp"), lax.axis_size("mp")
    data_index, model_index = lax.axis_index("dp"), lax.axis_index("mp")
    devices = data_size * model_size
    block_rows = token_ids.shape[0]
    tokens = block_rows * data_size
    width = table.shape[1]
    width_here = qkv_weight.shape[0]
    heads_here = qkv_weight.shape[2] // HEAD_DIM
    hidden_here = down_weight.shape[0] // data_size
    vocab_here = table.shape[0]
    device_index = data_index * model_size + model_index
    vocab_ids = device_index * vocab_here + jnp.arange(vocab_here, dtype=jnp.int32)
    score_scale = 1.0 / math.sqrt(HEAD_DIM)

    sharers = data_size // heads_here
    shares = sharers // 2
    share_slots = data_size // shares * R_DEV
    exit_here = data_index % sharers % 2
    share_here = data_index % sharers // 2
    slots_here = R_DEV // model_size
    rows_here = block_rows // model_size

    ints, gain_low = exchange(
        [
            jnp.concatenate([token_ids[None], target_ids[None], exit_mask]),
            jnp.pad(gains.astype(low), ((0, 13), (0, 0))),
        ],
        (True, True),
        0,
    )
    gain_rows = jnp.moveaxis(gain_low[:, :3], 0, 1).reshape(3, width).astype(jnp.float32)
    all_ids = ints[:, 0].reshape(tokens)
    mask_blocks = jnp.moveaxis(ints[:, 2:], 0, 1)
    slot_ids = jnp.arange(R_DEV, dtype=jnp.int32)
    slot_ranks = jnp.cumsum(mask_blocks, axis=2) - 1
    pick_int = (
        (slot_ranks[:, :, None, :] == slot_ids[:, None]) & (mask_blocks[:, :, None, :] == 1)
    ).astype(jnp.int32)
    pick_low = pick_int.astype(low)
    token_places = jnp.arange(tokens, dtype=jnp.int32)
    slot_targets = jnp.sum(pick_int * ints[:, 1][None, :, None, :], axis=3).reshape(2, -1)
    slot_places = jnp.sum(
        pick_int * token_places.reshape(1, data_size, 1, block_rows), axis=3
    ).reshape(2, -1)
    live = (slot_ids < jnp.sum(mask_blocks, axis=2)[:, :, None]).astype(jnp.float32).reshape(2, -1)
    counts = jnp.sum(live, axis=1)

    head_rows = jnp.moveaxis(
        qkv_weight.astype(low).reshape(width_here, 3, heads_here, HEAD_DIM), 0, 3
    )
    head_rows = jnp.concatenate(
        [
            jnp.moveaxis(head_rows, 0, 1).reshape(heads_here, 3 * HEAD_DIM, width_here),
            out_weight.astype(low).reshape(heads_here, HEAD_DIM, width_here),
        ],
        axis=1,
    )
    hidden_rows = jnp.moveaxis(
        gate_up_weight.astype(low).reshape(width_here, 2, data_size, hidden_here), 0, 3
    )
    hidden_rows = jnp.concatenate(
        [
            jnp.moveaxis(hidden_rows, 0, 1).reshape(data_size, 2 * hidden_here, width_here),
            down_weight.astype(low).reshape(data_size, hidden_here, width_here),
        ],
        axis=1,
    )

    head_rows = swap_blocks(after(jnp.repeat(head_rows, sharers, axis=0), ints))

    table_low = table.astype(low)
    id_hits = (all_ids[:, None] == vocab_ids[None, :]).astype(low)
    (resid_low,) = relay(
        dot(id_hits, table_low).astype(low),
        lambda p, total, extras: (total.astype(low), (), ()),
        1,
    )
    hidden_rows = swap_blocks(after(hidden_rows, resid_low))
    pick_share = lax.dynamic_slice_in_dim(
        lax.dynamic_index_in_dim(pick_low, exit_here, 0, keepdims=False),
        share_here * (data_size // shares),
        data_size // shares,
        0,
    )
    def share_of(per_slot):
        return lax.dynamic_slice(per_slot, (exit_here, share_here * share_slots), (1, share_slots))[
            0
        ]

    places_share, live_share = share_of(slot_places), share_of(live)
    cosine, sine_table = rotary(token_places, HEAD_DIM)
    cosine_share, sine_share = rotary(places_share, HEAD_DIM)

    def turns(cosines, sines):
        return (
            jnp.concatenate([cosines, cosines], axis=1),
            jnp.concatenate([-sines, sines], axis=1),
        )

    if kernel_mesh():
        attn_low, query_slots, key_low, value_low, attn_out, out_partial = attend(
            exit_here[None],
            resid_low,
            gain_rows[:1],
            head_rows,
            *turns(cosine, sine_table),
            pick_share,
            places_share[:, None],
            live_share[:, None],
            slots_here,
        )
        out_partial = out_partial.reshape(-1, width)
    else:
        qkv_head, out_head = head_rows[: 3 * HEAD_DIM], head_rows[3 * HEAD_DIM :]
        attn_low = norm_fwd(resid_low.astype(jnp.float32), gain_rows[0])[0].astype(low)

        projected = dot(attn_low, qkv_head, 1, 1)
        query_low = rotate_pairs(projected[:, :HEAD_DIM], cosine, sine_table).astype(low)
        key_low = rotate_pairs(projected[:, HEAD_DIM : 2 * HEAD_DIM], cosine, sine_table).astype(low)
        value_low = projected[:, 2 * HEAD_DIM :].astype(low)
        query_share = lax.dynamic_slice_in_dim(
            query_low.reshape(data_size, block_rows, HEAD_DIM),
            share_here * (data_size // shares),
            data_size // shares,
            0,
        )
        query_slots = (
            jnp.einsum("brt,btd->brd", pick_share, query_share, preferred_element_type=jnp.float32)
            .astype(low)
            .reshape(share_slots, HEAD_DIM)
        )

        scores = dot(query_slots, key_low, 1, 1) * score_scale
        allowed = token_places[None, :] <= places_share[:, None]
        scores = jnp.where(allowed, scores, NEG)
        weights = jnp.exp(scores - jnp.max(scores, axis=-1, keepdims=True))
        probs = weights / jnp.sum(weights, axis=-1, keepdims=True)
        probs_low = probs.astype(low)
        attn_out = (dot(probs_low, value_low) * live_share[:, None]).astype(low)

        def spread(per_share):
            if shares > 1:
                full = jnp.zeros((data_size * R_DEV, width), per_share.dtype)
                per_share = lax.dynamic_update_slice_in_dim(
                    full, per_share, share_here * share_slots, 0
                )
            exits = jnp.arange(2, dtype=jnp.int32)[None, :, None, None]
            rows = per_share.reshape(devices, 1, slots_here, width)
            return jnp.where(exits == exit_here, rows, 0).reshape(-1, width)
        out_partial = spread(dot(attn_out, out_head).astype(low))

    block_low = lax.dynamic_slice_in_dim(resid_low, data_index * block_rows, block_rows, 0)
    pick_here = lax.dynamic_slice(
        pick_low,
        (0, data_index, model_index * slots_here, 0),
        (2, 1, slots_here, block_rows),
    ).reshape(2 * slots_here, block_rows)

    def first_step(p, total, extras):
        resid = extras[0][p * GROUP : (p + 1) * GROUP] + total
        gain = 2 if p == 0 else 1
        return (norm_fwd(resid, extras[1][gain : gain + 1])[0].astype(low), (resid,), ())

    first_rows, resid_one = relay(
        out_partial,
        first_step,
        2,
        extras=[dot(pick_here, block_low), gain_rows],
        kept=1,
    )
    first_rows = first_rows.reshape(devices, 2, slots_here, width)
    exit_rows_one = first_rows[:, 0].reshape(-1, width)
    mlp_low = first_rows[:, 1].reshape(-1, width)

    gate_up_head, down_head = hidden_rows[: 2 * hidden_here], hidden_rows[2 * hidden_here :]
    gate_up = dot(mlp_low, gate_up_head, 1, 1)
    gate_part, up_part = gate_up[:, :hidden_here], gate_up[:, hidden_here:]
    gate_sigma = jax.nn.sigmoid(gate_part)
    hidden_low = (gate_part * gate_sigma * up_part).astype(low)

    def second_step(p, total, extras):
        resid = extras[0][GROUP : 2 * GROUP] + total
        return (norm_fwd(resid, extras[1][2:3])[0].astype(low), (resid,), ())

    exit_rows_two, resid_two = relay(
        dot(hidden_low, down_head).astype(low), second_step, 3, extras=[resid_one, gain_rows], kept=1
    )

    exit_rows = (exit_rows_one, exit_rows_two)
    logits = [dot(rows, table_low, 1, 1) for rows in exit_rows]
    hits = [slot_targets[e][:, None] == vocab_ids[None, :] for e in range(2)]
    tops = [jnp.max(values, axis=1) for values in logits]
    masses = [jnp.sum(jnp.exp(values - top[:, None]), axis=1) for values, top in zip(logits, tops)]
    found = [jnp.sum(jnp.where(hit, values, 0.0), axis=1) for hit, values in zip(hits, logits)]
    stats = jnp.concatenate(tops + masses + found).reshape(-1, 128)
    stats = gather_small(stats, 4).reshape(devices, 3, 2, -1)
    row_top = jnp.max(stats[:, 0], axis=0)
    row_mass = jnp.sum(stats[:, 1] * jnp.exp(stats[:, 0] - row_top), axis=0)
    row_lse = row_top + jnp.log(row_mass)
    entropy = row_lse - jnp.sum(stats[:, 2], axis=0)
    loss_sums = jnp.sum(entropy * live, axis=1)
    row_weight = live * (jnp.array(EXIT_SCALE, jnp.float32) / counts)[:, None]
    grad_logits = [
        (
            row_weight[e][:, None]
            * (jnp.exp(logits[e] - row_lse[e][:, None]) - hits[e].astype(jnp.float32))
        ).astype(low)
        for e in range(2)
    ]
    table_head = dot(grad_logits[0], exit_rows_one, 0, 0) + dot(grad_logits[1], exit_rows_two, 0, 0)
    row_terms = jnp.stack(
        [
            dot(grad, table_low).astype(low).reshape(devices, slots_here, width)
            for grad in grad_logits
        ],
        axis=1,
    )

    def head_step(p, total, extras):
        values = extras[0][:GROUP] if p == 0 else extras[1][...]
        gain = extras[2][2:3]
        _, unit, scale = norm_fwd(values, gain)
        back, gain_grad = norm_back(unit, scale, gain, total)
        return (None if p == 0 else back.astype(low), (back,), (gain_grad[None],))

    dtwo_low, dexits, final_grad = relay(
        row_terms.reshape(-1, width),
        head_step,
        5,
        extras=[resid_one, resid_two, gain_rows],
        kept=1,
        sums=1,
        order=[1, 0],
        slot=lambda p: None if p == 0 else 0,
    )
    down_local = dot(hidden_low, dtwo_low, 0, 0)
    dhidden = dot(dtwo_low, down_head, 1, 1)
    dgate = dhidden * up_part * gate_sigma * (1.0 + gate_part * (1.0 - gate_sigma))
    dup_part = dhidden * gate_part * gate_sigma
    dgate_up = jnp.concatenate([dgate, dup_part], axis=1).astype(low)
    gate_up_local = dot(dgate_up, mlp_low, 0, 0)

    def mlp_step(p, total, extras):
        gain = extras[2][1:2]
        _, unit, scale = norm_fwd(extras[0][GROUP : 2 * GROUP], gain)
        back, gain_grad = norm_back(unit, scale, gain, total)
        return ((extras[1][GROUP : 2 * GROUP] + back).astype(low), (), (gain_grad[None],))

    done_low, mlp_grad = relay(
        dot(dgate_up, gate_up_head).astype(low),
        mlp_step,
        6,
        extras=[resid_one, dexits, gain_rows],
        sums=1,
        slot=lambda p: 1,
        ready=dexits[:GROUP].astype(low),
    )
    hidden_parts = jnp.concatenate([gate_up_local.astype(low), down_local.astype(low)])
    hidden_parts = swap_blocks(after(hidden_parts, done_low))
    done_low = done_low.reshape(devices, 2, slots_here, width)

    if kernel_mesh():
        zero_partial, head_parts = attend_back(
            exit_here[None],
            done_low,
            head_rows,
            attn_out,
            query_slots,
            key_low,
            value_low,
            *turns(cosine, sine_table),
            turns(cosine_share, sine_share),
            pick_share,
            places_share[:, None],
            attn_low,
        )
    else:
        done_share = lax.dynamic_slice(
            lax.dynamic_index_in_dim(done_low, exit_here, 1, keepdims=False).reshape(-1, width),
            (share_here * share_slots, 0),
            (share_slots, width),
        )
        out_local = dot(attn_out, done_share, 0, 0)
        dattn_low = dot(done_share, out_head, 1, 1).astype(low)
        dprobs = dot(dattn_low, value_low, 1, 1)
        delta = jnp.sum(probs * dprobs, axis=-1, keepdims=True)
        dscores = (probs * (dprobs - delta)).astype(low)
        dquery = rotate_pairs(dot(dscores, key_low) * score_scale, cosine_share, -sine_share).astype(
            low
        )
        dquery_share = jnp.einsum(
            "brt,brd->btd",
            pick_share,
            dquery.reshape(-1, R_DEV, HEAD_DIM),
            preferred_element_type=jnp.float32,
        ).astype(low)
        if shares > 1:
            dquery_share = lax.dynamic_update_slice_in_dim(
                jnp.zeros((data_size, block_rows, HEAD_DIM), low),
                dquery_share,
                share_here * (data_size // shares),
                0,
            )
        dkey = rotate_pairs(dot(dscores, query_slots, 0, 0) * score_scale, cosine, -sine_table)
        dvalue = dot(probs_low, dattn_low, 0, 0)
        dprojected = jnp.concatenate(
            [dquery_share.reshape(tokens, HEAD_DIM), dkey.astype(low), dvalue.astype(low)], axis=1
        )
        head_parts = jnp.concatenate([dot(dprojected, attn_low, 0, 0).astype(low), out_local.astype(low)])
        zero_partial = dot(dprojected, qkv_head).astype(low)

    resid_here = lax.dynamic_slice_in_dim(resid_low, device_index * rows_here, rows_here, 0)
    done_block = lax.dynamic_slice_in_dim(done_low, data_index * model_size, model_size, 0)
    pick_block = lax.dynamic_slice(
        pick_low,
        (0, data_index, 0, model_index * rows_here),
        (2, 1, R_DEV, rows_here),
    ).reshape(2, model_size, slots_here, rows_here)
    dresid_here = jnp.einsum(
        "emst,mesd->td", pick_block, done_block, preferred_element_type=jnp.float32
    )

    def zero_step(p, total, extras):
        at = slice(p * GROUP, (p + 1) * GROUP)
        gain = extras[2][:1]
        _, unit, scale = norm_fwd(extras[0][at], gain)
        back, gain_grad = norm_back(unit, scale, gain, total)
        return ((extras[1][at] + back).astype(low), (), (gain_grad[None],))

    dzero_low, attn_grad = relay(
        after(zero_partial, head_parts, hidden_parts),
        zero_step,
        7,
        extras=[resid_here.astype(jnp.float32), dresid_here, gain_rows],
        sums=1,
    )
    head_parts = swap_blocks(after(head_parts, dzero_low))
    table_grad = table_head + dot(id_hits, dzero_low, 0, 0)

    head_grad = jnp.sum(
        head_parts.reshape(heads_here, sharers, 4, HEAD_DIM, width_here).astype(jnp.float32), axis=1
    )
    qkv_grad = placed(jnp.transpose(head_grad[:, :3], (3, 1, 0, 2)).reshape(qkv_weight.shape), (1, 0, 2))
    out_grad = head_grad[:, 3].reshape(out_weight.shape)
    hidden_parts = hidden_parts.astype(jnp.float32)
    gate_up_grad = hidden_parts[:, : 2 * hidden_here].reshape(
        data_size, 2, hidden_here, width_here
    )
    gate_up_grad = placed(
        jnp.transpose(gate_up_grad, (3, 1, 0, 2)).reshape(gate_up_weight.shape), (0, 1, 2)
    )
    down_grad = hidden_parts[:, 2 * hidden_here :].reshape(down_weight.shape)
    squares = (
        jnp.sum(table_grad * table_grad)
        + jnp.sum(qkv_grad * qkv_grad)
        + jnp.sum(out_grad * out_grad)
        + jnp.sum(gate_up_grad * gate_up_grad)
        + jnp.sum(down_grad * down_grad)
    )
    parts = jnp.concatenate(
        [
            jnp.concatenate([attn_grad, mlp_grad, final_grad]).reshape(-1, 128),
            jnp.full((8, 128), squares),
        ]
    )
    parts = jnp.sum(gather_small(parts, 8), axis=0)
    gain_sums = parts[:-8].reshape(3, width)
    gain_grad = lax.dynamic_slice_in_dim(gain_sums, data_index * width_here, width_here, 1)
    grad_norm = jnp.sqrt(parts[-1, 0] + jnp.sum(gain_sums * gain_sums))
    factor = jnp.minimum(1.0, CLIP / (grad_norm + 1e-06))
    table_new = adam_update(
        table, table_first, table_second, table_grad * factor, RATE_MATRIX, DECAY
    )
    qkv_new = adam_update(qkv_weight, qkv_first, qkv_second, qkv_grad * factor, RATE_MATRIX, DECAY)
    out_new = adam_update(out_weight, out_first, out_second, out_grad * factor, RATE_MATRIX, DECAY)
    gate_up_new = adam_update(
        gate_up_weight, gate_up_first, gate_up_second, gate_up_grad * factor, RATE_MATRIX, DECAY
    )
    down_new = adam_update(
        down_weight, down_first, down_second, down_grad * factor, RATE_MATRIX, DECAY
    )
    gains_new = adam_update(gains, gains_first, gains_second, gain_grad * factor, RATE_GAIN, 0.0)
    return (
        loss_sums,
        counts,
        grad_norm,
        *table_new,
        *qkv_new,
        *out_new,
        *gate_up_new,
        *down_new,
        *gains_new,
    )


def solution(mesh):
    rows, sides, cols, gain = P(BOTH, None), P("dp", None, "mp"), P("mp", "dp"), P(None, "dp")
    state = (rows,) * 3 + (sides,) * 3 + (cols,) * 3 + (sides,) * 3 + (cols,) * 3 + (gain,) * 3
    return jax.shard_map(
        body,
        mesh=mesh,
        in_specs=(P("dp"), P("dp"), P(None, "dp")) + state,
        out_specs=(P(), P(), P()) + state,
        check_vma=False,
    )
```

```python
import functools
import math

import jax
import jax.numpy as jnp
from jax import lax
from jax.experimental import pallas as pl
from jax.experimental.pallas import tpu as pltpu
from jax.sharding import PartitionSpec as P

HEAD_DIM = 128
R_DEV = 64
STEP = 10


EPS_NORM = 1e-05
BETA_ONE = 0.9
BETA_TWO = 0.95
ADAM_EPS = 1e-08
DECAY = 0.1
RATE_MATRIX = 0.02
RATE_GAIN = 1.0
CLIP = 0.02
EXIT_SCALE = (1.0 / 3.0, 2.0 / 3.0)
NEG = -1e30
BOTH = ("dp", "mp")
MESH = pl.DeviceIdType.MESH
VMEM_LIMIT = 60 * 1024 * 1024
ANY = pl.BlockSpec(memory_space=pl.ANY)
GROUP = 16
CARGO_CUTS = 2
CARGO_EARLY = 4
CARGO_LATE = 2


def kernel_mesh():
    return lax.axis_size("dp") == 8 and lax.axis_size("mp") == 4


def comm_params(ident):
    return pltpu.CompilerParams(
        collective_id=ident, has_side_effects=True, vmem_limit_bytes=VMEM_LIMIT
    )


class Links:
    def __init__(self, send_sem, recv_sem, cargo=False):
        data_index, model_index = lax.axis_index("dp"), lax.axis_index("mp")
        z, y, x, c = data_index // 2, data_index % 2, model_index // 2, model_index % 2
        self.c = c
        self.zs = (z, z + 1 - 2 * (z % 2), (z + 2) % 4, 3 - z)
        self.corners = ((y, x), (y, 1 - x), (1 - y, x), (1 - y, 1 - x))
        self.z_side = [(zd * 2 + y, model_index) for zd in self.zs]
        self.x_side = (data_index, (1 - x) * 2 + c)
        self.y_side = (z * 2 + 1 - y, model_index)
        self.c_side = (data_index, x * 2 + 1 - c)
        self.send_sem, self.recv_sem, self.sent, self.slots = send_sem, recv_sem, [], {}
        peers = self.z_side[1:] + [self.x_side, self.y_side, self.c_side]
        if cargo:
            peers += [(zd * 2 + 1 - y, model_index) for zd in self.zs[1:]]
        barrier = pltpu.get_barrier_semaphore()
        for peer in peers:
            pl.semaphore_signal(barrier, inc=1, device_id=peer, device_id_type=MESH)
        pl.semaphore_wait(barrier, len(peers))

    def first_row(self, rows, d, group, core=0):
        y, x = self.corners[group]
        c = 1 - self.c if core else self.c
        return ((self.zs[d] * 2 + y) * 4 + x * 2 + c) * rows

    def recv(self, name):
        return self.recv_sem.at[self.slots.setdefault(name, len(self.slots))]

    def send(self, source, target, device, name):
        copy = pltpu.make_async_remote_copy(
            src_ref=source,
            dst_ref=target,
            send_sem=self.send_sem.at[len(self.sent)],
            recv_sem=self.recv(name),
            device_id=device,
            device_id_type=MESH,
        )
        copy.start()
        self.sent.append(copy)

    def arrived(self, ref, name):
        pltpu.make_async_copy(ref, ref, self.recv(name)).wait()
        return ref

    def finish(self):
        for copy in self.sent:
            copy.wait_send()


class Cargo:
    def __init__(self, source, target, send_sem, recv_sem, own_sem):
        self.me, self.model_index = lax.axis_index("dp"), lax.axis_index("mp")
        self.source, self.target = source, target
        self.send_sem, self.recv_sem, self.sent = send_sem, recv_sem, []
        self.own = pltpu.make_async_copy(source.at[self.me], target.at[self.me], own_sem)
        self.own.start()
        size = source.shape[1] // CARGO_CUTS
        cuts = [pl.ds(cut * size, size) for cut in range(CARGO_CUTS)]
        self.cuts = [(shift, cut) for cut in cuts for shift in (4, 3, 5, 2, 6, 1, 7)]

    def load(self, count):
        for _ in range(count):
            index = len(self.sent)
            if index == len(self.cuts):
                return
            shift, cut = self.cuts[index]
            peer = lax.rem(self.me + shift, 8)
            copy = pltpu.make_async_remote_copy(
                src_ref=self.source.at[peer, cut],
                dst_ref=self.target.at[self.me, cut],
                send_sem=self.send_sem.at[index],
                recv_sem=self.recv_sem.at[index],
                device_id=(peer, self.model_index),
                device_id_type=MESH,
            )
            copy.start()
            self.sent.append(copy)

    def finish(self):
        self.load(len(self.cuts))
        self.own.wait()
        for index, (shift, cut) in enumerate(self.cuts):
            here = self.target.at[lax.rem(self.me + 8 - shift, 8), cut]
            pltpu.make_async_copy(here, here, self.recv_sem.at[index]).wait()
        for copy in self.sent:
            copy.wait_send()


class Gather:
    def __init__(self, link, outs, steps, own_sem):
        self.link, self.outs, self.steps, self.own_sem = link, outs, steps, own_sem
        self.owns = []

    def spot(self, g, d, group, core=0):
        if len(self.outs) > 1:
            out, start = self.outs[g], self.link.first_row(GROUP, d, group, core)
        else:
            out, start = self.outs[0], self.link.first_row(self.steps * GROUP, d, group, core)
            start = start + g * GROUP
        return out.at[pl.ds(pl.multiple_of(start, GROUP), GROUP)]

    def send(self, g, source, device, here, there):
        self.link.send(source, self.spot(g, *here), device, ("gather", g, *there))

    def arrived(self, g, d, group, core):
        return self.link.arrived(self.spot(g, d, group, core), ("gather", g, d, group, core))

    def begin(self, g, source):
        link = self.link
        own = pltpu.make_async_copy(source, self.spot(g, 0, 0), self.own_sem.at[g])
        own.start()
        self.owns.append(own)
        for d in (1, 2, 3):
            self.send(g, source, link.z_side[d], (0, 0), (d, 0, 0))
        self.send(g, source, link.x_side, (0, 0), (0, 1, 0))
        self.send(g, source, link.y_side, (0, 0), (0, 2, 0))
        self.send(g, source, link.c_side, (0, 0), (0, 0, 1))

    def from_z(self, g, d):
        here = self.arrived(g, d, 0, 0)
        self.send(g, here, self.link.x_side, (d, 0), (d, 1, 0))
        self.send(g, here, self.link.y_side, (d, 0), (d, 2, 0))
        self.send(g, here, self.link.c_side, (d, 0), (d, 0, 1))

    def from_sides(self, g, d):
        for group, side in ((1, self.link.y_side), (2, self.link.x_side)):
            here = self.arrived(g, d, group, 0)
            if (d % 2 == 0) == (group == 1):
                self.send(g, here, side, (d, group), (d, 3, 0))
            self.send(g, here, self.link.c_side, (d, group), (d, group, 1))

    def first(self, g):
        self.from_z(g, 1)
        self.from_sides(g, 0)
        self.from_z(g, 2)
        self.from_z(g, 3)

    def second(self, g):
        for d in (1, 2, 3):
            self.from_sides(g, d)

    def third(self, g):
        for d in range(4):
            here = self.arrived(g, d, 3, 0)
            self.send(g, here, self.link.c_side, (d, 3), (d, 3, 1))

    def finish(self):
        for g in range(self.steps):
            for d in range(4):
                for group in range(4):
                    self.arrived(g, d, group, 1)
        for own in self.owns:
            own.wait()


CORNER = [(d, 3) for d in range(4)]
SIDES = [(1, 1), (3, 1), (0, 2), (2, 2), (0, 1), (2, 1), (1, 2), (3, 2)]
COLUMN = [(d, 0) for d in (3, 2, 1)]


class Scatter:
    def __init__(self, link, partials, rows, order, buffers, own_sem):
        self.link, self.partials, self.rows = link, partials, rows
        self.mine, self.core, self.corner, self.side, self.column = buffers
        self.owns = {}
        for p in order:
            for d, group in CORNER + SIDES + COLUMN + [(0, 0)]:
                k = d * 4 + group
                here = self.mine.at[k, pl.ds(p * GROUP, GROUP)]
                own = pltpu.make_async_copy(self.spot(p, d, group), here, own_sem.at[p * 16 + k])
                own.start()
                self.owns[p, k] = own
                self.send(p, self.spot(p, d, group, 1), self.core, k, link.c_side, "core")

    def spot(self, p, d, group, core=0):
        if len(self.partials) > 1:
            partial, start = self.partials[p], self.link.first_row(GROUP, d, group, core)
        else:
            partial, start = self.partials[0], self.link.first_row(self.rows, d, group, core)
            start = start + p * GROUP
        return partial.at[pl.ds(pl.multiple_of(start, GROUP), GROUP)]

    def send(self, p, source, buffer, k, device, name):
        self.link.send(source, buffer.at[k, pl.ds(p * GROUP, GROUP)], device, (name, p, k))

    def term(self, p, buffer, k, name):
        return self.link.arrived(buffer.at[k, pl.ds(p * GROUP, GROUP)], (name, p, k))[...].astype(
            jnp.float32
        )

    def start_terms(self, p, k):
        self.owns[p, k].wait()
        own = self.mine[k, pl.ds(p * GROUP, GROUP)].astype(jnp.float32)
        return own + self.term(p, self.core, k, "core")

    def pass_on(self, p, k, total, buffer, there, device, name):
        here = self.mine.at[k, pl.ds(p * GROUP, GROUP)]
        here[...] = total.astype(here.dtype)
        self.send(p, here, buffer, there, device, name)

    def to_corner(self, p):
        for d, _ in CORNER:
            side = self.link.y_side if d % 2 == 0 else self.link.x_side
            k = d * 4 + 3
            self.pass_on(p, k, self.start_terms(p, k), self.corner, d, side, "corner")

    def to_sides(self, p):
        for d, group in SIDES:
            k = d * 4 + group
            total = self.start_terms(p, k)
            if (d % 2 == 0) == (group == 1):
                total = total + self.term(p, self.corner, d, "corner")
            side = self.link.x_side if group == 1 else self.link.y_side
            self.pass_on(p, k, total, self.side, d * 2 + group - 1, side, "side")

    def column_terms(self, p, d):
        total = self.start_terms(p, d * 4)
        for k in (d * 2, d * 2 + 1):
            total = total + self.term(p, self.side, k, "side")
        return total

    def to_column(self, p):
        for d, _ in COLUMN:
            total = self.column_terms(p, d)
            self.pass_on(p, d * 4, total, self.column, d - 1, self.link.z_side[d], "column")

    def total(self, p):
        total = self.column_terms(p, 0)
        for d in (1, 2, 3):
            total = total + self.term(p, self.column, d - 1, "column")
        return total


def relay_kernel(plan, row_step, *refs):
    refs = list(refs)

    def take(count):
        taken = refs[:count]
        del refs[:count]
        return taken

    partials = take(plan["partials"])
    ready = take(plan["ready"])
    extras = take(plan["extras"])
    cargo_in = take(plan["cargo"])
    gathered = take(plan["outs"])
    kept = take(plan["kept"])
    sums = take(plan["sums"])
    cargo_out = take(plan["cargo"])
    buffers = take(5)
    held, send_sem, recv_sem, load_sem, own_sem = take(5)
    order, steps = plan["order"], plan["steps"]
    link = Links(send_sem, recv_sem, plan["cargo"])
    gather = Gather(link, gathered, steps, own_sem)
    if ready:
        gather.begin(0, ready[0])
    scatter = Scatter(link, partials, plan["rows"], order, buffers, load_sem)
    cargo = Cargo(*cargo_in, *cargo_out, *refs) if cargo_in else None
    ticks = len(order) + 7
    agenda = [[] for _ in range(ticks)]
    if ready:
        for tick, step in enumerate((gather.first, gather.second, gather.third)):
            agenda[tick + 2].append((step, 0))

    def last(p):
        rows, keeps, adds = row_step(p, scatter.total(p), extras)
        for ref, value in zip(kept, keeps):
            ref[pl.ds(p * GROUP, GROUP)] = value
        for ref, value in zip(sums, adds):
            ref[...] = value if p == order[0] else ref[...] + value
        if rows is not None:
            g = plan["slot"](p)
            held[g] = rows
            gather.begin(g, held.at[g])

    for q, p in enumerate(order):
        for tick, step in enumerate(
            (scatter.to_corner, scatter.to_sides, scatter.to_column, last)
        ):
            agenda[q + tick].append((step, p))
        if plan["slot"](p) is not None:
            for tick, step in enumerate((gather.first, gather.second, gather.third)):
                agenda[q + 4 + tick].append((step, plan["slot"](p)))
    for number, tick in enumerate(agenda):
        if cargo:
            cargo.load(CARGO_EARLY if number < 4 else CARGO_LATE)
        for step, index in tick:
            step(index)
    gather.finish()
    link.finish()
    if cargo:
        cargo.finish()


def relay(
    partials,
    row_step,
    ident,
    extras=(),
    kept=0,
    sums=0,
    order=None,
    slot=None,
    ready=None,
    split=False,
    cargo=None,
):
    devices, width = lax.axis_size("dp") * lax.axis_size("mp"), partials[0].shape[1]
    rows = sum(partial.shape[0] for partial in partials) // devices
    groups = rows // GROUP
    order = list(range(groups)) if order is None else order
    slot = slot or (lambda p: p)
    steps = sum(slot(p) is not None for p in order) + (ready is not None)
    if not kernel_mesh():
        total = jnp.concatenate(
            [lax.psum_scatter(part, BOTH, scatter_dimension=0, tiled=True) for part in partials]
        )
        total = total.astype(jnp.float32)
        outs, keeps, adds = [None] * steps, [None] * groups, [0.0] * sums
        if ready is not None:
            outs[0] = ready
        for p in order:
            out, keeps[p], add = row_step(p, total[p * GROUP : (p + 1) * GROUP], extras)
            adds = [one + two for one, two in zip(adds, add)]
            if out is not None:
                outs[slot(p)] = out
        outs = outs if split else [jnp.concatenate(outs)]
        gathered = [lax.all_gather(out, BOTH, axis=0, tiled=True) for out in outs]
        keeps = [jnp.concatenate(parts) for parts in zip(*keeps)]
        moved = [] if cargo is None else [swap_blocks(cargo)]
        return [*gathered, *keeps, *adds, *moved]
    plan = dict(
        partials=len(partials),
        outs=steps if split else 1,
        cargo=int(cargo is not None),
        rows=rows,
        order=order,
        slot=slot,
        steps=steps,
        ready=int(ready is not None),
        extras=len(extras),
        kept=kept,
        sums=sums,
    )
    low = partials[0].dtype
    load = [] if cargo is None else [cargo]
    vmem = pl.BlockSpec(memory_space=pltpu.VMEM)
    copies = 31 * (groups + steps)
    out_rows = [devices * GROUP] * steps if split else [devices * steps * GROUP]
    shapes = [jax.ShapeDtypeStruct((count, width), low) for count in out_rows]
    shapes += [jax.ShapeDtypeStruct((rows, width), jnp.float32)] * kept
    shapes += [jax.ShapeDtypeStruct((1, width), jnp.float32)] * sums
    shapes += [jax.ShapeDtypeStruct(value.shape, value.dtype) for value in load]
    buffers = [pltpu.VMEM((count, rows, width), low) for count in (16, 16, 4, 8, 3)]
    semaphores = [pltpu.SemaphoreType.DMA((count,)) for count in (copies, copies, 16 * groups, steps)]
    if load:
        semaphores += [pltpu.SemaphoreType.DMA((7 * CARGO_CUTS,))] * 2 + [pltpu.SemaphoreType.DMA]
    return pl.pallas_call(
        functools.partial(relay_kernel, plan, row_step),
        out_shape=shapes,
        in_specs=[ANY] * (len(partials) + plan["ready"])
        + [vmem] * len(extras)
        + [ANY] * len(load),
        out_specs=[ANY] * len(out_rows) + [vmem] * (kept + sums) + [ANY] * len(load),
        scratch_shapes=buffers + [pltpu.VMEM((steps, GROUP, width), low)] + semaphores,
        compiler_params=comm_params(ident),
        cost_estimate=pl.CostEstimate(flops=1, bytes_accessed=1, transcendentals=0),
    )(*partials, *([] if ready is None else [ready]), *extras, *load)


def after(value, *first):
    return lax.optimization_barrier((value, *first))[0]


def swap_blocks(value):
    return lax.all_to_all(value, "dp", split_axis=0, concat_axis=0, tiled=True)


def small_gather_kernel(x_ref, o_ref, send_sem, recv_sem, own_sem):
    data_index, model_index = lax.axis_index("dp"), lax.axis_index("mp")
    me = data_index * 4 + model_index
    own = pltpu.make_async_copy(x_ref, o_ref.at[me], own_sem)
    own.start()
    peers = [lax.rem(me + shift, 32) for shift in range(1, 32)]
    barrier = pltpu.get_barrier_semaphore()
    for peer in peers:
        pl.semaphore_signal(
            barrier, inc=1, device_id=(peer // 4, peer % 4), device_id_type=MESH
        )
    pl.semaphore_wait(barrier, 31)
    sent = []
    for index, peer in enumerate(peers):
        copy = pltpu.make_async_remote_copy(
            src_ref=x_ref,
            dst_ref=o_ref.at[me],
            send_sem=send_sem.at[index],
            recv_sem=recv_sem.at[index],
            device_id=(peer // 4, peer % 4),
            device_id_type=MESH,
        )
        copy.start()
        sent.append(copy)
    for index in range(31):
        here = o_ref.at[lax.rem(me + 31 - index, 32)]
        pltpu.make_async_copy(here, here, recv_sem.at[index]).wait()
    own.wait()
    for copy in sent:
        copy.wait_send()


def gather_small(value, ident):
    if not kernel_mesh():
        return lax.all_gather(value, BOTH)
    vmem = pl.BlockSpec(memory_space=pltpu.VMEM)
    return pl.pallas_call(
        small_gather_kernel,
        out_shape=jax.ShapeDtypeStruct((32,) + value.shape, value.dtype),
        in_specs=[vmem],
        out_specs=vmem,
        scratch_shapes=[
            pltpu.SemaphoreType.DMA((31,)),
            pltpu.SemaphoreType.DMA((31,)),
            pltpu.SemaphoreType.DMA,
        ],
        compiler_params=comm_params(ident),
    )(value)


def greet(peers):
    barrier = pltpu.get_barrier_semaphore()
    for peer in peers:
        pl.semaphore_signal(barrier, inc=1, device_id=peer, device_id_type=MESH)
    pl.semaphore_wait(barrier, len(peers))


def exchange_kernel(count, whole, *refs):
    ins, outs = refs[: len(whole)], refs[len(whole) : 2 * len(whole)]
    send_sem, recv_sem, own_sem = refs[2 * len(whole) :]
    me, model_index = lax.axis_index("dp"), lax.axis_index("mp")
    peers = [lax.rem(me + shift, count) for shift in range(1, count)]
    greet([(peer, model_index) for peer in peers])
    owns, sent = [], []
    for array, keep in enumerate(whole):
        own = pltpu.make_async_copy(
            ins[array] if keep else ins[array].at[me], outs[array].at[me], own_sem.at[array]
        )
        own.start()
        owns.append(own)
        for shift in range(count - 1):
            copy = pltpu.make_async_remote_copy(
                src_ref=ins[array] if keep else ins[array].at[peers[shift]],
                dst_ref=outs[array].at[me],
                send_sem=send_sem.at[array, shift],
                recv_sem=recv_sem.at[array, shift],
                device_id=(peers[shift], model_index),
                device_id_type=MESH,
            )
            copy.start()
            sent.append(copy)
    for own in owns:
        own.wait()
    for array in range(len(whole)):
        for shift in range(count - 1):
            source = lax.rem(me + count - 1 - shift, count)
            here = outs[array].at[source]
            pltpu.make_async_copy(here, here, recv_sem.at[array, shift]).wait()
    for copy in sent:
        copy.wait_send()


def exchange(values, whole, ident):
    count = lax.axis_size("dp")
    if not kernel_mesh():
        return [
            lax.all_gather(value, "dp")
            if keep
            else lax.all_to_all(value, "dp", split_axis=0, concat_axis=0, tiled=True)
            for value, keep in zip(values, whole)
        ]
    shapes = [
        jax.ShapeDtypeStruct(((count,) if keep else ()) + value.shape, value.dtype)
        for value, keep in zip(values, whole)
    ]
    return pl.pallas_call(
        functools.partial(exchange_kernel, count, tuple(whole)),
        out_shape=shapes,
        in_specs=[ANY] * len(values),
        out_specs=[ANY] * len(values),
        scratch_shapes=[
            pltpu.SemaphoreType.DMA((len(values), count - 1)),
            pltpu.SemaphoreType.DMA((len(values), count - 1)),
            pltpu.SemaphoreType.DMA((len(values),)),
        ],
        compiler_params=comm_params(ident),
    )(*values)


def turned(values, cosine, sine_table):
    return values * cosine + pltpu.roll(values, HEAD_DIM // 2, 1) * sine_table


def to_column(row):
    return jnp.broadcast_to(row, (row.shape[1], row.shape[1])).T[:, :1]


def to_row(column):
    return jnp.broadcast_to(column, (column.shape[0], column.shape[0])).T[:1]


def softmax_rows(query, keys, places):
    scores = dot(query, keys, 1, 1) * (1.0 / math.sqrt(HEAD_DIM))
    columns = lax.broadcasted_iota(jnp.int32, scores.shape, 1)
    scores = jnp.where(columns <= places, scores, NEG)
    weights = jnp.exp(scores - jnp.max(scores, axis=-1, keepdims=True))
    return weights / jnp.sum(weights, axis=-1, keepdims=True)


def attend_kernel(
    exit_ref,
    resid_ref,
    gain_ref,
    head_ref,
    inner_ref,
    outer_ref,
    pick_ref,
    place_ref,
    live_ref,
    attn_ref,
    query_ref,
    key_ref,
    value_ref,
    out_ref,
    turn_ref,
    slot_turn_ref,
    partial_ref,
):
    block, blocks = pl.program_id(0), key_ref.shape[0] // resid_ref.shape[0]
    rows, slots = resid_ref.shape[0], pick_ref.shape[1]
    parts, columns = head_ref.shape[0], head_ref.shape[2]
    low = jnp.bfloat16
    attn = norm_fwd(resid_ref[...].astype(jnp.float32), gain_ref[...])[0].astype(low)
    attn_ref[...] = attn
    projected = jnp.zeros((rows, 3 * HEAD_DIM), jnp.float32)
    for part in range(parts):
        piece = attn[:, part * columns : (part + 1) * columns]
        projected = projected + dot(piece, head_ref[part, : 3 * HEAD_DIM], 1, 1)
    inner_cos, inner_sin = inner_ref[0], inner_ref[1]
    outer_cos, outer_sin = outer_ref[0, pl.ds(block, 1)], outer_ref[1, pl.ds(block, 1)]
    sign = jnp.where(lax.broadcasted_iota(jnp.int32, inner_cos.shape, 1) < HEAD_DIM // 2, -1.0, 1.0)
    cosine = inner_cos * outer_cos - inner_sin * outer_sin
    sine_table = (inner_sin * outer_cos + inner_cos * outer_sin) * sign
    at = pl.ds(pl.multiple_of(block * rows, rows), rows)
    turn_ref[0, at], turn_ref[1, at] = cosine, sine_table
    query = turned(projected[:, :HEAD_DIM], cosine, sine_table).astype(low)
    key_ref[at] = turned(projected[:, HEAD_DIM : 2 * HEAD_DIM], cosine, sine_table).astype(low)
    value_ref[at] = projected[:, 2 * HEAD_DIM :].astype(low)
    at = pl.ds(pl.multiple_of(block * slots, slots), slots)
    query_ref[at] = dot(pick_ref[0], query).astype(low)
    pick_wide = pick_ref[0].astype(jnp.float32)
    for index, table in enumerate((cosine, sine_table)):
        slot_turn_ref[index, at] = jnp.dot(
            pick_wide, table, precision=lax.Precision.HIGHEST, preferred_element_type=jnp.float32
        )

    @pl.when(block == blocks - 1)
    def _():
        exit_here = exit_ref[0]
        step = 2 * slots
        for index in range(blocks // 2):
            reach = (index + 1) * 2 * rows
            at = slice(index * step, (index + 1) * step)
            row = slice(index, index + 1)
            places, live = to_column(place_ref[row]), to_column(live_ref[row])
            probs = softmax_rows(query_ref[at], key_ref[:reach], places).astype(low)
            out = (dot(probs, value_ref[:reach]) * live).astype(low)
            out_ref[at] = out
            groups = step // partial_ref.shape[2]
            at = slice(index * groups, (index + 1) * groups)
            for part in range(parts):
                share = dot(out, head_ref[part, 3 * HEAD_DIM :]).astype(low)
                share = share.reshape(groups, 1, -1, columns)
                lanes = slice(part * columns, (part + 1) * columns)
                partial_ref[at, pl.ds(exit_here, 1), :, lanes] = share
                partial_ref[at, pl.ds(1 - exit_here, 1), :, lanes] = jnp.zeros_like(share)


def attend_back_kernel(
    exit_ref,
    done_ref,
    head_ref,
    out_ref,
    query_ref,
    key_ref,
    value_ref,
    turn_ref,
    slot_turn_ref,
    pick_ref,
    place_ref,
    attn_ref,
    partial_ref,
    parts_ref,
    key_sum,
    value_sum,
    turned_ref,
    head_sum,
):
    block, blocks = pl.program_id(0), key_ref.shape[0] // attn_ref.shape[0]
    rows, slots = attn_ref.shape[0], pick_ref.shape[1]
    parts, columns = head_ref.shape[0], head_ref.shape[2]
    low = jnp.bfloat16
    scale = 1.0 / math.sqrt(HEAD_DIM)

    @pl.when(block == 0)
    def _():
        key_sum[...] = jnp.zeros_like(key_sum)
        value_sum[...] = jnp.zeros_like(value_sum)
        step = 2 * slots
        width = done_ref.shape[-1]
        done = done_ref[...].reshape(-1, width)
        dout = jnp.zeros((done.shape[0], HEAD_DIM), jnp.float32)
        for part in range(parts):
            piece = done[:, part * columns : (part + 1) * columns]
            parts_ref[part, 3 * HEAD_DIM :] = dot(out_ref[...], piece, 0, 0).astype(low)
            dout = dout + dot(piece, head_ref[part, 3 * HEAD_DIM :], 1, 1)
        dout = dout.astype(low)
        for index in range(blocks // 2):
            reach = (index + 1) * 2 * rows
            at = slice(index * step, (index + 1) * step)
            places = to_column(place_ref[index : index + 1])
            probs = softmax_rows(query_ref[at], key_ref[:reach], places)
            dprobs = dot(dout[at], value_ref[:reach], 1, 1)
            delta = jnp.sum(probs * dprobs, axis=-1, keepdims=True)
            dscores = (probs * (dprobs - delta)).astype(low)
            dquery = dot(dscores, key_ref[:reach]) * scale
            dquery = turned(dquery, slot_turn_ref[0, at], -slot_turn_ref[1, at]).astype(low)
            for half in (0, 1):
                where = 2 * index + half
                turned_ref[where * rows : (where + 1) * rows, :HEAD_DIM] = dot(
                    pick_ref[where], dquery[half * slots : (half + 1) * slots], 0, 0
                ).astype(low)
            key_sum[:reach] += dot(dscores, query_ref[at], 0, 0)
            value_sum[:reach] += dot(probs.astype(low), dout[at], 0, 0)
        dkey = turned(key_sum[...] * scale, turn_ref[0], -turn_ref[1])
        turned_ref[:, HEAD_DIM : 2 * HEAD_DIM] = dkey.astype(low)
        turned_ref[:, 2 * HEAD_DIM :] = value_sum[...].astype(low)

    at = pl.ds(pl.multiple_of(block * rows, rows), rows)
    dprojected = turned_ref[at]
    for part in range(parts):
        lanes = slice(part * columns, (part + 1) * columns)
        partial_ref[:, lanes] = dot(dprojected, head_ref[part, : 3 * HEAD_DIM]).astype(low)
    term = dot(dprojected, attn_ref[...], 0, 0)

    @pl.when(block == 0)
    def _():
        head_sum[...] = term

    @pl.when(block > 0)
    def _():
        head_sum[...] += term

    @pl.when(block == blocks - 1)
    def _():
        for part in range(parts):
            lanes = slice(part * columns, (part + 1) * columns)
            parts_ref[part, : 3 * HEAD_DIM] = head_sum[:, lanes].astype(low)


def local_params():
    return dict(
        compiler_params=pltpu.CompilerParams(vmem_limit_bytes=VMEM_LIMIT),
        cost_estimate=pl.CostEstimate(flops=1, bytes_accessed=1, transcendentals=0),
    )


def whole_spec(value):
    return pl.BlockSpec(value.shape, lambda b, e: (0,) * len(value.shape))


def attend(exit_here, resid, gain, head, inner, outer, pick, places, live, slots_here):
    (tokens, width), (blocks, slots, rows) = resid.shape, pick.shape
    low = resid.dtype
    devices = blocks * slots // slots_here
    by_block = pl.BlockSpec((rows, width), lambda b, e: (b, 0))
    outs = [
        jax.ShapeDtypeStruct((tokens, width), low),
        jax.ShapeDtypeStruct((blocks * slots, HEAD_DIM), low),
        jax.ShapeDtypeStruct((tokens, HEAD_DIM), low),
        jax.ShapeDtypeStruct((tokens, HEAD_DIM), low),
        jax.ShapeDtypeStruct((blocks * slots, HEAD_DIM), low),
        jax.ShapeDtypeStruct((2, tokens, HEAD_DIM), jnp.float32),
        jax.ShapeDtypeStruct((2, blocks * slots, HEAD_DIM), jnp.float32),
        jax.ShapeDtypeStruct((devices, 2, slots_here, width), low),
    ]
    return pl.pallas_call(
        attend_kernel,
        out_shape=outs,
        grid_spec=pltpu.PrefetchScalarGridSpec(
            num_scalar_prefetch=1,
            grid=(blocks,),
            in_specs=[
                by_block,
                whole_spec(gain),
                whole_spec(head),
                whole_spec(inner),
                whole_spec(outer),
                pl.BlockSpec((1, slots, rows), lambda b, e: (b, 0, 0)),
                whole_spec(places),
                whole_spec(live),
            ],
            out_specs=[by_block] + [whole_spec(out) for out in outs[1:]],
        ),
        **local_params(),
    )(exit_here, resid, gain, head, inner, outer, pick, places, live)


def attend_back(exit_here, done, head, out, query, key, value, turn, slot_turn, pick, places, attn):
    (tokens, width), (blocks, slots, rows) = attn.shape, pick.shape
    low = attn.dtype
    devices, _, slots_here, _ = done.shape
    by_block = pl.BlockSpec((rows, width), lambda b, e: (b, 0))
    inner = [head, out, query, key, value, turn, slot_turn, pick, places]
    parts = jax.ShapeDtypeStruct(head.shape, low)
    return pl.pallas_call(
        attend_back_kernel,
        out_shape=[jax.ShapeDtypeStruct((tokens, width), low), parts],
        grid_spec=pltpu.PrefetchScalarGridSpec(
            num_scalar_prefetch=1,
            grid=(blocks,),
            in_specs=[
                pl.BlockSpec((devices, 1, slots_here, width), lambda b, e: (0, e[0], 0, 0))
            ]
            + [whole_spec(value) for value in inner]
            + [by_block],
            out_specs=[by_block, whole_spec(parts)],
            scratch_shapes=[
                pltpu.VMEM((tokens, HEAD_DIM), jnp.float32),
                pltpu.VMEM((tokens, HEAD_DIM), jnp.float32),
                pltpu.VMEM((tokens, 3 * HEAD_DIM), low),
                pltpu.VMEM((3 * HEAD_DIM, width), jnp.float32),
            ],
        ),
        **local_params(),
    )(exit_here, done, *inner, attn)


def local(kernel, outs, *values, scratch=()):
    vmem = pl.BlockSpec(memory_space=pltpu.VMEM)
    return pl.pallas_call(
        kernel,
        out_shape=[jax.ShapeDtypeStruct(shape, dtype) for shape, dtype in outs],
        in_specs=[vmem] * len(values),
        out_specs=[vmem] * len(outs),
        scratch_shapes=list(scratch),
        **local_params(),
    )(*values)


def pack_head_kernel(qkv_ref, out_ref, packed_ref):
    heads = out_ref.shape[0] // HEAD_DIM
    sharers = packed_ref.shape[0] // heads
    low = packed_ref.dtype
    for head in range(heads):
        lanes = slice(head * HEAD_DIM, (head + 1) * HEAD_DIM)
        for c in range(4):
            block = out_ref[lanes] if c == 3 else qkv_ref[c, :, lanes].T
            for sharer in range(sharers):
                packed_ref[head * sharers + sharer, c * HEAD_DIM : (c + 1) * HEAD_DIM] = block.astype(
                    low
                )


def pack_hidden_kernel(gate_up_ref, down_ref, packed_ref, turned_ref):
    parts, hidden = packed_ref.shape[0], packed_ref.shape[1] // 3
    low = packed_ref.dtype
    for c in range(2):
        for start in range(0, gate_up_ref.shape[2], 128):
            lanes = slice(start, start + 128)
            turned_ref[lanes] = gate_up_ref[:, c, lanes].T
        for part in range(parts):
            packed_ref[part, c * hidden : (c + 1) * hidden] = turned_ref[
                part * hidden : (part + 1) * hidden
            ].astype(low)
    for part in range(parts):
        packed_ref[part, 2 * hidden :] = down_ref[part * hidden : (part + 1) * hidden].astype(low)


def square_row(value):
    return jnp.sum(value * value, axis=0, keepdims=True)


def unpack_head_kernel(one_ref, two_ref, qkv_ref, out_ref, square_ref):
    heads = out_ref.shape[0] // HEAD_DIM
    sharers = one_ref.shape[0] // heads
    squares = jnp.zeros(square_ref.shape, jnp.float32)
    for head in range(heads):
        lanes = slice(head * HEAD_DIM, (head + 1) * HEAD_DIM)
        for c in range(4):
            parts_ref = one_ref if c < 2 else two_ref
            rows = slice(c % 2 * HEAD_DIM, (c % 2 + 1) * HEAD_DIM)
            total = parts_ref[head * sharers, rows].astype(jnp.float32)
            for sharer in range(1, sharers):
                total = total + parts_ref[head * sharers + sharer, rows].astype(jnp.float32)
            squares = squares + square_row(total)
            if c == 3:
                out_ref[lanes] = total
            else:
                qkv_ref[c, :, lanes] = total.T
    square_ref[...] = squares


def unpack_hidden_kernel(parts_ref, gate_up_ref, down_ref, square_ref, turned_ref):
    parts, hidden = parts_ref.shape[0], parts_ref.shape[1] // 3
    squares = jnp.zeros(square_ref.shape, jnp.float32)
    for c in range(3):
        target = down_ref if c == 2 else turned_ref
        for part in range(parts):
            block = parts_ref[part, c * hidden : (c + 1) * hidden].astype(jnp.float32)
            squares = squares + square_row(block)
            target[part * hidden : (part + 1) * hidden] = block
        if c < 2:
            for start in range(0, gate_up_ref.shape[2], 128):
                lanes = slice(start, start + 128)
                gate_up_ref[:, c, lanes] = turned_ref[lanes].T
    square_ref[...] = squares


def hidden_kernel(rows_ref, weight_ref, gate_ref, up_ref, hidden_ref, partial_ref):
    parts, columns = weight_ref.shape[0], weight_ref.shape[2]
    hidden = weight_ref.shape[1] // 3
    low = jnp.bfloat16
    gate = jnp.zeros(gate_ref.shape, jnp.float32)
    up = jnp.zeros(gate_ref.shape, jnp.float32)
    for part in range(parts):
        piece = rows_ref[:, part * columns : (part + 1) * columns]
        gate = gate + dot(piece, weight_ref[part, :hidden], 1, 1)
        up = up + dot(piece, weight_ref[part, hidden : 2 * hidden], 1, 1)
    gate_ref[...], up_ref[...] = gate, up
    value = (gate * jax.nn.sigmoid(gate) * up).astype(low)
    hidden_ref[...] = value
    for part in range(parts):
        partial_ref[:, part * columns : (part + 1) * columns] = dot(
            value, weight_ref[part, 2 * hidden :]
        ).astype(low)


def hidden_back_kernel(
    dtwo_ref, rows_ref, weight_ref, gate_ref, up_ref, hidden_ref, partial_ref, parts_ref
):
    parts, columns = weight_ref.shape[0], weight_ref.shape[2]
    hidden = weight_ref.shape[1] // 3
    low = jnp.bfloat16
    dhidden = jnp.zeros(gate_ref.shape, jnp.float32)
    for part in range(parts):
        piece = dtwo_ref[:, part * columns : (part + 1) * columns]
        dhidden = dhidden + dot(piece, weight_ref[part, 2 * hidden :], 1, 1)
        parts_ref[part, 2 * hidden :] = dot(hidden_ref[...], piece, 0, 0).astype(low)
    gate, up = gate_ref[...], up_ref[...]
    sigma = jax.nn.sigmoid(gate)
    dgate = (dhidden * up * sigma * (1.0 + gate * (1.0 - sigma))).astype(low)
    dup = (dhidden * gate * sigma).astype(low)
    for part in range(parts):
        lanes = slice(part * columns, (part + 1) * columns)
        partial_ref[:, lanes] = (
            dot(dgate, weight_ref[part, :hidden]) + dot(dup, weight_ref[part, hidden : 2 * hidden])
        ).astype(low)
        parts_ref[part, :hidden] = dot(dgate, rows_ref[:, lanes], 0, 0).astype(low)
        parts_ref[part, hidden : 2 * hidden] = dot(dup, rows_ref[:, lanes], 0, 0).astype(low)


def embed_kernel(base_ref, ids_ref, table_ref, partial_ref, low_ref, hits_ref):
    @pl.when(pl.program_id(0) == 0)
    def _():
        entries = base_ref[0] + lax.broadcasted_iota(jnp.int32, (1, table_ref.shape[0]), 1)
        hits_ref[...] = jnp.where(ids_ref[...] == entries, 1.0, 0.0).astype(hits_ref.dtype)

    table_low = table_ref[...].astype(low_ref.dtype)
    low_ref[...] = table_low
    partial_ref[...] = dot(hits_ref[...], table_low).astype(partial_ref.dtype)


def embed(base, ids, table):
    (entries, width), tokens, low = table.shape, ids.shape[0], jnp.bfloat16
    columns = 256
    by_columns = lambda rows: pl.BlockSpec((rows, columns), lambda b, e: (0, b))
    return pl.pallas_call(
        embed_kernel,
        out_shape=[
            jax.ShapeDtypeStruct((tokens, width), low),
            jax.ShapeDtypeStruct((entries, width), low),
        ],
        grid_spec=pltpu.PrefetchScalarGridSpec(
            num_scalar_prefetch=1,
            grid=(width // columns,),
            in_specs=[whole_spec(ids), by_columns(entries)],
            out_specs=[by_columns(tokens), by_columns(entries)],
            scratch_shapes=[pltpu.VMEM((tokens, entries), low)],
        ),
        **local_params(),
    )(base, ids, table)


def logits_kernel(one_ref, two_ref, table_ref, target_ref, entry_ref, logits_ref, stats_ref):
    slots, step, lanes = one_ref.shape[0], 256, stats_ref.shape[1]
    for e, rows_ref in enumerate((one_ref, two_ref)):
        for start in range(0, slots, step):
            values = dot(rows_ref[start : start + step], table_ref[...], 1, 1)
            logits_ref[e * slots + start : e * slots + start + step] = values
            top = jnp.max(values, axis=1, keepdims=True)
            mass = jnp.sum(jnp.exp(values - top), axis=1, keepdims=True)
            for part in range(0, step, lanes):
                row = (e * slots + start + part) // lanes
                at = slice(part, part + lanes)
                hit = to_column(target_ref[row : row + 1]) == entry_ref[...]
                found = jnp.sum(jnp.where(hit, values[at], 0.0), axis=1, keepdims=True)
                for stat, column in enumerate((top[at], mass[at], found)):
                    index = stat * (2 * slots // lanes) + row
                    stats_ref[index : index + 1] = to_row(column)


def head_grad_kernel(
    logits_ref, lse_ref, weight_ref, target_ref, entry_ref, table_ref, one_ref, two_ref, *terms
):
    slots, lanes, step = one_ref.shape[0], lse_ref.shape[1], 256
    low = jnp.bfloat16
    for e, grad_ref in enumerate((one_ref, two_ref)):
        for start in range(0, slots, lanes):
            row = (e * slots + start) // lanes
            lse, weight, target = (
                to_column(ref[row : row + 1]) for ref in (lse_ref, weight_ref, target_ref)
            )
            values = logits_ref[row * lanes : (row + 1) * lanes]
            hit = jnp.where(target == entry_ref[...], 1.0, 0.0)
            grad_ref[start : start + lanes] = (weight * (jnp.exp(values - lse) - hit)).astype(low)
        for start in range(0, slots, step):
            at = slice(start, start + step)
            terms[e][at] = dot(grad_ref[at], table_ref[...]).astype(low)


def table_grad_kernel(
    base_ref, ids_ref, one_ref, two_ref, rows_one, rows_two, dzero_ref, grad_ref, square_ref, left_ref
):
    slots = one_ref.shape[0]

    @pl.when(pl.program_id(0) == 0)
    def _():
        entries = base_ref[0] + lax.broadcasted_iota(jnp.int32, (left_ref.shape[0], 1), 0)
        left_ref[:, :slots] = one_ref[...].T
        left_ref[:, slots : 2 * slots] = two_ref[...].T
        hits = jnp.where(ids_ref[...] == entries, 1.0, 0.0)
        left_ref[:, 2 * slots :] = hits.astype(left_ref.dtype)

    grad = (
        dot(left_ref[:, :slots], rows_one[...])
        + dot(left_ref[:, slots : 2 * slots], rows_two[...])
        + dot(left_ref[:, 2 * slots :], dzero_ref[...])
    )
    grad_ref[...] = grad
    square_ref[...] = square_row(grad)


def table_gradient(base, ids, grads, rows, dzero):
    slots, entries = grads[0].shape
    tokens, width = dzero.shape
    columns = 256
    by_columns = lambda count: pl.BlockSpec((count, columns), lambda b, e: (0, b))
    return pl.pallas_call(
        table_grad_kernel,
        out_shape=[
            jax.ShapeDtypeStruct((entries, width), jnp.float32),
            jax.ShapeDtypeStruct((1, width), jnp.float32),
        ],
        grid_spec=pltpu.PrefetchScalarGridSpec(
            num_scalar_prefetch=1,
            grid=(width // columns,),
            in_specs=[whole_spec(ids), whole_spec(grads[0]), whole_spec(grads[1])]
            + [by_columns(slots), by_columns(slots), by_columns(tokens)],
            out_specs=[by_columns(entries), by_columns(1)],
            scratch_shapes=[pltpu.VMEM((entries, 2 * slots + tokens), dzero.dtype)],
        ),
        **local_params(),
    )(base, ids, *grads, *rows, dzero)


def norm_fwd(values, gain):
    row_scale = lax.rsqrt(jnp.mean(values * values, axis=-1, keepdims=True) + EPS_NORM)
    unit_rows = values * row_scale
    return (unit_rows * gain, unit_rows, row_scale)


def norm_back(unit_rows, row_scale, gain, gradient):
    weighted = gradient * gain
    back_rows = row_scale * (
        weighted - unit_rows * jnp.mean(weighted * unit_rows, axis=-1, keepdims=True)
    )
    return (back_rows, jnp.sum(gradient * unit_rows, axis=0))


def rotary(places, width):
    half_width = width // 2
    frequency = jnp.exp(
        jnp.arange(half_width, dtype=jnp.float32) * (-math.log(10000.0) / half_width)
    )
    angles = places.astype(jnp.float32)[:, None] * frequency[None, :]
    return (jnp.cos(angles), jnp.sin(angles))


def rotate_pairs(values, cosine, sine_table):
    half_width = values.shape[-1] // 2
    front_half = values[..., :half_width]
    back_half = values[..., half_width:]
    return jnp.concatenate(
        [
            front_half * cosine - back_half * sine_table,
            back_half * cosine + front_half * sine_table,
        ],
        axis=-1,
    )


def dot(left, right, left_dim=1, right_dim=0):
    return lax.dot_general(
        left, right, (((left_dim,), (right_dim,)), ((), ())), preferred_element_type=jnp.float32
    )


def adam_update(weight, moment_one, moment_two, gradient, rate, decay):
    moment_one = BETA_ONE * moment_one + (1.0 - BETA_ONE) * gradient
    moment_two = BETA_TWO * moment_two + (1.0 - BETA_TWO) * gradient * gradient
    ratio = (
        moment_one
        / (1.0 - BETA_ONE**STEP)
        / (jnp.sqrt(moment_two / (1.0 - BETA_TWO**STEP)) + ADAM_EPS)
    )
    return (weight - rate * (ratio + decay * weight), moment_one, moment_two)


def body(
    token_ids,
    target_ids,
    exit_mask,
    table,
    table_first,
    table_second,
    qkv_weight,
    qkv_first,
    qkv_second,
    out_weight,
    out_first,
    out_second,
    gate_up_weight,
    gate_up_first,
    gate_up_second,
    down_weight,
    down_first,
    down_second,
    gains,
    gains_first,
    gains_second,
):
    low = jnp.bfloat16
    data_size, model_size = lax.axis_size("dp"), lax.axis_size("mp")
    data_index, model_index = lax.axis_index("dp"), lax.axis_index("mp")
    devices = data_size * model_size
    block_rows = token_ids.shape[0]
    tokens = block_rows * data_size
    width = table.shape[1]
    width_here = qkv_weight.shape[0]
    heads_here = qkv_weight.shape[2] // HEAD_DIM
    hidden_here = down_weight.shape[0] // data_size
    vocab_here = table.shape[0]
    device_index = data_index * model_size + model_index
    vocab_ids = device_index * vocab_here + jnp.arange(vocab_here, dtype=jnp.int32)
    score_scale = 1.0 / math.sqrt(HEAD_DIM)

    sharers = data_size // heads_here
    shares = sharers // 2
    share_slots = data_size // shares * R_DEV
    exit_here = data_index % sharers % 2
    share_here = data_index % sharers // 2
    slots_here = R_DEV // model_size
    rows_here = block_rows // model_size

    ints, gain_low = exchange(
        [
            jnp.concatenate([token_ids[None], target_ids[None], exit_mask]),
            jnp.pad(gains.astype(low), ((0, 13), (0, 0))),
        ],
        (True, True),
        0,
    )
    gain_rows = jnp.moveaxis(gain_low[:, :3], 0, 1).reshape(3, width).astype(jnp.float32)
    all_ids = ints[:, 0].reshape(tokens)
    mask_blocks = jnp.moveaxis(ints[:, 2:], 0, 1)
    slot_ids = jnp.arange(R_DEV, dtype=jnp.int32)
    slot_ranks = jnp.cumsum(mask_blocks, axis=2) - 1
    pick_int = (
        (slot_ranks[:, :, None, :] == slot_ids[:, None]) & (mask_blocks[:, :, None, :] == 1)
    ).astype(jnp.int32)
    pick_low = pick_int.astype(low)
    token_places = jnp.arange(tokens, dtype=jnp.int32)
    slot_targets = jnp.sum(pick_int * ints[:, 1][None, :, None, :], axis=3).reshape(2, -1)
    slot_places = jnp.sum(
        pick_int * token_places.reshape(1, data_size, 1, block_rows), axis=3
    ).reshape(2, -1)
    live = (slot_ids < jnp.sum(mask_blocks, axis=2)[:, :, None]).astype(jnp.float32).reshape(2, -1)
    counts = jnp.sum(live, axis=1)

    packed = kernel_mesh()
    head_shape = (data_size, 4 * HEAD_DIM, width_here)
    hidden_shape = (data_size, 3 * hidden_here, width_here)
    if packed:
        (head_rows,) = local(
            pack_head_kernel,
            [(head_shape, low)],
            jnp.transpose(qkv_weight, (1, 0, 2)),
            out_weight,
        )
    else:
        head_rows = jnp.moveaxis(
            qkv_weight.astype(low).reshape(width_here, 3, heads_here, HEAD_DIM), 0, 3
        )
        head_rows = jnp.concatenate(
            [
                jnp.moveaxis(head_rows, 0, 1).reshape(heads_here, 3 * HEAD_DIM, width_here),
                out_weight.astype(low).reshape(heads_here, HEAD_DIM, width_here),
            ],
            axis=1,
        )
        head_rows = jnp.repeat(head_rows, sharers, axis=0)
    head_rows = swap_blocks(after(head_rows, ints))

    base = (device_index * vocab_here)[None]
    if packed:
        id_rows, table_low = embed(base, all_ids[:, None], table)
    else:
        table_low = table.astype(low)
        id_hits = (all_ids[:, None] == vocab_ids[None, :]).astype(low)
        id_rows = dot(id_hits, table_low).astype(low)
    if packed:
        (hidden_rows,) = local(
            pack_hidden_kernel,
            [(hidden_shape, low)],
            gate_up_weight,
            down_weight,
            scratch=[pltpu.VMEM((gate_up_weight.shape[2], width_here), jnp.float32)],
        )
    else:
        hidden_rows = jnp.moveaxis(
            gate_up_weight.astype(low).reshape(width_here, 2, data_size, hidden_here), 0, 3
        )
        hidden_rows = jnp.concatenate(
            [
                jnp.moveaxis(hidden_rows, 0, 1).reshape(data_size, 2 * hidden_here, width_here),
                down_weight.astype(low).reshape(data_size, hidden_here, width_here),
            ],
            axis=1,
        )
    (resid_low,) = relay([after(id_rows, hidden_rows)], lambda p, total, extras: (total.astype(low), (), ()), 1)

    hidden_rows = swap_blocks(after(hidden_rows, resid_low))

    pick_share = lax.dynamic_slice_in_dim(
        lax.dynamic_index_in_dim(pick_low, exit_here, 0, keepdims=False),
        share_here * (data_size // shares),
        data_size // shares,
        0,
    )
    def share_of(per_slot):
        return lax.dynamic_slice(per_slot, (exit_here, share_here * share_slots), (1, share_slots))[
            0
        ]

    places_share, live_share = share_of(slot_places), share_of(live)
    if packed:

        def turns(places):
            return jnp.stack([jnp.concatenate([part, part], axis=1) for part in rotary(places, HEAD_DIM)])

        attn_low, query_slots, key_low, value_low, attn_out, turn, slot_turn, out_partial = attend(
            exit_here[None],
            resid_low,
            gain_rows[:1],
            head_rows,
            turns(token_places[:block_rows]),
            turns(token_places[::block_rows]),
            pick_share,
            places_share.reshape(-1, 2 * R_DEV),
            live_share.reshape(-1, 2 * R_DEV),
            slots_here,
        )
        out_partial = out_partial.reshape(-1, width)
    else:
        head_rows = jnp.moveaxis(head_rows, 0, 1).reshape(4 * HEAD_DIM, width)
        qkv_head, out_head = head_rows[: 3 * HEAD_DIM], head_rows[3 * HEAD_DIM :]
        cosine, sine_table = rotary(token_places, HEAD_DIM)
        cosine_share, sine_share = rotary(places_share, HEAD_DIM)
        attn_low = norm_fwd(resid_low.astype(jnp.float32), gain_rows[0])[0].astype(low)

        projected = dot(attn_low, qkv_head, 1, 1)
        query_low = rotate_pairs(projected[:, :HEAD_DIM], cosine, sine_table).astype(low)
        key_low = rotate_pairs(projected[:, HEAD_DIM : 2 * HEAD_DIM], cosine, sine_table).astype(low)
        value_low = projected[:, 2 * HEAD_DIM :].astype(low)
        query_share = lax.dynamic_slice_in_dim(
            query_low.reshape(data_size, block_rows, HEAD_DIM),
            share_here * (data_size // shares),
            data_size // shares,
            0,
        )
        query_slots = (
            jnp.einsum("brt,btd->brd", pick_share, query_share, preferred_element_type=jnp.float32)
            .astype(low)
            .reshape(share_slots, HEAD_DIM)
        )

        scores = dot(query_slots, key_low, 1, 1) * score_scale
        allowed = token_places[None, :] <= places_share[:, None]
        scores = jnp.where(allowed, scores, NEG)
        weights = jnp.exp(scores - jnp.max(scores, axis=-1, keepdims=True))
        probs = weights / jnp.sum(weights, axis=-1, keepdims=True)
        probs_low = probs.astype(low)
        attn_out = (dot(probs_low, value_low) * live_share[:, None]).astype(low)

        def spread(per_share):
            if shares > 1:
                full = jnp.zeros((data_size * R_DEV, width), per_share.dtype)
                per_share = lax.dynamic_update_slice_in_dim(
                    full, per_share, share_here * share_slots, 0
                )
            exits = jnp.arange(2, dtype=jnp.int32)[None, :, None, None]
            rows = per_share.reshape(devices, 1, slots_here, width)
            return jnp.where(exits == exit_here, rows, 0).reshape(-1, width)
        out_partial = spread(dot(attn_out, out_head).astype(low))

    block_low = lax.dynamic_slice_in_dim(resid_low, data_index * block_rows, block_rows, 0)
    pick_here = lax.dynamic_slice(
        pick_low,
        (0, data_index, model_index * slots_here, 0),
        (2, 1, slots_here, block_rows),
    ).reshape(2 * slots_here, block_rows)

    def first_step(p, total, extras):
        resid = extras[0][p * GROUP : (p + 1) * GROUP] + total
        gain = 2 if p == 0 else 1
        return (norm_fwd(resid, extras[1][gain : gain + 1])[0].astype(low), (resid,), ())

    exit_rows_one, mlp_low, resid_one = relay(
        [out_partial],
        first_step,
        2,
        extras=[dot(pick_here, block_low), gain_rows],
        kept=1,
        split=True,
    )

    slots = mlp_low.shape[0]
    if packed:
        gate_part, up_part, hidden_low, mlp_partial = local(
            hidden_kernel,
            [
                ((slots, hidden_here), jnp.float32),
                ((slots, hidden_here), jnp.float32),
                ((slots, hidden_here), low),
                ((slots, width), low),
            ],
            mlp_low,
            hidden_rows,
        )
    else:
        hidden_rows = jnp.moveaxis(hidden_rows, 0, 1).reshape(3 * hidden_here, width)
        gate_up_head, down_head = hidden_rows[: 2 * hidden_here], hidden_rows[2 * hidden_here :]
        gate_up = dot(mlp_low, gate_up_head, 1, 1)
        gate_part, up_part = gate_up[:, :hidden_here], gate_up[:, hidden_here:]
        gate_sigma = jax.nn.sigmoid(gate_part)
        hidden_low = (gate_part * gate_sigma * up_part).astype(low)
        mlp_partial = dot(hidden_low, down_head).astype(low)

    def second_step(p, total, extras):
        resid = extras[0][GROUP : 2 * GROUP] + total
        return (norm_fwd(resid, extras[1][2:3])[0].astype(low), (resid,), ())

    exit_rows_two, resid_two = relay(
        [mlp_partial], second_step, 3, extras=[resid_one, gain_rows], kept=1
    )

    exit_rows = (exit_rows_one, exit_rows_two)
    if packed:
        target_rows, entry_row = slot_targets.reshape(-1, 128), vocab_ids[None]
        logits, stats = local(
            logits_kernel,
            [((2 * slots, vocab_here), jnp.float32), ((3 * 2 * slots // 128, 128), jnp.float32)],
            *exit_rows,
            table_low,
            target_rows,
            entry_row,
        )
    else:
        logits = [dot(rows, table_low, 1, 1) for rows in exit_rows]
        hits = [slot_targets[e][:, None] == vocab_ids[None, :] for e in range(2)]
        tops = [jnp.max(values, axis=1) for values in logits]
        masses = [
            jnp.sum(jnp.exp(values - top[:, None]), axis=1) for values, top in zip(logits, tops)
        ]
        found = [jnp.sum(jnp.where(hit, values, 0.0), axis=1) for hit, values in zip(hits, logits)]
        stats = jnp.concatenate(tops + masses + found).reshape(-1, 128)
    stats = gather_small(stats, 4).reshape(devices, 3, 2, -1)
    row_top = jnp.max(stats[:, 0], axis=0)
    row_mass = jnp.sum(stats[:, 1] * jnp.exp(stats[:, 0] - row_top), axis=0)
    row_lse = row_top + jnp.log(row_mass)
    entropy = row_lse - jnp.sum(stats[:, 2], axis=0)
    loss_sums = jnp.sum(entropy * live, axis=1)
    row_weight = live * (jnp.array(EXIT_SCALE, jnp.float32) / counts)[:, None]
    if packed:
        *grad_logits, one_terms, two_terms = local(
            head_grad_kernel,
            [((slots, vocab_here), low)] * 2 + [((slots, width), low)] * 2,
            logits,
            row_lse.reshape(-1, 128),
            row_weight.reshape(-1, 128),
            target_rows,
            entry_row,
            table_low,
        )
        row_terms = [one_terms, two_terms]
    else:
        grad_logits = [
            (
                row_weight[e][:, None]
                * (jnp.exp(logits[e] - row_lse[e][:, None]) - hits[e].astype(jnp.float32))
            ).astype(low)
            for e in range(2)
        ]
        row_terms = [dot(grad, table_low).astype(low) for grad in grad_logits]

    def head_step(p, total, extras):
        values = extras[0][:GROUP] if p == 0 else extras[1][...]
        gain = extras[2][2:3]
        _, unit, scale = norm_fwd(values, gain)
        back, gain_grad = norm_back(unit, scale, gain, total)
        return (None if p == 0 else back.astype(low), (back,), (gain_grad[None],))

    dtwo_low, dexits, final_grad = relay(
        row_terms,
        head_step,
        5,
        extras=[resid_one, resid_two, gain_rows],
        kept=1,
        sums=1,
        order=[1, 0],
        slot=lambda p: None if p == 0 else 0,
    )
    if packed:
        dmlp_partial, hidden_parts = local(
            hidden_back_kernel,
            [((slots, width), low), (hidden_shape, low)],
            dtwo_low,
            mlp_low,
            hidden_rows,
            gate_part,
            up_part,
            hidden_low,
        )
    else:
        down_local = dot(hidden_low, dtwo_low, 0, 0)
        dhidden = dot(dtwo_low, down_head, 1, 1)
        dgate = dhidden * up_part * gate_sigma * (1.0 + gate_part * (1.0 - gate_sigma))
        dup_part = dhidden * gate_part * gate_sigma
        dgate_up = jnp.concatenate([dgate, dup_part], axis=1).astype(low)
        gate_up_local = dot(dgate_up, mlp_low, 0, 0)
        dmlp_partial = dot(dgate_up, gate_up_head).astype(low)
        hidden_parts = jnp.concatenate([gate_up_local.astype(low), down_local.astype(low)])
        hidden_parts = jnp.moveaxis(hidden_parts.reshape(-1, data_size, width_here), 1, 0)

    def mlp_step(p, total, extras):
        gain = extras[2][1:2]
        _, unit, scale = norm_fwd(extras[0][GROUP : 2 * GROUP], gain)
        back, gain_grad = norm_back(unit, scale, gain, total)
        return ((extras[1][GROUP : 2 * GROUP] + back).astype(low), (), (gain_grad[None],))

    done_low, mlp_grad = relay(
        [dmlp_partial],
        mlp_step,
        6,
        extras=[resid_one, dexits, gain_rows],
        sums=1,
        slot=lambda p: 1,
        ready=dexits[:GROUP].astype(low),
    )
    hidden_parts = swap_blocks(after(hidden_parts, done_low))
    done_low = done_low.reshape(devices, 2, slots_here, width)

    if kernel_mesh():
        zero_partial, head_parts = attend_back(
            exit_here[None],
            done_low,
            head_rows,
            attn_out,
            query_slots,
            key_low,
            value_low,
            turn,
            slot_turn,
            pick_share,
            places_share.reshape(-1, 2 * R_DEV),
            attn_low,
        )
    else:
        done_share = lax.dynamic_slice(
            lax.dynamic_index_in_dim(done_low, exit_here, 1, keepdims=False).reshape(-1, width),
            (share_here * share_slots, 0),
            (share_slots, width),
        )
        out_local = dot(attn_out, done_share, 0, 0)
        dattn_low = dot(done_share, out_head, 1, 1).astype(low)
        dprobs = dot(dattn_low, value_low, 1, 1)
        delta = jnp.sum(probs * dprobs, axis=-1, keepdims=True)
        dscores = (probs * (dprobs - delta)).astype(low)
        dquery = rotate_pairs(dot(dscores, key_low) * score_scale, cosine_share, -sine_share).astype(
            low
        )
        dquery_share = jnp.einsum(
            "brt,brd->btd",
            pick_share,
            dquery.reshape(-1, R_DEV, HEAD_DIM),
            preferred_element_type=jnp.float32,
        ).astype(low)
        if shares > 1:
            dquery_share = lax.dynamic_update_slice_in_dim(
                jnp.zeros((data_size, block_rows, HEAD_DIM), low),
                dquery_share,
                share_here * (data_size // shares),
                0,
            )
        dkey = rotate_pairs(dot(dscores, query_slots, 0, 0) * score_scale, cosine, -sine_table)
        dvalue = dot(probs_low, dattn_low, 0, 0)
        dprojected = jnp.concatenate(
            [dquery_share.reshape(tokens, HEAD_DIM), dkey.astype(low), dvalue.astype(low)], axis=1
        )
        head_parts = jnp.concatenate([dot(dprojected, attn_low, 0, 0).astype(low), out_local.astype(low)])
        zero_partial = dot(dprojected, qkv_head).astype(low)
        head_parts = jnp.moveaxis(head_parts.reshape(-1, data_size, width_here), 1, 0)

    resid_here = lax.dynamic_slice_in_dim(resid_low, device_index * rows_here, rows_here, 0)
    done_block = lax.dynamic_slice_in_dim(done_low, data_index * model_size, model_size, 0)
    pick_block = lax.dynamic_slice(
        pick_low,
        (0, data_index, 0, model_index * rows_here),
        (2, 1, R_DEV, rows_here),
    ).reshape(2, model_size, slots_here, rows_here)
    dresid_here = jnp.einsum(
        "emst,mesd->td", pick_block, done_block, preferred_element_type=jnp.float32
    )

    def zero_step(p, total, extras):
        at = slice(p * GROUP, (p + 1) * GROUP)
        gain = extras[2][:1]
        _, unit, scale = norm_fwd(extras[0][at], gain)
        back, gain_grad = norm_back(unit, scale, gain, total)
        return ((extras[1][at] + back).astype(low), (), (gain_grad[None],))

    ride = 2 * HEAD_DIM
    dzero_low, attn_grad, ridden = relay(
        [after(zero_partial, hidden_parts)],
        zero_step,
        7,
        extras=[resid_here.astype(jnp.float32), dresid_here, gain_rows],
        sums=1,
        cargo=head_parts[:, :ride],
    )
    later = swap_blocks(after(head_parts[:, ride:], dzero_low))
    if packed:
        table_grad, squares = table_gradient(
            base, all_ids[None, :], grad_logits, exit_rows, dzero_low
        )
        squares = jnp.sum(squares)
    else:
        table_grad = dot(id_hits, dzero_low, 0, 0)
        for grad, rows in zip(grad_logits, exit_rows):
            table_grad = table_grad + dot(grad, rows, 0, 0)
        squares = jnp.sum(table_grad * table_grad)

    square_shape = ((1, width_here), jnp.float32)
    if packed:
        qkv_grad, out_grad, head_squares = local(
            unpack_head_kernel,
            [
                ((3, width_here, qkv_weight.shape[2]), jnp.float32),
                (out_weight.shape, jnp.float32),
                square_shape,
            ],
            ridden,
            later,
        )
        qkv_grad = jnp.transpose(qkv_grad, (1, 0, 2))
        gate_up_grad, down_grad, hidden_squares = local(
            unpack_hidden_kernel,
            [
                (gate_up_weight.shape, jnp.float32),
                (down_weight.shape, jnp.float32),
                square_shape,
            ],
            hidden_parts,
            scratch=[pltpu.VMEM((gate_up_weight.shape[2], width_here), jnp.float32)],
        )
        squares = squares + jnp.sum(head_squares) + jnp.sum(hidden_squares)
    else:
        head_grad = jnp.sum(
            jnp.concatenate([ridden, later], axis=1).reshape(heads_here, sharers, 4, HEAD_DIM, width_here).astype(jnp.float32),
            axis=1,
        )
        qkv_grad = jnp.transpose(head_grad[:, :3], (3, 1, 0, 2)).reshape(qkv_weight.shape)
        out_grad = head_grad[:, 3].reshape(out_weight.shape)
        hidden_parts = hidden_parts.astype(jnp.float32)
        gate_up_grad = hidden_parts[:, : 2 * hidden_here].reshape(
            data_size, 2, hidden_here, width_here
        )
        gate_up_grad = jnp.transpose(gate_up_grad, (3, 1, 0, 2)).reshape(gate_up_weight.shape)
        down_grad = hidden_parts[:, 2 * hidden_here :].reshape(down_weight.shape)
        squares = (
            squares
            + jnp.sum(qkv_grad * qkv_grad)
            + jnp.sum(out_grad * out_grad)
            + jnp.sum(gate_up_grad * gate_up_grad)
            + jnp.sum(down_grad * down_grad)
        )
    parts = jnp.concatenate(
        [
            jnp.concatenate([attn_grad, mlp_grad, final_grad]).reshape(-1, 128),
            jnp.full((8, 128), squares),
        ]
    )
    parts = jnp.sum(gather_small(parts, 8), axis=0)
    gain_sums = parts[:-8].reshape(3, width)
    gain_grad = lax.dynamic_slice_in_dim(gain_sums, data_index * width_here, width_here, 1)
    grad_norm = jnp.sqrt(parts[-1, 0] + jnp.sum(gain_sums * gain_sums))
    factor = jnp.minimum(1.0, CLIP / (grad_norm + 1e-06))
    table_new = adam_update(
        table, table_first, table_second, table_grad * factor, RATE_MATRIX, DECAY
    )
    qkv_new = adam_update(qkv_weight, qkv_first, qkv_second, qkv_grad * factor, RATE_MATRIX, DECAY)
    out_new = adam_update(out_weight, out_first, out_second, out_grad * factor, RATE_MATRIX, DECAY)
    gate_up_new = adam_update(
        gate_up_weight, gate_up_first, gate_up_second, gate_up_grad * factor, RATE_MATRIX, DECAY
    )
    down_new = adam_update(
        down_weight, down_first, down_second, down_grad * factor, RATE_MATRIX, DECAY
    )
    gains_new = adam_update(gains, gains_first, gains_second, gain_grad * factor, RATE_GAIN, 0.0)
    return (
        loss_sums,
        counts,
        grad_norm,
        *table_new,
        *qkv_new,
        *out_new,
        *gate_up_new,
        *down_new,
        *gains_new,
    )


def solution(mesh):
    rows, sides, cols, gain = P(BOTH, None), P("dp", None, "mp"), P("mp", "dp"), P(None, "dp")
    state = (rows,) * 3 + (sides,) * 3 + (cols,) * 3 + (sides,) * 3 + (cols,) * 3 + (gain,) * 3
    return jax.shard_map(
        body,
        mesh=mesh,
        in_specs=(P("dp"), P("dp"), P(None, "dp")) + state,
        out_specs=(P(), P(), P()) + state,
        check_vma=False,
    )
```

```python
import functools
import math

import jax
import jax.numpy as jnp
from jax import lax
from jax.experimental import pallas as pl
from jax.experimental.pallas import tpu as pltpu
from jax.sharding import PartitionSpec as P

HEAD_DIM = 128
R_DEV = 64
STEP = 10


EPS_NORM = 1e-05
BETA_ONE = 0.9
BETA_TWO = 0.95
ADAM_EPS = 1e-08
DECAY = 0.1
RATE_MATRIX = 0.02
RATE_GAIN = 1.0
CLIP = 0.02
EXIT_SCALE = (1.0 / 3.0, 2.0 / 3.0)
NEG = -1e30
BOTH = ("dp", "mp")
MESH = pl.DeviceIdType.MESH
MIB = 1024 * 1024
ANY = pl.BlockSpec(memory_space=pl.ANY)
GROUP = 16
CARGO_EARLY = 4
CARGO_LATE = 2


def kernel_mesh():
    return lax.axis_size("dp") == 8 and lax.axis_size("mp") == 4


def comm_params(ident, room):
    return pltpu.CompilerParams(
        collective_id=ident, has_side_effects=True, vmem_limit_bytes=room * MIB
    )


class Links:
    def __init__(self, send_sem, recv_sem, cargo=False):
        data_index, model_index = lax.axis_index("dp"), lax.axis_index("mp")
        z, y, x, c = data_index // 2, data_index % 2, model_index // 2, model_index % 2
        self.c = c
        self.zs = (z, z + 1 - 2 * (z % 2), (z + 2) % 4, 3 - z)
        self.corners = ((y, x), (y, 1 - x), (1 - y, x), (1 - y, 1 - x))
        self.z_side = [(zd * 2 + y, model_index) for zd in self.zs]
        self.x_side = (data_index, (1 - x) * 2 + c)
        self.y_side = (z * 2 + 1 - y, model_index)
        self.c_side = (data_index, x * 2 + 1 - c)
        self.send_sem, self.recv_sem, self.sent, self.slots = send_sem, recv_sem, [], {}
        peers = self.z_side[1:] + [self.x_side, self.y_side, self.c_side]
        if cargo:
            peers += [(zd * 2 + 1 - y, model_index) for zd in self.zs[1:]]
        barrier = pltpu.get_barrier_semaphore()
        for peer in peers:
            pl.semaphore_signal(barrier, inc=1, device_id=peer, device_id_type=MESH)
        pl.semaphore_wait(barrier, len(peers))

    def first_row(self, rows, d, group, core=0):
        y, x = self.corners[group]
        c = 1 - self.c if core else self.c
        return ((self.zs[d] * 2 + y) * 4 + x * 2 + c) * rows

    def recv(self, name):
        return self.recv_sem.at[self.slots.setdefault(name, len(self.slots))]

    def send(self, source, target, device, name):
        copy = pltpu.make_async_remote_copy(
            src_ref=source,
            dst_ref=target,
            send_sem=self.send_sem.at[len(self.sent)],
            recv_sem=self.recv(name),
            device_id=device,
            device_id_type=MESH,
        )
        copy.start()
        self.sent.append(copy)

    def arrived(self, ref, name):
        pltpu.make_async_copy(ref, ref, self.recv(name)).wait()
        return ref

    def finish(self):
        for copy in self.sent:
            copy.wait_send()


def cargo_cuts(shape):
    return 2 if shape[1] % 32 == 0 else 1


class Cargo:
    def __init__(self, source, target, send_sem, recv_sem, own_sem):
        self.me, self.model_index = lax.axis_index("dp"), lax.axis_index("mp")
        self.source, self.target = source, target
        self.send_sem, self.recv_sem, self.sent = send_sem, recv_sem, []
        self.own = pltpu.make_async_copy(source.at[self.me], target.at[self.me], own_sem)
        self.own.start()
        count = cargo_cuts(source.shape)
        size = source.shape[1] // count
        cuts = [pl.ds(cut * size, size) for cut in range(count)]
        self.cuts = [(shift, cut) for cut in cuts for shift in (4, 3, 5, 2, 6, 1, 7)]

    def load(self, count):
        for _ in range(count):
            index = len(self.sent)
            if index == len(self.cuts):
                return
            shift, cut = self.cuts[index]
            peer = lax.rem(self.me + shift, 8)
            copy = pltpu.make_async_remote_copy(
                src_ref=self.source.at[peer, cut],
                dst_ref=self.target.at[self.me, cut],
                send_sem=self.send_sem.at[index],
                recv_sem=self.recv_sem.at[index],
                device_id=(peer, self.model_index),
                device_id_type=MESH,
            )
            copy.start()
            self.sent.append(copy)

    def finish(self):
        self.load(len(self.cuts))
        self.own.wait()
        for index, (shift, cut) in enumerate(self.cuts):
            here = self.target.at[lax.rem(self.me + 8 - shift, 8), cut]
            pltpu.make_async_copy(here, here, self.recv_sem.at[index]).wait()
        for copy in self.sent:
            copy.wait_send()


class Gather:
    def __init__(self, link, outs, steps, own_sem):
        self.link, self.outs, self.steps, self.own_sem = link, outs, steps, own_sem
        self.owns = []

    def spot(self, g, d, group, core=0):
        if len(self.outs) > 1:
            out, start = self.outs[g], self.link.first_row(GROUP, d, group, core)
        else:
            out, start = self.outs[0], self.link.first_row(self.steps * GROUP, d, group, core)
            start = start + g * GROUP
        return out.at[pl.ds(pl.multiple_of(start, GROUP), GROUP)]

    def send(self, g, source, device, here, there):
        self.link.send(source, self.spot(g, *here), device, ("gather", g, *there))

    def arrived(self, g, d, group, core):
        return self.link.arrived(self.spot(g, d, group, core), ("gather", g, d, group, core))

    def begin(self, g, source):
        link = self.link
        own = pltpu.make_async_copy(source, self.spot(g, 0, 0), self.own_sem.at[g])
        own.start()
        self.owns.append(own)
        for d in (1, 2, 3):
            self.send(g, source, link.z_side[d], (0, 0), (d, 0, 0))
        self.send(g, source, link.x_side, (0, 0), (0, 1, 0))
        self.send(g, source, link.y_side, (0, 0), (0, 2, 0))
        self.send(g, source, link.c_side, (0, 0), (0, 0, 1))

    def from_z(self, g, d):
        here = self.arrived(g, d, 0, 0)
        self.send(g, here, self.link.x_side, (d, 0), (d, 1, 0))
        self.send(g, here, self.link.y_side, (d, 0), (d, 2, 0))
        self.send(g, here, self.link.c_side, (d, 0), (d, 0, 1))

    def from_sides(self, g, d):
        for group, side in ((1, self.link.y_side), (2, self.link.x_side)):
            here = self.arrived(g, d, group, 0)
            if (d % 2 == 0) == (group == 1):
                self.send(g, here, side, (d, group), (d, 3, 0))
            self.send(g, here, self.link.c_side, (d, group), (d, group, 1))

    def first(self, g):
        self.from_z(g, 1)
        self.from_sides(g, 0)
        self.from_z(g, 2)
        self.from_z(g, 3)

    def second(self, g):
        for d in (1, 2, 3):
            self.from_sides(g, d)

    def third(self, g):
        for d in range(4):
            here = self.arrived(g, d, 3, 0)
            self.send(g, here, self.link.c_side, (d, 3), (d, 3, 1))

    def finish(self):
        for g in range(self.steps):
            for d in range(4):
                for group in range(4):
                    self.arrived(g, d, group, 1)
        for own in self.owns:
            own.wait()


CORNER = [(d, 3) for d in range(4)]
SIDES = [(1, 1), (3, 1), (0, 2), (2, 2), (0, 1), (2, 1), (1, 2), (3, 2)]
COLUMN = [(d, 0) for d in (3, 2, 1)]


class Scatter:
    def __init__(self, link, partials, rows, order, buffers, own_sem):
        self.link, self.partials, self.rows = link, partials, rows
        self.mine, self.core, self.corner, self.side, self.column = buffers
        self.owns = {}
        for p in order:
            for d, group in CORNER + SIDES + COLUMN + [(0, 0)]:
                k = d * 4 + group
                here = self.mine.at[k, pl.ds(p * GROUP, GROUP)]
                own = pltpu.make_async_copy(self.spot(p, d, group), here, own_sem.at[p * 16 + k])
                own.start()
                self.owns[p, k] = own
                self.send(p, self.spot(p, d, group, 1), self.core, k, link.c_side, "core")

    def spot(self, p, d, group, core=0):
        if len(self.partials) > 1:
            partial, start = self.partials[p], self.link.first_row(GROUP, d, group, core)
        else:
            partial, start = self.partials[0], self.link.first_row(self.rows, d, group, core)
            start = start + p * GROUP
        return partial.at[pl.ds(pl.multiple_of(start, GROUP), GROUP)]

    def send(self, p, source, buffer, k, device, name):
        self.link.send(source, buffer.at[k, pl.ds(p * GROUP, GROUP)], device, (name, p, k))

    def term(self, p, buffer, k, name):
        return self.link.arrived(buffer.at[k, pl.ds(p * GROUP, GROUP)], (name, p, k))[...].astype(
            jnp.float32
        )

    def start_terms(self, p, k):
        self.owns[p, k].wait()
        own = self.mine[k, pl.ds(p * GROUP, GROUP)].astype(jnp.float32)
        return own + self.term(p, self.core, k, "core")

    def pass_on(self, p, k, total, buffer, there, device, name):
        here = self.mine.at[k, pl.ds(p * GROUP, GROUP)]
        here[...] = total.astype(here.dtype)
        self.send(p, here, buffer, there, device, name)

    def to_corner(self, p):
        for d, _ in CORNER:
            side = self.link.y_side if d % 2 == 0 else self.link.x_side
            k = d * 4 + 3
            self.pass_on(p, k, self.start_terms(p, k), self.corner, d, side, "corner")

    def to_sides(self, p):
        for d, group in SIDES:
            k = d * 4 + group
            total = self.start_terms(p, k)
            if (d % 2 == 0) == (group == 1):
                total = total + self.term(p, self.corner, d, "corner")
            side = self.link.x_side if group == 1 else self.link.y_side
            self.pass_on(p, k, total, self.side, d * 2 + group - 1, side, "side")

    def column_terms(self, p, d):
        total = self.start_terms(p, d * 4)
        for k in (d * 2, d * 2 + 1):
            total = total + self.term(p, self.side, k, "side")
        return total

    def to_column(self, p):
        for d, _ in COLUMN:
            total = self.column_terms(p, d)
            self.pass_on(p, d * 4, total, self.column, d - 1, self.link.z_side[d], "column")

    def total(self, p):
        total = self.column_terms(p, 0)
        for d in (1, 2, 3):
            total = total + self.term(p, self.column, d - 1, "column")
        return total


def relay_kernel(plan, row_step, *refs):
    refs = list(refs)

    def take(count):
        taken = refs[:count]
        del refs[:count]
        return taken

    partials = take(plan["partials"])
    ready = take(plan["ready"])
    extras = take(plan["extras"])
    cargo_in = take(plan["cargo"])
    gathered = take(plan["outs"])
    kept = take(plan["kept"])
    sums = take(plan["sums"])
    cargo_out = take(plan["cargo"])
    buffers = take(5)
    held, send_sem, recv_sem, load_sem, own_sem = take(5)
    order, steps = plan["order"], plan["steps"]
    link = Links(send_sem, recv_sem, plan["cargo"])
    gather = Gather(link, gathered, steps, own_sem)
    if ready:
        gather.begin(0, ready[0])
    scatter = Scatter(link, partials, plan["rows"], order, buffers, load_sem)
    cargo = Cargo(*cargo_in, *cargo_out, *refs) if cargo_in else None
    ticks = len(order) + 7
    agenda = [[] for _ in range(ticks)]
    if ready:
        for tick, step in enumerate((gather.first, gather.second, gather.third)):
            agenda[tick + 2].append((step, 0))

    def last(p):
        rows, keeps, adds = row_step(p, scatter.total(p), extras)
        for ref, value in zip(kept, keeps):
            ref[pl.ds(p * GROUP, GROUP)] = value
        for ref, value in zip(sums, adds):
            ref[...] = value if p == order[0] else ref[...] + value
        if rows is not None:
            g = plan["slot"](p)
            held[g] = rows
            gather.begin(g, held.at[g])

    for q, p in enumerate(order):
        for tick, step in enumerate(
            (scatter.to_corner, scatter.to_sides, scatter.to_column, last)
        ):
            agenda[q + tick].append((step, p))
        if plan["slot"](p) is not None:
            for tick, step in enumerate((gather.first, gather.second, gather.third)):
                agenda[q + 4 + tick].append((step, plan["slot"](p)))
    for number, tick in enumerate(agenda):
        if cargo:
            cargo.load(CARGO_EARLY if number < 4 else CARGO_LATE)
        for step, index in tick:
            step(index)
    gather.finish()
    link.finish()
    if cargo:
        cargo.finish()


def relay(
    partials,
    row_step,
    ident,
    extras=(),
    kept=0,
    sums=0,
    order=None,
    slot=None,
    ready=None,
    split=False,
    cargo=None,
):
    devices, width = lax.axis_size("dp") * lax.axis_size("mp"), partials[0].shape[1]
    rows = sum(partial.shape[0] for partial in partials) // devices
    groups = rows // GROUP
    order = list(range(groups)) if order is None else order
    slot = slot or (lambda p: p)
    steps = sum(slot(p) is not None for p in order) + (ready is not None)
    if not kernel_mesh():
        total = jnp.concatenate(
            [lax.psum_scatter(part, BOTH, scatter_dimension=0, tiled=True) for part in partials]
        )
        total = total.astype(jnp.float32)
        outs, keeps, adds = [None] * steps, [None] * groups, [0.0] * sums
        if ready is not None:
            outs[0] = ready
        for p in order:
            out, keeps[p], add = row_step(p, total[p * GROUP : (p + 1) * GROUP], extras)
            adds = [one + two for one, two in zip(adds, add)]
            if out is not None:
                outs[slot(p)] = out
        outs = outs if split else [jnp.concatenate(outs)]
        gathered = [lax.all_gather(out, BOTH, axis=0, tiled=True) for out in outs]
        keeps = [jnp.concatenate(parts) for parts in zip(*keeps)]
        moved = [] if cargo is None else [swap_blocks(cargo)]
        return [*gathered, *keeps, *adds, *moved]
    plan = dict(
        partials=len(partials),
        outs=steps if split else 1,
        cargo=int(cargo is not None),
        rows=rows,
        order=order,
        slot=slot,
        steps=steps,
        ready=int(ready is not None),
        extras=len(extras),
        kept=kept,
        sums=sums,
    )
    low = partials[0].dtype
    load = [] if cargo is None else [cargo]
    vmem = pl.BlockSpec(memory_space=pltpu.VMEM)
    copies = 31 * (groups + steps)
    out_rows = [devices * GROUP] * steps if split else [devices * steps * GROUP]
    shapes = [jax.ShapeDtypeStruct((count, width), low) for count in out_rows]
    shapes += [jax.ShapeDtypeStruct((rows, width), jnp.float32)] * kept
    shapes += [jax.ShapeDtypeStruct((1, width), jnp.float32)] * sums
    shapes += [jax.ShapeDtypeStruct(value.shape, value.dtype) for value in load]
    buffers = [pltpu.VMEM((count, rows, width), low) for count in (16, 16, 4, 8, 3)]
    semaphores = [pltpu.SemaphoreType.DMA((count,)) for count in (copies, copies, 16 * groups, steps)]
    if load:
        semaphores += [pltpu.SemaphoreType.DMA((7 * cargo_cuts(cargo.shape),))] * 2
        semaphores += [pltpu.SemaphoreType.DMA]
    return pl.pallas_call(
        functools.partial(relay_kernel, plan, row_step),
        out_shape=shapes,
        in_specs=[ANY] * (len(partials) + plan["ready"])
        + [vmem] * len(extras)
        + [ANY] * len(load),
        out_specs=[ANY] * len(out_rows) + [vmem] * (kept + sums) + [ANY] * len(load),
        scratch_shapes=buffers + [pltpu.VMEM((steps, GROUP, width), low)] + semaphores,
        compiler_params=comm_params(ident, 60 if rows > 32 else 6 + rows // 4),
        cost_estimate=pl.CostEstimate(flops=1, bytes_accessed=1, transcendentals=0),
    )(*partials, *([] if ready is None else [ready]), *extras, *load)


def after(value, *first):
    return lax.optimization_barrier((value, *first))[0]


def swap_blocks(value):
    return lax.all_to_all(value, "dp", split_axis=0, concat_axis=0, tiled=True)


def small_gather_kernel(x_ref, o_ref, send_sem, recv_sem, own_sem):
    data_index, model_index = lax.axis_index("dp"), lax.axis_index("mp")
    me = data_index * 4 + model_index
    own = pltpu.make_async_copy(x_ref, o_ref.at[me], own_sem)
    own.start()
    peers = [lax.rem(me + shift, 32) for shift in range(1, 32)]
    barrier = pltpu.get_barrier_semaphore()
    for peer in peers:
        pl.semaphore_signal(
            barrier, inc=1, device_id=(peer // 4, peer % 4), device_id_type=MESH
        )
    pl.semaphore_wait(barrier, 31)
    sent = []
    for index, peer in enumerate(peers):
        copy = pltpu.make_async_remote_copy(
            src_ref=x_ref,
            dst_ref=o_ref.at[me],
            send_sem=send_sem.at[index],
            recv_sem=recv_sem.at[index],
            device_id=(peer // 4, peer % 4),
            device_id_type=MESH,
        )
        copy.start()
        sent.append(copy)
    for index in range(31):
        here = o_ref.at[lax.rem(me + 31 - index, 32)]
        pltpu.make_async_copy(here, here, recv_sem.at[index]).wait()
    own.wait()
    for copy in sent:
        copy.wait_send()


def gather_small(value, ident):
    if not kernel_mesh():
        return lax.all_gather(value, BOTH)
    vmem = pl.BlockSpec(memory_space=pltpu.VMEM)
    return pl.pallas_call(
        small_gather_kernel,
        out_shape=jax.ShapeDtypeStruct((32,) + value.shape, value.dtype),
        in_specs=[vmem],
        out_specs=vmem,
        scratch_shapes=[
            pltpu.SemaphoreType.DMA((31,)),
            pltpu.SemaphoreType.DMA((31,)),
            pltpu.SemaphoreType.DMA,
        ],
        compiler_params=comm_params(ident, 2),
    )(value)


def greet(peers):
    barrier = pltpu.get_barrier_semaphore()
    for peer in peers:
        pl.semaphore_signal(barrier, inc=1, device_id=peer, device_id_type=MESH)
    pl.semaphore_wait(barrier, len(peers))


def exchange_kernel(count, whole, *refs):
    ins, outs = refs[: len(whole)], refs[len(whole) : 2 * len(whole)]
    send_sem, recv_sem, own_sem = refs[2 * len(whole) :]
    me, model_index = lax.axis_index("dp"), lax.axis_index("mp")
    peers = [lax.rem(me + shift, count) for shift in range(1, count)]
    greet([(peer, model_index) for peer in peers])
    owns, sent = [], []
    for array, keep in enumerate(whole):
        own = pltpu.make_async_copy(
            ins[array] if keep else ins[array].at[me], outs[array].at[me], own_sem.at[array]
        )
        own.start()
        owns.append(own)
        for shift in range(count - 1):
            copy = pltpu.make_async_remote_copy(
                src_ref=ins[array] if keep else ins[array].at[peers[shift]],
                dst_ref=outs[array].at[me],
                send_sem=send_sem.at[array, shift],
                recv_sem=recv_sem.at[array, shift],
                device_id=(peers[shift], model_index),
                device_id_type=MESH,
            )
            copy.start()
            sent.append(copy)
    for own in owns:
        own.wait()
    for array in range(len(whole)):
        for shift in range(count - 1):
            source = lax.rem(me + count - 1 - shift, count)
            here = outs[array].at[source]
            pltpu.make_async_copy(here, here, recv_sem.at[array, shift]).wait()
    for copy in sent:
        copy.wait_send()


def exchange(values, whole, ident):
    count = lax.axis_size("dp")
    if not kernel_mesh():
        return [
            lax.all_gather(value, "dp")
            if keep
            else lax.all_to_all(value, "dp", split_axis=0, concat_axis=0, tiled=True)
            for value, keep in zip(values, whole)
        ]
    shapes = [
        jax.ShapeDtypeStruct(((count,) if keep else ()) + value.shape, value.dtype)
        for value, keep in zip(values, whole)
    ]
    return pl.pallas_call(
        functools.partial(exchange_kernel, count, tuple(whole)),
        out_shape=shapes,
        in_specs=[ANY] * len(values),
        out_specs=[ANY] * len(values),
        scratch_shapes=[
            pltpu.SemaphoreType.DMA((len(values), count - 1)),
            pltpu.SemaphoreType.DMA((len(values), count - 1)),
            pltpu.SemaphoreType.DMA((len(values),)),
        ],
        compiler_params=comm_params(ident, 2),
    )(*values)


def turned(values, cosine, sine_table):
    return values * cosine + pltpu.roll(values, HEAD_DIM // 2, 1) * sine_table


def to_column(row):
    return jnp.broadcast_to(row, (row.shape[1], row.shape[1])).T[:, :1]


def to_row(column):
    return jnp.broadcast_to(column, (column.shape[0], column.shape[0])).T[:1]


def softmax_rows(query, keys, places):
    scores = dot(query, keys, 1, 1) * (1.0 / math.sqrt(HEAD_DIM))
    columns = lax.broadcasted_iota(jnp.int32, scores.shape, 1)
    scores = jnp.where(columns <= places, scores, NEG)
    weights = jnp.exp(scores - jnp.max(scores, axis=-1, keepdims=True))
    return weights / jnp.sum(weights, axis=-1, keepdims=True)


def attend_kernel(
    exit_ref,
    resid_ref,
    gain_ref,
    head_ref,
    inner_ref,
    outer_ref,
    pick_ref,
    place_ref,
    live_ref,
    attn_ref,
    query_ref,
    key_ref,
    value_ref,
    out_ref,
    turn_ref,
    slot_turn_ref,
    partial_ref,
):
    block, blocks = pl.program_id(0), key_ref.shape[0] // resid_ref.shape[0]
    rows, slots = resid_ref.shape[0], pick_ref.shape[1]
    parts, columns = head_ref.shape[0], head_ref.shape[2]
    low = jnp.bfloat16
    attn = norm_fwd(resid_ref[...].astype(jnp.float32), gain_ref[...])[0].astype(low)
    attn_ref[...] = attn
    projected = jnp.zeros((rows, 3 * HEAD_DIM), jnp.float32)
    for part in range(parts):
        piece = attn[:, part * columns : (part + 1) * columns]
        projected = projected + dot(piece, head_ref[part, : 3 * HEAD_DIM], 1, 1)
    inner_cos, inner_sin = inner_ref[0], inner_ref[1]
    outer_cos, outer_sin = outer_ref[0, pl.ds(block, 1)], outer_ref[1, pl.ds(block, 1)]
    sign = jnp.where(lax.broadcasted_iota(jnp.int32, inner_cos.shape, 1) < HEAD_DIM // 2, -1.0, 1.0)
    cosine = inner_cos * outer_cos - inner_sin * outer_sin
    sine_table = (inner_sin * outer_cos + inner_cos * outer_sin) * sign
    at = pl.ds(pl.multiple_of(block * rows, rows), rows)
    turn_ref[0, at], turn_ref[1, at] = cosine, sine_table
    query = turned(projected[:, :HEAD_DIM], cosine, sine_table).astype(low)
    key_ref[at] = turned(projected[:, HEAD_DIM : 2 * HEAD_DIM], cosine, sine_table).astype(low)
    value_ref[at] = projected[:, 2 * HEAD_DIM :].astype(low)
    at = pl.ds(pl.multiple_of(block * slots, slots), slots)
    query_ref[at] = dot(pick_ref[0], query).astype(low)
    pick_wide = pick_ref[0].astype(jnp.float32)
    for index, table in enumerate((cosine, sine_table)):
        slot_turn_ref[index, at] = jnp.dot(
            pick_wide, table, precision=lax.Precision.HIGHEST, preferred_element_type=jnp.float32
        )

    @pl.when(block == blocks - 1)
    def _():
        exit_here = exit_ref[0]
        step = 2 * slots
        for index in range(blocks // 2):
            reach = (index + 1) * 2 * rows
            at = slice(index * step, (index + 1) * step)
            row = slice(index, index + 1)
            places, live = to_column(place_ref[row]), to_column(live_ref[row])
            probs = softmax_rows(query_ref[at], key_ref[:reach], places).astype(low)
            out = (dot(probs, value_ref[:reach]) * live).astype(low)
            out_ref[at] = out
            groups = step // partial_ref.shape[2]
            at = slice(index * groups, (index + 1) * groups)
            for part in range(parts):
                share = dot(out, head_ref[part, 3 * HEAD_DIM :]).astype(low)
                share = share.reshape(groups, 1, -1, columns)
                lanes = slice(part * columns, (part + 1) * columns)
                partial_ref[at, pl.ds(exit_here, 1), :, lanes] = share
                partial_ref[at, pl.ds(1 - exit_here, 1), :, lanes] = jnp.zeros_like(share)


def attend_back_kernel(
    exit_ref,
    done_ref,
    head_ref,
    out_ref,
    query_ref,
    key_ref,
    value_ref,
    turn_ref,
    slot_turn_ref,
    pick_ref,
    place_ref,
    attn_ref,
    partial_ref,
    parts_ref,
    key_sum,
    value_sum,
    turned_ref,
    head_sum,
):
    block, blocks = pl.program_id(0), key_ref.shape[0] // attn_ref.shape[0]
    rows, slots = attn_ref.shape[0], pick_ref.shape[1]
    parts, columns = head_ref.shape[0], head_ref.shape[2]
    low = jnp.bfloat16
    scale = 1.0 / math.sqrt(HEAD_DIM)

    @pl.when(block == 0)
    def _():
        key_sum[...] = jnp.zeros_like(key_sum)
        value_sum[...] = jnp.zeros_like(value_sum)
        step = 2 * slots
        width = done_ref.shape[-1]
        done = done_ref[...].reshape(-1, width)
        dout = jnp.zeros((done.shape[0], HEAD_DIM), jnp.float32)
        for part in range(parts):
            piece = done[:, part * columns : (part + 1) * columns]
            parts_ref[part, 3 * HEAD_DIM :] = dot(out_ref[...], piece, 0, 0).astype(low)
            dout = dout + dot(piece, head_ref[part, 3 * HEAD_DIM :], 1, 1)
        dout = dout.astype(low)
        for index in range(blocks // 2):
            reach = (index + 1) * 2 * rows
            at = slice(index * step, (index + 1) * step)
            places = to_column(place_ref[index : index + 1])
            probs = softmax_rows(query_ref[at], key_ref[:reach], places)
            dprobs = dot(dout[at], value_ref[:reach], 1, 1)
            delta = jnp.sum(probs * dprobs, axis=-1, keepdims=True)
            dscores = (probs * (dprobs - delta)).astype(low)
            dquery = dot(dscores, key_ref[:reach]) * scale
            dquery = turned(dquery, slot_turn_ref[0, at], -slot_turn_ref[1, at]).astype(low)
            for half in (0, 1):
                where = 2 * index + half
                turned_ref[where * rows : (where + 1) * rows, :HEAD_DIM] = dot(
                    pick_ref[where], dquery[half * slots : (half + 1) * slots], 0, 0
                ).astype(low)
            key_sum[:reach] += dot(dscores, query_ref[at], 0, 0)
            value_sum[:reach] += dot(probs.astype(low), dout[at], 0, 0)
        dkey = turned(key_sum[...] * scale, turn_ref[0], -turn_ref[1])
        turned_ref[:, HEAD_DIM : 2 * HEAD_DIM] = dkey.astype(low)
        turned_ref[:, 2 * HEAD_DIM :] = value_sum[...].astype(low)

    at = pl.ds(pl.multiple_of(block * rows, rows), rows)
    dprojected = turned_ref[at]
    for part in range(parts):
        lanes = slice(part * columns, (part + 1) * columns)
        partial_ref[:, lanes] = dot(dprojected, head_ref[part, : 3 * HEAD_DIM]).astype(low)
    term = dot(dprojected, attn_ref[...], 0, 0)

    @pl.when(block == 0)
    def _():
        head_sum[...] = term

    @pl.when(block > 0)
    def _():
        head_sum[...] += term

    @pl.when(block == blocks - 1)
    def _():
        for part in range(parts):
            lanes = slice(part * columns, (part + 1) * columns)
            parts_ref[part, : 3 * HEAD_DIM] = head_sum[:, lanes].astype(low)


def local_params(room):
    return dict(
        compiler_params=pltpu.CompilerParams(vmem_limit_bytes=room * MIB),
        cost_estimate=pl.CostEstimate(flops=1, bytes_accessed=1, transcendentals=0),
    )


def whole_spec(value):
    return pl.BlockSpec(value.shape, lambda b, e: (0,) * len(value.shape))


def attend(exit_here, resid, gain, head, inner, outer, pick, places, live, slots_here):
    (tokens, width), (blocks, slots, rows) = resid.shape, pick.shape
    low = resid.dtype
    devices = blocks * slots // slots_here
    by_block = pl.BlockSpec((rows, width), lambda b, e: (b, 0))
    outs = [
        jax.ShapeDtypeStruct((tokens, width), low),
        jax.ShapeDtypeStruct((blocks * slots, HEAD_DIM), low),
        jax.ShapeDtypeStruct((tokens, HEAD_DIM), low),
        jax.ShapeDtypeStruct((tokens, HEAD_DIM), low),
        jax.ShapeDtypeStruct((blocks * slots, HEAD_DIM), low),
        jax.ShapeDtypeStruct((2, tokens, HEAD_DIM), jnp.float32),
        jax.ShapeDtypeStruct((2, blocks * slots, HEAD_DIM), jnp.float32),
        jax.ShapeDtypeStruct((devices, 2, slots_here, width), low),
    ]
    return pl.pallas_call(
        attend_kernel,
        out_shape=outs,
        grid_spec=pltpu.PrefetchScalarGridSpec(
            num_scalar_prefetch=1,
            grid=(blocks,),
            in_specs=[
                by_block,
                whole_spec(gain),
                whole_spec(head),
                whole_spec(inner),
                whole_spec(outer),
                pl.BlockSpec((1, slots, rows), lambda b, e: (b, 0, 0)),
                whole_spec(places),
                whole_spec(live),
            ],
            out_specs=[by_block] + [whole_spec(out) for out in outs[1:]],
        ),
        **local_params(60),
    )(exit_here, resid, gain, head, inner, outer, pick, places, live)


def attend_back(exit_here, done, head, out, query, key, value, turn, slot_turn, pick, places, attn):
    (tokens, width), (blocks, slots, rows) = attn.shape, pick.shape
    low = attn.dtype
    devices, _, slots_here, _ = done.shape
    by_block = pl.BlockSpec((rows, width), lambda b, e: (b, 0))
    inner = [head, out, query, key, value, turn, slot_turn, pick, places]
    parts = jax.ShapeDtypeStruct(head.shape, low)
    return pl.pallas_call(
        attend_back_kernel,
        out_shape=[jax.ShapeDtypeStruct((tokens, width), low), parts],
        grid_spec=pltpu.PrefetchScalarGridSpec(
            num_scalar_prefetch=1,
            grid=(blocks,),
            in_specs=[
                pl.BlockSpec((devices, 1, slots_here, width), lambda b, e: (0, e[0], 0, 0))
            ]
            + [whole_spec(value) for value in inner]
            + [by_block],
            out_specs=[by_block, whole_spec(parts)],
            scratch_shapes=[
                pltpu.VMEM((tokens, HEAD_DIM), jnp.float32),
                pltpu.VMEM((tokens, HEAD_DIM), jnp.float32),
                pltpu.VMEM((tokens, 3 * HEAD_DIM), low),
                pltpu.VMEM((3 * HEAD_DIM, width), jnp.float32),
            ],
        ),
        **local_params(60),
    )(exit_here, done, *inner, attn)


def local(kernel, room, outs, *values, scratch=()):
    vmem = pl.BlockSpec(memory_space=pltpu.VMEM)
    return pl.pallas_call(
        kernel,
        out_shape=[jax.ShapeDtypeStruct(shape, dtype) for shape, dtype in outs],
        in_specs=[vmem] * len(values),
        out_specs=[vmem] * len(outs),
        scratch_shapes=list(scratch),
        **local_params(room),
    )(*values)


def pack_head_kernel(qkv_ref, out_ref, packed_ref):
    heads = out_ref.shape[0] // HEAD_DIM
    sharers = packed_ref.shape[0] // heads
    low = packed_ref.dtype
    for head in range(heads):
        lanes = slice(head * HEAD_DIM, (head + 1) * HEAD_DIM)
        for c in range(4):
            block = out_ref[lanes] if c == 3 else qkv_ref[c, :, lanes].T
            for sharer in range(sharers):
                packed_ref[head * sharers + sharer, c * HEAD_DIM : (c + 1) * HEAD_DIM] = block.astype(
                    low
                )


def pack_hidden_kernel(gate_up_ref, down_ref, packed_ref, turned_ref):
    parts, hidden = packed_ref.shape[0], packed_ref.shape[1] // 3
    low = packed_ref.dtype
    for c in range(2):
        for start in range(0, gate_up_ref.shape[2], 128):
            lanes = slice(start, start + 128)
            turned_ref[lanes] = gate_up_ref[:, c, lanes].T
        for part in range(parts):
            packed_ref[part, c * hidden : (c + 1) * hidden] = turned_ref[
                part * hidden : (part + 1) * hidden
            ].astype(low)
    for part in range(parts):
        packed_ref[part, 2 * hidden :] = down_ref[part * hidden : (part + 1) * hidden].astype(low)


def square_row(value):
    return jnp.sum(value * value, axis=0, keepdims=True)


def unpack_head_kernel(one_ref, two_ref, qkv_ref, out_ref, square_ref):
    heads = out_ref.shape[0] // HEAD_DIM
    sharers = one_ref.shape[0] // heads
    squares = jnp.zeros(square_ref.shape, jnp.float32)
    for head in range(heads):
        lanes = slice(head * HEAD_DIM, (head + 1) * HEAD_DIM)
        for c in range(4):
            parts_ref = one_ref if c < 2 else two_ref
            rows = slice(c % 2 * HEAD_DIM, (c % 2 + 1) * HEAD_DIM)
            total = parts_ref[head * sharers, rows].astype(jnp.float32)
            for sharer in range(1, sharers):
                total = total + parts_ref[head * sharers + sharer, rows].astype(jnp.float32)
            squares = squares + square_row(total)
            if c == 3:
                out_ref[lanes] = total
            else:
                qkv_ref[c, :, lanes] = total.T
    square_ref[...] = squares


def unpack_hidden_kernel(parts_ref, down_parts_ref, gate_up_ref, down_ref, square_ref, turned_ref):
    parts, hidden = down_parts_ref.shape[:2]
    squares = jnp.zeros(square_ref.shape, jnp.float32)
    for c in range(3):
        target = down_ref if c == 2 else turned_ref
        for part in range(parts):
            block = down_parts_ref[part] if c == 2 else parts_ref[part, c * hidden : (c + 1) * hidden]
            block = block.astype(jnp.float32)
            squares = squares + square_row(block)
            target[part * hidden : (part + 1) * hidden] = block
        if c < 2:
            for start in range(0, gate_up_ref.shape[2], 128):
                lanes = slice(start, start + 128)
                gate_up_ref[:, c, lanes] = turned_ref[lanes].T
    square_ref[...] = squares


def hidden_kernel(rows_ref, weight_ref, gate_ref, up_ref, hidden_ref, partial_ref):
    parts, columns = weight_ref.shape[0], weight_ref.shape[2]
    hidden = weight_ref.shape[1] // 3
    low = jnp.bfloat16
    gate = jnp.zeros(gate_ref.shape, jnp.float32)
    up = jnp.zeros(gate_ref.shape, jnp.float32)
    for part in range(parts):
        piece = rows_ref[:, part * columns : (part + 1) * columns]
        gate = gate + dot(piece, weight_ref[part, :hidden], 1, 1)
        up = up + dot(piece, weight_ref[part, hidden : 2 * hidden], 1, 1)
    gate_ref[...], up_ref[...] = gate, up
    value = (gate * jax.nn.sigmoid(gate) * up).astype(low)
    hidden_ref[...] = value
    for part in range(parts):
        partial_ref[:, part * columns : (part + 1) * columns] = dot(
            value, weight_ref[part, 2 * hidden :]
        ).astype(low)


def hidden_back_kernel(
    dtwo_ref,
    rows_ref,
    weight_ref,
    gate_ref,
    up_ref,
    hidden_ref,
    partial_ref,
    parts_ref,
    down_parts_ref,
):
    parts, hidden, columns = down_parts_ref.shape
    low = jnp.bfloat16
    dhidden = jnp.zeros(gate_ref.shape, jnp.float32)
    for part in range(parts):
        piece = dtwo_ref[:, part * columns : (part + 1) * columns]
        dhidden = dhidden + dot(piece, weight_ref[part, 2 * hidden :], 1, 1)
        down_parts_ref[part] = dot(hidden_ref[...], piece, 0, 0).astype(low)
    gate, up = gate_ref[...], up_ref[...]
    sigma = jax.nn.sigmoid(gate)
    dgate = (dhidden * up * sigma * (1.0 + gate * (1.0 - sigma))).astype(low)
    dup = (dhidden * gate * sigma).astype(low)
    for part in range(parts):
        lanes = slice(part * columns, (part + 1) * columns)
        partial_ref[:, lanes] = (
            dot(dgate, weight_ref[part, :hidden]) + dot(dup, weight_ref[part, hidden : 2 * hidden])
        ).astype(low)
        parts_ref[part, :hidden] = dot(dgate, rows_ref[:, lanes], 0, 0).astype(low)
        parts_ref[part, hidden : 2 * hidden] = dot(dup, rows_ref[:, lanes], 0, 0).astype(low)


def embed_kernel(base_ref, ids_ref, table_ref, partial_ref, low_ref, hits_ref):
    @pl.when(pl.program_id(0) == 0)
    def _():
        entries = base_ref[0] + lax.broadcasted_iota(jnp.int32, (1, table_ref.shape[0]), 1)
        hits_ref[...] = jnp.where(ids_ref[...] == entries, 1.0, 0.0).astype(hits_ref.dtype)

    table_low = table_ref[...].astype(low_ref.dtype)
    low_ref[...] = table_low
    partial_ref[...] = dot(hits_ref[...], table_low).astype(partial_ref.dtype)


def embed(base, ids, table):
    (entries, width), tokens, low = table.shape, ids.shape[0], jnp.bfloat16
    columns = 256
    by_columns = lambda rows: pl.BlockSpec((rows, columns), lambda b, e: (0, b))
    return pl.pallas_call(
        embed_kernel,
        out_shape=[
            jax.ShapeDtypeStruct((tokens, width), low),
            jax.ShapeDtypeStruct((entries, width), low),
        ],
        grid_spec=pltpu.PrefetchScalarGridSpec(
            num_scalar_prefetch=1,
            grid=(width // columns,),
            in_specs=[whole_spec(ids), by_columns(entries)],
            out_specs=[by_columns(tokens), by_columns(entries)],
            scratch_shapes=[pltpu.VMEM((tokens, entries), low)],
        ),
        **local_params(60),
    )(base, ids, table)


def logits_kernel(one_ref, two_ref, table_ref, target_ref, entry_ref, logits_ref, stats_ref):
    slots, step, lanes = one_ref.shape[0], 256, stats_ref.shape[1]
    for e, rows_ref in enumerate((one_ref, two_ref)):
        for start in range(0, slots, step):
            values = dot(rows_ref[start : start + step], table_ref[...], 1, 1)
            logits_ref[e * slots + start : e * slots + start + step] = values
            top = jnp.max(values, axis=1, keepdims=True)
            mass = jnp.sum(jnp.exp(values - top), axis=1, keepdims=True)
            for part in range(0, step, lanes):
                row = (e * slots + start + part) // lanes
                at = slice(part, part + lanes)
                hit = to_column(target_ref[row : row + 1]) == entry_ref[...]
                found = jnp.sum(jnp.where(hit, values[at], 0.0), axis=1, keepdims=True)
                for stat, column in enumerate((top[at], mass[at], found)):
                    index = stat * (2 * slots // lanes) + row
                    stats_ref[index : index + 1] = to_row(column)


def head_grad_kernel(
    logits_ref, lse_ref, weight_ref, target_ref, entry_ref, table_ref, one_ref, two_ref, *terms
):
    slots, lanes, step = one_ref.shape[0], lse_ref.shape[1], 256
    low = jnp.bfloat16
    for e, grad_ref in enumerate((one_ref, two_ref)):
        for start in range(0, slots, lanes):
            row = (e * slots + start) // lanes
            lse, weight, target = (
                to_column(ref[row : row + 1]) for ref in (lse_ref, weight_ref, target_ref)
            )
            values = logits_ref[row * lanes : (row + 1) * lanes]
            hit = jnp.where(target == entry_ref[...], 1.0, 0.0)
            grad_ref[start : start + lanes] = (weight * (jnp.exp(values - lse) - hit)).astype(low)
        for start in range(0, slots, step):
            at = slice(start, start + step)
            terms[e][at] = dot(grad_ref[at], table_ref[...]).astype(low)


def table_grad_kernel(
    base_ref, ids_ref, one_ref, two_ref, rows_one, rows_two, dzero_ref, grad_ref, square_ref, left_ref
):
    slots = one_ref.shape[0]

    @pl.when(pl.program_id(0) == 0)
    def _():
        entries = base_ref[0] + lax.broadcasted_iota(jnp.int32, (left_ref.shape[0], 1), 0)
        left_ref[:, :slots] = one_ref[...].T
        left_ref[:, slots : 2 * slots] = two_ref[...].T
        hits = jnp.where(ids_ref[...] == entries, 1.0, 0.0)
        left_ref[:, 2 * slots :] = hits.astype(left_ref.dtype)

    grad = (
        dot(left_ref[:, :slots], rows_one[...])
        + dot(left_ref[:, slots : 2 * slots], rows_two[...])
        + dot(left_ref[:, 2 * slots :], dzero_ref[...])
    )
    grad_ref[...] = grad
    square_ref[...] = square_row(grad)


def table_gradient(base, ids, grads, rows, dzero):
    slots, entries = grads[0].shape
    tokens, width = dzero.shape
    columns = 256
    by_columns = lambda count: pl.BlockSpec((count, columns), lambda b, e: (0, b))
    return pl.pallas_call(
        table_grad_kernel,
        out_shape=[
            jax.ShapeDtypeStruct((entries, width), jnp.float32),
            jax.ShapeDtypeStruct((1, width), jnp.float32),
        ],
        grid_spec=pltpu.PrefetchScalarGridSpec(
            num_scalar_prefetch=1,
            grid=(width // columns,),
            in_specs=[whole_spec(ids), whole_spec(grads[0]), whole_spec(grads[1])]
            + [by_columns(slots), by_columns(slots), by_columns(tokens)],
            out_specs=[by_columns(entries), by_columns(1)],
            scratch_shapes=[pltpu.VMEM((entries, 2 * slots + tokens), dzero.dtype)],
        ),
        **local_params(60),
    )(base, ids, *grads, *rows, dzero)


def norm_fwd(values, gain):
    row_scale = lax.rsqrt(jnp.mean(values * values, axis=-1, keepdims=True) + EPS_NORM)
    unit_rows = values * row_scale
    return (unit_rows * gain, unit_rows, row_scale)


def norm_back(unit_rows, row_scale, gain, gradient):
    weighted = gradient * gain
    back_rows = row_scale * (
        weighted - unit_rows * jnp.mean(weighted * unit_rows, axis=-1, keepdims=True)
    )
    return (back_rows, jnp.sum(gradient * unit_rows, axis=0))


def rotary(places, width):
    half_width = width // 2
    frequency = jnp.exp(
        jnp.arange(half_width, dtype=jnp.float32) * (-math.log(10000.0) / half_width)
    )
    angles = places.astype(jnp.float32)[:, None] * frequency[None, :]
    return (jnp.cos(angles), jnp.sin(angles))


def rotate_pairs(values, cosine, sine_table):
    half_width = values.shape[-1] // 2
    front_half = values[..., :half_width]
    back_half = values[..., half_width:]
    return jnp.concatenate(
        [
            front_half * cosine - back_half * sine_table,
            back_half * cosine + front_half * sine_table,
        ],
        axis=-1,
    )


def dot(left, right, left_dim=1, right_dim=0):
    return lax.dot_general(
        left, right, (((left_dim,), (right_dim,)), ((), ())), preferred_element_type=jnp.float32
    )


def adam_update(weight, moment_one, moment_two, gradient, rate, decay):
    moment_one = BETA_ONE * moment_one + (1.0 - BETA_ONE) * gradient
    moment_two = BETA_TWO * moment_two + (1.0 - BETA_TWO) * gradient * gradient
    ratio = (
        moment_one
        / (1.0 - BETA_ONE**STEP)
        / (jnp.sqrt(moment_two / (1.0 - BETA_TWO**STEP)) + ADAM_EPS)
    )
    return (weight - rate * (ratio + decay * weight), moment_one, moment_two)


def small_sum_kernel(x_ref, o_ref, held, got, send_sem, recv_sem):
    data_index, model_index = lax.axis_index("dp"), lax.axis_index("mp")
    z, y = data_index // 2, data_index % 2
    x, c = model_index // 2, model_index % 2
    peers = [
        (data_index, x * 2 + 1 - c),
        (data_index, (1 - x) * 2 + c),
        (z * 2 + 1 - y, model_index),
        ((z + 1 - 2 * (z % 2)) * 2 + y, model_index),
        (lax.rem(z + 2, 4) * 2 + y, model_index),
    ]
    greet(peers)
    held[0] = x_ref[...]
    sent = []
    for step, peer in enumerate(peers):
        copy = pltpu.make_async_remote_copy(
            src_ref=held.at[step],
            dst_ref=got.at[step],
            send_sem=send_sem.at[step],
            recv_sem=recv_sem.at[step],
            device_id=peer,
            device_id_type=MESH,
        )
        copy.start()
        copy.wait_recv()
        sent.append(copy)
        held[step + 1] = held[step] + got[step]
    o_ref[...] = held[len(peers)]
    for copy in sent:
        copy.wait_send()


def sum_small(value, ident):
    if not kernel_mesh():
        return lax.psum(value, BOTH)
    vmem = pl.BlockSpec(memory_space=pltpu.VMEM)
    return pl.pallas_call(
        small_sum_kernel,
        out_shape=jax.ShapeDtypeStruct(value.shape, value.dtype),
        in_specs=[vmem],
        out_specs=vmem,
        scratch_shapes=[
            pltpu.VMEM((6,) + value.shape, value.dtype),
            pltpu.VMEM((5,) + value.shape, value.dtype),
            pltpu.SemaphoreType.DMA((5,)),
            pltpu.SemaphoreType.DMA((5,)),
        ],
        compiler_params=comm_params(ident, 2),
    )(value)


def body(
    token_ids,
    target_ids,
    exit_mask,
    table,
    table_first,
    table_second,
    qkv_weight,
    qkv_first,
    qkv_second,
    out_weight,
    out_first,
    out_second,
    gate_up_weight,
    gate_up_first,
    gate_up_second,
    down_weight,
    down_first,
    down_second,
    gains,
    gains_first,
    gains_second,
):
    low = jnp.bfloat16
    data_size, model_size = lax.axis_size("dp"), lax.axis_size("mp")
    data_index, model_index = lax.axis_index("dp"), lax.axis_index("mp")
    devices = data_size * model_size
    block_rows = token_ids.shape[0]
    tokens = block_rows * data_size
    width = table.shape[1]
    width_here = qkv_weight.shape[0]
    heads_here = qkv_weight.shape[2] // HEAD_DIM
    hidden_here = down_weight.shape[0] // data_size
    vocab_here = table.shape[0]
    device_index = data_index * model_size + model_index
    vocab_ids = device_index * vocab_here + jnp.arange(vocab_here, dtype=jnp.int32)
    score_scale = 1.0 / math.sqrt(HEAD_DIM)

    sharers = data_size // heads_here
    shares = sharers // 2
    share_slots = data_size // shares * R_DEV
    exit_here = data_index % sharers % 2
    share_here = data_index % sharers // 2
    slots_here = R_DEV // model_size
    rows_here = block_rows // model_size

    ints, gain_low = exchange(
        [
            jnp.concatenate([token_ids[None], target_ids[None], exit_mask]),
            jnp.pad(gains.astype(low), ((0, 13), (0, 0))),
        ],
        (True, True),
        0,
    )
    gain_rows = jnp.moveaxis(gain_low[:, :3], 0, 1).reshape(3, width).astype(jnp.float32)
    all_ids = ints[:, 0].reshape(tokens)
    mask_blocks = jnp.moveaxis(ints[:, 2:], 0, 1)
    slot_ids = jnp.arange(R_DEV, dtype=jnp.int32)
    slot_ranks = jnp.cumsum(mask_blocks, axis=2) - 1
    pick_int = (
        (slot_ranks[:, :, None, :] == slot_ids[:, None]) & (mask_blocks[:, :, None, :] == 1)
    ).astype(jnp.int32)
    pick_low = pick_int.astype(low)
    token_places = jnp.arange(tokens, dtype=jnp.int32)
    slot_targets = jnp.sum(pick_int * ints[:, 1][None, :, None, :], axis=3).reshape(2, -1)
    slot_places = jnp.sum(
        pick_int * token_places.reshape(1, data_size, 1, block_rows), axis=3
    ).reshape(2, -1)
    live = (slot_ids < jnp.sum(mask_blocks, axis=2)[:, :, None]).astype(jnp.float32).reshape(2, -1)
    counts = jnp.sum(live, axis=1)

    packed = kernel_mesh()
    head_shape = (data_size, 4 * HEAD_DIM, width_here)
    hidden_shape = (data_size, 2 * hidden_here, width_here)
    down_shape = (data_size, hidden_here, width_here)
    if packed:
        (head_rows,) = local(
            pack_head_kernel,
            10,
            [(head_shape, low)],
            jnp.transpose(qkv_weight, (1, 0, 2)),
            out_weight,
        )
    else:
        head_rows = jnp.moveaxis(
            qkv_weight.astype(low).reshape(width_here, 3, heads_here, HEAD_DIM), 0, 3
        )
        head_rows = jnp.concatenate(
            [
                jnp.moveaxis(head_rows, 0, 1).reshape(heads_here, 3 * HEAD_DIM, width_here),
                out_weight.astype(low).reshape(heads_here, HEAD_DIM, width_here),
            ],
            axis=1,
        )
        head_rows = jnp.repeat(head_rows, sharers, axis=0)
    head_rows = swap_blocks(after(head_rows, ints))

    base = (device_index * vocab_here)[None]
    if packed:
        id_rows, table_low = embed(base, all_ids[:, None], table)
    else:
        table_low = table.astype(low)
        id_hits = (all_ids[:, None] == vocab_ids[None, :]).astype(low)
        id_rows = dot(id_hits, table_low).astype(low)
    if packed:
        (hidden_rows,) = local(
            pack_hidden_kernel,
            16,
            [((data_size, 3 * hidden_here, width_here), low)],
            gate_up_weight,
            down_weight,
            scratch=[pltpu.VMEM((gate_up_weight.shape[2], width_here), jnp.float32)],
        )
    else:
        hidden_rows = jnp.moveaxis(
            gate_up_weight.astype(low).reshape(width_here, 2, data_size, hidden_here), 0, 3
        )
        hidden_rows = jnp.concatenate(
            [
                jnp.moveaxis(hidden_rows, 0, 1).reshape(hidden_shape),
                down_weight.astype(low).reshape(down_shape),
            ],
            axis=1,
        )
    (resid_low,) = relay([after(id_rows, hidden_rows)], lambda p, total, extras: (total.astype(low), (), ()), 1)

    hidden_rows = swap_blocks(after(hidden_rows, resid_low))

    pick_share = lax.dynamic_slice_in_dim(
        lax.dynamic_index_in_dim(pick_low, exit_here, 0, keepdims=False),
        share_here * (data_size // shares),
        data_size // shares,
        0,
    )
    def share_of(per_slot):
        return lax.dynamic_slice(per_slot, (exit_here, share_here * share_slots), (1, share_slots))[
            0
        ]

    places_share, live_share = share_of(slot_places), share_of(live)
    if packed:

        def turns(places):
            return jnp.stack([jnp.concatenate([part, part], axis=1) for part in rotary(places, HEAD_DIM)])

        attn_low, query_slots, key_low, value_low, attn_out, turn, slot_turn, out_partial = attend(
            exit_here[None],
            resid_low,
            gain_rows[:1],
            head_rows,
            turns(token_places[:block_rows]),
            turns(token_places[::block_rows]),
            pick_share,
            places_share.reshape(-1, 2 * R_DEV),
            live_share.reshape(-1, 2 * R_DEV),
            slots_here,
        )
        out_partial = out_partial.reshape(-1, width)
    else:
        head_rows = jnp.moveaxis(head_rows, 0, 1).reshape(4 * HEAD_DIM, width)
        qkv_head, out_head = head_rows[: 3 * HEAD_DIM], head_rows[3 * HEAD_DIM :]
        cosine, sine_table = rotary(token_places, HEAD_DIM)
        cosine_share, sine_share = rotary(places_share, HEAD_DIM)
        attn_low = norm_fwd(resid_low.astype(jnp.float32), gain_rows[0])[0].astype(low)

        projected = dot(attn_low, qkv_head, 1, 1)
        query_low = rotate_pairs(projected[:, :HEAD_DIM], cosine, sine_table).astype(low)
        key_low = rotate_pairs(projected[:, HEAD_DIM : 2 * HEAD_DIM], cosine, sine_table).astype(low)
        value_low = projected[:, 2 * HEAD_DIM :].astype(low)
        query_share = lax.dynamic_slice_in_dim(
            query_low.reshape(data_size, block_rows, HEAD_DIM),
            share_here * (data_size // shares),
            data_size // shares,
            0,
        )
        query_slots = (
            jnp.einsum("brt,btd->brd", pick_share, query_share, preferred_element_type=jnp.float32)
            .astype(low)
            .reshape(share_slots, HEAD_DIM)
        )

        scores = dot(query_slots, key_low, 1, 1) * score_scale
        allowed = token_places[None, :] <= places_share[:, None]
        scores = jnp.where(allowed, scores, NEG)
        weights = jnp.exp(scores - jnp.max(scores, axis=-1, keepdims=True))
        probs = weights / jnp.sum(weights, axis=-1, keepdims=True)
        probs_low = probs.astype(low)
        attn_out = (dot(probs_low, value_low) * live_share[:, None]).astype(low)

        def spread(per_share):
            if shares > 1:
                full = jnp.zeros((data_size * R_DEV, width), per_share.dtype)
                per_share = lax.dynamic_update_slice_in_dim(
                    full, per_share, share_here * share_slots, 0
                )
            exits = jnp.arange(2, dtype=jnp.int32)[None, :, None, None]
            rows = per_share.reshape(devices, 1, slots_here, width)
            return jnp.where(exits == exit_here, rows, 0).reshape(-1, width)
        out_partial = spread(dot(attn_out, out_head).astype(low))

    block_low = lax.dynamic_slice_in_dim(resid_low, data_index * block_rows, block_rows, 0)
    pick_here = lax.dynamic_slice(
        pick_low,
        (0, data_index, model_index * slots_here, 0),
        (2, 1, slots_here, block_rows),
    ).reshape(2 * slots_here, block_rows)

    def first_step(p, total, extras):
        resid = extras[0][p * GROUP : (p + 1) * GROUP] + total
        gain = 2 if p == 0 else 1
        return (norm_fwd(resid, extras[1][gain : gain + 1])[0].astype(low), (resid,), ())

    exit_rows_one, mlp_low, resid_one = relay(
        [out_partial],
        first_step,
        2,
        extras=[dot(pick_here, block_low), gain_rows],
        kept=1,
        split=True,
    )

    slots = mlp_low.shape[0]
    if packed:
        gate_part, up_part, hidden_low, mlp_partial = local(
            hidden_kernel,
            20,
            [
                ((slots, hidden_here), jnp.float32),
                ((slots, hidden_here), jnp.float32),
                ((slots, hidden_here), low),
                ((slots, width), low),
            ],
            mlp_low,
            hidden_rows,
        )
    else:
        hidden_rows = jnp.moveaxis(hidden_rows, 0, 1).reshape(3 * hidden_here, width)
        gate_up_head, down_head = hidden_rows[: 2 * hidden_here], hidden_rows[2 * hidden_here :]
        gate_up = dot(mlp_low, gate_up_head, 1, 1)
        gate_part, up_part = gate_up[:, :hidden_here], gate_up[:, hidden_here:]
        gate_sigma = jax.nn.sigmoid(gate_part)
        hidden_low = (gate_part * gate_sigma * up_part).astype(low)
        mlp_partial = dot(hidden_low, down_head).astype(low)

    def second_step(p, total, extras):
        resid = extras[0][GROUP : 2 * GROUP] + total
        return (norm_fwd(resid, extras[1][2:3])[0].astype(low), (resid,), ())

    exit_rows_two, resid_two = relay(
        [mlp_partial], second_step, 3, extras=[resid_one, gain_rows], kept=1
    )

    exit_rows = (exit_rows_one, exit_rows_two)
    if packed:
        target_rows, entry_row = slot_targets.reshape(-1, 128), vocab_ids[None]
        logits, stats = local(
            logits_kernel,
            28,
            [((2 * slots, vocab_here), jnp.float32), ((3 * 2 * slots // 128, 128), jnp.float32)],
            *exit_rows,
            table_low,
            target_rows,
            entry_row,
        )
    else:
        logits = [dot(rows, table_low, 1, 1) for rows in exit_rows]
        hits = [slot_targets[e][:, None] == vocab_ids[None, :] for e in range(2)]
        tops = [jnp.max(values, axis=1) for values in logits]
        masses = [
            jnp.sum(jnp.exp(values - top[:, None]), axis=1) for values, top in zip(logits, tops)
        ]
        found = [jnp.sum(jnp.where(hit, values, 0.0), axis=1) for hit, values in zip(hits, logits)]
        stats = jnp.concatenate(tops + masses + found).reshape(-1, 128)
    stats = gather_small(stats, 4).reshape(devices, 3, 2, -1)
    row_top = jnp.max(stats[:, 0], axis=0)
    row_mass = jnp.sum(stats[:, 1] * jnp.exp(stats[:, 0] - row_top), axis=0)
    row_lse = row_top + jnp.log(row_mass)
    entropy = row_lse - jnp.sum(stats[:, 2], axis=0)
    loss_sums = jnp.sum(entropy * live, axis=1)
    row_weight = live * (jnp.array(EXIT_SCALE, jnp.float32) / counts)[:, None]
    if packed:
        *grad_logits, one_terms, two_terms = local(
            head_grad_kernel,
            28,
            [((slots, vocab_here), low)] * 2 + [((slots, width), low)] * 2,
            logits,
            row_lse.reshape(-1, 128),
            row_weight.reshape(-1, 128),
            target_rows,
            entry_row,
            table_low,
        )
        row_terms = [one_terms, two_terms]
    else:
        grad_logits = [
            (
                row_weight[e][:, None]
                * (jnp.exp(logits[e] - row_lse[e][:, None]) - hits[e].astype(jnp.float32))
            ).astype(low)
            for e in range(2)
        ]
        row_terms = [dot(grad, table_low).astype(low) for grad in grad_logits]

    def head_step(p, total, extras):
        values = extras[0][:GROUP] if p == 0 else extras[1][...]
        gain = extras[2][2:3]
        _, unit, scale = norm_fwd(values, gain)
        back, gain_grad = norm_back(unit, scale, gain, total)
        return (None if p == 0 else back.astype(low), (back,), (gain_grad[None],))

    dtwo_low, dexits, final_grad = relay(
        row_terms,
        head_step,
        5,
        extras=[resid_one, resid_two, gain_rows],
        kept=1,
        sums=1,
        order=[1, 0],
        slot=lambda p: None if p == 0 else 0,
    )
    if packed:
        dmlp_partial, hidden_parts, down_parts = local(
            hidden_back_kernel,
            28,
            [((slots, width), low), (hidden_shape, low), (down_shape, low)],
            dtwo_low,
            mlp_low,
            hidden_rows,
            gate_part,
            up_part,
            hidden_low,
        )
    else:
        down_local = dot(hidden_low, dtwo_low, 0, 0)
        dhidden = dot(dtwo_low, down_head, 1, 1)
        dgate = dhidden * up_part * gate_sigma * (1.0 + gate_part * (1.0 - gate_sigma))
        dup_part = dhidden * gate_part * gate_sigma
        dgate_up = jnp.concatenate([dgate, dup_part], axis=1).astype(low)
        gate_up_local = dot(dgate_up, mlp_low, 0, 0)
        dmlp_partial = dot(dgate_up, gate_up_head).astype(low)
        hidden_parts, down_parts = (
            jnp.moveaxis(value.astype(low).reshape(-1, data_size, width_here), 1, 0)
            for value in (gate_up_local, down_local)
        )

    def mlp_step(p, total, extras):
        gain = extras[2][1:2]
        _, unit, scale = norm_fwd(extras[0][GROUP : 2 * GROUP], gain)
        back, gain_grad = norm_back(unit, scale, gain, total)
        return ((extras[1][GROUP : 2 * GROUP] + back).astype(low), (), (gain_grad[None],))

    done_low, mlp_grad, down_parts = relay(
        [dmlp_partial],
        mlp_step,
        6,
        extras=[resid_one, dexits, gain_rows],
        sums=1,
        slot=lambda p: 1,
        ready=dexits[:GROUP].astype(low),
        cargo=down_parts,
    )
    hidden_parts = swap_blocks(after(hidden_parts, done_low))
    done_low = done_low.reshape(devices, 2, slots_here, width)

    if kernel_mesh():
        zero_partial, head_parts = attend_back(
            exit_here[None],
            done_low,
            head_rows,
            attn_out,
            query_slots,
            key_low,
            value_low,
            turn,
            slot_turn,
            pick_share,
            places_share.reshape(-1, 2 * R_DEV),
            attn_low,
        )
    else:
        done_share = lax.dynamic_slice(
            lax.dynamic_index_in_dim(done_low, exit_here, 1, keepdims=False).reshape(-1, width),
            (share_here * share_slots, 0),
            (share_slots, width),
        )
        out_local = dot(attn_out, done_share, 0, 0)
        dattn_low = dot(done_share, out_head, 1, 1).astype(low)
        dprobs = dot(dattn_low, value_low, 1, 1)
        delta = jnp.sum(probs * dprobs, axis=-1, keepdims=True)
        dscores = (probs * (dprobs - delta)).astype(low)
        dquery = rotate_pairs(dot(dscores, key_low) * score_scale, cosine_share, -sine_share).astype(
            low
        )
        dquery_share = jnp.einsum(
            "brt,brd->btd",
            pick_share,
            dquery.reshape(-1, R_DEV, HEAD_DIM),
            preferred_element_type=jnp.float32,
        ).astype(low)
        if shares > 1:
            dquery_share = lax.dynamic_update_slice_in_dim(
                jnp.zeros((data_size, block_rows, HEAD_DIM), low),
                dquery_share,
                share_here * (data_size // shares),
                0,
            )
        dkey = rotate_pairs(dot(dscores, query_slots, 0, 0) * score_scale, cosine, -sine_table)
        dvalue = dot(probs_low, dattn_low, 0, 0)
        dprojected = jnp.concatenate(
            [dquery_share.reshape(tokens, HEAD_DIM), dkey.astype(low), dvalue.astype(low)], axis=1
        )
        head_parts = jnp.concatenate([dot(dprojected, attn_low, 0, 0).astype(low), out_local.astype(low)])
        zero_partial = dot(dprojected, qkv_head).astype(low)
        head_parts = jnp.moveaxis(head_parts.reshape(-1, data_size, width_here), 1, 0)

    resid_here = lax.dynamic_slice_in_dim(resid_low, device_index * rows_here, rows_here, 0)
    done_block = lax.dynamic_slice_in_dim(done_low, data_index * model_size, model_size, 0)
    pick_block = lax.dynamic_slice(
        pick_low,
        (0, data_index, 0, model_index * rows_here),
        (2, 1, R_DEV, rows_here),
    ).reshape(2, model_size, slots_here, rows_here)
    dresid_here = jnp.einsum(
        "emst,mesd->td", pick_block, done_block, preferred_element_type=jnp.float32
    )

    def zero_step(p, total, extras):
        at = slice(p * GROUP, (p + 1) * GROUP)
        gain = extras[2][:1]
        _, unit, scale = norm_fwd(extras[0][at], gain)
        back, gain_grad = norm_back(unit, scale, gain, total)
        return ((extras[1][at] + back).astype(low), (), (gain_grad[None],))

    ride = 2 * HEAD_DIM
    dzero_low, attn_grad, ridden = relay(
        [after(zero_partial, hidden_parts)],
        zero_step,
        7,
        extras=[resid_here.astype(jnp.float32), dresid_here, gain_rows],
        sums=1,
        cargo=head_parts[:, :ride],
    )
    later = swap_blocks(after(head_parts[:, ride:], dzero_low))
    if packed:
        table_grad, squares = table_gradient(
            base, all_ids[None, :], grad_logits, exit_rows, dzero_low
        )
        squares = jnp.sum(squares)
    else:
        table_grad = dot(id_hits, dzero_low, 0, 0)
        for grad, rows in zip(grad_logits, exit_rows):
            table_grad = table_grad + dot(grad, rows, 0, 0)
        squares = jnp.sum(table_grad * table_grad)

    square_shape = ((1, width_here), jnp.float32)
    if packed:
        qkv_grad, out_grad, head_squares = local(
            unpack_head_kernel,
            12,
            [
                ((3, width_here, qkv_weight.shape[2]), jnp.float32),
                (out_weight.shape, jnp.float32),
                square_shape,
            ],
            ridden,
            later,
        )
        gate_up_grad, down_grad, hidden_squares = local(
            unpack_hidden_kernel,
            20,
            [
                (gate_up_weight.shape, jnp.float32),
                (down_weight.shape, jnp.float32),
                square_shape,
            ],
            hidden_parts,
            down_parts,
            scratch=[pltpu.VMEM((gate_up_weight.shape[2], width_here), jnp.float32)],
        )
        qkv_grad = jnp.transpose(qkv_grad, (1, 0, 2))
        squares = squares + jnp.sum(head_squares) + jnp.sum(hidden_squares)
    else:
        head_grad = jnp.sum(
            jnp.concatenate([ridden, later], axis=1).reshape(heads_here, sharers, 4, HEAD_DIM, width_here).astype(jnp.float32),
            axis=1,
        )
        qkv_grad = jnp.transpose(head_grad[:, :3], (3, 1, 0, 2)).reshape(qkv_weight.shape)
        out_grad = head_grad[:, 3].reshape(out_weight.shape)
        hidden_parts = hidden_parts.astype(jnp.float32)
        gate_up_grad = hidden_parts.reshape(data_size, 2, hidden_here, width_here)
        gate_up_grad = jnp.transpose(gate_up_grad, (3, 1, 0, 2)).reshape(gate_up_weight.shape)
        down_grad = down_parts.reshape(down_weight.shape).astype(jnp.float32)
        squares = (
            squares
            + jnp.sum(qkv_grad * qkv_grad)
            + jnp.sum(out_grad * out_grad)
            + jnp.sum(gate_up_grad * gate_up_grad)
            + jnp.sum(down_grad * down_grad)
        )
    parts = jnp.concatenate(
        [
            jnp.concatenate([attn_grad, mlp_grad, final_grad]).reshape(-1, 128),
            jnp.full((8, 128), squares),
        ]
    )
    parts = sum_small(parts, 8)
    gain_sums = parts[:-8].reshape(3, width)
    gain_grad = lax.dynamic_slice_in_dim(gain_sums, data_index * width_here, width_here, 1)
    grad_norm = jnp.sqrt(parts[-1, 0] + jnp.sum(gain_sums * gain_sums))
    factor = jnp.minimum(1.0, CLIP / (grad_norm + 1e-06))
    table_new, qkv_new, out_new, gate_up_new, down_new = (
        adam_update(weight, first, second, grad * factor, RATE_MATRIX, DECAY)
        for weight, first, second, grad in (
            (table, table_first, table_second, table_grad),
            (qkv_weight, qkv_first, qkv_second, qkv_grad),
            (out_weight, out_first, out_second, out_grad),
            (gate_up_weight, gate_up_first, gate_up_second, gate_up_grad),
            (down_weight, down_first, down_second, down_grad),
        )
    )
    gains_new = adam_update(gains, gains_first, gains_second, gain_grad * factor, RATE_GAIN, 0.0)
    return (
        loss_sums,
        counts,
        grad_norm,
        *table_new,
        *qkv_new,
        *out_new,
        *gate_up_new,
        *down_new,
        *gains_new,
    )


def solution(mesh):
    rows, sides, cols, gain = P(BOTH, None), P("dp", None, "mp"), P("mp", "dp"), P(None, "dp")
    state = (rows,) * 3 + (sides,) * 3 + (cols,) * 3 + (sides,) * 3 + (cols,) * 3 + (gain,) * 3
    return jax.shard_map(
        body,
        mesh=mesh,
        in_specs=(P("dp"), P("dp"), P(None, "dp")) + state,
        out_specs=(P(), P(), P()) + state,
        check_vma=False,
    )
```

```python
import functools
import math

import jax
import jax.numpy as jnp
from jax import lax
from jax.experimental import pallas as pl
from jax.experimental.pallas import tpu as pltpu
from jax.sharding import PartitionSpec as P

HEAD_DIM = 128
R_DEV = 64
STEP = 10


EPS_NORM = 1e-05
BETA_ONE = 0.9
BETA_TWO = 0.95
ADAM_EPS = 1e-08
DECAY = 0.1
RATE_MATRIX = 0.02
RATE_GAIN = 1.0
CLIP = 0.02
EXIT_SCALE = (1.0 / 3.0, 2.0 / 3.0)
NEG = -1e30
BOTH = ("dp", "mp")
MESH = pl.DeviceIdType.MESH
MIB = 1024 * 1024
ANY = pl.BlockSpec(memory_space=pl.ANY)
GROUP = 16
CARGO_EARLY = 4
CARGO_LATE = 2


def kernel_mesh():
    return lax.axis_size("dp") == 8 and lax.axis_size("mp") == 4


def comm_params(ident, room):
    return pltpu.CompilerParams(
        collective_id=ident, has_side_effects=True, vmem_limit_bytes=room * MIB
    )


class Links:
    def __init__(self, send_sem, recv_sem, cargo=False):
        data_index, model_index = lax.axis_index("dp"), lax.axis_index("mp")
        z, y, x, c = data_index // 2, data_index % 2, model_index // 2, model_index % 2
        self.c = c
        self.zs = (z, z + 1 - 2 * (z % 2), (z + 2) % 4, 3 - z)
        self.corners = ((y, x), (y, 1 - x), (1 - y, x), (1 - y, 1 - x))
        self.z_side = [(zd * 2 + y, model_index) for zd in self.zs]
        self.x_side = (data_index, (1 - x) * 2 + c)
        self.y_side = (z * 2 + 1 - y, model_index)
        self.c_side = (data_index, x * 2 + 1 - c)
        self.send_sem, self.recv_sem, self.sent, self.slots = send_sem, recv_sem, [], {}
        peers = self.z_side[1:] + [self.x_side, self.y_side, self.c_side]
        if cargo:
            peers += [(zd * 2 + 1 - y, model_index) for zd in self.zs[1:]]
        barrier = pltpu.get_barrier_semaphore()
        for peer in peers:
            pl.semaphore_signal(barrier, inc=1, device_id=peer, device_id_type=MESH)
        pl.semaphore_wait(barrier, len(peers))

    def first_row(self, rows, d, group, core=0):
        y, x = self.corners[group]
        c = 1 - self.c if core else self.c
        return ((self.zs[d] * 2 + y) * 4 + x * 2 + c) * rows

    def recv(self, name):
        return self.recv_sem.at[self.slots.setdefault(name, len(self.slots))]

    def send(self, source, target, device, name):
        copy = pltpu.make_async_remote_copy(
            src_ref=source,
            dst_ref=target,
            send_sem=self.send_sem.at[len(self.sent)],
            recv_sem=self.recv(name),
            device_id=device,
            device_id_type=MESH,
        )
        copy.start()
        self.sent.append(copy)

    def arrived(self, ref, name):
        pltpu.make_async_copy(ref, ref, self.recv(name)).wait()
        return ref

    def finish(self):
        for copy in self.sent:
            copy.wait_send()


def cargo_cuts(shape):
    return 2 if shape[1] % 32 == 0 else 1


class Cargo:
    def __init__(self, source, target, send_sem, recv_sem, own_sem):
        self.me, self.model_index = lax.axis_index("dp"), lax.axis_index("mp")
        self.source, self.target = source, target
        self.send_sem, self.recv_sem, self.sent = send_sem, recv_sem, []
        self.own = pltpu.make_async_copy(source.at[self.me], target.at[self.me], own_sem)
        self.own.start()
        count = cargo_cuts(source.shape)
        size = source.shape[1] // count
        cuts = [pl.ds(cut * size, size) for cut in range(count)]
        self.cuts = [(shift, cut) for cut in cuts for shift in (4, 3, 5, 2, 6, 1, 7)]

    def load(self, count):
        for _ in range(count):
            index = len(self.sent)
            if index == len(self.cuts):
                return
            shift, cut = self.cuts[index]
            peer = lax.rem(self.me + shift, 8)
            copy = pltpu.make_async_remote_copy(
                src_ref=self.source.at[peer, cut],
                dst_ref=self.target.at[self.me, cut],
                send_sem=self.send_sem.at[index],
                recv_sem=self.recv_sem.at[index],
                device_id=(peer, self.model_index),
                device_id_type=MESH,
            )
            copy.start()
            self.sent.append(copy)

    def finish(self):
        self.load(len(self.cuts))
        self.own.wait()
        for index, (shift, cut) in enumerate(self.cuts):
            here = self.target.at[lax.rem(self.me + 8 - shift, 8), cut]
            pltpu.make_async_copy(here, here, self.recv_sem.at[index]).wait()
        for copy in self.sent:
            copy.wait_send()


class Gather:
    def __init__(self, link, outs, steps, own_sem):
        self.link, self.outs, self.steps, self.own_sem = link, outs, steps, own_sem
        self.owns = []

    def spot(self, g, d, group, core=0):
        if len(self.outs) > 1:
            out, start = self.outs[g], self.link.first_row(GROUP, d, group, core)
        else:
            out, start = self.outs[0], self.link.first_row(self.steps * GROUP, d, group, core)
            start = start + g * GROUP
        return out.at[pl.ds(pl.multiple_of(start, GROUP), GROUP)]

    def send(self, g, source, device, here, there):
        self.link.send(source, self.spot(g, *here), device, ("gather", g, *there))

    def arrived(self, g, d, group, core):
        return self.link.arrived(self.spot(g, d, group, core), ("gather", g, d, group, core))

    def begin(self, g, source):
        link = self.link
        own = pltpu.make_async_copy(source, self.spot(g, 0, 0), self.own_sem.at[g])
        own.start()
        self.owns.append(own)
        for d in (1, 2, 3):
            self.send(g, source, link.z_side[d], (0, 0), (d, 0, 0))
        self.send(g, source, link.x_side, (0, 0), (0, 1, 0))
        self.send(g, source, link.y_side, (0, 0), (0, 2, 0))
        self.send(g, source, link.c_side, (0, 0), (0, 0, 1))

    def from_z(self, g, d):
        here = self.arrived(g, d, 0, 0)
        self.send(g, here, self.link.x_side, (d, 0), (d, 1, 0))
        self.send(g, here, self.link.y_side, (d, 0), (d, 2, 0))
        self.send(g, here, self.link.c_side, (d, 0), (d, 0, 1))

    def from_sides(self, g, d):
        for group, side in ((1, self.link.y_side), (2, self.link.x_side)):
            here = self.arrived(g, d, group, 0)
            if (d % 2 == 0) == (group == 1):
                self.send(g, here, side, (d, group), (d, 3, 0))
            self.send(g, here, self.link.c_side, (d, group), (d, group, 1))

    def first(self, g):
        self.from_z(g, 1)
        self.from_sides(g, 0)
        self.from_z(g, 2)
        self.from_z(g, 3)

    def second(self, g):
        for d in (1, 2, 3):
            self.from_sides(g, d)

    def third(self, g):
        for d in range(4):
            here = self.arrived(g, d, 3, 0)
            self.send(g, here, self.link.c_side, (d, 3), (d, 3, 1))

    def finish(self):
        for g in range(self.steps):
            for d in range(4):
                for group in range(4):
                    self.arrived(g, d, group, 1)
        for own in self.owns:
            own.wait()


CORNER = [(d, 3) for d in range(4)]
SIDES = [(1, 1), (3, 1), (0, 2), (2, 2), (0, 1), (2, 1), (1, 2), (3, 2)]
COLUMN = [(d, 0) for d in (3, 2, 1)]


class Scatter:
    def __init__(self, link, partials, rows, order, buffers, own_sem):
        self.link, self.partials, self.rows = link, partials, rows
        self.mine, self.core, self.corner, self.side, self.column = buffers
        self.owns = {}
        for p in order:
            for d, group in CORNER + SIDES + COLUMN + [(0, 0)]:
                k = d * 4 + group
                here = self.mine.at[k, pl.ds(p * GROUP, GROUP)]
                own = pltpu.make_async_copy(self.spot(p, d, group), here, own_sem.at[p * 16 + k])
                own.start()
                self.owns[p, k] = own
                self.send(p, self.spot(p, d, group, 1), self.core, k, link.c_side, "core")

    def spot(self, p, d, group, core=0):
        if len(self.partials) > 1:
            partial, start = self.partials[p], self.link.first_row(GROUP, d, group, core)
        else:
            partial, start = self.partials[0], self.link.first_row(self.rows, d, group, core)
            start = start + p * GROUP
        return partial.at[pl.ds(pl.multiple_of(start, GROUP), GROUP)]

    def send(self, p, source, buffer, k, device, name):
        self.link.send(source, buffer.at[k, pl.ds(p * GROUP, GROUP)], device, (name, p, k))

    def term(self, p, buffer, k, name):
        return self.link.arrived(buffer.at[k, pl.ds(p * GROUP, GROUP)], (name, p, k))[...].astype(
            jnp.float32
        )

    def start_terms(self, p, k):
        self.owns[p, k].wait()
        own = self.mine[k, pl.ds(p * GROUP, GROUP)].astype(jnp.float32)
        return own + self.term(p, self.core, k, "core")

    def pass_on(self, p, k, total, buffer, there, device, name):
        here = self.mine.at[k, pl.ds(p * GROUP, GROUP)]
        here[...] = total.astype(here.dtype)
        self.send(p, here, buffer, there, device, name)

    def to_corner(self, p):
        for d, _ in CORNER:
            side = self.link.y_side if d % 2 == 0 else self.link.x_side
            k = d * 4 + 3
            self.pass_on(p, k, self.start_terms(p, k), self.corner, d, side, "corner")

    def to_sides(self, p):
        for d, group in SIDES:
            k = d * 4 + group
            total = self.start_terms(p, k)
            if (d % 2 == 0) == (group == 1):
                total = total + self.term(p, self.corner, d, "corner")
            side = self.link.x_side if group == 1 else self.link.y_side
            self.pass_on(p, k, total, self.side, d * 2 + group - 1, side, "side")

    def column_terms(self, p, d):
        total = self.start_terms(p, d * 4)
        for k in (d * 2, d * 2 + 1):
            total = total + self.term(p, self.side, k, "side")
        return total

    def to_column(self, p):
        for d, _ in COLUMN:
            total = self.column_terms(p, d)
            self.pass_on(p, d * 4, total, self.column, d - 1, self.link.z_side[d], "column")

    def total(self, p):
        total = self.column_terms(p, 0)
        for d in (1, 2, 3):
            total = total + self.term(p, self.column, d - 1, "column")
        return total


def relay_kernel(plan, row_step, *refs):
    refs = list(refs)

    def take(count):
        taken = refs[:count]
        del refs[:count]
        return taken

    partials = take(plan["partials"])
    ready = take(plan["ready"])
    extras = take(plan["extras"])
    cargo_in = take(plan["cargo"])
    gathered = take(plan["outs"])
    kept = take(plan["kept"])
    sums = take(plan["sums"])
    cargo_out = take(plan["cargo"])
    buffers = take(5)
    held, send_sem, recv_sem, load_sem, own_sem = take(5)
    order, steps = plan["order"], plan["steps"]
    link = Links(send_sem, recv_sem, plan["cargo"])
    gather = Gather(link, gathered, steps, own_sem)
    if ready:
        gather.begin(0, ready[0])
    scatter = Scatter(link, partials, plan["rows"], order, buffers, load_sem)
    cargo = Cargo(*cargo_in, *cargo_out, *refs) if cargo_in else None
    ticks = len(order) + 7
    agenda = [[] for _ in range(ticks)]
    if ready:
        for tick, step in enumerate((gather.first, gather.second, gather.third)):
            agenda[tick + 2].append((step, 0))

    def last(p):
        rows, keeps, adds = row_step(p, scatter.total(p), extras)
        for ref, value in zip(kept, keeps):
            ref[pl.ds(p * GROUP, GROUP)] = value
        for ref, value in zip(sums, adds):
            ref[...] = value if p == order[0] else ref[...] + value
        if rows is not None:
            g = plan["slot"](p)
            held[g] = rows
            gather.begin(g, held.at[g])

    for q, p in enumerate(order):
        for tick, step in enumerate(
            (scatter.to_corner, scatter.to_sides, scatter.to_column, last)
        ):
            agenda[q + tick].append((step, p))
        if plan["slot"](p) is not None:
            for tick, step in enumerate((gather.first, gather.second, gather.third)):
                agenda[q + 4 + tick].append((step, plan["slot"](p)))
    for number, tick in enumerate(agenda):
        if cargo:
            cargo.load(CARGO_EARLY if number < 4 else CARGO_LATE)
        for step, index in tick:
            step(index)
    gather.finish()
    link.finish()
    if cargo:
        cargo.finish()


def relay(
    partials,
    row_step,
    ident,
    extras=(),
    kept=0,
    sums=0,
    order=None,
    slot=None,
    ready=None,
    split=False,
    cargo=None,
):
    devices, width = lax.axis_size("dp") * lax.axis_size("mp"), partials[0].shape[1]
    rows = sum(partial.shape[0] for partial in partials) // devices
    groups = rows // GROUP
    order = list(range(groups)) if order is None else order
    slot = slot or (lambda p: p)
    steps = sum(slot(p) is not None for p in order) + (ready is not None)
    if not kernel_mesh():
        total = jnp.concatenate(
            [lax.psum_scatter(part, BOTH, scatter_dimension=0, tiled=True) for part in partials]
        )
        total = total.astype(jnp.float32)
        outs, keeps, adds = [None] * steps, [None] * groups, [0.0] * sums
        if ready is not None:
            outs[0] = ready
        for p in order:
            out, keeps[p], add = row_step(p, total[p * GROUP : (p + 1) * GROUP], extras)
            adds = [one + two for one, two in zip(adds, add)]
            if out is not None:
                outs[slot(p)] = out
        outs = outs if split else [jnp.concatenate(outs)]
        gathered = [lax.all_gather(out, BOTH, axis=0, tiled=True) for out in outs]
        keeps = [jnp.concatenate(parts) for parts in zip(*keeps)]
        moved = [] if cargo is None else [swap_blocks(cargo)]
        return [*gathered, *keeps, *adds, *moved]
    plan = dict(
        partials=len(partials),
        outs=steps if split else 1,
        cargo=int(cargo is not None),
        rows=rows,
        order=order,
        slot=slot,
        steps=steps,
        ready=int(ready is not None),
        extras=len(extras),
        kept=kept,
        sums=sums,
    )
    low = partials[0].dtype
    load = [] if cargo is None else [cargo]
    vmem = pl.BlockSpec(memory_space=pltpu.VMEM)
    copies = 31 * (groups + steps)
    out_rows = [devices * GROUP] * steps if split else [devices * steps * GROUP]
    shapes = [jax.ShapeDtypeStruct((count, width), low) for count in out_rows]
    shapes += [jax.ShapeDtypeStruct((rows, width), jnp.float32)] * kept
    shapes += [jax.ShapeDtypeStruct((1, width), jnp.float32)] * sums
    shapes += [jax.ShapeDtypeStruct(value.shape, value.dtype) for value in load]
    buffers = [pltpu.VMEM((count, rows, width), low) for count in (16, 16, 4, 8, 3)]
    semaphores = [pltpu.SemaphoreType.DMA((count,)) for count in (copies, copies, 16 * groups, steps)]
    if load:
        semaphores += [pltpu.SemaphoreType.DMA((7 * cargo_cuts(cargo.shape),))] * 2
        semaphores += [pltpu.SemaphoreType.DMA]
    return pl.pallas_call(
        functools.partial(relay_kernel, plan, row_step),
        out_shape=shapes,
        in_specs=[ANY] * (len(partials) + plan["ready"])
        + [vmem] * len(extras)
        + [ANY] * len(load),
        out_specs=[ANY] * len(out_rows) + [vmem] * (kept + sums) + [ANY] * len(load),
        scratch_shapes=buffers + [pltpu.VMEM((steps, GROUP, width), low)] + semaphores,
        compiler_params=comm_params(ident, 60 if rows > 32 else 6 + rows // 4),
        cost_estimate=pl.CostEstimate(flops=1, bytes_accessed=1, transcendentals=0),
    )(*partials, *([] if ready is None else [ready]), *extras, *load)


def after(value, *first):
    return lax.optimization_barrier((value, *first))[0]


def swap_blocks(value):
    return lax.all_to_all(value, "dp", split_axis=0, concat_axis=0, tiled=True)


def small_gather_kernel(then, x_ref, result_ref, o_ref, send_sem, recv_sem, own_sem):
    data_index, model_index = lax.axis_index("dp"), lax.axis_index("mp")
    me = data_index * 4 + model_index
    own = pltpu.make_async_copy(x_ref, o_ref.at[me], own_sem)
    own.start()
    peers = [lax.rem(me + shift, 32) for shift in range(1, 32)]
    barrier = pltpu.get_barrier_semaphore()
    for peer in peers:
        pl.semaphore_signal(
            barrier, inc=1, device_id=(peer // 4, peer % 4), device_id_type=MESH
        )
    pl.semaphore_wait(barrier, 31)
    sent = []
    for index, peer in enumerate(peers):
        copy = pltpu.make_async_remote_copy(
            src_ref=x_ref,
            dst_ref=o_ref.at[me],
            send_sem=send_sem.at[index],
            recv_sem=recv_sem.at[index],
            device_id=(peer // 4, peer % 4),
            device_id_type=MESH,
        )
        copy.start()
        sent.append(copy)
    for index in range(31):
        here = o_ref.at[lax.rem(me + 31 - index, 32)]
        pltpu.make_async_copy(here, here, recv_sem.at[index]).wait()
    own.wait()
    result_ref[...] = then(o_ref)
    for copy in sent:
        copy.wait_send()


def gather_small(value, then, shape, ident):
    if not kernel_mesh():
        return then(lax.all_gather(value, BOTH))
    vmem = pl.BlockSpec(memory_space=pltpu.VMEM)
    return pl.pallas_call(
        functools.partial(small_gather_kernel, then),
        out_shape=jax.ShapeDtypeStruct(shape, value.dtype),
        in_specs=[vmem],
        out_specs=vmem,
        scratch_shapes=[
            pltpu.VMEM((32,) + value.shape, value.dtype),
            pltpu.SemaphoreType.DMA((31,)),
            pltpu.SemaphoreType.DMA((31,)),
            pltpu.SemaphoreType.DMA,
        ],
        compiler_params=comm_params(ident, 2),
    )(value)


def greet(peers):
    barrier = pltpu.get_barrier_semaphore()
    for peer in peers:
        pl.semaphore_signal(barrier, inc=1, device_id=peer, device_id_type=MESH)
    pl.semaphore_wait(barrier, len(peers))


def exchange_kernel(count, whole, *refs):
    ins, outs = refs[: len(whole)], refs[len(whole) : 2 * len(whole)]
    send_sem, recv_sem, own_sem = refs[2 * len(whole) :]
    me, model_index = lax.axis_index("dp"), lax.axis_index("mp")
    peers = [lax.rem(me + shift, count) for shift in range(1, count)]
    greet([(peer, model_index) for peer in peers])
    owns, sent = [], []
    for array, keep in enumerate(whole):
        own = pltpu.make_async_copy(
            ins[array] if keep else ins[array].at[me], outs[array].at[me], own_sem.at[array]
        )
        own.start()
        owns.append(own)
        for shift in range(count - 1):
            copy = pltpu.make_async_remote_copy(
                src_ref=ins[array] if keep else ins[array].at[peers[shift]],
                dst_ref=outs[array].at[me],
                send_sem=send_sem.at[array, shift],
                recv_sem=recv_sem.at[array, shift],
                device_id=(peers[shift], model_index),
                device_id_type=MESH,
            )
            copy.start()
            sent.append(copy)
    for own in owns:
        own.wait()
    for array in range(len(whole)):
        for shift in range(count - 1):
            source = lax.rem(me + count - 1 - shift, count)
            here = outs[array].at[source]
            pltpu.make_async_copy(here, here, recv_sem.at[array, shift]).wait()
    for copy in sent:
        copy.wait_send()


def exchange(values, whole, ident):
    count = lax.axis_size("dp")
    if not kernel_mesh():
        return [
            lax.all_gather(value, "dp")
            if keep
            else lax.all_to_all(value, "dp", split_axis=0, concat_axis=0, tiled=True)
            for value, keep in zip(values, whole)
        ]
    shapes = [
        jax.ShapeDtypeStruct(((count,) if keep else ()) + value.shape, value.dtype)
        for value, keep in zip(values, whole)
    ]
    return pl.pallas_call(
        functools.partial(exchange_kernel, count, tuple(whole)),
        out_shape=shapes,
        in_specs=[ANY] * len(values),
        out_specs=[ANY] * len(values),
        scratch_shapes=[
            pltpu.SemaphoreType.DMA((len(values), count - 1)),
            pltpu.SemaphoreType.DMA((len(values), count - 1)),
            pltpu.SemaphoreType.DMA((len(values),)),
        ],
        compiler_params=comm_params(ident, 2),
    )(*values)


def turned(values, cosine, sine_table):
    return values * cosine + pltpu.roll(values, HEAD_DIM // 2, 1) * sine_table


def to_column(row):
    return jnp.broadcast_to(row, (row.shape[1], row.shape[1])).T[:, :1]


def to_row(column):
    return jnp.broadcast_to(column, (column.shape[0], column.shape[0])).T[:1]


def softmax_rows(query, keys, places):
    scores = dot(query, keys, 1, 1) * (1.0 / math.sqrt(HEAD_DIM))
    columns = lax.broadcasted_iota(jnp.int32, scores.shape, 1)
    scores = jnp.where(columns <= places, scores, NEG)
    weights = jnp.exp(scores - jnp.max(scores, axis=-1, keepdims=True))
    return weights / jnp.sum(weights, axis=-1, keepdims=True)


def attend_kernel(
    exit_ref,
    resid_ref,
    gain_ref,
    head_ref,
    inner_ref,
    outer_ref,
    pick_ref,
    place_ref,
    live_ref,
    attn_ref,
    query_ref,
    key_ref,
    value_ref,
    out_ref,
    turn_ref,
    slot_turn_ref,
    partial_ref,
):
    block, blocks = pl.program_id(0), key_ref.shape[0] // resid_ref.shape[0]
    rows, slots = resid_ref.shape[0], pick_ref.shape[1]
    parts, columns = head_ref.shape[0], head_ref.shape[2]
    low = jnp.bfloat16
    attn = norm_fwd(resid_ref[...].astype(jnp.float32), gain_ref[...])[0].astype(low)
    attn_ref[...] = attn
    projected = jnp.zeros((rows, 3 * HEAD_DIM), jnp.float32)
    for part in range(parts):
        piece = attn[:, part * columns : (part + 1) * columns]
        projected = projected + dot(piece, head_ref[part, : 3 * HEAD_DIM], 1, 1)
    inner_cos, inner_sin = inner_ref[0], inner_ref[1]
    outer_cos, outer_sin = outer_ref[0, pl.ds(block, 1)], outer_ref[1, pl.ds(block, 1)]
    sign = jnp.where(lax.broadcasted_iota(jnp.int32, inner_cos.shape, 1) < HEAD_DIM // 2, -1.0, 1.0)
    cosine = inner_cos * outer_cos - inner_sin * outer_sin
    sine_table = (inner_sin * outer_cos + inner_cos * outer_sin) * sign
    at = pl.ds(pl.multiple_of(block * rows, rows), rows)
    turn_ref[0, at], turn_ref[1, at] = cosine, sine_table
    query = turned(projected[:, :HEAD_DIM], cosine, sine_table).astype(low)
    key_ref[at] = turned(projected[:, HEAD_DIM : 2 * HEAD_DIM], cosine, sine_table).astype(low)
    value_ref[at] = projected[:, 2 * HEAD_DIM :].astype(low)
    at = pl.ds(pl.multiple_of(block * slots, slots), slots)
    query_ref[at] = dot(pick_ref[0], query).astype(low)
    pick_wide = pick_ref[0].astype(jnp.float32)
    for index, table in enumerate((cosine, sine_table)):
        slot_turn_ref[index, at] = jnp.dot(
            pick_wide, table, precision=lax.Precision.HIGHEST, preferred_element_type=jnp.float32
        )

    @pl.when(block == blocks - 1)
    def _():
        exit_here = exit_ref[0]
        step = 2 * slots
        for index in range(blocks // 2):
            reach = (index + 1) * 2 * rows
            at = slice(index * step, (index + 1) * step)
            row = slice(index, index + 1)
            places, live = to_column(place_ref[row]), to_column(live_ref[row])
            probs = softmax_rows(query_ref[at], key_ref[:reach], places).astype(low)
            out = (dot(probs, value_ref[:reach]) * live).astype(low)
            out_ref[at] = out
            groups = step // partial_ref.shape[2]
            at = slice(index * groups, (index + 1) * groups)
            for part in range(parts):
                share = dot(out, head_ref[part, 3 * HEAD_DIM :]).astype(low)
                share = share.reshape(groups, 1, -1, columns)
                lanes = slice(part * columns, (part + 1) * columns)
                partial_ref[at, pl.ds(exit_here, 1), :, lanes] = share
                partial_ref[at, pl.ds(1 - exit_here, 1), :, lanes] = jnp.zeros_like(share)


def attend_back_kernel(
    exit_ref,
    done_ref,
    head_ref,
    out_ref,
    query_ref,
    key_ref,
    value_ref,
    turn_ref,
    slot_turn_ref,
    pick_ref,
    place_ref,
    attn_ref,
    partial_ref,
    parts_ref,
    key_sum,
    value_sum,
    turned_ref,
    head_sum,
):
    block, blocks = pl.program_id(0), key_ref.shape[0] // attn_ref.shape[0]
    rows, slots = attn_ref.shape[0], pick_ref.shape[1]
    parts, columns = head_ref.shape[0], head_ref.shape[2]
    low = jnp.bfloat16
    scale = 1.0 / math.sqrt(HEAD_DIM)

    @pl.when(block == 0)
    def _():
        key_sum[...] = jnp.zeros_like(key_sum)
        value_sum[...] = jnp.zeros_like(value_sum)
        step = 2 * slots
        width = done_ref.shape[-1]
        done = done_ref[...].reshape(-1, width)
        dout = jnp.zeros((done.shape[0], HEAD_DIM), jnp.float32)
        for part in range(parts):
            piece = done[:, part * columns : (part + 1) * columns]
            parts_ref[part, 3 * HEAD_DIM :] = dot(out_ref[...], piece, 0, 0).astype(low)
            dout = dout + dot(piece, head_ref[part, 3 * HEAD_DIM :], 1, 1)
        dout = dout.astype(low)
        for index in range(blocks // 2):
            reach = (index + 1) * 2 * rows
            at = slice(index * step, (index + 1) * step)
            places = to_column(place_ref[index : index + 1])
            probs = softmax_rows(query_ref[at], key_ref[:reach], places)
            dprobs = dot(dout[at], value_ref[:reach], 1, 1)
            delta = jnp.sum(probs * dprobs, axis=-1, keepdims=True)
            dscores = (probs * (dprobs - delta)).astype(low)
            dquery = dot(dscores, key_ref[:reach]) * scale
            dquery = turned(dquery, slot_turn_ref[0, at], -slot_turn_ref[1, at]).astype(low)
            for half in (0, 1):
                where = 2 * index + half
                turned_ref[where * rows : (where + 1) * rows, :HEAD_DIM] = dot(
                    pick_ref[where], dquery[half * slots : (half + 1) * slots], 0, 0
                ).astype(low)
            key_sum[:reach] += dot(dscores, query_ref[at], 0, 0)
            value_sum[:reach] += dot(probs.astype(low), dout[at], 0, 0)
        dkey = turned(key_sum[...] * scale, turn_ref[0], -turn_ref[1])
        turned_ref[:, HEAD_DIM : 2 * HEAD_DIM] = dkey.astype(low)
        turned_ref[:, 2 * HEAD_DIM :] = value_sum[...].astype(low)

    at = pl.ds(pl.multiple_of(block * rows, rows), rows)
    dprojected = turned_ref[at]
    for part in range(parts):
        lanes = slice(part * columns, (part + 1) * columns)
        partial_ref[:, lanes] = dot(dprojected, head_ref[part, : 3 * HEAD_DIM]).astype(low)
    term = dot(dprojected, attn_ref[...], 0, 0)

    @pl.when(block == 0)
    def _():
        head_sum[...] = term

    @pl.when(block > 0)
    def _():
        head_sum[...] += term

    @pl.when(block == blocks - 1)
    def _():
        for part in range(parts):
            lanes = slice(part * columns, (part + 1) * columns)
            parts_ref[part, : 3 * HEAD_DIM] = head_sum[:, lanes].astype(low)


def local_params(room):
    return dict(
        compiler_params=pltpu.CompilerParams(vmem_limit_bytes=room * MIB),
        cost_estimate=pl.CostEstimate(flops=1, bytes_accessed=1, transcendentals=0),
    )


def whole_spec(value):
    return pl.BlockSpec(value.shape, lambda b, e: (0,) * len(value.shape))


def attend(exit_here, resid, gain, head, inner, outer, pick, places, live, slots_here):
    (tokens, width), (blocks, slots, rows) = resid.shape, pick.shape
    low = resid.dtype
    devices = blocks * slots // slots_here
    by_block = pl.BlockSpec((rows, width), lambda b, e: (b, 0))
    outs = [
        jax.ShapeDtypeStruct((tokens, width), low),
        jax.ShapeDtypeStruct((blocks * slots, HEAD_DIM), low),
        jax.ShapeDtypeStruct((tokens, HEAD_DIM), low),
        jax.ShapeDtypeStruct((tokens, HEAD_DIM), low),
        jax.ShapeDtypeStruct((blocks * slots, HEAD_DIM), low),
        jax.ShapeDtypeStruct((2, tokens, HEAD_DIM), jnp.float32),
        jax.ShapeDtypeStruct((2, blocks * slots, HEAD_DIM), jnp.float32),
        jax.ShapeDtypeStruct((devices, 2, slots_here, width), low),
    ]
    return pl.pallas_call(
        attend_kernel,
        out_shape=outs,
        grid_spec=pltpu.PrefetchScalarGridSpec(
            num_scalar_prefetch=1,
            grid=(blocks,),
            in_specs=[
                by_block,
                whole_spec(gain),
                whole_spec(head),
                whole_spec(inner),
                whole_spec(outer),
                pl.BlockSpec((1, slots, rows), lambda b, e: (b, 0, 0)),
                whole_spec(places),
                whole_spec(live),
            ],
            out_specs=[by_block] + [whole_spec(out) for out in outs[1:]],
        ),
        **local_params(60),
    )(exit_here, resid, gain, head, inner, outer, pick, places, live)


def attend_back(exit_here, done, head, out, query, key, value, turn, slot_turn, pick, places, attn):
    (tokens, width), (blocks, slots, rows) = attn.shape, pick.shape
    low = attn.dtype
    devices, _, slots_here, _ = done.shape
    by_block = pl.BlockSpec((rows, width), lambda b, e: (b, 0))
    inner = [head, out, query, key, value, turn, slot_turn, pick, places]
    parts = jax.ShapeDtypeStruct(head.shape, low)
    return pl.pallas_call(
        attend_back_kernel,
        out_shape=[jax.ShapeDtypeStruct((tokens, width), low), parts],
        grid_spec=pltpu.PrefetchScalarGridSpec(
            num_scalar_prefetch=1,
            grid=(blocks,),
            in_specs=[
                pl.BlockSpec((devices, 1, slots_here, width), lambda b, e: (0, e[0], 0, 0))
            ]
            + [whole_spec(value) for value in inner]
            + [by_block],
            out_specs=[by_block, whole_spec(parts)],
            scratch_shapes=[
                pltpu.VMEM((tokens, HEAD_DIM), jnp.float32),
                pltpu.VMEM((tokens, HEAD_DIM), jnp.float32),
                pltpu.VMEM((tokens, 3 * HEAD_DIM), low),
                pltpu.VMEM((3 * HEAD_DIM, width), jnp.float32),
            ],
        ),
        **local_params(60),
    )(exit_here, done, *inner, attn)


def local(kernel, room, outs, *values, scratch=()):
    vmem = pl.BlockSpec(memory_space=pltpu.VMEM)
    return pl.pallas_call(
        kernel,
        out_shape=[jax.ShapeDtypeStruct(shape, dtype) for shape, dtype in outs],
        in_specs=[vmem] * len(values),
        out_specs=[vmem] * len(outs),
        scratch_shapes=list(scratch),
        **local_params(room),
    )(*values)


def slots_kernel(ints_ref, pick_ref, place_ref, target_ref, live_ref, weight_ref):
    blocks, _, rows = ints_ref.shape
    slots, lanes = pick_ref.shape[2], place_ref.shape[1]
    low = jnp.bfloat16
    across = lax.broadcasted_iota(jnp.int32, (rows, rows), 1)
    down = lax.broadcasted_iota(jnp.int32, (rows, rows), 0)
    until = jnp.where(down <= across, 1.0, 0.0).astype(low)
    slot = lax.broadcasted_iota(jnp.int32, (slots, rows), 0).astype(jnp.float32)
    kind = lax.broadcasted_iota(jnp.int32, (8, rows), 0)
    inner = lax.broadcasted_iota(jnp.int32, (1, rows), 1).astype(jnp.float32)
    for e in range(2):
        mask = ints_ref[:, 2 + e].astype(jnp.float32)
        ranks = dot(mask.astype(low), until) - 1.0
        for block in range(blocks):
            at = slice(block, block + 1)
            pick = jnp.where((ranks[at] == slot) & (mask[at] == 1.0), 1.0, 0.0).astype(low)
            pick_ref[e, block] = pick
            target = ints_ref[block, 1:2]
            high = (target >> 8).astype(jnp.float32)
            rest = (target & 255).astype(jnp.float32)
            facts = jnp.where(kind == 0, inner, jnp.where(kind == 1, high, rest))
            facts = jnp.where(kind == 3, 1.0, facts).astype(low)
            found = dot(facts, pick, 1, 1)
            live = found[3:4]
            row = slice((e * blocks + block) * slots // lanes, (e * blocks + block) * slots // lanes + 1)
            lane = slice(block * slots % lanes, block * slots % lanes + slots)
            place = found[0:1] + live * float(block * rows)
            place_ref[row, lane] = place.astype(jnp.int32)
            target_ref[row, lane] = (found[1:2] * 256.0 + found[2:3]).astype(jnp.int32)
            live_ref[row, lane] = live
        half = slice(e * blocks * slots // lanes, (e + 1) * blocks * slots // lanes)
        live = live_ref[half]
        weight_ref[half] = live * (EXIT_SCALE[e] / jnp.sum(live, keepdims=True))


def pack_head_kernel(qkv_ref, out_ref, packed_ref):
    heads = out_ref.shape[0] // HEAD_DIM
    sharers = packed_ref.shape[0] // heads
    low = packed_ref.dtype
    for head in range(heads):
        lanes = slice(head * HEAD_DIM, (head + 1) * HEAD_DIM)
        for c in range(4):
            block = out_ref[lanes] if c == 3 else qkv_ref[c, :, lanes].T
            for sharer in range(sharers):
                packed_ref[head * sharers + sharer, c * HEAD_DIM : (c + 1) * HEAD_DIM] = block.astype(
                    low
                )


def pack_hidden_kernel(gate_up_ref, down_ref, packed_ref, turned_ref):
    parts, hidden = packed_ref.shape[0], packed_ref.shape[1] // 3
    low = packed_ref.dtype
    for c in range(2):
        for start in range(0, gate_up_ref.shape[2], 128):
            lanes = slice(start, start + 128)
            turned_ref[lanes] = gate_up_ref[:, c, lanes].T
        for part in range(parts):
            packed_ref[part, c * hidden : (c + 1) * hidden] = turned_ref[
                part * hidden : (part + 1) * hidden
            ].astype(low)
    for part in range(parts):
        packed_ref[part, 2 * hidden :] = down_ref[part * hidden : (part + 1) * hidden].astype(low)


def square_row(value):
    return jnp.sum(value * value, axis=0, keepdims=True)


def unpack_head_kernel(one_ref, two_ref, qkv_ref, out_ref, square_ref):
    heads = out_ref.shape[0] // HEAD_DIM
    sharers = one_ref.shape[0] // heads
    squares = jnp.zeros(square_ref.shape, jnp.float32)
    for head in range(heads):
        lanes = slice(head * HEAD_DIM, (head + 1) * HEAD_DIM)
        for c in range(4):
            parts_ref = one_ref if c < 2 else two_ref
            rows = slice(c % 2 * HEAD_DIM, (c % 2 + 1) * HEAD_DIM)
            total = parts_ref[head * sharers, rows].astype(jnp.float32)
            for sharer in range(1, sharers):
                total = total + parts_ref[head * sharers + sharer, rows].astype(jnp.float32)
            squares = squares + square_row(total)
            if c == 3:
                out_ref[lanes] = total
            else:
                qkv_ref[c, :, lanes] = total.T
    square_ref[...] = squares


def unpack_hidden_kernel(parts_ref, down_parts_ref, gate_up_ref, down_ref, square_ref, turned_ref):
    parts, hidden = down_parts_ref.shape[:2]
    squares = jnp.zeros(square_ref.shape, jnp.float32)
    for c in range(3):
        target = down_ref if c == 2 else turned_ref
        for part in range(parts):
            block = down_parts_ref[part] if c == 2 else parts_ref[part, c * hidden : (c + 1) * hidden]
            block = block.astype(jnp.float32)
            squares = squares + square_row(block)
            target[part * hidden : (part + 1) * hidden] = block
        if c < 2:
            for start in range(0, gate_up_ref.shape[2], 128):
                lanes = slice(start, start + 128)
                gate_up_ref[:, c, lanes] = turned_ref[lanes].T
    square_ref[...] = squares


def hidden_kernel(rows_ref, weight_ref, gate_ref, up_ref, hidden_ref, partial_ref):
    parts, columns = weight_ref.shape[0], weight_ref.shape[2]
    hidden = weight_ref.shape[1] // 3
    low = jnp.bfloat16
    gate = jnp.zeros(gate_ref.shape, jnp.float32)
    up = jnp.zeros(gate_ref.shape, jnp.float32)
    for part in range(parts):
        piece = rows_ref[:, part * columns : (part + 1) * columns]
        gate = gate + dot(piece, weight_ref[part, :hidden], 1, 1)
        up = up + dot(piece, weight_ref[part, hidden : 2 * hidden], 1, 1)
    gate_ref[...], up_ref[...] = gate, up
    value = (gate * jax.nn.sigmoid(gate) * up).astype(low)
    hidden_ref[...] = value
    for part in range(parts):
        partial_ref[:, part * columns : (part + 1) * columns] = dot(
            value, weight_ref[part, 2 * hidden :]
        ).astype(low)


def hidden_back_kernel(
    dtwo_ref,
    rows_ref,
    weight_ref,
    gate_ref,
    up_ref,
    hidden_ref,
    partial_ref,
    parts_ref,
    down_parts_ref,
):
    parts, hidden, columns = down_parts_ref.shape
    low = jnp.bfloat16
    dhidden = jnp.zeros(gate_ref.shape, jnp.float32)
    for part in range(parts):
        piece = dtwo_ref[:, part * columns : (part + 1) * columns]
        dhidden = dhidden + dot(piece, weight_ref[part, 2 * hidden :], 1, 1)
        down_parts_ref[part] = dot(hidden_ref[...], piece, 0, 0).astype(low)
    gate, up = gate_ref[...], up_ref[...]
    sigma = jax.nn.sigmoid(gate)
    dgate = (dhidden * up * sigma * (1.0 + gate * (1.0 - sigma))).astype(low)
    dup = (dhidden * gate * sigma).astype(low)
    for part in range(parts):
        lanes = slice(part * columns, (part + 1) * columns)
        partial_ref[:, lanes] = (
            dot(dgate, weight_ref[part, :hidden]) + dot(dup, weight_ref[part, hidden : 2 * hidden])
        ).astype(low)
        parts_ref[part, :hidden] = dot(dgate, rows_ref[:, lanes], 0, 0).astype(low)
        parts_ref[part, hidden : 2 * hidden] = dot(dup, rows_ref[:, lanes], 0, 0).astype(low)


def embed_kernel(base_ref, ids_ref, table_ref, partial_ref, low_ref, hits_ref):
    @pl.when(pl.program_id(0) == 0)
    def _():
        entries = base_ref[0] + lax.broadcasted_iota(jnp.int32, (1, table_ref.shape[0]), 1)
        hits_ref[...] = jnp.where(ids_ref[...] == entries, 1.0, 0.0).astype(hits_ref.dtype)

    table_low = table_ref[...].astype(low_ref.dtype)
    low_ref[...] = table_low
    partial_ref[...] = dot(hits_ref[...], table_low).astype(partial_ref.dtype)


def embed(base, ids, table):
    (entries, width), tokens, low = table.shape, ids.shape[0], jnp.bfloat16
    columns = 256
    by_columns = lambda rows: pl.BlockSpec((rows, columns), lambda b, e: (0, b))
    return pl.pallas_call(
        embed_kernel,
        out_shape=[
            jax.ShapeDtypeStruct((tokens, width), low),
            jax.ShapeDtypeStruct((entries, width), low),
        ],
        grid_spec=pltpu.PrefetchScalarGridSpec(
            num_scalar_prefetch=1,
            grid=(width // columns,),
            in_specs=[whole_spec(ids), by_columns(entries)],
            out_specs=[by_columns(tokens), by_columns(entries)],
            scratch_shapes=[pltpu.VMEM((tokens, entries), low)],
        ),
        **local_params(60),
    )(base, ids, table)


def logits_kernel(one_ref, two_ref, table_ref, target_ref, entry_ref, logits_ref, stats_ref):
    slots, step, lanes = one_ref.shape[0], 256, stats_ref.shape[1]
    for e, rows_ref in enumerate((one_ref, two_ref)):
        for start in range(0, slots, step):
            values = dot(rows_ref[start : start + step], table_ref[...], 1, 1)
            logits_ref[e * slots + start : e * slots + start + step] = values
            top = jnp.max(values, axis=1, keepdims=True)
            mass = jnp.sum(jnp.exp(values - top), axis=1, keepdims=True)
            for part in range(0, step, lanes):
                row = (e * slots + start + part) // lanes
                at = slice(part, part + lanes)
                hit = to_column(target_ref[row : row + 1]) == entry_ref[...]
                found = jnp.sum(jnp.where(hit, values[at], 0.0), axis=1, keepdims=True)
                for stat, column in enumerate((top[at], mass[at], found)):
                    index = stat * (2 * slots // lanes) + row
                    stats_ref[index : index + 1] = to_row(column)


def head_grad_kernel(
    logits_ref, lse_ref, weight_ref, target_ref, entry_ref, table_ref, one_ref, two_ref, *terms
):
    slots, lanes, step = one_ref.shape[0], lse_ref.shape[1], 256
    low = jnp.bfloat16
    for e, grad_ref in enumerate((one_ref, two_ref)):
        for start in range(0, slots, lanes):
            row = (e * slots + start) // lanes
            lse, weight, target = (
                to_column(ref[row : row + 1]) for ref in (lse_ref, weight_ref, target_ref)
            )
            values = logits_ref[row * lanes : (row + 1) * lanes]
            hit = jnp.where(target == entry_ref[...], 1.0, 0.0)
            grad_ref[start : start + lanes] = (weight * (jnp.exp(values - lse) - hit)).astype(low)
        for start in range(0, slots, step):
            at = slice(start, start + step)
            terms[e][at] = dot(grad_ref[at], table_ref[...]).astype(low)


def table_grad_kernel(
    base_ref, ids_ref, one_ref, two_ref, rows_one, rows_two, dzero_ref, grad_ref, square_ref, left_ref
):
    slots = one_ref.shape[0]

    @pl.when(pl.program_id(0) == 0)
    def _():
        entries = base_ref[0] + lax.broadcasted_iota(jnp.int32, (left_ref.shape[0], 1), 0)
        left_ref[:, :slots] = one_ref[...].T
        left_ref[:, slots : 2 * slots] = two_ref[...].T
        hits = jnp.where(ids_ref[...] == entries, 1.0, 0.0)
        left_ref[:, 2 * slots :] = hits.astype(left_ref.dtype)

    grad = (
        dot(left_ref[:, :slots], rows_one[...])
        + dot(left_ref[:, slots : 2 * slots], rows_two[...])
        + dot(left_ref[:, 2 * slots :], dzero_ref[...])
    )
    grad_ref[...] = grad
    square_ref[...] = square_row(grad)


def table_gradient(base, ids, grads, rows, dzero):
    slots, entries = grads[0].shape
    tokens, width = dzero.shape
    columns = 256
    by_columns = lambda count: pl.BlockSpec((count, columns), lambda b, e: (0, b))
    return pl.pallas_call(
        table_grad_kernel,
        out_shape=[
            jax.ShapeDtypeStruct((entries, width), jnp.float32),
            jax.ShapeDtypeStruct((1, width), jnp.float32),
        ],
        grid_spec=pltpu.PrefetchScalarGridSpec(
            num_scalar_prefetch=1,
            grid=(width // columns,),
            in_specs=[whole_spec(ids), whole_spec(grads[0]), whole_spec(grads[1])]
            + [by_columns(slots), by_columns(slots), by_columns(tokens)],
            out_specs=[by_columns(entries), by_columns(1)],
            scratch_shapes=[pltpu.VMEM((entries, 2 * slots + tokens), dzero.dtype)],
        ),
        **local_params(60),
    )(base, ids, *grads, *rows, dzero)


def norm_fwd(values, gain):
    row_scale = lax.rsqrt(jnp.mean(values * values, axis=-1, keepdims=True) + EPS_NORM)
    unit_rows = values * row_scale
    return (unit_rows * gain, unit_rows, row_scale)


def norm_back(unit_rows, row_scale, gain, gradient):
    weighted = gradient * gain
    back_rows = row_scale * (
        weighted - unit_rows * jnp.mean(weighted * unit_rows, axis=-1, keepdims=True)
    )
    return (back_rows, jnp.sum(gradient * unit_rows, axis=0))


def rotary(places, width):
    half_width = width // 2
    frequency = jnp.exp(
        jnp.arange(half_width, dtype=jnp.float32) * (-math.log(10000.0) / half_width)
    )
    angles = places.astype(jnp.float32)[:, None] * frequency[None, :]
    return (jnp.cos(angles), jnp.sin(angles))


def rotate_pairs(values, cosine, sine_table):
    half_width = values.shape[-1] // 2
    front_half = values[..., :half_width]
    back_half = values[..., half_width:]
    return jnp.concatenate(
        [
            front_half * cosine - back_half * sine_table,
            back_half * cosine + front_half * sine_table,
        ],
        axis=-1,
    )


def dot(left, right, left_dim=1, right_dim=0):
    return lax.dot_general(
        left, right, (((left_dim,), (right_dim,)), ((), ())), preferred_element_type=jnp.float32
    )


def adam_update(weight, moment_one, moment_two, gradient, rate, decay):
    moment_one = BETA_ONE * moment_one + (1.0 - BETA_ONE) * gradient
    moment_two = BETA_TWO * moment_two + (1.0 - BETA_TWO) * gradient * gradient
    ratio = (
        moment_one
        / (1.0 - BETA_ONE**STEP)
        / (jnp.sqrt(moment_two / (1.0 - BETA_TWO**STEP)) + ADAM_EPS)
    )
    return (weight - rate * (ratio + decay * weight), moment_one, moment_two)


def small_sum_kernel(x_ref, o_ref, held, plane, column, send_sem, recv_sem):
    data_index, model_index = lax.axis_index("dp"), lax.axis_index("mp")
    z, y = data_index // 2, data_index % 2
    x, c = model_index // 2, model_index % 2
    core = (data_index, x * 2 + 1 - c)
    corners = [
        (data_index, (1 - x) * 2 + c),
        (z * 2 + 1 - y, model_index),
        (z * 2 + 1 - y, (1 - x) * 2 + c),
    ]
    zs = (z + 1 - 2 * (z % 2), (z + 2) % 4, 3 - z)
    greet([core] + corners + [(zd * 2 + y, model_index) for zd in zs])
    sent = []

    def send(source, target, device):
        index = len(sent)
        copy = pltpu.make_async_remote_copy(
            src_ref=source,
            dst_ref=target,
            send_sem=send_sem.at[index],
            recv_sem=recv_sem.at[index],
            device_id=device,
            device_id_type=MESH,
        )
        copy.start()
        sent.append(copy)
        return copy

    held[0] = x_ref[...]
    send(held.at[0], held.at[1], core).wait_recv()
    mine = y * 2 + x
    plane[mine] = held[0] + held[1]
    for copy in [send(plane.at[mine], plane.at[mine], device) for device in corners]:
        copy.wait_recv()
    column[z] = (plane[0] + plane[1]) + (plane[2] + plane[3])
    for copy in [send(column.at[z], column.at[z], (zd * 2 + y, model_index)) for zd in zs]:
        copy.wait_recv()
    o_ref[...] = (column[0] + column[1]) + (column[2] + column[3])
    for copy in sent:
        copy.wait_send()


def sum_small(value, ident):
    if not kernel_mesh():
        return lax.psum(value, BOTH)
    vmem = pl.BlockSpec(memory_space=pltpu.VMEM)
    return pl.pallas_call(
        small_sum_kernel,
        out_shape=jax.ShapeDtypeStruct(value.shape, value.dtype),
        in_specs=[vmem],
        out_specs=vmem,
        scratch_shapes=[
            pltpu.VMEM((2,) + value.shape, value.dtype),
            pltpu.VMEM((4,) + value.shape, value.dtype),
            pltpu.VMEM((4,) + value.shape, value.dtype),
            pltpu.SemaphoreType.DMA((7,)),
            pltpu.SemaphoreType.DMA((7,)),
        ],
        compiler_params=comm_params(ident, 2),
    )(value)


def body(
    token_ids,
    target_ids,
    exit_mask,
    table,
    table_first,
    table_second,
    qkv_weight,
    qkv_first,
    qkv_second,
    out_weight,
    out_first,
    out_second,
    gate_up_weight,
    gate_up_first,
    gate_up_second,
    down_weight,
    down_first,
    down_second,
    gains,
    gains_first,
    gains_second,
):
    low = jnp.bfloat16
    data_size, model_size = lax.axis_size("dp"), lax.axis_size("mp")
    data_index, model_index = lax.axis_index("dp"), lax.axis_index("mp")
    devices = data_size * model_size
    block_rows = token_ids.shape[0]
    tokens = block_rows * data_size
    width = table.shape[1]
    width_here = qkv_weight.shape[0]
    heads_here = qkv_weight.shape[2] // HEAD_DIM
    hidden_here = down_weight.shape[0] // data_size
    vocab_here = table.shape[0]
    device_index = data_index * model_size + model_index
    vocab_ids = device_index * vocab_here + jnp.arange(vocab_here, dtype=jnp.int32)
    score_scale = 1.0 / math.sqrt(HEAD_DIM)

    sharers = data_size // heads_here
    shares = sharers // 2
    share_slots = data_size // shares * R_DEV
    exit_here = data_index % sharers % 2
    share_here = data_index % sharers // 2
    slots_here = R_DEV // model_size
    rows_here = block_rows // model_size

    ints, gain_low = exchange(
        [
            jnp.concatenate([token_ids[None], target_ids[None], exit_mask]),
            jnp.pad(gains.astype(low), ((0, 13), (0, 0))),
        ],
        (True, True),
        0,
    )
    gain_rows = jnp.moveaxis(gain_low[:, :3], 0, 1).reshape(3, width).astype(jnp.float32)
    all_ids = ints[:, 0].reshape(tokens)
    token_places = jnp.arange(tokens, dtype=jnp.int32)
    packed = kernel_mesh()
    slot_shape = (2 * data_size * R_DEV // 128, 128)
    if packed:
        pick_low, place_rows, target_rows, live_rows, weight_rows = local(
            slots_kernel,
            16,
            [
                ((2, data_size, R_DEV, block_rows), low),
                (slot_shape, jnp.int32),
                (slot_shape, jnp.int32),
                (slot_shape, jnp.float32),
                (slot_shape, jnp.float32),
            ],
            ints,
        )
    else:
        mask_blocks = jnp.moveaxis(ints[:, 2:], 0, 1)
        slot_ids = jnp.arange(R_DEV, dtype=jnp.int32)
        slot_ranks = jnp.cumsum(mask_blocks, axis=2) - 1
        pick_int = (
            (slot_ranks[:, :, None, :] == slot_ids[:, None]) & (mask_blocks[:, :, None, :] == 1)
        ).astype(jnp.int32)
        pick_low = pick_int.astype(low)
        target_rows = jnp.sum(pick_int * ints[:, 1][None, :, None, :], axis=3).reshape(slot_shape)
        place_rows = jnp.sum(
            pick_int * token_places.reshape(1, data_size, 1, block_rows), axis=3
        ).reshape(slot_shape)
        live_rows = (slot_ids < jnp.sum(mask_blocks, axis=2)[:, :, None]).astype(jnp.float32)
        live_rows = live_rows.reshape(slot_shape)
        scales = jnp.array(EXIT_SCALE, jnp.float32) / jnp.sum(live_rows.reshape(2, -1), axis=1)
        weight_rows = live_rows * jnp.repeat(scales, slot_shape[0] // 2)[:, None]
    slot_targets, live = target_rows.reshape(2, -1), live_rows.reshape(2, -1)
    row_weight = weight_rows.reshape(2, -1)
    counts = jnp.sum(live, axis=1)

    head_shape = (data_size, 4 * HEAD_DIM, width_here)
    hidden_shape = (data_size, 2 * hidden_here, width_here)
    down_shape = (data_size, hidden_here, width_here)
    if packed:
        (head_rows,) = local(
            pack_head_kernel,
            10,
            [(head_shape, low)],
            jnp.transpose(qkv_weight, (1, 0, 2)),
            out_weight,
        )
    else:
        head_rows = jnp.moveaxis(
            qkv_weight.astype(low).reshape(width_here, 3, heads_here, HEAD_DIM), 0, 3
        )
        head_rows = jnp.concatenate(
            [
                jnp.moveaxis(head_rows, 0, 1).reshape(heads_here, 3 * HEAD_DIM, width_here),
                out_weight.astype(low).reshape(heads_here, HEAD_DIM, width_here),
            ],
            axis=1,
        )
        head_rows = jnp.repeat(head_rows, sharers, axis=0)
    head_rows = swap_blocks(after(head_rows, ints))

    base = (device_index * vocab_here)[None]
    if packed:
        id_rows, table_low = embed(base, all_ids[:, None], table)
    else:
        table_low = table.astype(low)
        id_hits = (all_ids[:, None] == vocab_ids[None, :]).astype(low)
        id_rows = dot(id_hits, table_low).astype(low)
    if packed:
        (hidden_rows,) = local(
            pack_hidden_kernel,
            16,
            [((data_size, 3 * hidden_here, width_here), low)],
            gate_up_weight,
            down_weight,
            scratch=[pltpu.VMEM((gate_up_weight.shape[2], width_here), jnp.float32)],
        )
    else:
        hidden_rows = jnp.moveaxis(
            gate_up_weight.astype(low).reshape(width_here, 2, data_size, hidden_here), 0, 3
        )
        hidden_rows = jnp.concatenate(
            [
                jnp.moveaxis(hidden_rows, 0, 1).reshape(hidden_shape),
                down_weight.astype(low).reshape(down_shape),
            ],
            axis=1,
        )
    (resid_low,) = relay([after(id_rows, hidden_rows)], lambda p, total, extras: (total.astype(low), (), ()), 1)

    hidden_rows, resid_low = lax.optimization_barrier((hidden_rows, resid_low))
    hidden_rows = swap_blocks(hidden_rows)

    pick_share = lax.dynamic_slice_in_dim(
        lax.dynamic_index_in_dim(pick_low, exit_here, 0, keepdims=False),
        share_here * (data_size // shares),
        data_size // shares,
        0,
    )
    def share_of(rows):
        count = share_slots // 128
        return lax.dynamic_slice_in_dim(rows, (exit_here * shares + share_here) * count, count, 0)

    place_share, live_rows_share = share_of(place_rows), share_of(live_rows)
    if packed:

        def turns(places):
            return jnp.stack([jnp.concatenate([part, part], axis=1) for part in rotary(places, HEAD_DIM)])

        attn_low, query_slots, key_low, value_low, attn_out, turn, slot_turn, out_partial = attend(
            exit_here[None],
            resid_low,
            gain_rows[:1],
            head_rows,
            turns(token_places[:block_rows]),
            turns(token_places[::block_rows]),
            pick_share,
            place_share,
            live_rows_share,
            slots_here,
        )
        out_partial = out_partial.reshape(-1, width)
    else:
        head_rows = jnp.moveaxis(head_rows, 0, 1).reshape(4 * HEAD_DIM, width)
        qkv_head, out_head = head_rows[: 3 * HEAD_DIM], head_rows[3 * HEAD_DIM :]
        cosine, sine_table = rotary(token_places, HEAD_DIM)
        places_share, live_share = place_share.reshape(-1), live_rows_share.reshape(-1)
        cosine_share, sine_share = rotary(places_share, HEAD_DIM)
        attn_low = norm_fwd(resid_low.astype(jnp.float32), gain_rows[0])[0].astype(low)

        projected = dot(attn_low, qkv_head, 1, 1)
        query_low = rotate_pairs(projected[:, :HEAD_DIM], cosine, sine_table).astype(low)
        key_low = rotate_pairs(projected[:, HEAD_DIM : 2 * HEAD_DIM], cosine, sine_table).astype(low)
        value_low = projected[:, 2 * HEAD_DIM :].astype(low)
        query_share = lax.dynamic_slice_in_dim(
            query_low.reshape(data_size, block_rows, HEAD_DIM),
            share_here * (data_size // shares),
            data_size // shares,
            0,
        )
        query_slots = (
            jnp.einsum("brt,btd->brd", pick_share, query_share, preferred_element_type=jnp.float32)
            .astype(low)
            .reshape(share_slots, HEAD_DIM)
        )

        scores = dot(query_slots, key_low, 1, 1) * score_scale
        allowed = token_places[None, :] <= places_share[:, None]
        scores = jnp.where(allowed, scores, NEG)
        weights = jnp.exp(scores - jnp.max(scores, axis=-1, keepdims=True))
        probs = weights / jnp.sum(weights, axis=-1, keepdims=True)
        probs_low = probs.astype(low)
        attn_out = (dot(probs_low, value_low) * live_share[:, None]).astype(low)

        def spread(per_share):
            if shares > 1:
                full = jnp.zeros((data_size * R_DEV, width), per_share.dtype)
                per_share = lax.dynamic_update_slice_in_dim(
                    full, per_share, share_here * share_slots, 0
                )
            exits = jnp.arange(2, dtype=jnp.int32)[None, :, None, None]
            rows = per_share.reshape(devices, 1, slots_here, width)
            return jnp.where(exits == exit_here, rows, 0).reshape(-1, width)
        out_partial = spread(dot(attn_out, out_head).astype(low))

    block_low = lax.dynamic_slice_in_dim(resid_low, data_index * block_rows, block_rows, 0)
    pick_here = lax.dynamic_slice(
        pick_low,
        (0, data_index, model_index * slots_here, 0),
        (2, 1, slots_here, block_rows),
    ).reshape(2 * slots_here, block_rows)

    def first_step(p, total, extras):
        resid = extras[0][p * GROUP : (p + 1) * GROUP] + total
        gain = 2 if p == 0 else 1
        return (norm_fwd(resid, extras[1][gain : gain + 1])[0].astype(low), (resid,), ())

    exit_rows_one, mlp_low, resid_one = relay(
        [out_partial],
        first_step,
        2,
        extras=[dot(pick_here, block_low), gain_rows],
        kept=1,
        split=True,
    )

    slots = mlp_low.shape[0]
    if packed:
        gate_part, up_part, hidden_low, mlp_partial = local(
            hidden_kernel,
            20,
            [
                ((slots, hidden_here), jnp.float32),
                ((slots, hidden_here), jnp.float32),
                ((slots, hidden_here), low),
                ((slots, width), low),
            ],
            mlp_low,
            hidden_rows,
        )
    else:
        hidden_rows = jnp.moveaxis(hidden_rows, 0, 1).reshape(3 * hidden_here, width)
        gate_up_head, down_head = hidden_rows[: 2 * hidden_here], hidden_rows[2 * hidden_here :]
        gate_up = dot(mlp_low, gate_up_head, 1, 1)
        gate_part, up_part = gate_up[:, :hidden_here], gate_up[:, hidden_here:]
        gate_sigma = jax.nn.sigmoid(gate_part)
        hidden_low = (gate_part * gate_sigma * up_part).astype(low)
        mlp_partial = dot(hidden_low, down_head).astype(low)

    def second_step(p, total, extras):
        resid = extras[0][GROUP : 2 * GROUP] + total
        return (norm_fwd(resid, extras[1][2:3])[0].astype(low), (resid,), ())

    exit_rows_two, resid_two = relay(
        [mlp_partial], second_step, 3, extras=[resid_one, gain_rows], kept=1
    )

    exit_rows = (exit_rows_one, exit_rows_two)
    if packed:
        entry_row = vocab_ids[None]
        logits, stats = local(
            logits_kernel,
            28,
            [((2 * slots, vocab_here), jnp.float32), ((3 * 2 * slots // 128, 128), jnp.float32)],
            *exit_rows,
            table_low,
            target_rows,
            entry_row,
        )
    else:
        logits = [dot(rows, table_low, 1, 1) for rows in exit_rows]
        hits = [slot_targets[e][:, None] == vocab_ids[None, :] for e in range(2)]
        tops = [jnp.max(values, axis=1) for values in logits]
        masses = [
            jnp.sum(jnp.exp(values - top[:, None]), axis=1) for values, top in zip(logits, tops)
        ]
        found = [jnp.sum(jnp.where(hit, values, 0.0), axis=1) for hit, values in zip(hits, logits)]
        stats = jnp.concatenate(tops + masses + found).reshape(-1, 128)
    part = stats.shape[0] // 3

    def joined(stats):
        tops, masses, found = (stats[:, k * part : (k + 1) * part] for k in range(3))
        top = jnp.max(tops, axis=0)
        lse = top + jnp.log(jnp.sum(masses * jnp.exp(tops - top), axis=0))
        return jnp.concatenate([lse, lse - jnp.sum(found, axis=0)])

    joint = gather_small(stats, joined, (2 * part, 128), 4)
    row_lse, entropy = joint[:part].reshape(2, -1), joint[part:].reshape(2, -1)
    loss_sums = jnp.sum(entropy * live, axis=1)
    if packed:
        *grad_logits, one_terms, two_terms = local(
            head_grad_kernel,
            28,
            [((slots, vocab_here), low)] * 2 + [((slots, width), low)] * 2,
            logits,
            joint[:part],
            weight_rows,
            target_rows,
            entry_row,
            table_low,
        )
        row_terms = [one_terms, two_terms]
    else:
        grad_logits = [
            (
                row_weight[e][:, None]
                * (jnp.exp(logits[e] - row_lse[e][:, None]) - hits[e].astype(jnp.float32))
            ).astype(low)
            for e in range(2)
        ]
        row_terms = [dot(grad, table_low).astype(low) for grad in grad_logits]

    def head_step(p, total, extras):
        values = extras[0][:GROUP] if p == 0 else extras[1][...]
        gain = extras[2][2:3]
        _, unit, scale = norm_fwd(values, gain)
        back, gain_grad = norm_back(unit, scale, gain, total)
        return (None if p == 0 else back.astype(low), (back,), (gain_grad[None],))

    dtwo_low, dexits, final_grad = relay(
        row_terms,
        head_step,
        5,
        extras=[resid_one, resid_two, gain_rows],
        kept=1,
        sums=1,
        order=[1, 0],
        slot=lambda p: None if p == 0 else 0,
    )
    if packed:
        dmlp_partial, hidden_parts, down_parts = local(
            hidden_back_kernel,
            28,
            [((slots, width), low), (hidden_shape, low), (down_shape, low)],
            dtwo_low,
            mlp_low,
            hidden_rows,
            gate_part,
            up_part,
            hidden_low,
        )
    else:
        down_local = dot(hidden_low, dtwo_low, 0, 0)
        dhidden = dot(dtwo_low, down_head, 1, 1)
        dgate = dhidden * up_part * gate_sigma * (1.0 + gate_part * (1.0 - gate_sigma))
        dup_part = dhidden * gate_part * gate_sigma
        dgate_up = jnp.concatenate([dgate, dup_part], axis=1).astype(low)
        gate_up_local = dot(dgate_up, mlp_low, 0, 0)
        dmlp_partial = dot(dgate_up, gate_up_head).astype(low)
        hidden_parts, down_parts = (
            jnp.moveaxis(value.astype(low).reshape(-1, data_size, width_here), 1, 0)
            for value in (gate_up_local, down_local)
        )

    def mlp_step(p, total, extras):
        gain = extras[2][1:2]
        _, unit, scale = norm_fwd(extras[0][GROUP : 2 * GROUP], gain)
        back, gain_grad = norm_back(unit, scale, gain, total)
        return ((extras[1][GROUP : 2 * GROUP] + back).astype(low), (), (gain_grad[None],))

    done_low, mlp_grad, down_parts = relay(
        [dmlp_partial],
        mlp_step,
        6,
        extras=[resid_one, dexits, gain_rows],
        sums=1,
        slot=lambda p: 1,
        ready=dexits[:GROUP].astype(low),
        cargo=down_parts,
    )
    hidden_parts, done_low = lax.optimization_barrier((hidden_parts, done_low))
    hidden_parts = swap_blocks(hidden_parts)
    done_low = done_low.reshape(devices, 2, slots_here, width)

    if kernel_mesh():
        zero_partial, head_parts = attend_back(
            exit_here[None],
            done_low,
            head_rows,
            attn_out,
            query_slots,
            key_low,
            value_low,
            turn,
            slot_turn,
            pick_share,
            place_share,
            attn_low,
        )
    else:
        done_share = lax.dynamic_slice(
            lax.dynamic_index_in_dim(done_low, exit_here, 1, keepdims=False).reshape(-1, width),
            (share_here * share_slots, 0),
            (share_slots, width),
        )
        out_local = dot(attn_out, done_share, 0, 0)
        dattn_low = dot(done_share, out_head, 1, 1).astype(low)
        dprobs = dot(dattn_low, value_low, 1, 1)
        delta = jnp.sum(probs * dprobs, axis=-1, keepdims=True)
        dscores = (probs * (dprobs - delta)).astype(low)
        dquery = rotate_pairs(dot(dscores, key_low) * score_scale, cosine_share, -sine_share).astype(
            low
        )
        dquery_share = jnp.einsum(
            "brt,brd->btd",
            pick_share,
            dquery.reshape(-1, R_DEV, HEAD_DIM),
            preferred_element_type=jnp.float32,
        ).astype(low)
        if shares > 1:
            dquery_share = lax.dynamic_update_slice_in_dim(
                jnp.zeros((data_size, block_rows, HEAD_DIM), low),
                dquery_share,
                share_here * (data_size // shares),
                0,
            )
        dkey = rotate_pairs(dot(dscores, query_slots, 0, 0) * score_scale, cosine, -sine_table)
        dvalue = dot(probs_low, dattn_low, 0, 0)
        dprojected = jnp.concatenate(
            [dquery_share.reshape(tokens, HEAD_DIM), dkey.astype(low), dvalue.astype(low)], axis=1
        )
        head_parts = jnp.concatenate([dot(dprojected, attn_low, 0, 0).astype(low), out_local.astype(low)])
        zero_partial = dot(dprojected, qkv_head).astype(low)
        head_parts = jnp.moveaxis(head_parts.reshape(-1, data_size, width_here), 1, 0)

    resid_here = lax.dynamic_slice_in_dim(resid_low, device_index * rows_here, rows_here, 0)
    done_block = lax.dynamic_slice_in_dim(done_low, data_index * model_size, model_size, 0)
    pick_block = lax.dynamic_slice(
        pick_low,
        (0, data_index, 0, model_index * rows_here),
        (2, 1, R_DEV, rows_here),
    ).reshape(2, model_size, slots_here, rows_here)
    dresid_here = jnp.einsum(
        "emst,mesd->td", pick_block, done_block, preferred_element_type=jnp.float32
    )

    def zero_step(p, total, extras):
        at = slice(p * GROUP, (p + 1) * GROUP)
        gain = extras[2][:1]
        _, unit, scale = norm_fwd(extras[0][at], gain)
        back, gain_grad = norm_back(unit, scale, gain, total)
        return ((extras[1][at] + back).astype(low), (), (gain_grad[None],))

    ride = 2 * HEAD_DIM
    dzero_low, attn_grad, ridden = relay(
        [after(zero_partial, hidden_parts)],
        zero_step,
        7,
        extras=[resid_here.astype(jnp.float32), dresid_here, gain_rows],
        sums=1,
        cargo=head_parts[:, :ride],
    )
    later, dzero_low = lax.optimization_barrier((head_parts[:, ride:], dzero_low))
    later = swap_blocks(later)
    if packed:
        table_grad, squares = table_gradient(
            base, all_ids[None, :], grad_logits, exit_rows, dzero_low
        )
        squares = jnp.sum(squares)
    else:
        table_grad = dot(id_hits, dzero_low, 0, 0)
        for grad, rows in zip(grad_logits, exit_rows):
            table_grad = table_grad + dot(grad, rows, 0, 0)
        squares = jnp.sum(table_grad * table_grad)

    square_shape = ((1, width_here), jnp.float32)
    if packed:
        qkv_grad, out_grad, head_squares = local(
            unpack_head_kernel,
            12,
            [
                ((3, width_here, qkv_weight.shape[2]), jnp.float32),
                (out_weight.shape, jnp.float32),
                square_shape,
            ],
            ridden,
            later,
        )
        gate_up_grad, down_grad, hidden_squares = local(
            unpack_hidden_kernel,
            20,
            [
                (gate_up_weight.shape, jnp.float32),
                (down_weight.shape, jnp.float32),
                square_shape,
            ],
            hidden_parts,
            down_parts,
            scratch=[pltpu.VMEM((gate_up_weight.shape[2], width_here), jnp.float32)],
        )
        qkv_grad = jnp.transpose(qkv_grad, (1, 0, 2))
        squares = squares + jnp.sum(head_squares) + jnp.sum(hidden_squares)
    else:
        head_grad = jnp.sum(
            jnp.concatenate([ridden, later], axis=1).reshape(heads_here, sharers, 4, HEAD_DIM, width_here).astype(jnp.float32),
            axis=1,
        )
        qkv_grad = jnp.transpose(head_grad[:, :3], (3, 1, 0, 2)).reshape(qkv_weight.shape)
        out_grad = head_grad[:, 3].reshape(out_weight.shape)
        hidden_parts = hidden_parts.astype(jnp.float32)
        gate_up_grad = hidden_parts.reshape(data_size, 2, hidden_here, width_here)
        gate_up_grad = jnp.transpose(gate_up_grad, (3, 1, 0, 2)).reshape(gate_up_weight.shape)
        down_grad = down_parts.reshape(down_weight.shape).astype(jnp.float32)
        squares = (
            squares
            + jnp.sum(qkv_grad * qkv_grad)
            + jnp.sum(out_grad * out_grad)
            + jnp.sum(gate_up_grad * gate_up_grad)
            + jnp.sum(down_grad * down_grad)
        )
    parts = jnp.concatenate(
        [
            jnp.concatenate([attn_grad, mlp_grad, final_grad]).reshape(-1, 128),
            jnp.full((8, 128), squares),
        ]
    )
    parts = sum_small(parts, 8)
    gain_sums = parts[:-8].reshape(3, width)
    gain_grad = lax.dynamic_slice_in_dim(gain_sums, data_index * width_here, width_here, 1)
    grad_norm = jnp.sqrt(parts[-1, 0] + jnp.sum(gain_sums * gain_sums))
    factor = jnp.minimum(1.0, CLIP / (grad_norm + 1e-06))
    table_new, qkv_new, out_new, gate_up_new, down_new = (
        adam_update(weight, first, second, grad * factor, RATE_MATRIX, DECAY)
        for weight, first, second, grad in (
            (table, table_first, table_second, table_grad),
            (qkv_weight, qkv_first, qkv_second, qkv_grad),
            (out_weight, out_first, out_second, out_grad),
            (gate_up_weight, gate_up_first, gate_up_second, gate_up_grad),
            (down_weight, down_first, down_second, down_grad),
        )
    )
    gains_new = adam_update(gains, gains_first, gains_second, gain_grad * factor, RATE_GAIN, 0.0)
    return (
        loss_sums,
        counts,
        grad_norm,
        *table_new,
        *qkv_new,
        *out_new,
        *gate_up_new,
        *down_new,
        *gains_new,
    )


def solution(mesh):
    rows, sides, cols, gain = P(BOTH, None), P("dp", None, "mp"), P("mp", "dp"), P(None, "dp")
    state = (rows,) * 3 + (sides,) * 3 + (cols,) * 3 + (sides,) * 3 + (cols,) * 3 + (gain,) * 3
    return jax.shard_map(
        body,
        mesh=mesh,
        in_specs=(P("dp"), P("dp"), P(None, "dp")) + state,
        out_specs=(P(), P(), P()) + state,
        check_vma=False,
    )
```

```python
import functools
import math

import jax
import jax.numpy as jnp
from jax import lax
from jax.experimental import pallas as pl
from jax.experimental.pallas import tpu as pltpu
from jax.sharding import PartitionSpec as P

HEAD_DIM = 128
R_DEV = 64
STEP = 10


EPS_NORM = 1e-05
BETA_ONE = 0.9
BETA_TWO = 0.95
ADAM_EPS = 1e-08
DECAY = 0.1
RATE_MATRIX = 0.02
RATE_GAIN = 1.0
CLIP = 0.02
EXIT_SCALE = (1.0 / 3.0, 2.0 / 3.0)
NEG = -1e30
BOTH = ("dp", "mp")
MESH = pl.DeviceIdType.MESH
MIB = 1024 * 1024
ANY = pl.BlockSpec(memory_space=pl.ANY)
GROUP = 16
CARGO_EARLY = 4
CARGO_LATE = 2


def kernel_mesh():
    return lax.axis_size("dp") == 8 and lax.axis_size("mp") == 4


def comm_params(ident, room):
    return pltpu.CompilerParams(
        collective_id=ident, has_side_effects=True, vmem_limit_bytes=room * MIB
    )


class Links:
    def __init__(self, send_sem, recv_sem, cargo=False):
        data_index, model_index = lax.axis_index("dp"), lax.axis_index("mp")
        z, y, x, c = data_index // 2, data_index % 2, model_index // 2, model_index % 2
        self.c = c
        self.zs = (z, z + 1 - 2 * (z % 2), (z + 2) % 4, 3 - z)
        self.corners = ((y, x), (y, 1 - x), (1 - y, x), (1 - y, 1 - x))
        self.z_side = [(zd * 2 + y, model_index) for zd in self.zs]
        self.x_side = (data_index, (1 - x) * 2 + c)
        self.y_side = (z * 2 + 1 - y, model_index)
        self.c_side = (data_index, x * 2 + 1 - c)
        self.send_sem, self.recv_sem, self.sent, self.slots = send_sem, recv_sem, [], {}
        peers = self.z_side[1:] + [self.x_side, self.y_side, self.c_side]
        if cargo:
            peers += [(zd * 2 + 1 - y, model_index) for zd in self.zs[1:]]
        barrier = pltpu.get_barrier_semaphore()
        for peer in peers:
            pl.semaphore_signal(barrier, inc=1, device_id=peer, device_id_type=MESH)
        pl.semaphore_wait(barrier, len(peers))

    def first_row(self, rows, d, group, core=0):
        y, x = self.corners[group]
        c = 1 - self.c if core else self.c
        return ((self.zs[d] * 2 + y) * 4 + x * 2 + c) * rows

    def recv(self, name):
        return self.recv_sem.at[self.slots.setdefault(name, len(self.slots))]

    def send(self, source, target, device, name):
        copy = pltpu.make_async_remote_copy(
            src_ref=source,
            dst_ref=target,
            send_sem=self.send_sem.at[len(self.sent)],
            recv_sem=self.recv(name),
            device_id=device,
            device_id_type=MESH,
        )
        copy.start()
        self.sent.append(copy)

    def arrived(self, ref, name):
        pltpu.make_async_copy(ref, ref, self.recv(name)).wait()
        return ref

    def finish(self):
        for copy in self.sent:
            copy.wait_send()


def cargo_cuts(shape):
    return 2 if shape[1] % 32 == 0 else 1


class Cargo:
    def __init__(self, source, target, send_sem, recv_sem, own_sem):
        self.me, self.model_index = lax.axis_index("dp"), lax.axis_index("mp")
        self.source, self.target = source, target
        self.send_sem, self.recv_sem, self.sent = send_sem, recv_sem, []
        self.own = pltpu.make_async_copy(source.at[self.me], target.at[self.me], own_sem)
        self.own.start()
        count = cargo_cuts(source.shape)
        size = source.shape[1] // count
        cuts = [pl.ds(cut * size, size) for cut in range(count)]
        self.cuts = [(shift, cut) for cut in cuts for shift in (4, 3, 5, 2, 6, 1, 7)]

    def load(self, count):
        for _ in range(count):
            index = len(self.sent)
            if index == len(self.cuts):
                return
            shift, cut = self.cuts[index]
            peer = lax.rem(self.me + shift, 8)
            copy = pltpu.make_async_remote_copy(
                src_ref=self.source.at[peer, cut],
                dst_ref=self.target.at[self.me, cut],
                send_sem=self.send_sem.at[index],
                recv_sem=self.recv_sem.at[index],
                device_id=(peer, self.model_index),
                device_id_type=MESH,
            )
            copy.start()
            self.sent.append(copy)

    def finish(self):
        self.load(len(self.cuts))
        self.own.wait()
        for index, (shift, cut) in enumerate(self.cuts):
            here = self.target.at[lax.rem(self.me + 8 - shift, 8), cut]
            pltpu.make_async_copy(here, here, self.recv_sem.at[index]).wait()
        for copy in self.sent:
            copy.wait_send()


class Gather:
    def __init__(self, link, outs, steps, own_sem):
        self.link, self.outs, self.steps, self.own_sem = link, outs, steps, own_sem
        self.owns = []

    def spot(self, g, d, group, core=0):
        if len(self.outs) > 1:
            out, start = self.outs[g], self.link.first_row(GROUP, d, group, core)
        else:
            out, start = self.outs[0], self.link.first_row(self.steps * GROUP, d, group, core)
            start = start + g * GROUP
        return out.at[pl.ds(pl.multiple_of(start, GROUP), GROUP)]

    def send(self, g, source, device, here, there):
        self.link.send(source, self.spot(g, *here), device, ("gather", g, *there))

    def arrived(self, g, d, group, core):
        return self.link.arrived(self.spot(g, d, group, core), ("gather", g, d, group, core))

    def begin(self, g, source):
        link = self.link
        own = pltpu.make_async_copy(source, self.spot(g, 0, 0), self.own_sem.at[g])
        own.start()
        self.owns.append(own)
        for d in (1, 2, 3):
            self.send(g, source, link.z_side[d], (0, 0), (d, 0, 0))
        self.send(g, source, link.x_side, (0, 0), (0, 1, 0))
        self.send(g, source, link.y_side, (0, 0), (0, 2, 0))
        self.send(g, source, link.c_side, (0, 0), (0, 0, 1))

    def from_z(self, g, d):
        here = self.arrived(g, d, 0, 0)
        self.send(g, here, self.link.x_side, (d, 0), (d, 1, 0))
        self.send(g, here, self.link.y_side, (d, 0), (d, 2, 0))
        self.send(g, here, self.link.c_side, (d, 0), (d, 0, 1))

    def from_sides(self, g, d):
        for group, side in ((1, self.link.y_side), (2, self.link.x_side)):
            here = self.arrived(g, d, group, 0)
            if (d % 2 == 0) == (group == 1):
                self.send(g, here, side, (d, group), (d, 3, 0))
            self.send(g, here, self.link.c_side, (d, group), (d, group, 1))

    def first(self, g):
        self.from_z(g, 1)
        self.from_sides(g, 0)
        self.from_z(g, 2)
        self.from_z(g, 3)

    def second(self, g):
        for d in (1, 2, 3):
            self.from_sides(g, d)

    def third(self, g):
        for d in range(4):
            here = self.arrived(g, d, 3, 0)
            self.send(g, here, self.link.c_side, (d, 3), (d, 3, 1))

    def finish(self):
        for g in range(self.steps):
            for d in range(4):
                for group in range(4):
                    self.arrived(g, d, group, 1)
        for own in self.owns:
            own.wait()


CORNER = [(d, 3) for d in range(4)]
SIDES = [(1, 1), (3, 1), (0, 2), (2, 2), (0, 1), (2, 1), (1, 2), (3, 2)]
COLUMN = [(d, 0) for d in (3, 2, 1)]


class Scatter:
    def __init__(self, link, partials, rows, order, buffers, own_sem):
        self.link, self.partials, self.rows = link, partials, rows
        self.mine, self.core, self.corner, self.side, self.column = buffers
        self.owns = {}
        for p in order:
            for d, group in CORNER + SIDES + COLUMN + [(0, 0)]:
                k = d * 4 + group
                here = self.mine.at[k, pl.ds(p * GROUP, GROUP)]
                own = pltpu.make_async_copy(self.spot(p, d, group), here, own_sem.at[p * 16 + k])
                own.start()
                self.owns[p, k] = own
                self.send(p, self.spot(p, d, group, 1), self.core, k, link.c_side, "core")

    def spot(self, p, d, group, core=0):
        if len(self.partials) > 1:
            partial, start = self.partials[p], self.link.first_row(GROUP, d, group, core)
        else:
            partial, start = self.partials[0], self.link.first_row(self.rows, d, group, core)
            start = start + p * GROUP
        return partial.at[pl.ds(pl.multiple_of(start, GROUP), GROUP)]

    def send(self, p, source, buffer, k, device, name):
        self.link.send(source, buffer.at[k, pl.ds(p * GROUP, GROUP)], device, (name, p, k))

    def term(self, p, buffer, k, name):
        return self.link.arrived(buffer.at[k, pl.ds(p * GROUP, GROUP)], (name, p, k))[...].astype(
            jnp.float32
        )

    def start_terms(self, p, k):
        self.owns[p, k].wait()
        own = self.mine[k, pl.ds(p * GROUP, GROUP)].astype(jnp.float32)
        return own + self.term(p, self.core, k, "core")

    def pass_on(self, p, k, total, buffer, there, device, name):
        here = self.mine.at[k, pl.ds(p * GROUP, GROUP)]
        here[...] = total.astype(here.dtype)
        self.send(p, here, buffer, there, device, name)

    def to_corner(self, p):
        for d, _ in CORNER:
            side = self.link.y_side if d % 2 == 0 else self.link.x_side
            k = d * 4 + 3
            self.pass_on(p, k, self.start_terms(p, k), self.corner, d, side, "corner")

    def to_sides(self, p):
        for d, group in SIDES:
            k = d * 4 + group
            total = self.start_terms(p, k)
            if (d % 2 == 0) == (group == 1):
                total = total + self.term(p, self.corner, d, "corner")
            side = self.link.x_side if group == 1 else self.link.y_side
            self.pass_on(p, k, total, self.side, d * 2 + group - 1, side, "side")

    def column_terms(self, p, d):
        total = self.start_terms(p, d * 4)
        for k in (d * 2, d * 2 + 1):
            total = total + self.term(p, self.side, k, "side")
        return total

    def to_column(self, p):
        for d, _ in COLUMN:
            total = self.column_terms(p, d)
            self.pass_on(p, d * 4, total, self.column, d - 1, self.link.z_side[d], "column")

    def total(self, p):
        total = self.column_terms(p, 0)
        for d in (1, 2, 3):
            total = total + self.term(p, self.column, d - 1, "column")
        return total


def relay_kernel(plan, row_step, *refs):
    refs = list(refs)

    def take(count):
        taken = refs[:count]
        del refs[:count]
        return taken

    partials = take(plan["partials"])
    ready = take(plan["ready"])
    extras = take(plan["extras"])
    cargo_in = take(plan["cargo"])
    gathered = take(plan["outs"])
    kept = take(plan["kept"])
    sums = take(plan["sums"])
    cargo_out = take(plan["cargo"])
    buffers = take(5)
    held, send_sem, recv_sem, load_sem, own_sem = take(5)
    order, steps = plan["order"], plan["steps"]
    link = Links(send_sem, recv_sem, plan["cargo"])
    gather = Gather(link, gathered, steps, own_sem)
    if ready:
        gather.begin(0, ready[0])
    scatter = Scatter(link, partials, plan["rows"], order, buffers, load_sem)
    cargo = Cargo(*cargo_in, *cargo_out, *refs) if cargo_in else None
    ticks = len(order) + 7
    agenda = [[] for _ in range(ticks)]
    if ready:
        for tick, step in enumerate((gather.first, gather.second, gather.third)):
            agenda[tick + 2].append((step, 0))

    def last(p):
        rows, keeps, adds = row_step(p, scatter.total(p), extras)
        for ref, value in zip(kept, keeps):
            ref[pl.ds(p * GROUP, GROUP)] = value
        for ref, value in zip(sums, adds):
            ref[...] = value if p == order[0] else ref[...] + value
        if rows is not None:
            g = plan["slot"](p)
            held[g] = rows
            gather.begin(g, held.at[g])

    for q, p in enumerate(order):
        for tick, step in enumerate(
            (scatter.to_corner, scatter.to_sides, scatter.to_column, last)
        ):
            agenda[q + tick].append((step, p))
        if plan["slot"](p) is not None:
            for tick, step in enumerate((gather.first, gather.second, gather.third)):
                agenda[q + 4 + tick].append((step, plan["slot"](p)))
    for number, tick in enumerate(agenda):
        if cargo:
            cargo.load(CARGO_EARLY if number < 4 else CARGO_LATE)
        for step, index in tick:
            step(index)
    gather.finish()
    link.finish()
    if cargo:
        cargo.finish()


def wide_sum(value):
    pieces = jnp.moveaxis(value.reshape(value.shape[0], 4, -1), 1, 0)
    sums = lax.map(
        lambda piece: lax.psum_scatter(
            piece.astype(jnp.float32), BOTH, scatter_dimension=0, tiled=True
        ),
        pieces,
    )
    return jnp.moveaxis(sums, 0, 1).reshape(sums.shape[1], -1)


def relay(
    partials,
    row_step,
    ident,
    extras=(),
    kept=0,
    sums=0,
    order=None,
    slot=None,
    ready=None,
    split=False,
    cargo=None,
):
    devices, width = lax.axis_size("dp") * lax.axis_size("mp"), partials[0].shape[1]
    rows = sum(partial.shape[0] for partial in partials) // devices
    groups = rows // GROUP
    order = list(range(groups)) if order is None else order
    slot = slot or (lambda p: p)
    steps = sum(slot(p) is not None for p in order) + (ready is not None)
    if not kernel_mesh():
        total = jnp.concatenate(
            [wide_sum(part) for part in partials]
        )
        outs, keeps, adds = [None] * steps, [None] * groups, [0.0] * sums
        if ready is not None:
            outs[0] = ready
        for p in order:
            out, keeps[p], add = row_step(p, total[p * GROUP : (p + 1) * GROUP], extras)
            adds = [one + two for one, two in zip(adds, add)]
            if out is not None:
                outs[slot(p)] = out
        outs = outs if split else [jnp.concatenate(outs)]
        gathered = [lax.all_gather(out, BOTH, axis=0, tiled=True) for out in outs]
        keeps = [jnp.concatenate(parts) for parts in zip(*keeps)]
        moved = [] if cargo is None else [swap_blocks(cargo)]
        return [*gathered, *keeps, *adds, *moved]
    plan = dict(
        partials=len(partials),
        outs=steps if split else 1,
        cargo=int(cargo is not None),
        rows=rows,
        order=order,
        slot=slot,
        steps=steps,
        ready=int(ready is not None),
        extras=len(extras),
        kept=kept,
        sums=sums,
    )
    low = partials[0].dtype
    load = [] if cargo is None else [cargo]
    vmem = pl.BlockSpec(memory_space=pltpu.VMEM)
    copies = 31 * (groups + steps)
    out_rows = [devices * GROUP] * steps if split else [devices * steps * GROUP]
    shapes = [jax.ShapeDtypeStruct((count, width), low) for count in out_rows]
    shapes += [jax.ShapeDtypeStruct((rows, width), jnp.float32)] * kept
    shapes += [jax.ShapeDtypeStruct((1, width), jnp.float32)] * sums
    shapes += [jax.ShapeDtypeStruct(value.shape, value.dtype) for value in load]
    buffers = [pltpu.VMEM((count, rows, width), low) for count in (16, 16, 4, 8, 3)]
    semaphores = [pltpu.SemaphoreType.DMA((count,)) for count in (copies, copies, 16 * groups, steps)]
    if load:
        semaphores += [pltpu.SemaphoreType.DMA((7 * cargo_cuts(cargo.shape),))] * 2
        semaphores += [pltpu.SemaphoreType.DMA]
    return pl.pallas_call(
        functools.partial(relay_kernel, plan, row_step),
        out_shape=shapes,
        in_specs=[ANY] * (len(partials) + plan["ready"])
        + [vmem] * len(extras)
        + [ANY] * len(load),
        out_specs=[ANY] * len(out_rows) + [vmem] * (kept + sums) + [ANY] * len(load),
        scratch_shapes=buffers + [pltpu.VMEM((steps, GROUP, width), low)] + semaphores,
        compiler_params=comm_params(ident, 60 if rows > 32 else 6 + rows // 4),
        cost_estimate=pl.CostEstimate(flops=1, bytes_accessed=1, transcendentals=0),
    )(*partials, *([] if ready is None else [ready]), *extras, *load)


def after(value, *first):
    return lax.optimization_barrier((value, *first))[0]


def swap_blocks(value):
    return lax.all_to_all(value, "dp", split_axis=0, concat_axis=0, tiled=True)


def small_gather_kernel(then, x_ref, result_ref, o_ref, send_sem, recv_sem, own_sem):
    data_index, model_index = lax.axis_index("dp"), lax.axis_index("mp")
    me = data_index * 4 + model_index
    own = pltpu.make_async_copy(x_ref, o_ref.at[me], own_sem)
    own.start()
    peers = [lax.rem(me + shift, 32) for shift in range(1, 32)]
    barrier = pltpu.get_barrier_semaphore()
    for peer in peers:
        pl.semaphore_signal(
            barrier, inc=1, device_id=(peer // 4, peer % 4), device_id_type=MESH
        )
    pl.semaphore_wait(barrier, 31)
    sent = []
    for index, peer in enumerate(peers):
        copy = pltpu.make_async_remote_copy(
            src_ref=x_ref,
            dst_ref=o_ref.at[me],
            send_sem=send_sem.at[index],
            recv_sem=recv_sem.at[index],
            device_id=(peer // 4, peer % 4),
            device_id_type=MESH,
        )
        copy.start()
        sent.append(copy)
    for index in range(31):
        here = o_ref.at[lax.rem(me + 31 - index, 32)]
        pltpu.make_async_copy(here, here, recv_sem.at[index]).wait()
    own.wait()
    result_ref[...] = then(o_ref)
    for copy in sent:
        copy.wait_send()


def gather_small(value, then, shape, ident):
    if not kernel_mesh():
        return then(lax.all_gather(value, BOTH))
    vmem = pl.BlockSpec(memory_space=pltpu.VMEM)
    return pl.pallas_call(
        functools.partial(small_gather_kernel, then),
        out_shape=jax.ShapeDtypeStruct(shape, value.dtype),
        in_specs=[vmem],
        out_specs=vmem,
        scratch_shapes=[
            pltpu.VMEM((32,) + value.shape, value.dtype),
            pltpu.SemaphoreType.DMA((31,)),
            pltpu.SemaphoreType.DMA((31,)),
            pltpu.SemaphoreType.DMA,
        ],
        compiler_params=comm_params(ident, 2),
    )(value)


def greet(peers):
    barrier = pltpu.get_barrier_semaphore()
    for peer in peers:
        pl.semaphore_signal(barrier, inc=1, device_id=peer, device_id_type=MESH)
    pl.semaphore_wait(barrier, len(peers))


def exchange_kernel(count, whole, *refs):
    ins, outs = refs[: len(whole)], refs[len(whole) : 2 * len(whole)]
    send_sem, recv_sem, own_sem = refs[2 * len(whole) :]
    me, model_index = lax.axis_index("dp"), lax.axis_index("mp")
    peers = [lax.rem(me + shift, count) for shift in range(1, count)]
    greet([(peer, model_index) for peer in peers])
    owns, sent = [], []
    for array, keep in enumerate(whole):
        own = pltpu.make_async_copy(
            ins[array] if keep else ins[array].at[me], outs[array].at[me], own_sem.at[array]
        )
        own.start()
        owns.append(own)
        for shift in range(count - 1):
            copy = pltpu.make_async_remote_copy(
                src_ref=ins[array] if keep else ins[array].at[peers[shift]],
                dst_ref=outs[array].at[me],
                send_sem=send_sem.at[array, shift],
                recv_sem=recv_sem.at[array, shift],
                device_id=(peers[shift], model_index),
                device_id_type=MESH,
            )
            copy.start()
            sent.append(copy)
    for own in owns:
        own.wait()
    for array in range(len(whole)):
        for shift in range(count - 1):
            source = lax.rem(me + count - 1 - shift, count)
            here = outs[array].at[source]
            pltpu.make_async_copy(here, here, recv_sem.at[array, shift]).wait()
    for copy in sent:
        copy.wait_send()


def exchange(values, whole, ident):
    count = lax.axis_size("dp")
    if not kernel_mesh():
        return [
            lax.all_gather(value, "dp")
            if keep
            else lax.all_to_all(value, "dp", split_axis=0, concat_axis=0, tiled=True)
            for value, keep in zip(values, whole)
        ]
    shapes = [
        jax.ShapeDtypeStruct(((count,) if keep else ()) + value.shape, value.dtype)
        for value, keep in zip(values, whole)
    ]
    return pl.pallas_call(
        functools.partial(exchange_kernel, count, tuple(whole)),
        out_shape=shapes,
        in_specs=[ANY] * len(values),
        out_specs=[ANY] * len(values),
        scratch_shapes=[
            pltpu.SemaphoreType.DMA((len(values), count - 1)),
            pltpu.SemaphoreType.DMA((len(values), count - 1)),
            pltpu.SemaphoreType.DMA((len(values),)),
        ],
        compiler_params=comm_params(ident, 2),
    )(*values)


def turned(values, cosine, sine_table):
    return values * cosine + pltpu.roll(values, HEAD_DIM // 2, 1) * sine_table


def to_column(row):
    return jnp.broadcast_to(row, (row.shape[1], row.shape[1])).T[:, :1]


def to_row(column):
    return jnp.broadcast_to(column, (column.shape[0], column.shape[0])).T[:1]


def softmax_rows(query, keys, places):
    scores = dot(query, keys, 1, 1) * (1.0 / math.sqrt(HEAD_DIM))
    columns = lax.broadcasted_iota(jnp.int32, scores.shape, 1)
    scores = jnp.where(columns <= places, scores, NEG)
    weights = jnp.exp(scores - jnp.max(scores, axis=-1, keepdims=True))
    return weights / jnp.sum(weights, axis=-1, keepdims=True)


def attend_kernel(
    exit_ref,
    resid_ref,
    gain_ref,
    head_ref,
    inner_ref,
    outer_ref,
    pick_ref,
    place_ref,
    live_ref,
    attn_ref,
    query_ref,
    key_ref,
    value_ref,
    out_ref,
    turn_ref,
    slot_turn_ref,
    partial_ref,
):
    block, blocks = pl.program_id(0), key_ref.shape[0] // resid_ref.shape[0]
    rows, slots = resid_ref.shape[0], pick_ref.shape[1]
    parts, columns = head_ref.shape[0], head_ref.shape[2]
    low = jnp.bfloat16
    attn = norm_fwd(resid_ref[...].astype(jnp.float32), gain_ref[...])[0].astype(low)
    attn_ref[...] = attn
    projected = jnp.zeros((rows, 3 * HEAD_DIM), jnp.float32)
    for part in range(parts):
        piece = attn[:, part * columns : (part + 1) * columns]
        projected = projected + dot(piece, head_ref[part, : 3 * HEAD_DIM], 1, 1)
    inner_cos, inner_sin = inner_ref[0], inner_ref[1]
    outer_cos, outer_sin = outer_ref[0, pl.ds(block, 1)], outer_ref[1, pl.ds(block, 1)]
    sign = jnp.where(lax.broadcasted_iota(jnp.int32, inner_cos.shape, 1) < HEAD_DIM // 2, -1.0, 1.0)
    cosine = inner_cos * outer_cos - inner_sin * outer_sin
    sine_table = (inner_sin * outer_cos + inner_cos * outer_sin) * sign
    at = pl.ds(pl.multiple_of(block * rows, rows), rows)
    turn_ref[0, at], turn_ref[1, at] = cosine, sine_table
    query = turned(projected[:, :HEAD_DIM], cosine, sine_table).astype(low)
    key_ref[at] = turned(projected[:, HEAD_DIM : 2 * HEAD_DIM], cosine, sine_table).astype(low)
    value_ref[at] = projected[:, 2 * HEAD_DIM :].astype(low)
    at = pl.ds(pl.multiple_of(block * slots, slots), slots)
    query_ref[at] = dot(pick_ref[0], query).astype(low)
    pick_wide = pick_ref[0].astype(jnp.float32)
    for index, table in enumerate((cosine, sine_table)):
        slot_turn_ref[index, at] = jnp.dot(
            pick_wide, table, precision=lax.Precision.HIGHEST, preferred_element_type=jnp.float32
        )

    @pl.when(block == blocks - 1)
    def _():
        exit_here = exit_ref[0]
        step = 2 * slots
        for index in range(blocks // 2):
            reach = (index + 1) * 2 * rows
            at = slice(index * step, (index + 1) * step)
            row = slice(index, index + 1)
            places, live = to_column(place_ref[row]), to_column(live_ref[row])
            probs = softmax_rows(query_ref[at], key_ref[:reach], places).astype(low)
            out = (dot(probs, value_ref[:reach]) * live).astype(low)
            out_ref[at] = out
            groups = step // partial_ref.shape[2]
            at = slice(index * groups, (index + 1) * groups)
            for part in range(parts):
                share = dot(out, head_ref[part, 3 * HEAD_DIM :]).astype(low)
                share = share.reshape(groups, 1, -1, columns)
                lanes = slice(part * columns, (part + 1) * columns)
                partial_ref[at, pl.ds(exit_here, 1), :, lanes] = share
                partial_ref[at, pl.ds(1 - exit_here, 1), :, lanes] = jnp.zeros_like(share)


def attend_back_kernel(
    exit_ref,
    done_ref,
    head_ref,
    out_ref,
    query_ref,
    key_ref,
    value_ref,
    turn_ref,
    slot_turn_ref,
    pick_ref,
    place_ref,
    attn_ref,
    partial_ref,
    parts_ref,
    key_sum,
    value_sum,
    turned_ref,
    head_sum,
):
    block, blocks = pl.program_id(0), key_ref.shape[0] // attn_ref.shape[0]
    rows, slots = attn_ref.shape[0], pick_ref.shape[1]
    parts, columns = head_ref.shape[0], head_ref.shape[2]
    low = jnp.bfloat16
    scale = 1.0 / math.sqrt(HEAD_DIM)

    @pl.when(block == 0)
    def _():
        key_sum[...] = jnp.zeros_like(key_sum)
        value_sum[...] = jnp.zeros_like(value_sum)
        step = 2 * slots
        width = done_ref.shape[-1]
        done = done_ref[...].reshape(-1, width)
        dout = jnp.zeros((done.shape[0], HEAD_DIM), jnp.float32)
        for part in range(parts):
            piece = done[:, part * columns : (part + 1) * columns]
            parts_ref[part, 3 * HEAD_DIM :] = dot(out_ref[...], piece, 0, 0).astype(low)
            dout = dout + dot(piece, head_ref[part, 3 * HEAD_DIM :], 1, 1)
        dout = dout.astype(low)
        for index in range(blocks // 2):
            reach = (index + 1) * 2 * rows
            at = slice(index * step, (index + 1) * step)
            places = to_column(place_ref[index : index + 1])
            probs = softmax_rows(query_ref[at], key_ref[:reach], places)
            dprobs = dot(dout[at], value_ref[:reach], 1, 1)
            delta = jnp.sum(probs * dprobs, axis=-1, keepdims=True)
            dscores = (probs * (dprobs - delta)).astype(low)
            dquery = dot(dscores, key_ref[:reach]) * scale
            dquery = turned(dquery, slot_turn_ref[0, at], -slot_turn_ref[1, at]).astype(low)
            for half in (0, 1):
                where = 2 * index + half
                turned_ref[where * rows : (where + 1) * rows, :HEAD_DIM] = dot(
                    pick_ref[where], dquery[half * slots : (half + 1) * slots], 0, 0
                ).astype(low)
            key_sum[:reach] += dot(dscores, query_ref[at], 0, 0)
            value_sum[:reach] += dot(probs.astype(low), dout[at], 0, 0)
        dkey = turned(key_sum[...] * scale, turn_ref[0], -turn_ref[1])
        turned_ref[:, HEAD_DIM : 2 * HEAD_DIM] = dkey.astype(low)
        turned_ref[:, 2 * HEAD_DIM :] = value_sum[...].astype(low)

    at = pl.ds(pl.multiple_of(block * rows, rows), rows)
    dprojected = turned_ref[at]
    for part in range(parts):
        lanes = slice(part * columns, (part + 1) * columns)
        partial_ref[:, lanes] = dot(dprojected, head_ref[part, : 3 * HEAD_DIM]).astype(low)
    term = dot(dprojected, attn_ref[...], 0, 0)

    @pl.when(block == 0)
    def _():
        head_sum[...] = term

    @pl.when(block > 0)
    def _():
        head_sum[...] += term

    @pl.when(block == blocks - 1)
    def _():
        for part in range(parts):
            lanes = slice(part * columns, (part + 1) * columns)
            parts_ref[part, : 3 * HEAD_DIM] = head_sum[:, lanes].astype(low)


def local_params(room):
    return dict(
        compiler_params=pltpu.CompilerParams(vmem_limit_bytes=room * MIB),
        cost_estimate=pl.CostEstimate(flops=1, bytes_accessed=1, transcendentals=0),
    )


def whole_spec(value):
    return pl.BlockSpec(value.shape, lambda b, e: (0,) * len(value.shape))


def attend(exit_here, resid, gain, head, inner, outer, pick, places, live, slots_here):
    (tokens, width), (blocks, slots, rows) = resid.shape, pick.shape
    low = resid.dtype
    devices = blocks * slots // slots_here
    by_block = pl.BlockSpec((rows, width), lambda b, e: (b, 0))
    outs = [
        jax.ShapeDtypeStruct((tokens, width), low),
        jax.ShapeDtypeStruct((blocks * slots, HEAD_DIM), low),
        jax.ShapeDtypeStruct((tokens, HEAD_DIM), low),
        jax.ShapeDtypeStruct((tokens, HEAD_DIM), low),
        jax.ShapeDtypeStruct((blocks * slots, HEAD_DIM), low),
        jax.ShapeDtypeStruct((2, tokens, HEAD_DIM), jnp.float32),
        jax.ShapeDtypeStruct((2, blocks * slots, HEAD_DIM), jnp.float32),
        jax.ShapeDtypeStruct((devices, 2, slots_here, width), low),
    ]
    return pl.pallas_call(
        attend_kernel,
        out_shape=outs,
        grid_spec=pltpu.PrefetchScalarGridSpec(
            num_scalar_prefetch=1,
            grid=(blocks,),
            in_specs=[
                by_block,
                whole_spec(gain),
                whole_spec(head),
                whole_spec(inner),
                whole_spec(outer),
                pl.BlockSpec((1, slots, rows), lambda b, e: (b, 0, 0)),
                whole_spec(places),
                whole_spec(live),
            ],
            out_specs=[by_block] + [whole_spec(out) for out in outs[1:]],
        ),
        **local_params(60),
    )(exit_here, resid, gain, head, inner, outer, pick, places, live)


def attend_back(exit_here, done, head, out, query, key, value, turn, slot_turn, pick, places, attn):
    (tokens, width), (blocks, slots, rows) = attn.shape, pick.shape
    low = attn.dtype
    devices, _, slots_here, _ = done.shape
    by_block = pl.BlockSpec((rows, width), lambda b, e: (b, 0))
    inner = [head, out, query, key, value, turn, slot_turn, pick, places]
    parts = jax.ShapeDtypeStruct(head.shape, low)
    return pl.pallas_call(
        attend_back_kernel,
        out_shape=[jax.ShapeDtypeStruct((tokens, width), low), parts],
        grid_spec=pltpu.PrefetchScalarGridSpec(
            num_scalar_prefetch=1,
            grid=(blocks,),
            in_specs=[
                pl.BlockSpec((devices, 1, slots_here, width), lambda b, e: (0, e[0], 0, 0))
            ]
            + [whole_spec(value) for value in inner]
            + [by_block],
            out_specs=[by_block, whole_spec(parts)],
            scratch_shapes=[
                pltpu.VMEM((tokens, HEAD_DIM), jnp.float32),
                pltpu.VMEM((tokens, HEAD_DIM), jnp.float32),
                pltpu.VMEM((tokens, 3 * HEAD_DIM), low),
                pltpu.VMEM((3 * HEAD_DIM, width), jnp.float32),
            ],
        ),
        **local_params(60),
    )(exit_here, done, *inner, attn)


def local(kernel, room, outs, *values, scratch=()):
    vmem = pl.BlockSpec(memory_space=pltpu.VMEM)
    return pl.pallas_call(
        kernel,
        out_shape=[jax.ShapeDtypeStruct(shape, dtype) for shape, dtype in outs],
        in_specs=[vmem] * len(values),
        out_specs=[vmem] * len(outs),
        scratch_shapes=list(scratch),
        **local_params(room),
    )(*values)


def slots_kernel(ints_ref, pick_ref, place_ref, target_ref, live_ref, weight_ref):
    blocks, _, rows = ints_ref.shape
    slots, lanes = pick_ref.shape[2], place_ref.shape[1]
    low = jnp.bfloat16
    across = lax.broadcasted_iota(jnp.int32, (rows, rows), 1)
    down = lax.broadcasted_iota(jnp.int32, (rows, rows), 0)
    until = jnp.where(down <= across, 1.0, 0.0).astype(low)
    slot = lax.broadcasted_iota(jnp.int32, (slots, rows), 0).astype(jnp.float32)
    kind = lax.broadcasted_iota(jnp.int32, (8, rows), 0)
    inner = lax.broadcasted_iota(jnp.int32, (1, rows), 1).astype(jnp.float32)
    for e in range(2):
        mask = ints_ref[:, 2 + e].astype(jnp.float32)
        ranks = dot(mask.astype(low), until) - 1.0
        for block in range(blocks):
            at = slice(block, block + 1)
            pick = jnp.where((ranks[at] == slot) & (mask[at] == 1.0), 1.0, 0.0).astype(low)
            pick_ref[e, block] = pick
            target = ints_ref[block, 1:2]
            high = (target >> 8).astype(jnp.float32)
            rest = (target & 255).astype(jnp.float32)
            facts = jnp.where(kind == 0, inner, jnp.where(kind == 1, high, rest))
            facts = jnp.where(kind == 3, 1.0, facts).astype(low)
            found = dot(facts, pick, 1, 1)
            live = found[3:4]
            row = slice((e * blocks + block) * slots // lanes, (e * blocks + block) * slots // lanes + 1)
            lane = slice(block * slots % lanes, block * slots % lanes + slots)
            place = found[0:1] + live * float(block * rows)
            place_ref[row, lane] = place.astype(jnp.int32)
            target_ref[row, lane] = (found[1:2] * 256.0 + found[2:3]).astype(jnp.int32)
            live_ref[row, lane] = live
        half = slice(e * blocks * slots // lanes, (e + 1) * blocks * slots // lanes)
        live = live_ref[half]
        weight_ref[half] = live * (EXIT_SCALE[e] / jnp.sum(live, keepdims=True))


def pack_head_kernel(qkv_ref, out_ref, packed_ref):
    heads = out_ref.shape[0] // HEAD_DIM
    sharers = packed_ref.shape[0] // heads
    low = packed_ref.dtype
    for head in range(heads):
        lanes = slice(head * HEAD_DIM, (head + 1) * HEAD_DIM)
        for c in range(4):
            block = out_ref[lanes] if c == 3 else qkv_ref[c, :, lanes].T
            for sharer in range(sharers):
                packed_ref[head * sharers + sharer, c * HEAD_DIM : (c + 1) * HEAD_DIM] = block.astype(
                    low
                )


def pack_hidden_kernel(gate_up_ref, down_ref, packed_ref, turned_ref):
    parts, hidden = packed_ref.shape[0], packed_ref.shape[1] // 3
    low = packed_ref.dtype
    for c in range(2):
        for start in range(0, gate_up_ref.shape[2], 128):
            lanes = slice(start, start + 128)
            turned_ref[lanes] = gate_up_ref[:, c, lanes].T
        for part in range(parts):
            packed_ref[part, c * hidden : (c + 1) * hidden] = turned_ref[
                part * hidden : (part + 1) * hidden
            ].astype(low)
    for part in range(parts):
        packed_ref[part, 2 * hidden :] = down_ref[part * hidden : (part + 1) * hidden].astype(low)


def square_row(value):
    return jnp.sum(value * value, axis=0, keepdims=True)


def unpack_head_kernel(one_ref, two_ref, qkv_ref, out_ref, square_ref):
    heads = out_ref.shape[0] // HEAD_DIM
    sharers = one_ref.shape[0] // heads
    squares = jnp.zeros(square_ref.shape, jnp.float32)
    for head in range(heads):
        lanes = slice(head * HEAD_DIM, (head + 1) * HEAD_DIM)
        for c in range(4):
            parts_ref = one_ref if c < 2 else two_ref
            rows = slice(c % 2 * HEAD_DIM, (c % 2 + 1) * HEAD_DIM)
            total = parts_ref[head * sharers, rows].astype(jnp.float32)
            for sharer in range(1, sharers):
                total = total + parts_ref[head * sharers + sharer, rows].astype(jnp.float32)
            squares = squares + square_row(total)
            if c == 3:
                out_ref[lanes] = total
            else:
                qkv_ref[c, :, lanes] = total.T
    square_ref[...] = squares


def unpack_hidden_kernel(parts_ref, down_parts_ref, gate_up_ref, down_ref, square_ref, turned_ref):
    parts, hidden = down_parts_ref.shape[:2]
    squares = jnp.zeros(square_ref.shape, jnp.float32)
    for c in range(3):
        target = down_ref if c == 2 else turned_ref
        for part in range(parts):
            block = down_parts_ref[part] if c == 2 else parts_ref[part, c * hidden : (c + 1) * hidden]
            block = block.astype(jnp.float32)
            squares = squares + square_row(block)
            target[part * hidden : (part + 1) * hidden] = block
        if c < 2:
            for start in range(0, gate_up_ref.shape[2], 128):
                lanes = slice(start, start + 128)
                gate_up_ref[:, c, lanes] = turned_ref[lanes].T
    square_ref[...] = squares


def hidden_kernel(rows_ref, weight_ref, gate_ref, up_ref, hidden_ref, partial_ref):
    parts, columns = weight_ref.shape[0], weight_ref.shape[2]
    hidden = weight_ref.shape[1] // 3
    low = jnp.bfloat16
    gate = jnp.zeros(gate_ref.shape, jnp.float32)
    up = jnp.zeros(gate_ref.shape, jnp.float32)
    for part in range(parts):
        piece = rows_ref[:, part * columns : (part + 1) * columns]
        gate = gate + dot(piece, weight_ref[part, :hidden], 1, 1)
        up = up + dot(piece, weight_ref[part, hidden : 2 * hidden], 1, 1)
    gate_ref[...], up_ref[...] = gate, up
    value = (gate * jax.nn.sigmoid(gate) * up).astype(low)
    hidden_ref[...] = value
    for part in range(parts):
        partial_ref[:, part * columns : (part + 1) * columns] = dot(
            value, weight_ref[part, 2 * hidden :]
        ).astype(low)


def hidden_back_kernel(
    dtwo_ref,
    rows_ref,
    weight_ref,
    gate_ref,
    up_ref,
    hidden_ref,
    partial_ref,
    parts_ref,
    down_parts_ref,
):
    parts, hidden, columns = down_parts_ref.shape
    low = jnp.bfloat16
    dhidden = jnp.zeros(gate_ref.shape, jnp.float32)
    for part in range(parts):
        piece = dtwo_ref[:, part * columns : (part + 1) * columns]
        dhidden = dhidden + dot(piece, weight_ref[part, 2 * hidden :], 1, 1)
        down_parts_ref[part] = dot(hidden_ref[...], piece, 0, 0).astype(low)
    gate, up = gate_ref[...], up_ref[...]
    sigma = jax.nn.sigmoid(gate)
    dgate = (dhidden * up * sigma * (1.0 + gate * (1.0 - sigma))).astype(low)
    dup = (dhidden * gate * sigma).astype(low)
    for part in range(parts):
        lanes = slice(part * columns, (part + 1) * columns)
        partial_ref[:, lanes] = (
            dot(dgate, weight_ref[part, :hidden]) + dot(dup, weight_ref[part, hidden : 2 * hidden])
        ).astype(low)
        parts_ref[part, :hidden] = dot(dgate, rows_ref[:, lanes], 0, 0).astype(low)
        parts_ref[part, hidden : 2 * hidden] = dot(dup, rows_ref[:, lanes], 0, 0).astype(low)


def embed_kernel(base_ref, ids_ref, table_ref, partial_ref, low_ref, hits_ref):
    @pl.when(pl.program_id(0) == 0)
    def _():
        entries = base_ref[0] + lax.broadcasted_iota(jnp.int32, (1, table_ref.shape[0]), 1)
        hits_ref[...] = jnp.where(ids_ref[...] == entries, 1.0, 0.0).astype(hits_ref.dtype)

    table_low = table_ref[...].astype(low_ref.dtype)
    low_ref[...] = table_low
    partial_ref[...] = dot(hits_ref[...], table_low).astype(partial_ref.dtype)


def embed(base, ids, table):
    (entries, width), tokens, low = table.shape, ids.shape[0], jnp.bfloat16
    columns = 256
    by_columns = lambda rows: pl.BlockSpec((rows, columns), lambda b, e: (0, b))
    return pl.pallas_call(
        embed_kernel,
        out_shape=[
            jax.ShapeDtypeStruct((tokens, width), low),
            jax.ShapeDtypeStruct((entries, width), low),
        ],
        grid_spec=pltpu.PrefetchScalarGridSpec(
            num_scalar_prefetch=1,
            grid=(width // columns,),
            in_specs=[whole_spec(ids), by_columns(entries)],
            out_specs=[by_columns(tokens), by_columns(entries)],
            scratch_shapes=[pltpu.VMEM((tokens, entries), low)],
        ),
        **local_params(60),
    )(base, ids, table)


def logits_kernel(one_ref, two_ref, table_ref, target_ref, entry_ref, logits_ref, stats_ref):
    slots, step, lanes = one_ref.shape[0], 256, stats_ref.shape[1]
    for e, rows_ref in enumerate((one_ref, two_ref)):
        for start in range(0, slots, step):
            values = dot(rows_ref[start : start + step], table_ref[...], 1, 1)
            logits_ref[e * slots + start : e * slots + start + step] = values
            top = jnp.max(values, axis=1, keepdims=True)
            mass = jnp.sum(jnp.exp(values - top), axis=1, keepdims=True)
            for part in range(0, step, lanes):
                row = (e * slots + start + part) // lanes
                at = slice(part, part + lanes)
                hit = to_column(target_ref[row : row + 1]) == entry_ref[...]
                found = jnp.sum(jnp.where(hit, values[at], 0.0), axis=1, keepdims=True)
                for stat, column in enumerate((top[at], mass[at], found)):
                    index = stat * (2 * slots // lanes) + row
                    stats_ref[index : index + 1] = to_row(column)


def head_grad_kernel(
    logits_ref, lse_ref, weight_ref, target_ref, entry_ref, table_ref, one_ref, two_ref, *terms
):
    slots, lanes, step = one_ref.shape[0], lse_ref.shape[1], 256
    low = jnp.bfloat16
    for e, grad_ref in enumerate((one_ref, two_ref)):
        for start in range(0, slots, lanes):
            row = (e * slots + start) // lanes
            lse, weight, target = (
                to_column(ref[row : row + 1]) for ref in (lse_ref, weight_ref, target_ref)
            )
            values = logits_ref[row * lanes : (row + 1) * lanes]
            hit = jnp.where(target == entry_ref[...], 1.0, 0.0)
            grad_ref[start : start + lanes] = (weight * (jnp.exp(values - lse) - hit)).astype(low)
        for start in range(0, slots, step):
            at = slice(start, start + step)
            terms[e][at] = dot(grad_ref[at], table_ref[...]).astype(low)


def table_grad_kernel(
    base_ref, ids_ref, one_ref, two_ref, rows_one, rows_two, dzero_ref, grad_ref, square_ref, left_ref
):
    slots = one_ref.shape[0]

    @pl.when(pl.program_id(0) == 0)
    def _():
        entries = base_ref[0] + lax.broadcasted_iota(jnp.int32, (left_ref.shape[0], 1), 0)
        left_ref[:, :slots] = one_ref[...].T
        left_ref[:, slots : 2 * slots] = two_ref[...].T
        hits = jnp.where(ids_ref[...] == entries, 1.0, 0.0)
        left_ref[:, 2 * slots :] = hits.astype(left_ref.dtype)

    grad = (
        dot(left_ref[:, :slots], rows_one[...])
        + dot(left_ref[:, slots : 2 * slots], rows_two[...])
        + dot(left_ref[:, 2 * slots :], dzero_ref[...])
    )
    grad_ref[...] = grad
    square_ref[...] = square_row(grad)


def table_gradient(base, ids, grads, rows, dzero):
    slots, entries = grads[0].shape
    tokens, width = dzero.shape
    columns = 256
    by_columns = lambda count: pl.BlockSpec((count, columns), lambda b, e: (0, b))
    return pl.pallas_call(
        table_grad_kernel,
        out_shape=[
            jax.ShapeDtypeStruct((entries, width), jnp.float32),
            jax.ShapeDtypeStruct((1, width), jnp.float32),
        ],
        grid_spec=pltpu.PrefetchScalarGridSpec(
            num_scalar_prefetch=1,
            grid=(width // columns,),
            in_specs=[whole_spec(ids), whole_spec(grads[0]), whole_spec(grads[1])]
            + [by_columns(slots), by_columns(slots), by_columns(tokens)],
            out_specs=[by_columns(entries), by_columns(1)],
            scratch_shapes=[pltpu.VMEM((entries, 2 * slots + tokens), dzero.dtype)],
        ),
        **local_params(60),
    )(base, ids, *grads, *rows, dzero)


def norm_fwd(values, gain):
    row_scale = lax.rsqrt(jnp.mean(values * values, axis=-1, keepdims=True) + EPS_NORM)
    unit_rows = values * row_scale
    return (unit_rows * gain, unit_rows, row_scale)


def norm_back(unit_rows, row_scale, gain, gradient):
    weighted = gradient * gain
    back_rows = row_scale * (
        weighted - unit_rows * jnp.mean(weighted * unit_rows, axis=-1, keepdims=True)
    )
    return (back_rows, jnp.sum(gradient * unit_rows, axis=0))


def rotary(places, width):
    half_width = width // 2
    frequency = jnp.exp(
        jnp.arange(half_width, dtype=jnp.float32) * (-math.log(10000.0) / half_width)
    )
    angles = places.astype(jnp.float32)[:, None] * frequency[None, :]
    return (jnp.cos(angles), jnp.sin(angles))


def rotate_pairs(values, cosine, sine_table):
    half_width = values.shape[-1] // 2
    front_half = values[..., :half_width]
    back_half = values[..., half_width:]
    return jnp.concatenate(
        [
            front_half * cosine - back_half * sine_table,
            back_half * cosine + front_half * sine_table,
        ],
        axis=-1,
    )


def dot(left, right, left_dim=1, right_dim=0):
    return lax.dot_general(
        left, right, (((left_dim,), (right_dim,)), ((), ())), preferred_element_type=jnp.float32
    )


def adam_update(weight, moment_one, moment_two, gradient, rate, decay):
    moment_one = BETA_ONE * moment_one + (1.0 - BETA_ONE) * gradient
    moment_two = BETA_TWO * moment_two + (1.0 - BETA_TWO) * gradient * gradient
    ratio = (
        moment_one
        / (1.0 - BETA_ONE**STEP)
        / (jnp.sqrt(moment_two / (1.0 - BETA_TWO**STEP)) + ADAM_EPS)
    )
    return (weight - rate * (ratio + decay * weight), moment_one, moment_two)


def small_sum_kernel(x_ref, o_ref, held, plane, column, send_sem, recv_sem):
    data_index, model_index = lax.axis_index("dp"), lax.axis_index("mp")
    z, y = data_index // 2, data_index % 2
    x, c = model_index // 2, model_index % 2
    core = (data_index, x * 2 + 1 - c)
    corners = [
        (data_index, (1 - x) * 2 + c),
        (z * 2 + 1 - y, model_index),
        (z * 2 + 1 - y, (1 - x) * 2 + c),
    ]
    zs = (z + 1 - 2 * (z % 2), (z + 2) % 4, 3 - z)
    greet([core] + corners + [(zd * 2 + y, model_index) for zd in zs])
    sent = []

    def send(source, target, device):
        index = len(sent)
        copy = pltpu.make_async_remote_copy(
            src_ref=source,
            dst_ref=target,
            send_sem=send_sem.at[index],
            recv_sem=recv_sem.at[index],
            device_id=device,
            device_id_type=MESH,
        )
        copy.start()
        sent.append(copy)
        return copy

    held[0] = x_ref[...]
    send(held.at[0], held.at[1], core).wait_recv()
    mine = y * 2 + x
    plane[mine] = held[0] + held[1]
    for copy in [send(plane.at[mine], plane.at[mine], device) for device in corners]:
        copy.wait_recv()
    column[z] = (plane[0] + plane[1]) + (plane[2] + plane[3])
    for copy in [send(column.at[z], column.at[z], (zd * 2 + y, model_index)) for zd in zs]:
        copy.wait_recv()
    o_ref[...] = (column[0] + column[1]) + (column[2] + column[3])
    for copy in sent:
        copy.wait_send()


def sum_small(value, ident):
    if not kernel_mesh():
        return lax.psum(value, BOTH)
    vmem = pl.BlockSpec(memory_space=pltpu.VMEM)
    return pl.pallas_call(
        small_sum_kernel,
        out_shape=jax.ShapeDtypeStruct(value.shape, value.dtype),
        in_specs=[vmem],
        out_specs=vmem,
        scratch_shapes=[
            pltpu.VMEM((2,) + value.shape, value.dtype),
            pltpu.VMEM((4,) + value.shape, value.dtype),
            pltpu.VMEM((4,) + value.shape, value.dtype),
            pltpu.SemaphoreType.DMA((7,)),
            pltpu.SemaphoreType.DMA((7,)),
        ],
        compiler_params=comm_params(ident, 2),
    )(value)


def body(
    token_ids,
    target_ids,
    exit_mask,
    table,
    table_first,
    table_second,
    qkv_weight,
    qkv_first,
    qkv_second,
    out_weight,
    out_first,
    out_second,
    gate_up_weight,
    gate_up_first,
    gate_up_second,
    down_weight,
    down_first,
    down_second,
    gains,
    gains_first,
    gains_second,
):
    low = jnp.bfloat16
    data_size, model_size = lax.axis_size("dp"), lax.axis_size("mp")
    data_index, model_index = lax.axis_index("dp"), lax.axis_index("mp")
    devices = data_size * model_size
    block_rows = token_ids.shape[0]
    tokens = block_rows * data_size
    width = table.shape[1]
    width_here = qkv_weight.shape[0]
    heads_here = qkv_weight.shape[2] // HEAD_DIM
    hidden_here = down_weight.shape[0] // data_size
    vocab_here = table.shape[0]
    device_index = data_index * model_size + model_index
    vocab_ids = device_index * vocab_here + jnp.arange(vocab_here, dtype=jnp.int32)
    score_scale = 1.0 / math.sqrt(HEAD_DIM)

    sharers = data_size // heads_here
    shares = sharers // 2
    share_slots = data_size // shares * R_DEV
    exit_here = data_index % sharers % 2
    share_here = data_index % sharers // 2
    slots_here = R_DEV // model_size
    rows_here = block_rows // model_size

    ints, gain_low = exchange(
        [
            jnp.concatenate([token_ids[None], target_ids[None], exit_mask]),
            jnp.pad(gains.astype(low), ((0, 13), (0, 0))),
        ],
        (True, True),
        0,
    )
    gain_rows = jnp.moveaxis(gain_low[:, :3], 0, 1).reshape(3, width).astype(jnp.float32)
    all_ids = ints[:, 0].reshape(tokens)
    token_places = jnp.arange(tokens, dtype=jnp.int32)
    packed = kernel_mesh()
    slot_shape = (2 * data_size * R_DEV // 128, 128)
    if packed:
        pick_low, place_rows, target_rows, live_rows, weight_rows = local(
            slots_kernel,
            16,
            [
                ((2, data_size, R_DEV, block_rows), low),
                (slot_shape, jnp.int32),
                (slot_shape, jnp.int32),
                (slot_shape, jnp.float32),
                (slot_shape, jnp.float32),
            ],
            ints,
        )
    else:
        mask_blocks = jnp.moveaxis(ints[:, 2:], 0, 1)
        slot_ids = jnp.arange(R_DEV, dtype=jnp.int32)
        slot_ranks = jnp.cumsum(mask_blocks, axis=2) - 1
        pick_int = (
            (slot_ranks[:, :, None, :] == slot_ids[:, None]) & (mask_blocks[:, :, None, :] == 1)
        ).astype(jnp.int32)
        pick_low = pick_int.astype(low)
        target_rows = jnp.sum(pick_int * ints[:, 1][None, :, None, :], axis=3).reshape(slot_shape)
        place_rows = jnp.sum(
            pick_int * token_places.reshape(1, data_size, 1, block_rows), axis=3
        ).reshape(slot_shape)
        live_rows = (slot_ids < jnp.sum(mask_blocks, axis=2)[:, :, None]).astype(jnp.float32)
        live_rows = live_rows.reshape(slot_shape)
        scales = jnp.array(EXIT_SCALE, jnp.float32) / jnp.sum(live_rows.reshape(2, -1), axis=1)
        weight_rows = live_rows * jnp.repeat(scales, slot_shape[0] // 2)[:, None]
    slot_targets, live = target_rows.reshape(2, -1), live_rows.reshape(2, -1)
    row_weight = weight_rows.reshape(2, -1)
    counts = jnp.sum(live, axis=1)

    head_shape = (data_size, 4 * HEAD_DIM, width_here)
    hidden_shape = (data_size, 2 * hidden_here, width_here)
    down_shape = (data_size, hidden_here, width_here)
    if packed:
        (head_rows,) = local(
            pack_head_kernel,
            10,
            [(head_shape, low)],
            jnp.transpose(qkv_weight, (1, 0, 2)),
            out_weight,
        )
    else:
        head_rows = jnp.moveaxis(
            qkv_weight.astype(low).reshape(width_here, 3, heads_here, HEAD_DIM), 0, 3
        )
        head_rows = jnp.concatenate(
            [
                jnp.moveaxis(head_rows, 0, 1).reshape(heads_here, 3 * HEAD_DIM, width_here),
                out_weight.astype(low).reshape(heads_here, HEAD_DIM, width_here),
            ],
            axis=1,
        )
        head_rows = jnp.repeat(head_rows, sharers, axis=0)
    head_rows = swap_blocks(after(head_rows, ints))

    base = (device_index * vocab_here)[None]
    if packed:
        id_rows, table_low = embed(base, all_ids[:, None], table)
    else:
        table_low = table.astype(low)
        id_hits = (all_ids[:, None] == vocab_ids[None, :]).astype(low)
        id_rows = dot(id_hits, table_low).astype(low)
    if packed:
        (hidden_rows,) = local(
            pack_hidden_kernel,
            16,
            [((data_size, 3 * hidden_here, width_here), low)],
            gate_up_weight,
            down_weight,
            scratch=[pltpu.VMEM((gate_up_weight.shape[2], width_here), jnp.float32)],
        )
    else:
        hidden_rows = jnp.moveaxis(
            gate_up_weight.astype(low).reshape(width_here, 2, data_size, hidden_here), 0, 3
        )
        hidden_rows = jnp.concatenate(
            [
                jnp.moveaxis(hidden_rows, 0, 1).reshape(hidden_shape),
                down_weight.astype(low).reshape(down_shape),
            ],
            axis=1,
        )
    (resid_low,) = relay([after(id_rows, hidden_rows)], lambda p, total, extras: (total.astype(low), (), ()), 1)

    hidden_rows, resid_low = lax.optimization_barrier((hidden_rows, resid_low))
    hidden_rows = swap_blocks(hidden_rows)

    pick_share = lax.dynamic_slice_in_dim(
        lax.dynamic_index_in_dim(pick_low, exit_here, 0, keepdims=False),
        share_here * (data_size // shares),
        data_size // shares,
        0,
    )
    def share_of(rows):
        count = share_slots // 128
        return lax.dynamic_slice_in_dim(rows, (exit_here * shares + share_here) * count, count, 0)

    place_share, live_rows_share = share_of(place_rows), share_of(live_rows)
    if packed:

        def turns(places):
            return jnp.stack([jnp.concatenate([part, part], axis=1) for part in rotary(places, HEAD_DIM)])

        attn_low, query_slots, key_low, value_low, attn_out, turn, slot_turn, out_partial = attend(
            exit_here[None],
            resid_low,
            gain_rows[:1],
            head_rows,
            turns(token_places[:block_rows]),
            turns(token_places[::block_rows]),
            pick_share,
            place_share,
            live_rows_share,
            slots_here,
        )
        out_partial = out_partial.reshape(-1, width)
    else:
        head_rows = jnp.moveaxis(head_rows, 0, 1).reshape(4 * HEAD_DIM, width)
        qkv_head, out_head = head_rows[: 3 * HEAD_DIM], head_rows[3 * HEAD_DIM :]
        cosine, sine_table = rotary(token_places, HEAD_DIM)
        places_share, live_share = place_share.reshape(-1), live_rows_share.reshape(-1)
        cosine_share, sine_share = rotary(places_share, HEAD_DIM)
        attn_low = norm_fwd(resid_low.astype(jnp.float32), gain_rows[0])[0].astype(low)

        projected = dot(attn_low, qkv_head, 1, 1)
        query_low = rotate_pairs(projected[:, :HEAD_DIM], cosine, sine_table).astype(low)
        key_low = rotate_pairs(projected[:, HEAD_DIM : 2 * HEAD_DIM], cosine, sine_table).astype(low)
        value_low = projected[:, 2 * HEAD_DIM :].astype(low)
        query_share = lax.dynamic_slice_in_dim(
            query_low.reshape(data_size, block_rows, HEAD_DIM),
            share_here * (data_size // shares),
            data_size // shares,
            0,
        )
        query_slots = (
            jnp.einsum("brt,btd->brd", pick_share, query_share, preferred_element_type=jnp.float32)
            .astype(low)
            .reshape(share_slots, HEAD_DIM)
        )

        scores = dot(query_slots, key_low, 1, 1) * score_scale
        allowed = token_places[None, :] <= places_share[:, None]
        scores = jnp.where(allowed, scores, NEG)
        weights = jnp.exp(scores - jnp.max(scores, axis=-1, keepdims=True))
        probs = weights / jnp.sum(weights, axis=-1, keepdims=True)
        probs_low = probs.astype(low)
        attn_out = (dot(probs_low, value_low) * live_share[:, None]).astype(low)

        def spread(per_share):
            if shares > 1:
                full = jnp.zeros((data_size * R_DEV, width), per_share.dtype)
                per_share = lax.dynamic_update_slice_in_dim(
                    full, per_share, share_here * share_slots, 0
                )
            exits = jnp.arange(2, dtype=jnp.int32)[None, :, None, None]
            rows = per_share.reshape(devices, 1, slots_here, width)
            return jnp.where(exits == exit_here, rows, 0).reshape(-1, width)
        out_partial = spread(dot(attn_out, out_head).astype(low))

    block_low = lax.dynamic_slice_in_dim(resid_low, data_index * block_rows, block_rows, 0)
    pick_here = lax.dynamic_slice(
        pick_low,
        (0, data_index, model_index * slots_here, 0),
        (2, 1, slots_here, block_rows),
    ).reshape(2 * slots_here, block_rows)

    def first_step(p, total, extras):
        resid = extras[0][p * GROUP : (p + 1) * GROUP] + total
        gain = 2 if p == 0 else 1
        return (norm_fwd(resid, extras[1][gain : gain + 1])[0].astype(low), (resid,), ())

    exit_rows_one, mlp_low, resid_one = relay(
        [out_partial],
        first_step,
        2,
        extras=[dot(pick_here, block_low), gain_rows],
        kept=1,
        split=True,
    )

    slots = mlp_low.shape[0]
    if packed:
        gate_part, up_part, hidden_low, mlp_partial = local(
            hidden_kernel,
            20,
            [
                ((slots, hidden_here), jnp.float32),
                ((slots, hidden_here), jnp.float32),
                ((slots, hidden_here), low),
                ((slots, width), low),
            ],
            mlp_low,
            hidden_rows,
        )
    else:
        hidden_rows = jnp.moveaxis(hidden_rows, 0, 1).reshape(3 * hidden_here, width)
        gate_up_head, down_head = hidden_rows[: 2 * hidden_here], hidden_rows[2 * hidden_here :]
        gate_up = dot(mlp_low, gate_up_head, 1, 1)
        gate_part, up_part = gate_up[:, :hidden_here], gate_up[:, hidden_here:]
        gate_sigma = jax.nn.sigmoid(gate_part)
        hidden_low = (gate_part * gate_sigma * up_part).astype(low)
        mlp_partial = dot(hidden_low, down_head).astype(low)

    def second_step(p, total, extras):
        resid = extras[0][GROUP : 2 * GROUP] + total
        return (norm_fwd(resid, extras[1][2:3])[0].astype(low), (resid,), ())

    exit_rows_two, resid_two = relay(
        [mlp_partial], second_step, 3, extras=[resid_one, gain_rows], kept=1
    )

    exit_rows = (exit_rows_one, exit_rows_two)
    if packed:
        entry_row = vocab_ids[None]
        logits, stats = local(
            logits_kernel,
            28,
            [((2 * slots, vocab_here), jnp.float32), ((3 * 2 * slots // 128, 128), jnp.float32)],
            *exit_rows,
            table_low,
            target_rows,
            entry_row,
        )
    else:
        logits = [dot(rows, table_low, 1, 1) for rows in exit_rows]
        hits = [slot_targets[e][:, None] == vocab_ids[None, :] for e in range(2)]
        tops = [jnp.max(values, axis=1) for values in logits]
        masses = [
            jnp.sum(jnp.exp(values - top[:, None]), axis=1) for values, top in zip(logits, tops)
        ]
        found = [jnp.sum(jnp.where(hit, values, 0.0), axis=1) for hit, values in zip(hits, logits)]
        stats = jnp.concatenate(tops + masses + found).reshape(-1, 128)
    part = stats.shape[0] // 3

    def joined(stats):
        tops, masses, found = (stats[:, k * part : (k + 1) * part] for k in range(3))
        top = jnp.max(tops, axis=0)
        lse = top + jnp.log(jnp.sum(masses * jnp.exp(tops - top), axis=0))
        return jnp.concatenate([lse, lse - jnp.sum(found, axis=0)])

    joint = gather_small(stats, joined, (2 * part, 128), 4)
    row_lse, entropy = joint[:part].reshape(2, -1), joint[part:].reshape(2, -1)
    loss_sums = jnp.sum(entropy * live, axis=1)
    if packed:
        *grad_logits, one_terms, two_terms = local(
            head_grad_kernel,
            28,
            [((slots, vocab_here), low)] * 2 + [((slots, width), low)] * 2,
            logits,
            joint[:part],
            weight_rows,
            target_rows,
            entry_row,
            table_low,
        )
        row_terms = [one_terms, two_terms]
    else:
        grad_logits = [
            (
                row_weight[e][:, None]
                * (jnp.exp(logits[e] - row_lse[e][:, None]) - hits[e].astype(jnp.float32))
            ).astype(low)
            for e in range(2)
        ]
        row_terms = [dot(grad, table_low).astype(low) for grad in grad_logits]

    def head_step(p, total, extras):
        values = extras[0][:GROUP] if p == 0 else extras[1][...]
        gain = extras[2][2:3]
        _, unit, scale = norm_fwd(values, gain)
        back, gain_grad = norm_back(unit, scale, gain, total)
        return (None if p == 0 else back.astype(low), (back,), (gain_grad[None],))

    dtwo_low, dexits, final_grad = relay(
        row_terms,
        head_step,
        5,
        extras=[resid_one, resid_two, gain_rows],
        kept=1,
        sums=1,
        order=[1, 0],
        slot=lambda p: None if p == 0 else 0,
    )
    if packed:
        dmlp_partial, hidden_parts, down_parts = local(
            hidden_back_kernel,
            28,
            [((slots, width), low), (hidden_shape, low), (down_shape, low)],
            dtwo_low,
            mlp_low,
            hidden_rows,
            gate_part,
            up_part,
            hidden_low,
        )
    else:
        down_local = dot(hidden_low, dtwo_low, 0, 0)
        dhidden = dot(dtwo_low, down_head, 1, 1)
        dgate = dhidden * up_part * gate_sigma * (1.0 + gate_part * (1.0 - gate_sigma))
        dup_part = dhidden * gate_part * gate_sigma
        dgate_up = jnp.concatenate([dgate, dup_part], axis=1).astype(low)
        gate_up_local = dot(dgate_up, mlp_low, 0, 0)
        dmlp_partial = dot(dgate_up, gate_up_head).astype(low)
        hidden_parts, down_parts = (
            jnp.moveaxis(value.astype(low).reshape(-1, data_size, width_here), 1, 0)
            for value in (gate_up_local, down_local)
        )

    def mlp_step(p, total, extras):
        gain = extras[2][1:2]
        _, unit, scale = norm_fwd(extras[0][GROUP : 2 * GROUP], gain)
        back, gain_grad = norm_back(unit, scale, gain, total)
        return ((extras[1][GROUP : 2 * GROUP] + back).astype(low), (), (gain_grad[None],))

    done_low, mlp_grad, down_parts = relay(
        [dmlp_partial],
        mlp_step,
        6,
        extras=[resid_one, dexits, gain_rows],
        sums=1,
        slot=lambda p: 1,
        ready=dexits[:GROUP].astype(low),
        cargo=down_parts,
    )
    hidden_parts, done_low = lax.optimization_barrier((hidden_parts, done_low))
    hidden_parts = swap_blocks(hidden_parts)
    done_low = done_low.reshape(devices, 2, slots_here, width)

    if kernel_mesh():
        zero_partial, head_parts = attend_back(
            exit_here[None],
            done_low,
            head_rows,
            attn_out,
            query_slots,
            key_low,
            value_low,
            turn,
            slot_turn,
            pick_share,
            place_share,
            attn_low,
        )
    else:
        done_share = lax.dynamic_slice(
            lax.dynamic_index_in_dim(done_low, exit_here, 1, keepdims=False).reshape(-1, width),
            (share_here * share_slots, 0),
            (share_slots, width),
        )
        out_local = dot(attn_out, done_share, 0, 0)
        dattn_low = dot(done_share, out_head, 1, 1).astype(low)
        dprobs = dot(dattn_low, value_low, 1, 1)
        delta = jnp.sum(probs * dprobs, axis=-1, keepdims=True)
        dscores = (probs * (dprobs - delta)).astype(low)
        dquery = rotate_pairs(dot(dscores, key_low) * score_scale, cosine_share, -sine_share).astype(
            low
        )
        dquery_share = jnp.einsum(
            "brt,brd->btd",
            pick_share,
            dquery.reshape(-1, R_DEV, HEAD_DIM),
            preferred_element_type=jnp.float32,
        ).astype(low)
        if shares > 1:
            dquery_share = lax.dynamic_update_slice_in_dim(
                jnp.zeros((data_size, block_rows, HEAD_DIM), low),
                dquery_share,
                share_here * (data_size // shares),
                0,
            )
        dkey = rotate_pairs(dot(dscores, query_slots, 0, 0) * score_scale, cosine, -sine_table)
        dvalue = dot(probs_low, dattn_low, 0, 0)
        dprojected = jnp.concatenate(
            [dquery_share.reshape(tokens, HEAD_DIM), dkey.astype(low), dvalue.astype(low)], axis=1
        )
        head_parts = jnp.concatenate([dot(dprojected, attn_low, 0, 0).astype(low), out_local.astype(low)])
        zero_partial = dot(dprojected, qkv_head).astype(low)
        head_parts = jnp.moveaxis(head_parts.reshape(-1, data_size, width_here), 1, 0)

    resid_here = lax.dynamic_slice_in_dim(resid_low, device_index * rows_here, rows_here, 0)
    done_block = lax.dynamic_slice_in_dim(done_low, data_index * model_size, model_size, 0)
    pick_block = lax.dynamic_slice(
        pick_low,
        (0, data_index, 0, model_index * rows_here),
        (2, 1, R_DEV, rows_here),
    ).reshape(2, model_size, slots_here, rows_here)
    dresid_here = jnp.einsum(
        "emst,mesd->td", pick_block, done_block, preferred_element_type=jnp.float32
    )

    def zero_step(p, total, extras):
        at = slice(p * GROUP, (p + 1) * GROUP)
        gain = extras[2][:1]
        _, unit, scale = norm_fwd(extras[0][at], gain)
        back, gain_grad = norm_back(unit, scale, gain, total)
        return ((extras[1][at] + back).astype(low), (), (gain_grad[None],))

    ride = 2 * HEAD_DIM
    dzero_low, attn_grad, ridden = relay(
        [after(zero_partial, hidden_parts)],
        zero_step,
        7,
        extras=[resid_here.astype(jnp.float32), dresid_here, gain_rows],
        sums=1,
        cargo=head_parts[:, :ride],
    )
    later, dzero_low = lax.optimization_barrier((head_parts[:, ride:], dzero_low))
    later = swap_blocks(later)
    if packed:
        table_grad, squares = table_gradient(
            base, all_ids[None, :], grad_logits, exit_rows, dzero_low
        )
        squares = jnp.sum(squares)
    else:
        table_grad = dot(id_hits, dzero_low, 0, 0)
        for grad, rows in zip(grad_logits, exit_rows):
            table_grad = table_grad + dot(grad, rows, 0, 0)
        squares = jnp.sum(table_grad * table_grad)

    square_shape = ((1, width_here), jnp.float32)
    if packed:
        qkv_grad, out_grad, head_squares = local(
            unpack_head_kernel,
            12,
            [
                ((3, width_here, qkv_weight.shape[2]), jnp.float32),
                (out_weight.shape, jnp.float32),
                square_shape,
            ],
            ridden,
            later,
        )
        gate_up_grad, down_grad, hidden_squares = local(
            unpack_hidden_kernel,
            20,
            [
                (gate_up_weight.shape, jnp.float32),
                (down_weight.shape, jnp.float32),
                square_shape,
            ],
            hidden_parts,
            down_parts,
            scratch=[pltpu.VMEM((gate_up_weight.shape[2], width_here), jnp.float32)],
        )
        qkv_grad = jnp.transpose(qkv_grad, (1, 0, 2))
        squares = squares + jnp.sum(head_squares) + jnp.sum(hidden_squares)
    else:
        head_grad = jnp.sum(
            jnp.concatenate([ridden, later], axis=1).reshape(heads_here, sharers, 4, HEAD_DIM, width_here).astype(jnp.float32),
            axis=1,
        )
        qkv_grad = jnp.transpose(head_grad[:, :3], (3, 1, 0, 2)).reshape(qkv_weight.shape)
        out_grad = head_grad[:, 3].reshape(out_weight.shape)
        hidden_parts = hidden_parts.astype(jnp.float32)
        gate_up_grad = hidden_parts.reshape(data_size, 2, hidden_here, width_here)
        gate_up_grad = jnp.transpose(gate_up_grad, (3, 1, 0, 2)).reshape(gate_up_weight.shape)
        down_grad = down_parts.reshape(down_weight.shape).astype(jnp.float32)
        squares = (
            squares
            + jnp.sum(qkv_grad * qkv_grad)
            + jnp.sum(out_grad * out_grad)
            + jnp.sum(gate_up_grad * gate_up_grad)
            + jnp.sum(down_grad * down_grad)
        )
    parts = jnp.concatenate(
        [
            jnp.concatenate([attn_grad, mlp_grad, final_grad]).reshape(-1, 128),
            jnp.full((8, 128), squares),
        ]
    )
    parts = sum_small(parts, 8)
    gain_sums = parts[:-8].reshape(3, width)
    gain_grad = lax.dynamic_slice_in_dim(gain_sums, data_index * width_here, width_here, 1)
    grad_norm = jnp.sqrt(parts[-1, 0] + jnp.sum(gain_sums * gain_sums))
    factor = jnp.minimum(1.0, CLIP / (grad_norm + 1e-06))
    table_new, qkv_new, out_new, gate_up_new, down_new = (
        adam_update(weight, first, second, grad * factor, RATE_MATRIX, DECAY)
        for weight, first, second, grad in (
            (table, table_first, table_second, table_grad),
            (qkv_weight, qkv_first, qkv_second, qkv_grad),
            (out_weight, out_first, out_second, out_grad),
            (gate_up_weight, gate_up_first, gate_up_second, gate_up_grad),
            (down_weight, down_first, down_second, down_grad),
        )
    )
    gains_new = adam_update(gains, gains_first, gains_second, gain_grad * factor, RATE_GAIN, 0.0)
    return (
        loss_sums,
        counts,
        grad_norm,
        *table_new,
        *qkv_new,
        *out_new,
        *gate_up_new,
        *down_new,
        *gains_new,
    )


def solution(mesh):
    rows, sides, cols, gain = P(BOTH, None), P("dp", None, "mp"), P("mp", "dp"), P(None, "dp")
    state = (rows,) * 3 + (sides,) * 3 + (cols,) * 3 + (sides,) * 3 + (cols,) * 3 + (gain,) * 3
    return jax.shard_map(
        body,
        mesh=mesh,
        in_specs=(P("dp"), P("dp"), P(None, "dp")) + state,
        out_specs=(P(), P(), P()) + state,
        check_vma=False,
    )
```
